32 devices in a mesh: pipe: 2 (over core), dp: 4 (over z), tensor: 4 (over y, x).
Axes of the slice: x: 2, y: 2, z: 4, core: 2. Of those that a mesh axis runs over, the one named last changes fastest.
Arguments:
- tokens: bfloat16 [2, 4, 256, 768], P(None, 'dp', 'tensor'), may hold values from -6 to 6
- conditions: bfloat16 [2, 4, 768], P(None, 'dp', 'tensor'), may hold values from -6 to 6
- cotangent: bfloat16 [2, 4, 256, 768], P(None, 'dp', 'tensor'), may hold values from -6 to 6
- modulation_weight: bfloat16 [2, 768, 4608], P('pipe', 'tensor', 'dp'), may hold values from -0.21875 to 0.21875
- modulation_bias: float32 [2, 4608], P('pipe'), may hold values from -3 to 3
- joint_weight: bfloat16 [2, 768, 3, 768], P('pipe', 'dp', None, 'tensor'), may hold values from -0.21875 to 0.21875
- joint_bias: float32 [2, 2, 768], P('pipe', None, 'tensor'), may hold values from -3 to 3
- output_weight: bfloat16 [2, 768, 768], P('pipe', 'tensor', 'dp'), may hold values from -0.875 to 0.875
- output_bias: float32 [2, 768], P('pipe'), may hold values from -3 to 3
- expand_weight: bfloat16 [2, 768, 3072], P('pipe', 'dp', 'tensor'), may hold values from -0.21875 to 0.21875
- expand_bias: float32 [2, 3072], P('pipe', 'tensor'), may hold values from -3 to 3
- shrink_weight: bfloat16 [2, 3072, 768], P('pipe', 'tensor', 'dp'), may hold values from -0.109375 to 0.109375
- shrink_bias: float32 [2, 768], P('pipe'), may hold values from -3 to 3
Outputs:
- layer_outputs: bfloat16 [2, 2, 4, 256, 768], P('pipe', None, 'dp', 'tensor')
- input_grads: bfloat16 [2, 2, 4, 256, 768], P('pipe', None, 'dp', 'tensor')
- condition_grads: float32 [2, 2, 4, 768], P('pipe', None, 'dp', 'tensor')
- modulation_weight_grad: float32 [2, 768, 4608], P('pipe', 'tensor', 'dp')
- modulation_bias_grad: float32 [2, 4608], P('pipe')
- joint_weight_grad: float32 [2, 768, 3, 768], P('pipe', 'dp', None, 'tensor')
- joint_bias_grad: float32 [2, 2, 768], P('pipe', None, 'tensor')
- output_weight_grad: float32 [2, 768, 768], P('pipe', 'tensor', 'dp')
- output_bias_grad: float32 [2, 768], P('pipe')
- expand_weight_grad: float32 [2, 768, 3072], P('pipe', 'dp', 'tensor')
- expand_bias_grad: float32 [2, 3072], P('pipe', 'tensor')
- shrink_weight_grad: float32 [2, 3072, 768], P('pipe', 'tensor', 'dp')
- shrink_bias_grad: float32 [2, 768], P('pipe')
The draws below stay inside these ranges and needn't reach their ends.
All inputs are finite; a program needn't handle non-finite values.
Results may differ from the reference program's by a relative error of at most 0.025.
Values may be sent and summed in bfloat16 or wider, within the bound.
No kernel may reach another device: no remote copies, remote signals or barrier semaphores. Data moves between devices by JAX's collectives and lax.ppermute only.
A program may use at most 128 MiB of HBM per device.

```python
import math
import jax
import jax.numpy as jnp
from jax import lax

D = 768
HEAD = 64
FF = 3072
SEQ = 256
MICRO = 2
LATENTS = 4
SECTIONS = 2


def shard_levels(own_key, extent, split, smallest, top_value):
    def one(position, blocks):
        steps = jax.random.uniform(jax.random.fold_in(jax.random.fold_in(own_key, 6), position), (blocks,), jnp.float32, smallest / len(split), top_value / len(split))
        return jnp.repeat(jnp.exp(steps), extent[position] // blocks).reshape((-1,) + (1,) * (len(extent) - position - 1))

    factor_of = one(*split[0])
    for cut in split[1:]:
        factor_of = factor_of * one(*cut)
    return factor_of


def normal_values(rng, shape, width, reach, pieces=(), held_as=jnp.bfloat16):
    result = jax.random.normal(rng, shape, jnp.float32) * width
    if len(pieces) > 0:
        result = shard_levels(rng, shape, pieces, -0.22, 0.18) * result
    return jnp.clip(result, min=-reach, max=reach).astype(held_as)


def setup_inputs(seed: int = 0) -> dict:
    arg_keys = jax.random.split(jax.random.key(seed), 14)
    return {
        "tokens": normal_values(arg_keys[0], (MICRO, LATENTS, SEQ, D), 1.0, 6.0, ((1, 4), (2, 4))),
        "conditions": normal_values(arg_keys[1], (MICRO, LATENTS, D), 1.0, 6.0, ((1, 4), (2, 4))),
        "cotangent": normal_values(arg_keys[2], (MICRO, LATENTS, SEQ, D), 1.0, 6.0, ((1, 4), (2, 4))),
        "modulation_weight": normal_values(arg_keys[3], (SECTIONS, D, 6 * D), D ** -0.5, 0.21875, ((0, 2), (1, 4), (2, 4))),
        "modulation_bias": normal_values(arg_keys[4], (SECTIONS, 6 * D), 0.5, 3.0, ((0, 2),), jnp.float32),
        "joint_weight": normal_values(arg_keys[5], (SECTIONS, D, 3, D), D ** -0.5, 0.21875, ((0, 2), (1, 4), (3, 4))),
        "joint_bias": normal_values(arg_keys[6], (SECTIONS, 2, D), 0.5, 3.0, ((0, 2), (2, 4)), jnp.float32),
        "output_weight": normal_values(arg_keys[7], (SECTIONS, D, D), (D // 16) ** -0.5, 0.875, ((0, 2), (1, 4), (2, 4))),
        "output_bias": normal_values(arg_keys[8], (SECTIONS, D), 0.5, 3.0, ((0, 2),), jnp.float32),
        "expand_weight": normal_values(arg_keys[9], (SECTIONS, D, FF), D ** -0.5, 0.21875, ((0, 2), (1, 4), (2, 4))),
        "expand_bias": normal_values(arg_keys[10], (SECTIONS, FF), 0.5, 3.0, ((0, 2), (1, 4)), jnp.float32),
        "shrink_weight": normal_values(arg_keys[11], (SECTIONS, FF, D), FF ** -0.5, 0.109375, ((0, 2), (1, 4), (2, 4))),
        "shrink_bias": normal_values(arg_keys[12], (SECTIONS, D), 0.5, 3.0, ((0, 2),), jnp.float32),
    }


@jax.custom_vjp
def low(v):
    return lax.optimization_barrier(v.astype(jnp.bfloat16)).astype(jnp.float32)

@jax.custom_vjp
def low_back(v):
    return v

def low_keep(v):
    return (low(v), None)

def low_pass(kept, grad):
    return (grad,)

def back_keep(v):
    return (v, None)

def back_low(kept, grad):
    return (low(grad),)
low.defvjp(low_keep, low_pass)
low_back.defvjp(back_keep, back_low)

def round_both(values):
    return low(low_back(values))

def layer_norm(values):
    centre = lax.optimization_barrier(jnp.mean(values, axis=-1, keepdims=True))
    centred = values - centre
    spread = lax.optimization_barrier(jnp.mean(centred * centred, axis=-1, keepdims=True))
    return centred * lax.rsqrt(spread + 1e-06)

def product(left, right):
    return jnp.matmul(left, right, precision=lax.Precision.HIGHEST)

def diffusion_transformer_layer(layer_input, condition_input, adaptive_norm_weight, adaptive_norm_bias, combined_weight, combined_bias, final_output_weight, final_output_bias, widen_weight, widen_bias, narrow_weight, narrow_bias):
    group_size = layer_input.shape[0]
    seq_len = layer_input.shape[1]
    model_width = layer_input.shape[2]
    activated = low(jax.nn.silu(condition_input))
    modulation = low_back(product(activated, adaptive_norm_weight) + adaptive_norm_bias)
    mod_parts = [modulation[:, None, part_index * model_width:(part_index + 1) * model_width] for part_index in range(6)]
    shift_attn, scale_attn, gate_attn, shift_mlp, scale_mlp, gate_mlp = mod_parts
    attn_in = low(layer_norm(layer_input) * (1.0 + scale_attn) + shift_attn)
    joint_out = jnp.einsum('gsd,dce->gsce', attn_in, combined_weight, precision=lax.Precision.HIGHEST)
    head_shape = (group_size, seq_len, model_width // HEAD, HEAD)
    query_block = round_both(joint_out[:, :, 0] + combined_bias[0]).reshape(head_shape)
    key_block = round_both(joint_out[:, :, 1]).reshape(head_shape)
    value_block = round_both(joint_out[:, :, 2] + combined_bias[1]).reshape(head_shape)
    scores = low_back(jnp.einsum('gqhe,gkhe->ghqk', query_block, key_block, precision=lax.Precision.HIGHEST) * HEAD ** (-0.5))
    row_max = lax.optimization_barrier(jnp.max(scores, axis=-1, keepdims=True))
    weights_exp = jnp.exp(scores - row_max)
    attn_probs = weights_exp / lax.optimization_barrier(jnp.sum(weights_exp, axis=-1, keepdims=True))
    mixed_heads = round_both(jnp.einsum('ghqk,gkhe->gqhe', low(attn_probs), value_block, precision=lax.Precision.HIGHEST))
    mixed_heads = mixed_heads.reshape(group_size, seq_len, model_width)
    attended = low_back(product(mixed_heads, final_output_weight) + final_output_bias)
    middle = layer_input + gate_attn * attended
    mlp_in = low(layer_norm(middle) * (1.0 + scale_mlp) + shift_mlp)
    pre_act = low_back(product(mlp_in, widen_weight) + widen_bias)
    hidden = low(jax.nn.gelu(pre_act, approximate=True))
    shrunk = low_back(product(hidden, narrow_weight) + narrow_bias)
    return middle + gate_mlp * shrunk

def network(params, layer_input, condition_first_layer, condition_second_layer, offset):
    first_layer_parameters = tuple((member[0] for member in params))
    second_layer_parameters = tuple((member[1] for member in params))
    first_layer_output = diffusion_transformer_layer(layer_input, condition_first_layer, *first_layer_parameters)
    passed = low(first_layer_output)
    second_layer_input = low_back(passed) + offset
    second_layer_output = diffusion_transformer_layer(second_layer_input, condition_second_layer, *second_layer_parameters)
    return (passed, second_layer_output)

def reference(tokens, conditions, cotangent, modulation_weight, modulation_bias, joint_weight, joint_bias, output_weight, output_bias, expand_weight, expand_bias, shrink_weight, shrink_bias):
    total_latents = MICRO * LATENTS
    group_size = math.gcd(total_latents, 16)
    group_count = total_latents // group_size
    token_groups = tokens.astype(jnp.float32).reshape(group_count, group_size, SEQ, D)
    cond_groups = conditions.astype(jnp.float32).reshape(group_count, group_size, D)
    cot_groups = cotangent.astype(jnp.float32).reshape(group_count, group_size, SEQ, D)
    params = tuple((member.astype(jnp.float32) for member in (modulation_weight, modulation_bias, joint_weight, joint_bias, output_weight, output_bias, expand_weight, expand_bias, shrink_weight, shrink_bias)))

    def one_group(totals, group_in):
        layer_input, condition_input, cot_in = group_in
        offset = jnp.zeros_like(layer_input)
        outputs, pullback = jax.vjp(network, params, layer_input, condition_input, condition_input, offset)
        grads = pullback((jnp.zeros_like(outputs[0]), cot_in))
        totals = jax.tree.map(jnp.add, totals, grads[0])
        return (totals, (outputs[0], outputs[1], grads[1], grads[4], grads[2], grads[3]))
    start_totals = jax.tree.map(jnp.zeros_like, params)
    totals, per_group = lax.scan(one_group, start_totals, (token_groups, cond_groups, cot_groups))
    first_layer_output, second_layer_output, first_grad, second_grad, condition_first_layer, condition_second_layer = per_group
    act_shape = (MICRO, LATENTS, SEQ, D)
    layer_outputs = jnp.stack([first_layer_output.reshape(act_shape), second_layer_output.reshape(act_shape)]).astype(jnp.bfloat16)
    input_grads = jnp.stack([first_grad.reshape(act_shape), second_grad.reshape(act_shape)]).astype(jnp.bfloat16)
    condition_grads = jnp.stack([condition_first_layer.reshape(MICRO, LATENTS, D), condition_second_layer.reshape(MICRO, LATENTS, D)])
    return (layer_outputs, input_grads, condition_grads, totals[0], totals[1], totals[2], totals[3], totals[4], totals[5], totals[6], totals[7], totals[8], totals[9])
```

```python
import jax
import jax.numpy as jnp
from jax import lax
from jax.sharding import PartitionSpec as P

HEAD = 64
EPS = 1e-06
F32 = jnp.float32
BF16 = jnp.bfloat16
LINE_LIMIT = 8


def swap(value, axis, mask):
    pairs = [(source, source ^ mask) for source in range(lax.axis_size(axis))]
    return lax.ppermute(value, axis, pairs)


def exchange(parts, axis):
    return [parts[0]] + [swap(parts[k], axis, k) for k in range(1, len(parts))]


def gather(value, axis):
    return exchange([value] * lax.axis_size(axis), axis)


def tree_sum(parts):
    parts = list(parts)
    while len(parts) > 1:
        parts = [parts[k] + parts[k + 1] for k in range(0, len(parts), 2)]
    return parts[0]


def gather_rows(value):
    return jnp.concatenate(gather(value, "tensor"), axis=0)


def scatter_rows(partial, own):
    blocks = partial.reshape(-1, own, partial.shape[-1])
    received = exchange([blocks[k] for k in range(blocks.shape[0])], "tensor")
    return tree_sum([block.astype(F32) for block in received])


def flip_blocks(values, index, count):
    lead = values.shape[:-1]
    blocks = values.reshape(lead + (count, values.shape[-1] // count))
    bit = 1
    while bit < count:
        paired = blocks.reshape(lead + (count // (2 * bit), 2, bit, blocks.shape[-1]))
        flipped = paired[..., ::-1, :, :].reshape(blocks.shape)
        blocks = jnp.where((index & bit) != 0, flipped, blocks)
        bit *= 2
    return blocks.reshape(values.shape)


def dot(left, right):
    return jnp.dot(left, right, preferred_element_type=F32)


def dot_t(left, right):
    return lax.dot_general(left, right, (((1,), (1,)), ((), ())), preferred_element_type=F32)


def t_dot(left, right):
    return lax.dot_general(left, right, (((0,), (0,)), ((), ())), preferred_element_type=F32)


def normalize(values):
    centred = values - jnp.mean(values, axis=-1, keepdims=True)
    rstd = lax.rsqrt(jnp.mean(centred * centred, axis=-1, keepdims=True) + EPS)
    return centred * rstd, rstd


def normalize_back(grad, normed, rstd):
    return rstd * (
        grad
        - jnp.mean(grad, axis=-1, keepdims=True)
        - normed * jnp.mean(grad * normed, axis=-1, keepdims=True)
    )


def tanh_gelu(values):
    return jax.nn.gelu(values, approximate=True)


def layer_forward(h, parts, weights, biases):
    w_joint, w_out, w_expand, w_shrink = weights
    joint_bias, out_bias, expand_bias, shrink_bias = biases
    shift_attn, scale_attn, gate_attn, shift_mlp, scale_mlp, gate_mlp = parts
    own = h.shape[0]
    width = w_out.shape[0]
    normed, _ = normalize(h)
    attn_rows = gather_rows((normed * (1.0 + scale_attn) + shift_attn).astype(BF16))
    joint = dot(attn_rows, w_joint)
    heads = (attn_rows.shape[0], width // HEAD, HEAD)
    query = (joint[:, :width] + joint_bias[0]).astype(BF16).reshape(heads)
    key = joint[:, width : 2 * width].astype(BF16).reshape(heads)
    value = (joint[:, 2 * width :] + joint_bias[1]).astype(BF16).reshape(heads)
    scores = jnp.einsum("qhe,khe->hqk", query, key, preferred_element_type=F32) * HEAD**-0.5
    powers = jnp.exp(scores - jnp.max(scores, axis=-1, keepdims=True))
    probs = powers / jnp.sum(powers, axis=-1, keepdims=True)
    mixed = jnp.einsum("hqk,khe->qhe", probs.astype(BF16), value, preferred_element_type=F32)
    mixed = mixed.astype(BF16).reshape(attn_rows.shape[0], width)
    attended = scatter_rows(dot(mixed, w_out).astype(BF16), own) + out_bias
    middle = h + gate_attn * attended
    normed, _ = normalize(middle)
    mlp_rows = gather_rows((normed * (1.0 + scale_mlp) + shift_mlp).astype(BF16))
    pre = dot(mlp_rows, w_expand) + expand_bias
    hidden = tanh_gelu(pre).astype(BF16)
    shrunk = scatter_rows(dot(hidden, w_shrink).astype(BF16), own) + shrink_bias
    kept = (h, attn_rows, query, key, value, probs, mixed, attended, middle, mlp_rows, pre, hidden, shrunk)
    return middle + gate_mlp * shrunk, kept


def layer_backward(g_y, kept, parts, weights):
    w_joint, w_out, w_expand, w_shrink = weights
    h, attn_rows, query, key, value, probs, mixed, attended, middle, mlp_rows, pre, hidden, shrunk = kept
    shift_attn, scale_attn, gate_attn, shift_mlp, scale_mlp, gate_mlp = parts
    own = h.shape[0]
    rows = attn_rows.shape[0]
    width = w_out.shape[0]
    g_gate_mlp = jnp.sum(g_y * shrunk, axis=0)
    g_shrunk = (gate_mlp * g_y).astype(BF16)
    shrink_bias_grad = jnp.sum(g_shrunk.astype(F32), axis=0)
    shrunk_rows = gather_rows(g_shrunk)
    _, gelu_back = jax.vjp(tanh_gelu, pre)
    g_pre = gelu_back(dot_t(shrunk_rows, w_shrink))[0].astype(BF16)
    expand_bias_grad = jnp.sum(g_pre.astype(F32), axis=0)
    g_mlp_in = scatter_rows(dot_t(g_pre, w_expand).astype(BF16), own)
    w_shrink_grad = t_dot(hidden, shrunk_rows)
    w_expand_grad = t_dot(mlp_rows, g_pre)
    normed, rstd = normalize(middle)
    g_shift_mlp = jnp.sum(g_mlp_in, axis=0)
    g_scale_mlp = jnp.sum(g_mlp_in * normed, axis=0)
    g_middle = g_y + normalize_back(g_mlp_in * (1.0 + scale_mlp), normed, rstd)
    g_gate_attn = jnp.sum(g_middle * attended, axis=0)
    g_attended = (gate_attn * g_middle).astype(BF16)
    out_bias_grad = jnp.sum(g_attended.astype(F32), axis=0)
    attended_rows = gather_rows(g_attended)
    g_mixed = dot_t(attended_rows, w_out).astype(BF16)
    g_heads = g_mixed.reshape(query.shape)
    g_probs = jnp.einsum("qhe,khe->hqk", g_heads, value, preferred_element_type=F32)
    row_dot = jnp.sum(probs * g_probs, axis=-1, keepdims=True)
    g_scores = (probs * (g_probs - row_dot)).astype(BF16)
    g_value = jnp.einsum("hqk,qhe->khe", probs.astype(BF16), g_heads, preferred_element_type=F32)
    g_query = jnp.einsum("hqk,khe->qhe", g_scores, key, preferred_element_type=F32) * HEAD**-0.5
    g_key = jnp.einsum("hqk,qhe->khe", g_scores, query, preferred_element_type=F32) * HEAD**-0.5
    g_joint = jnp.concatenate(
        [part.astype(BF16).reshape(rows, width) for part in (g_query, g_key, g_value)], axis=1
    )
    g_attn_in = scatter_rows(dot_t(g_joint, w_joint).astype(BF16), own)
    joint_sum = jnp.sum(g_joint.astype(F32), axis=0)
    joint_bias_grad = jnp.concatenate([joint_sum[:width], joint_sum[2 * width :]])
    w_out_grad = t_dot(mixed, attended_rows)
    w_joint_grad = t_dot(attn_rows, g_joint)
    normed, rstd = normalize(h)
    g_shift_attn = jnp.sum(g_attn_in, axis=0)
    g_scale_attn = jnp.sum(g_attn_in * normed, axis=0)
    g_h = g_middle + normalize_back(g_attn_in * (1.0 + scale_attn), normed, rstd)
    part_grads = (g_shift_attn, g_scale_attn, g_gate_attn, g_shift_mlp, g_scale_mlp, g_gate_mlp)
    weight_grads = (w_joint_grad, w_out_grad, w_expand_grad, w_shrink_grad)
    bias_grads = (joint_bias_grad, out_bias_grad, expand_bias_grad, shrink_bias_grad)
    return g_h, part_grads, weight_grads, bias_grads


def on_device(
    tokens,
    conditions,
    cotangent,
    modulation_weight,
    modulation_bias,
    joint_weight,
    joint_bias,
    output_weight,
    output_bias,
    expand_weight,
    expand_bias,
    shrink_weight,
    shrink_bias,
):
    core = lax.axis_index("pipe")
    first = core == 0
    line = lax.axis_index("dp")
    line_size = lax.axis_size("dp")
    direct = line_size <= LINE_LIMIT
    micro, _, own, model = tokens.shape
    head_width = output_weight.shape[1]
    hidden_width = expand_weight.shape[2]
    half_hidden = hidden_width // 2
    chunk = model // line_size
    half_chunk = head_width // 2
    ordinal = lambda values: flip_blocks(values, line, line_size) if direct else values

    def mine(pair):
        return jnp.where(first, pair[0], pair[1])

    def other(pair):
        return jnp.where(first, pair[1], pair[0])

    def both_layers(value):
        received = swap(value, "pipe", 1)
        return jnp.where(first, value, received), jnp.where(first, received, value)

    def halves_of_layers(halves):
        keep, give = mine(halves), other(halves)
        received = swap(give, "pipe", 1)
        return jnp.where(first, keep, received), jnp.where(first, received, keep)

    def along_line(value):
        if direct:
            return jnp.stack(gather(value, "dp"))
        return lax.all_gather(value, "dp", axis=0)

    def sum_along_line(blocks):
        blocks = blocks.astype(BF16)
        if direct:
            received = exchange([blocks[k] for k in range(line_size)], "dp")
            return tree_sum([block.astype(F32) for block in received])
        return lax.psum_scatter(blocks, "dp", scatter_dimension=0, tiled=False).astype(F32)

    activated = jax.nn.silu(conditions[:, 0].astype(F32)).astype(BF16)
    activated_all = (
        jnp.stack(gather(activated, "dp")) if direct else lax.all_gather(activated, "dp", axis=0)
    )
    own_rows = modulation_weight[0]
    flat_activated = activated_all.reshape(line_size * micro, -1)
    mod_partial = dot(flat_activated, own_rows)
    mod_sum = tree_sum(gather(mod_partial, "tensor"))
    mod_sum = mod_sum.reshape(line_size, micro, -1)
    mod_columns = mod_sum.shape[-1]
    if direct:
        pieces = jnp.stack(exchange([mod_sum[k] for k in range(line_size)], "dp"), axis=1)
        pieces = pieces.reshape(micro, -1)
        mod_layer = flip_blocks(pieces, line, line_size)
    else:
        mod_layer = lax.all_to_all(mod_sum, "dp", split_axis=0, concat_axis=0)
        mod_layer = jnp.swapaxes(mod_layer, 0, 1).reshape(micro, -1)
    mod_layer = mod_layer + modulation_bias[0]
    mod_received = swap(other(mod_layer), "pipe", 1)
    mod_own = mine(mod_layer)
    mod_layers = (jnp.where(first, mod_own, mod_received), jnp.where(first, mod_received, mod_own))
    parts = [
        [ordinal(part) for part in mod.reshape(6, model)] for mod in mod_layers
    ]

    attn_pack = jnp.concatenate(
        [joint_weight[0].reshape(chunk, -1), output_weight[0].reshape(chunk, -1)], axis=1
    )
    halves_attn = halves_of_layers(
        (attn_pack[: chunk // 2], attn_pack[chunk // 2 :])
    )
    halves_expand = halves_of_layers(
        (expand_weight[0][:, :half_hidden], expand_weight[0][:, half_hidden:])
    )
    halves_shrink = halves_of_layers(
        (shrink_weight[0][:half_hidden], shrink_weight[0][half_hidden:])
    )
    bias_pack = jnp.concatenate(
        [joint_bias[0].reshape(-1), output_bias[0], expand_bias[0], shrink_bias[0]]
    )
    bias_layers = both_layers(bias_pack)

    def order_halves(own_half, other_half, axis):
        return jnp.where(
            first,
            jnp.concatenate([own_half, other_half], axis=axis),
            jnp.concatenate([other_half, own_half], axis=axis),
        )

    def roll_hidden(values):
        return jnp.where(
            first, values, jnp.concatenate([values[half_hidden:], values[:half_hidden]])
        )

    joint_cols = 3 * head_width

    def attn_weights(half):
        lined = along_line(half)
        whole = order_halves(lined, swap(lined, "pipe", 1), 1)
        w_joint = whole[:, :, :joint_cols].reshape(model, joint_cols)
        w_out = whole[:, :, joint_cols:].reshape(line_size, head_width, chunk)
        w_out = jnp.swapaxes(w_out, 0, 1).reshape(head_width, model)
        return w_joint, w_out

    def expand_whole(half):
        lined = along_line(half)
        return jnp.concatenate([lined, swap(lined, "pipe", 1)], axis=2).reshape(model, hidden_width)

    def shrink_whole(half):
        lined = along_line(half)
        both = jnp.stack([lined, swap(lined, "pipe", 1)])
        return jnp.transpose(both, (0, 2, 1, 3)).reshape(hidden_width, model)

    def after(value, earlier):
        return lax.optimization_barrier((value, earlier))

    weights = []
    previous = None
    for layer in range(2):
        half_attn, half_expand, half_shrink = halves_attn[layer], halves_expand[layer], halves_shrink[layer]
        if previous is not None:
            half_attn, _ = after(half_attn, previous)
        w_joint, w_out = attn_weights(half_attn)
        half_expand, w_joint = after(half_expand, w_joint)
        w_expand = expand_whole(half_expand)
        half_shrink, w_expand = after(half_shrink, w_expand)
        w_shrink = shrink_whole(half_shrink)
        previous = w_shrink
        weights.append((w_joint, w_out, w_expand, w_shrink))
    biases = []
    for packed in bias_layers:
        split = 2 * head_width
        biases.append(
            (
                packed[:split].reshape(2, head_width),
                ordinal(packed[split : split + model]),
                roll_hidden(packed[split + model : split + model + hidden_width]),
                ordinal(packed[split + model + hidden_width :]),
            )
        )

    h = ordinal(mine(tokens[:, 0])).astype(F32)
    g_y = ordinal(mine(cotangent[:, 0])).astype(F32)
    y, kept_first = layer_forward(h, parts[0], weights[0], biases[0])
    passed = y.astype(BF16)
    y, kept_second = layer_forward(passed.astype(F32), parts[1], weights[1], biases[1])
    outputs = (passed, y.astype(BF16))

    def reduced(weight_grads):
        w_joint_grad, w_out_grad, w_expand_grad, w_shrink_grad = weight_grads
        blocks = jnp.swapaxes(w_out_grad.reshape(head_width, line_size, chunk), 0, 1)
        attn = jnp.concatenate(
            [
                w_joint_grad.reshape(line_size, chunk, joint_cols),
                blocks.reshape(line_size, chunk, head_width),
            ],
            axis=2,
        )
        attn_halves = (attn[:, : chunk // 2], attn[:, chunk // 2 :])
        attn_own = mine(attn_halves) + swap(other(attn_halves).astype(BF16), "pipe", 1).astype(F32)
        expand = w_expand_grad.reshape(line_size, chunk, hidden_width)
        expand_own = expand[:, :, :half_hidden] + swap(
            expand[:, :, half_hidden:].astype(BF16), "pipe", 1
        ).astype(F32)
        shrink = jnp.swapaxes(w_shrink_grad.reshape(hidden_width, line_size, chunk), 0, 1)
        shrink_own = shrink[:, :half_hidden] + swap(
            shrink[:, half_hidden:].astype(BF16), "pipe", 1
        ).astype(F32)
        return sum_along_line(attn_own), sum_along_line(expand_own), sum_along_line(shrink_own)

    g_h, part_grads_second, weight_grads, bias_grads_second = layer_backward(
        g_y, kept_second, parts[1], weights[1]
    )
    reduced_second = reduced(weight_grads)
    g_passed = g_h.astype(BF16)
    g_h, part_grads_first, weight_grads, bias_grads_first = layer_backward(
        g_passed.astype(F32), kept_first, parts[0], weights[0]
    )
    reduced_first = reduced(weight_grads)
    grads_in = (g_h.astype(BF16), g_passed)

    def own_layer(pair):
        received = swap(other(pair), "pipe", 1)
        return mine(pair), received

    attn_grad = order_halves(*own_layer((reduced_first[0], reduced_second[0])), 0)
    expand_grad = order_halves(*own_layer((reduced_first[1], reduced_second[1])), 1)
    shrink_grad = order_halves(*own_layer((reduced_first[2], reduced_second[2])), 0)
    joint_grad = attn_grad[:, :joint_cols].reshape(joint_weight[0].shape)
    output_grad = attn_grad[:, joint_cols:].reshape(output_weight[0].shape)

    def own_layer_of_micros(pair):
        mine_now, received = own_layer(pair)
        return jnp.stack([jnp.where(first, mine_now, received), jnp.where(first, received, mine_now)])

    layer_outputs = own_layer_of_micros(tuple(ordinal(value) for value in outputs))
    input_grads = own_layer_of_micros(tuple(ordinal(value) for value in grads_in))

    part_packs = tuple(
        jnp.concatenate([ordinal(part) for part in grads])
        for grads in (part_grads_first, part_grads_second)
    )
    mod_grad_layers = jnp.stack(part_packs)
    mod_grad_sum = tree_sum(gather(mod_grad_layers, "tensor")).astype(BF16)
    mod_grad = own_layer_of_micros((mod_grad_sum[0], mod_grad_sum[1]))
    mod_grad_all = (
        jnp.stack(gather(mod_grad, "dp")) if direct else lax.all_gather(mod_grad, "dp", axis=0)
    ).reshape(line_size * micro, -1)
    by_line = mod_grad_all.reshape(line_size, micro, -1).astype(F32)
    ada_bias_grad = tree_sum([jnp.sum(by_line[k], axis=0) for k in range(line_size)])
    mod_grad_own = lax.dynamic_slice_in_dim(mod_grad_all, line * mod_columns, mod_columns, 1)
    ada_grad = t_dot(flat_activated, mod_grad_own)
    act_partial = dot_t(mod_grad_own, own_rows).reshape(line_size, micro, -1)
    if direct:
        act_grad = tree_sum(
            exchange([act_partial[k] for k in range(line_size)], "dp")
        )
    else:
        act_grad = lax.psum_scatter(act_partial, "dp", scatter_dimension=0, tiled=False)
    _, silu_back = jax.vjp(jax.nn.silu, conditions[:, 0].astype(F32))
    cond_grad = silu_back(act_grad)[0]

    def pack_biases(grads):
        joint_bias_grad, out_bias_grad, expand_bias_grad, shrink_bias_grad = grads
        return (
            jnp.concatenate([joint_bias_grad, roll_hidden(expand_bias_grad)]),
            jnp.concatenate([ordinal(out_bias_grad), ordinal(shrink_bias_grad)]),
        )

    packs_first, packs_second = pack_biases(bias_grads_first), pack_biases(bias_grads_second)
    token_sums = jnp.stack([packs_first[1], packs_second[1]])
    token_sums = tree_sum(gather(token_sums, "tensor"))
    bias_first = jnp.concatenate([packs_first[0], token_sums[0]])
    bias_second = jnp.concatenate([packs_second[0], token_sums[1]])
    bias_own = tree_sum(own_layer((bias_first, bias_second)))
    bias_sum = (
        tree_sum(gather(bias_own, "dp")) if direct else lax.psum(bias_own, "dp")
    )
    split = 2 * head_width
    joint_bias_grad = bias_sum[:split].reshape(2, head_width)
    expand_bias_grad = bias_sum[split : split + hidden_width]
    out_bias_grad = bias_sum[split + hidden_width : split + hidden_width + model]
    shrink_bias_grad = bias_sum[split + hidden_width + model :]
    return (
        layer_outputs[None, :, None],
        input_grads[None, :, None],
        cond_grad[None, :, None],
        ada_grad[None],
        ada_bias_grad[None],
        joint_grad[None],
        joint_bias_grad[None],
        output_grad[None],
        out_bias_grad[None],
        expand_grad[None],
        expand_bias_grad[None],
        shrink_grad[None],
        shrink_bias_grad[None],
    )


def solution(mesh):
    in_specs = (
        P(None, "dp", "tensor", None),
        P(None, "dp", "tensor"),
        P(None, "dp", "tensor", None),
        P("pipe", "tensor", "dp"),
        P("pipe", None),
        P("pipe", "dp", None, "tensor"),
        P("pipe", None, "tensor"),
        P("pipe", "tensor", "dp"),
        P("pipe", None),
        P("pipe", "dp", "tensor"),
        P("pipe", "tensor"),
        P("pipe", "tensor", "dp"),
        P("pipe", None),
    )
    out_specs = (
        P("pipe", None, "dp", "tensor", None),
        P("pipe", None, "dp", "tensor", None),
        P("pipe", None, "dp", "tensor"),
        P("pipe", "tensor", "dp"),
        P("pipe", None),
        P("pipe", "dp", None, "tensor"),
        P("pipe", None, "tensor"),
        P("pipe", "tensor", "dp"),
        P("pipe", None),
        P("pipe", "dp", "tensor"),
        P("pipe", "tensor"),
        P("pipe", "tensor", "dp"),
        P("pipe", None),
    )
    return jax.shard_map(
        on_device, mesh=mesh, in_specs=in_specs, out_specs=out_specs, check_vma=False
    )
```

```python
import functools

import jax
import jax.numpy as jnp
from jax import lax
from jax.experimental import pallas as pl
from jax.experimental.pallas import tpu as pltpu
from jax.sharding import PartitionSpec as P

HEAD = 64
EPS = 1e-06
F32 = jnp.float32
BF16 = jnp.bfloat16
LINE = 4
VMEM_BYTES = 24 * 1024 * 1024
GELU_A = 0.7978845608028654
GELU_B = 0.044715


def swap(value, axis, mask):
    pairs = [(source, source ^ mask) for source in range(lax.axis_size(axis))]
    return lax.ppermute(value, axis, pairs)


def exchange(parts, axis):
    return [parts[0]] + [swap(parts[k], axis, k) for k in range(1, len(parts))]


def gather(value, axis):
    return exchange([value] * lax.axis_size(axis), axis)


def tree_sum(parts):
    parts = list(parts)
    while len(parts) > 1:
        parts = [parts[k] + parts[k + 1] for k in range(0, len(parts), 2)]
    return parts[0]


def shape(dims, dtype):
    return jax.ShapeDtypeStruct(dims, dtype)


def run(name, body, outs, args, place=None):
    specs = [pl.BlockSpec(memory_space=pltpu.VMEM) for _ in args]
    if place is not None:
        specs = [pl.BlockSpec(memory_space=pltpu.SMEM)] + specs
        args = [place] + list(args)
    return pl.pallas_call(
        body,
        out_shape=outs,
        in_specs=specs,
        out_specs=[pl.BlockSpec(memory_space=pltpu.VMEM) for _ in outs],
        compiler_params=pltpu.CompilerParams(vmem_limit_bytes=VMEM_BYTES),
        name=name,
    )(*args)


def dot(left, right):
    return jnp.dot(left, right, preferred_element_type=F32)


def dot_t(left, right):
    return lax.dot_general(left, right, (((1,), (1,)), ((), ())), preferred_element_type=F32)


def t_dot(left, right):
    return lax.dot_general(left, right, (((0,), (0,)), ((), ())), preferred_element_type=F32)


def normalize(values):
    centred = values - jnp.mean(values, axis=-1, keepdims=True)
    rstd = lax.rsqrt(jnp.mean(centred * centred, axis=-1, keepdims=True) + EPS)
    return centred * rstd, rstd


def normalize_back(grad, normed, rstd):
    return rstd * (
        grad
        - jnp.mean(grad, axis=-1, keepdims=True)
        - normed * jnp.mean(grad * normed, axis=-1, keepdims=True)
    )


def total(refs):
    return tree_sum([ref[...].astype(F32) for ref in refs])


def column_sum(values):
    return jnp.sum(values, axis=0, keepdims=True)


def part(mod_ref, index):
    width = mod_ref.shape[1] // 6
    return mod_ref[:, index * width : (index + 1) * width]


def gelu(pre):
    return 0.5 * pre * (1.0 + jnp.tanh(GELU_A * (pre + GELU_B * (pre * pre * pre))))


def gelu_slope(pre):
    square = pre * pre
    bent = jnp.tanh(GELU_A * (pre + GELU_B * (square * pre)))
    return 0.5 * (1.0 + bent) + 0.5 * pre * (1.0 - bent * bent) * (
        GELU_A * (1.0 + 3.0 * GELU_B * square)
    )


def put_rows(ref, refs):
    own = refs[0].shape[0]
    for k, source in enumerate(refs):
        ref[k * own : (k + 1) * own] = source[...]
    return ref[...]


def put_blocks(refs, values):
    own = refs[0].shape[0]
    for k, ref in enumerate(refs):
        ref[...] = values[k * own : (k + 1) * own].astype(ref.dtype)


def enter_body(place, tokens, cotangent, mod0, mod1, h_out, attn_in, g_y_out, g_shrunk):
    core = place[0]
    h = tokens[core].astype(F32)
    h_out[...] = h
    normed, _ = normalize(h)
    attn_in[...] = (normed * (1.0 + part(mod0, 1)) + part(mod0, 0)).astype(BF16)
    g_y = cotangent[core].astype(F32)
    g_y_out[...] = g_y
    g_shrunk[...] = (part(mod1, 5) * g_y).astype(BF16)


def pick_attn(place, own, received):
    first = place[0] == 0
    width = own.shape[1] // 2
    mine, other = own[...], received[...]
    front = jnp.where(first, mine, other)
    back = jnp.where(first, other, mine)
    return front, back[:, :width], back[:, width:]


def attn_body(count, place, *refs):
    chunks = refs[:count]
    w_own, w_received, bias = refs[count : count + 3]
    rows_out, qkv_out, probs_out, mixed_out = refs[count + 3 : count + 7]
    partial = refs[count + 7 :]
    rows = put_rows(rows_out, chunks)
    w_front, w_value, w_out = pick_attn(place, w_own, w_received)
    width = w_value.shape[1]
    front = (dot(rows, w_front) + bias[:, : 2 * width]).astype(BF16)
    value = (dot(rows, w_value) + bias[:, 2 * width :]).astype(BF16)
    qkv_out[:, : 2 * width] = front
    qkv_out[:, 2 * width :] = value
    mixed = []
    for head in range(width // HEAD):
        at = head * HEAD
        query = front[:, at : at + HEAD]
        key = front[:, width + at : width + at + HEAD]
        scores = dot_t(query, key) * HEAD**-0.5
        powers = jnp.exp(scores - jnp.max(scores, axis=-1, keepdims=True))
        probs = powers / jnp.sum(powers, axis=-1, keepdims=True)
        probs_out[head] = probs
        mixed.append(dot(probs.astype(BF16), value[:, at : at + HEAD]))
    mixed = jnp.concatenate(mixed, axis=1).astype(BF16)
    mixed_out[...] = mixed
    put_blocks(partial, dot_t(mixed, w_out))


def middle_body(count, *refs):
    parts, (bias, h, mod, attended_out, middle_out, mlp_in) = refs[:count], refs[count:]
    attended = total(parts) + bias[...]
    attended_out[...] = attended
    middle = h[...] + part(mod, 2) * attended
    middle_out[...] = middle
    normed, _ = normalize(middle)
    mlp_in[...] = (normed * (1.0 + part(mod, 4)) + part(mod, 3)).astype(BF16)


def mlp_body(count, *refs):
    chunks = refs[:count]
    w_own, w_received, bias, rows_out, pre_out, hidden_out = refs[count : count + 6]
    partial = refs[count + 6 :]
    rows = put_rows(rows_out, chunks)
    half = w_own.shape[1] // 2
    shrunk = None
    for index, weight in enumerate((w_own, w_received)):
        at = index * half
        pre = dot(rows, weight[:, :half]) + bias[:, at : at + half]
        pre_out[:, at : at + half] = pre
        hidden = gelu(pre).astype(BF16)
        hidden_out[:, at : at + half] = hidden
        term = dot_t(hidden, weight[:, half:])
        shrunk = term if shrunk is None else shrunk + term
    put_blocks(partial, shrunk)


def mlp_both_body(count, *refs):
    chunks, g_chunks = refs[:count], refs[count : 2 * count]
    w_own, w_received, bias, rows_out, g_rows_out, hidden_out, g_pre_out, bias_grad = refs[
        2 * count : 2 * count + 8
    ]
    partial = refs[2 * count + 8 : 3 * count + 8]
    g_partial = refs[3 * count + 8 :]
    rows = put_rows(rows_out, chunks)
    g_rows = put_rows(g_rows_out, g_chunks)
    half = w_own.shape[1] // 2
    shrunk, g_in = None, None
    for index, weight in enumerate((w_own, w_received)):
        at = index * half
        pre = dot(rows, weight[:, :half]) + bias[:, at : at + half]
        hidden = gelu(pre).astype(BF16)
        hidden_out[:, at : at + half] = hidden
        g_pre = (dot(g_rows, weight[:, half:]) * gelu_slope(pre)).astype(BF16)
        g_pre_out[:, at : at + half] = g_pre
        bias_grad[:, at : at + half] = column_sum(g_pre.astype(F32))
        term = dot_t(hidden, weight[:, half:])
        g_term = dot_t(g_pre, weight[:, :half])
        shrunk = term if shrunk is None else shrunk + term
        g_in = g_term if g_in is None else g_in + g_term
    put_blocks(g_partial, g_in)
    put_blocks(partial, shrunk)


def mlp_back_body(count, *refs):
    g_chunks = refs[:count]
    w_own, w_received, pre_ref, g_rows_out, g_pre_out, bias_grad = refs[count : count + 6]
    g_partial = refs[count + 6 :]
    g_rows = put_rows(g_rows_out, g_chunks)
    half = w_own.shape[1] // 2
    g_in = None
    for index, weight in enumerate((w_own, w_received)):
        at = index * half
        pre = pre_ref[:, at : at + half]
        g_pre = (dot(g_rows, weight[:, half:]) * gelu_slope(pre)).astype(BF16)
        g_pre_out[:, at : at + half] = g_pre
        bias_grad[:, at : at + half] = column_sum(g_pre.astype(F32))
        g_term = dot_t(g_pre, weight[:, :half])
        g_in = g_term if g_in is None else g_in + g_term
    put_blocks(g_partial, g_in)


def between_body(count, *refs):
    parts = refs[:count]
    bias, middle, mod0, mod1, shrunk_out, passed_out, h_out, attn_in = refs[count:]
    shrunk = total(parts) + bias[...]
    shrunk_out[...] = shrunk
    passed = (middle[...] + part(mod0, 5) * shrunk).astype(BF16)
    passed_out[...] = passed
    h = passed.astype(F32)
    h_out[...] = h
    normed, _ = normalize(h)
    attn_in[...] = (normed * (1.0 + part(mod1, 1)) + part(mod1, 0)).astype(BF16)


def leave_body(count, *refs):
    parts = refs[:count]
    bias, middle, mod, g_y_ref, g_shrunk, y_out, g_gate, bias_grad = refs[count:]
    shrunk = total(parts) + bias[...]
    y_out[...] = (middle[...] + part(mod, 5) * shrunk).astype(BF16)
    g_gate[...] = column_sum(g_y_ref[...] * shrunk)
    bias_grad[...] = column_sum(g_shrunk[...].astype(F32))


def middle_back_body(count, *refs):
    parts = refs[:count]
    middle, mod, g_y, attended, g_middle_out, g_attended_out, g_shift, g_scale, g_gate, bias_grad = refs[
        count:
    ]
    g_in = total(parts)
    normed, rstd = normalize(middle[...])
    g_shift[...] = column_sum(g_in)
    g_scale[...] = column_sum(g_in * normed)
    g_middle = g_y[...] + normalize_back(g_in * (1.0 + part(mod, 4)), normed, rstd)
    g_middle_out[...] = g_middle
    g_gate[...] = column_sum(g_middle * attended[...])
    g_attended = (part(mod, 2) * g_middle).astype(BF16)
    g_attended_out[...] = g_attended
    bias_grad[...] = column_sum(g_attended.astype(F32))


def attn_back_body(count, place, *refs):
    g_chunks = refs[:count]
    w_own, w_received, qkv, probs_ref = refs[count : count + 4]
    g_rows_out, g_joint_out, bias_grad = refs[count + 4 : count + 7]
    g_partial = refs[count + 7 :]
    g_rows = put_rows(g_rows_out, g_chunks)
    w_front, w_value, w_out = pick_attn(place, w_own, w_received)
    width = w_value.shape[1]
    g_mixed = dot(g_rows, w_out).astype(BF16)
    g_query, g_key, g_value = [], [], []
    for head in range(width // HEAD):
        at = head * HEAD
        query = qkv[:, at : at + HEAD]
        key = qkv[:, width + at : width + at + HEAD]
        value = qkv[:, 2 * width + at : 2 * width + at + HEAD]
        probs = probs_ref[head]
        g_head = g_mixed[:, at : at + HEAD]
        g_probs = dot_t(g_head, value)
        row_dot = jnp.sum(probs * g_probs, axis=-1, keepdims=True)
        g_scores = (probs * (g_probs - row_dot)).astype(BF16)
        g_value.append(t_dot(probs.astype(BF16), g_head))
        g_query.append(dot(g_scores, key) * HEAD**-0.5)
        g_key.append(t_dot(g_scores, query) * HEAD**-0.5)
    g_front = jnp.concatenate(g_query + g_key, axis=1).astype(BF16)
    g_value = jnp.concatenate(g_value, axis=1).astype(BF16)
    g_joint_out[:, : 2 * width] = g_front
    g_joint_out[:, 2 * width :] = g_value
    bias_grad[:, :width] = column_sum(g_front[:, :width].astype(F32))
    bias_grad[:, width:] = column_sum(g_value.astype(F32))
    put_blocks(g_partial, dot_t(g_front, w_front) + dot_t(g_value, w_value))


def input_grad(parts, h, mod, g_middle, g_shift, g_scale):
    g_in = total(parts)
    normed, rstd = normalize(h[...])
    g_shift[...] = column_sum(g_in)
    g_scale[...] = column_sum(g_in * normed)
    return (g_middle[...] + normalize_back(g_in * (1.0 + part(mod, 1)), normed, rstd)).astype(BF16)


def between_back_body(count, *refs):
    parts = refs[:count]
    h, mod1, mod0, g_middle, shrunk, g_h_out, g_y_out, g_shrunk_out = refs[count : count + 8]
    g_shift, g_scale, g_gate, bias_grad = refs[count + 8 :]
    g_h = input_grad(parts, h, mod1, g_middle, g_shift, g_scale)
    g_h_out[...] = g_h
    g_y = g_h.astype(F32)
    g_y_out[...] = g_y
    g_gate[...] = column_sum(g_y * shrunk[...])
    g_shrunk = (part(mod0, 5) * g_y).astype(BF16)
    g_shrunk_out[...] = g_shrunk
    bias_grad[...] = column_sum(g_shrunk.astype(F32))


def finish_back_body(count, *refs):
    parts = refs[:count]
    h, mod, g_middle, g_h_out, g_shift, g_scale = refs[count:]
    g_h_out[...] = input_grad(parts, h, mod, g_middle, g_shift, g_scale)


def mlp_weights_body(rows, g_pre, g_rows, hidden, keep, give):
    half = keep.shape[1] // 2
    keep[:, :half] = t_dot(rows[...], g_pre[:, :half])
    keep[:, half:] = t_dot(g_rows[...], hidden[:, :half])
    give[:, :half] = t_dot(rows[...], g_pre[:, half:]).astype(BF16)
    give[:, half:] = t_dot(g_rows[...], hidden[:, half:]).astype(BF16)


def attn_weights_body(place, rows, g_joint, g_rows, mixed, keep, give):
    width = mixed.shape[1]
    first = place[0] == 0
    front = t_dot(rows[...], g_joint[:, : 2 * width])
    back = jnp.concatenate(
        [t_dot(rows[...], g_joint[:, 2 * width :]), t_dot(g_rows[...], mixed[...])], axis=1
    )
    keep[...] = jnp.where(first, front, back)
    give[...] = jnp.where(first, back, front).astype(BF16)


def line_blocks(place, k, rows):
    return pl.ds(pl.multiple_of((place[1] ^ k) * rows, 16), rows)


def stack_body(place, *refs):
    out = refs[-1]
    for k, ref in enumerate(refs[:-1]):
        out[line_blocks(place, k, ref.shape[0])] = ref[...]


def line_parts_body(place, keep, received, near, far, own):
    rows = own.shape[0]

    def block(k):
        at = line_blocks(place, k, rows)
        return keep[at] + received[at].astype(F32)

    near[0] = block(1).astype(BF16)
    near[1] = block(3).astype(BF16)
    far[...] = block(2)
    own[...] = block(0)


def mod_first_body(a0, a1, a2, a3, weight, out):
    rows = jnp.concatenate([a0[...], a1[...], a2[...], a3[...]], axis=0)
    out[...] = dot(rows, weight[...])


def mod_sum_body(count, *refs):
    values = total(refs[:count])
    outs = refs[count:]
    micro = outs[0].shape[0]
    for k, out in enumerate(outs):
        out[...] = values[k * micro : (k + 1) * micro]


def mod_join_body(place, p0, p1, p2, p3, bias, mine, other, scratch):
    for k, ref in enumerate((p0, p1, p2, p3)):
        scratch[place[1] ^ k] = ref[...]
    values = jnp.concatenate([scratch[j] for j in range(LINE)], axis=1) + bias[...]
    first = place[0] == 0
    mine[...] = jnp.where(first, values[0:1], values[1:2])
    other[...] = jnp.where(first, values[1:2], values[0:1])


def pack_body(*refs):
    out, pieces = refs[-1], refs[:-1]
    count = len(pieces) // 2
    for row in range(2):
        at = 0
        for ref in pieces[row * count : (row + 1) * count]:
            out[row : row + 1, at : at + ref.shape[1]] = ref[...]
            at += ref.shape[1]


def grads_sum_body(count, place, *refs):
    parts = refs[:count]
    joint0, expand0, joint1, expand1, keep, give = refs[count:]
    first = place[0] == 0
    values = total(parts)
    hidden = expand0.shape[1]
    mod_width = values.shape[1] // 8 * 6
    rounded = values[:, :mod_width].astype(BF16).astype(F32)
    sums = values[:, mod_width:]
    half = hidden // 2

    def natural(ref):
        now = ref[...]
        return jnp.where(first, now, jnp.concatenate([now[:, half:], now[:, :half]], axis=1))

    rows = []
    for row, (joint, expand) in enumerate(((joint0, expand0), (joint1, expand1))):
        rows.append(
            jnp.concatenate(
                [rounded[row : row + 1], joint[...], natural(expand), sums[row : row + 1]], axis=1
            )
        )
    keep[...] = jnp.where(first, rows[0], rows[1])
    give[...] = jnp.where(first, rows[1], rows[0])


def grads_join_body(place, keep, received, out):
    mods = out.shape[1] - keep.shape[1]
    first = place[0] == 0
    own, other = keep[...], received[...]
    out[:, :mods] = jnp.where(first, own, other)[:, :mods]
    out[:, mods : 2 * mods] = jnp.where(first, other, own)[:, :mods]
    out[:, 2 * mods :] = own[:, mods:] + other[:, mods:]


def mod_back_body(place, g0, g1, g2, g3, a0, a1, a2, a3, weight, w_grad, b_grad, bias, c0, c1, c2, c3):
    columns = weight.shape[1]
    mods = columns * LINE
    grads = (g0, g1, g2, g3)
    at = pl.multiple_of(place[1] * columns, 128)
    rows = []
    for ref in grads:
        rows.append(ref[:, pl.ds(at, columns)])
        rows.append(ref[:, pl.ds(pl.multiple_of(at + mods, 128), columns)])
    picked = jnp.concatenate(rows, axis=0).astype(BF16)
    activated = jnp.concatenate([a0[...], a1[...], a2[...], a3[...]], axis=0)
    w_grad[...] = t_dot(activated, picked)
    act = dot_t(picked, weight[...])
    for k, out in enumerate((c0, c1, c2, c3)):
        out[...] = act[2 * k : 2 * k + 2]
    b_grad[...] = tree_sum([ref[:, :mods] + ref[:, mods : 2 * mods] for ref in grads])
    bias[...] = tree_sum([ref[:, 2 * mods :] for ref in grads])


def on_device(
    tokens,
    conditions,
    cotangent,
    modulation_weight,
    modulation_bias,
    joint_weight,
    joint_bias,
    output_weight,
    output_bias,
    expand_weight,
    expand_bias,
    shrink_weight,
    shrink_bias,
):
    core = lax.axis_index("pipe")
    first = core == 0
    line = lax.axis_index("dp")
    place = jnp.stack([core, line]).astype(jnp.int32)
    line_size = lax.axis_size("dp")
    count = lax.axis_size("tensor")
    direct = line_size == LINE
    micro, _, own, model = tokens.shape
    width = output_weight.shape[1]
    hidden = expand_weight.shape[2]
    chunk = model // line_size
    rows = own * count
    columns = modulation_weight.shape[2]
    mods = 6 * model
    bias_width = 2 * width + hidden + 2 * model
    own_rows = modulation_weight[0]

    def mine(pair):
        return jnp.where(first, pair[0], pair[1])

    def other(pair):
        return jnp.where(first, pair[1], pair[0])

    def both_layers(kept, received):
        return jnp.where(first, kept, received), jnp.where(first, received, kept)

    def after(value, earlier):
        return lax.optimization_barrier((value, earlier))[0]

    attn_pack = jnp.concatenate(
        [joint_weight[0].reshape(chunk, 3 * width), output_weight[0].T], axis=1
    )
    shrink_t = shrink_weight[0].T
    expand = expand_weight[0]

    def column_half(index):
        return jnp.concatenate(
            [
                attn_pack[:, index * 2 * width : (index + 1) * 2 * width],
                expand[:, index * (hidden // 2) : (index + 1) * (hidden // 2)],
                shrink_t[:, index * (hidden // 2) : (index + 1) * (hidden // 2)],
            ],
            axis=1,
        )

    halves = (column_half(0), column_half(1))
    halves_of_layers = both_layers(mine(halves), swap(other(halves), "pipe", 1))
    split = 2 * width

    bias_pack = jnp.concatenate(
        [
            joint_bias[0].reshape(-1),
            expand_bias[0],
            output_bias[0],
            shrink_bias[0],
        ]
    )[None]
    bias_layers = both_layers(bias_pack, swap(bias_pack, "pipe", 1))
    biases = []
    for packed in bias_layers:
        at = 2 * width
        joint = jnp.concatenate(
            [packed[:, :width], jnp.zeros((1, width), F32), packed[:, width:at]], axis=1
        )
        grown = packed[:, at : at + hidden]
        rolled = jnp.concatenate([grown[:, hidden // 2 :], grown[:, : hidden // 2]], axis=1)
        grown = jnp.where(first, grown, rolled)
        at += hidden
        biases.append((joint, packed[:, at : at + model], grown, packed[:, at + model :]))

    def along_line(value, earlier):
        if earlier is not None:
            value = after(value, earlier)
        if direct:
            near = swap(value, "dp", 1)
            far = swap(value, "dp", 2)
            farther = swap(far, "dp", 1)
            lined = run(
                "stack_line",
                stack_body,
                [shape((model, value.shape[1]), BF16)],
                [value, near, far, farther],
                place,
            )[0]
            mark = far
        else:
            lined = lax.all_gather(value, "dp", axis=0, tiled=True)
            mark = lined
        return (lined, swap(lined, "pipe", 1)), mark

    weights = []
    mark = None
    for layer in range(2):
        attn, mark = along_line(halves_of_layers[layer][:, :split], mark)
        mlp, mark = along_line(halves_of_layers[layer][:, split:], mark)
        weights.append((attn, mlp))

    activated = jax.nn.silu(conditions[:, 0].astype(F32)).astype(BF16)
    if direct:
        activated_all = gather(activated, "dp")
        mod_partial = run(
            "mod_first",
            mod_first_body,
            [shape((micro * LINE, columns), F32)],
            activated_all + [own_rows],
        )[0]
        pieces = run(
            "mod_sum",
            functools.partial(mod_sum_body, count),
            [shape((micro, columns), F32)] * LINE,
            gather(mod_partial, "tensor"),
        )
        mod_mine, mod_other = pl.pallas_call(
            mod_join_body,
            out_shape=[shape((1, mods), F32)] * 2,
            in_specs=[pl.BlockSpec(memory_space=pltpu.SMEM)]
            + [pl.BlockSpec(memory_space=pltpu.VMEM)] * 5,
            out_specs=[pl.BlockSpec(memory_space=pltpu.VMEM)] * 2,
            scratch_shapes=[pltpu.VMEM((LINE, micro, columns), F32)],
            name="mod_join",
        )(place, *exchange(pieces, "dp"), modulation_bias)
    else:
        activated_all = lax.all_gather(activated, "dp", axis=0).reshape(line_size * micro, -1)
        mod_partial = dot(activated_all, own_rows)
        mod_sum = tree_sum(gather(mod_partial, "tensor")).reshape(line_size, micro, -1)
        mod_layer = lax.all_to_all(mod_sum, "dp", split_axis=0, concat_axis=0)
        mod_layer = jnp.swapaxes(mod_layer, 0, 1).reshape(micro, -1) + modulation_bias
        mod_mine, mod_other = mine(mod_layer)[None], other(mod_layer)[None]
    mod0, mod1 = both_layers(mod_mine, swap(mod_other, "pipe", 1))

    own_f32 = shape((own, model), F32)
    own_bf16 = shape((own, model), BF16)
    blocks = [own_bf16] * count
    vector = shape((1, model), F32)
    h0, attn_in, g_y1, g_shrunk1 = run(
        "enter",
        enter_body,
        [own_f32, own_bf16, own_f32, own_bf16],
        [tokens[:, 0], cotangent[:, 0], mod0, mod1],
        place,
    )

    def attention(attn_in, weight, bias):
        outs = run(
            "attention",
            functools.partial(attn_body, count),
            [
                shape((rows, model), BF16),
                shape((rows, 3 * width), BF16),
                shape((width // HEAD, rows, rows), F32),
                shape((rows, width), BF16),
            ]
            + blocks,
            gather(attn_in, "tensor") + [weight[0], weight[1], bias],
            place,
        )
        return outs[:4], exchange(outs[4:], "tensor")

    def middle_of(parts, bias, h, mod):
        return run(
            "middle",
            functools.partial(middle_body, count),
            [own_f32, own_f32, own_bf16],
            parts + [bias, h, mod],
        )

    kept_attn0, parts = attention(attn_in, weights[0][0], biases[0][0])
    attended0, middle0, mlp_in = middle_of(parts, biases[0][1], h0, mod0)
    outs = run(
        "feed_forward",
        functools.partial(mlp_body, count),
        [shape((rows, model), BF16), shape((rows, hidden), F32), shape((rows, hidden), BF16)] + blocks,
        gather(mlp_in, "tensor") + [weights[0][1][0], weights[0][1][1], biases[0][2]],
    )
    mlp_rows0, pre0, hidden0 = outs[:3]
    shrunk0, passed, h1, attn_in = run(
        "between",
        functools.partial(between_body, count),
        [own_f32, own_bf16, own_f32, own_bf16],
        exchange(outs[3:], "tensor") + [biases[0][3], middle0, mod0, mod1],
    )

    g_shrunk_rows = gather(g_shrunk1, "tensor")
    kept_attn1, parts = attention(attn_in, weights[1][0], biases[1][0])
    attended1, middle1, mlp_in = middle_of(parts, biases[1][1], h1, mod1)
    outs = run(
        "feed_forward_both",
        functools.partial(mlp_both_body, count),
        [
            shape((rows, model), BF16),
            shape((rows, model), BF16),
            shape((rows, hidden), BF16),
            shape((rows, hidden), BF16),
            shape((1, hidden), F32),
        ]
        + blocks
        + blocks,
        gather(mlp_in, "tensor")
        + g_shrunk_rows
        + [weights[1][1][0], weights[1][1][1], biases[1][2]],
    )
    mlp_rows1, g_rows1, hidden1, g_pre1, expand_grad1 = outs[:5]
    y_parts, g_parts = outs[5 : 5 + count], outs[5 + count :]

    def middle_back(parts, middle, mod, g_y, attended):
        return run(
            "middle_back",
            functools.partial(middle_back_body, count),
            [own_f32, own_bf16] + [vector] * 4,
            parts + [middle, mod, g_y, attended],
        )

    def attention_back(g_attended, weight, kept):
        outs = run(
            "attention_back",
            functools.partial(attn_back_body, count),
            [
                shape((rows, model), BF16),
                shape((rows, 3 * width), BF16),
                shape((1, 2 * width), F32),
            ]
            + blocks,
            gather(g_attended, "tensor") + [weight[0], weight[1], kept[1], kept[2]],
            place,
        )
        return outs[:3], exchange(outs[3:], "tensor")

    def reduce_line(keep, give):
        received = swap(give, "pipe", 1)
        if not direct:
            whole = (keep + received.astype(F32)).astype(BF16)
            return lax.psum_scatter(whole, "dp", scatter_dimension=0, tiled=True).astype(F32)
        wide = keep.shape[1]
        near, far, own_part = run(
            "line_parts",
            line_parts_body,
            [
                shape((2, chunk, wide), BF16),
                shape((chunk, wide), F32),
                shape((chunk, wide), F32),
            ],
            [keep, received],
            place,
        )
        near = swap(near, "dp", 1)
        far = swap((far + near[1].astype(F32)).astype(BF16), "dp", 2)
        return own_part + near[0].astype(F32) + far.astype(F32)

    def mlp_weight_grads(mlp_rows, g_pre, g_rows, hidden_rows):
        keep, give = run(
            "mlp_weight_grads",
            mlp_weights_body,
            [shape((model, hidden), F32), shape((model, hidden), BF16)],
            [mlp_rows, g_pre, g_rows, hidden_rows],
        )
        return reduce_line(keep, give)

    def attn_weight_grads(attn_rows, g_joint, g_rows, mixed):
        keep, give = run(
            "attn_weight_grads",
            attn_weights_body,
            [shape((model, 2 * width), F32), shape((model, 2 * width), BF16)],
            [attn_rows, g_joint, g_rows, mixed],
            place,
        )
        return reduce_line(keep, give)

    g_middle1, g_attended, g_shift_mlp1, g_scale_mlp1, g_gate_attn1, out_grad1 = middle_back(
        exchange(g_parts, "tensor"), middle1, mod1, g_y1, attended1
    )
    mlp_grad1 = mlp_weight_grads(mlp_rows1, g_pre1, g_rows1, hidden1)
    y1, g_gate_mlp1, shrink_grad1 = run(
        "leave",
        functools.partial(leave_body, count),
        [own_bf16, vector, vector],
        exchange(y_parts, "tensor") + [biases[1][3], middle1, mod1, g_y1, g_shrunk1],
    )
    (g_rows, g_joint, joint_grad1), parts = attention_back(g_attended, weights[1][0], kept_attn1)
    g_passed, g_y0, g_shrunk0, g_shift_attn1, g_scale_attn1, g_gate_mlp0, shrink_grad0 = run(
        "between_back",
        functools.partial(between_back_body, count),
        [own_bf16, own_f32, own_bf16] + [vector] * 4,
        parts + [h1, mod1, mod0, g_middle1, shrunk0],
    )
    attn_grad1 = attn_weight_grads(kept_attn1[0], g_joint, g_rows, kept_attn1[3])

    outs = run(
        "feed_forward_back",
        functools.partial(mlp_back_body, count),
        [shape((rows, model), BF16), shape((rows, hidden), BF16), shape((1, hidden), F32)] + blocks,
        gather(g_shrunk0, "tensor") + [weights[0][1][0], weights[0][1][1], pre0],
    )
    g_rows0, g_pre0, expand_grad0 = outs[:3]
    g_middle0, g_attended, g_shift_mlp0, g_scale_mlp0, g_gate_attn0, out_grad0 = middle_back(
        exchange(outs[3:], "tensor"), middle0, mod0, g_y0, attended0
    )
    mlp_grad0 = mlp_weight_grads(mlp_rows0, g_pre0, g_rows0, hidden0)
    (g_rows, g_joint, joint_grad0), parts = attention_back(g_attended, weights[0][0], kept_attn0)
    g_h0, g_shift_attn0, g_scale_attn0 = run(
        "finish_back",
        functools.partial(finish_back_body, count),
        [own_bf16, vector, vector],
        parts + [h0, mod0, g_middle0],
    )
    attn_grad0 = attn_weight_grads(kept_attn0[0], g_joint, g_rows, kept_attn0[3])

    def own_layer_of_micros(pair):
        return jnp.stack(both_layers(mine(pair), swap(other(pair), "pipe", 1)))

    layer_outputs = own_layer_of_micros((passed, y1))
    input_grads = own_layer_of_micros((g_h0, g_passed))

    def own_columns(pair):
        return both_layers(mine(pair), swap(other(pair), "pipe", 1))

    mlp_halves = own_columns((mlp_grad0, mlp_grad1))
    half = hidden // 2
    expand_w_grad = jnp.concatenate([part[:, :half] for part in mlp_halves], axis=1)
    shrink_w_grad = jnp.concatenate([part[:, half:] for part in mlp_halves], axis=1).T
    front, back = own_columns((attn_grad0, attn_grad1))
    joint_w_grad = jnp.concatenate([front, back[:, :width]], axis=1).reshape(chunk, 3, width)
    output_w_grad = back[:, width:].T

    packed = run(
        "pack_grads",
        pack_body,
        [shape((2, mods + 2 * model), F32)],
        [
            g_shift_attn0,
            g_scale_attn0,
            g_gate_attn0,
            g_shift_mlp0,
            g_scale_mlp0,
            g_gate_mlp0,
            out_grad0,
            shrink_grad0,
            g_shift_attn1,
            g_scale_attn1,
            g_gate_attn1,
            g_shift_mlp1,
            g_scale_mlp1,
            g_gate_mlp1,
            out_grad1,
            shrink_grad1,
        ],
    )[0]
    keep, give = run(
        "grads_sum",
        functools.partial(grads_sum_body, count),
        [shape((1, mods + bias_width), F32)] * 2,
        gather(packed, "tensor") + [joint_grad0, expand_grad0, joint_grad1, expand_grad1],
        place,
    )
    joined = run(
        "grads_join",
        grads_join_body,
        [shape((1, 2 * mods + bias_width), F32)],
        [keep, swap(give, "pipe", 1)],
        place,
    )[0]
    if direct:
        outs = run(
            "mod_back",
            mod_back_body,
            [shape(own_rows.shape, F32), shape((1, mods), F32), shape((1, bias_width), F32)]
            + [shape((micro, own_rows.shape[0]), F32)] * LINE,
            gather(joined, "dp") + activated_all + [own_rows],
            place,
        )
        ada_grad, ada_bias_grad, bias_sum = outs[:3]
        act_grad = tree_sum(exchange(outs[3:], "dp"))
    else:
        joined_all = lax.all_gather(joined, "dp", axis=0, tiled=True)
        mod_grads = joined_all[:, : 2 * mods].reshape(line_size * micro, mods)
        bias_sum = jnp.sum(joined_all[:, 2 * mods :], axis=0, keepdims=True)
        ada_bias_grad = jnp.sum(mod_grads, axis=0, keepdims=True)
        picked = lax.dynamic_slice_in_dim(mod_grads, line * columns, columns, 1).astype(BF16)
        ada_grad = t_dot(activated_all, picked)
        act_partial = dot_t(picked, own_rows).reshape(line_size, micro, -1)
        act_grad = lax.psum_scatter(act_partial, "dp", scatter_dimension=0, tiled=False)
    _, silu_back = jax.vjp(jax.nn.silu, conditions[:, 0].astype(F32))
    cond_grad = silu_back(act_grad)[0]
    at = 2 * width
    return (
        layer_outputs[None, :, None],
        input_grads[None, :, None],
        cond_grad[None, :, None],
        ada_grad[None],
        ada_bias_grad,
        joint_w_grad[None],
        bias_sum[:, :at].reshape(1, 2, width),
        output_w_grad[None],
        bias_sum[:, at + hidden : at + hidden + model],
        expand_w_grad[None],
        bias_sum[:, at : at + hidden],
        shrink_w_grad[None],
        bias_sum[:, at + hidden + model :],
    )


def solution(mesh):
    in_specs = (
        P(None, "dp", "tensor", None),
        P(None, "dp", "tensor"),
        P(None, "dp", "tensor", None),
        P("pipe", "tensor", "dp"),
        P("pipe", None),
        P("pipe", "dp", None, "tensor"),
        P("pipe", None, "tensor"),
        P("pipe", "tensor", "dp"),
        P("pipe", None),
        P("pipe", "dp", "tensor"),
        P("pipe", "tensor"),
        P("pipe", "tensor", "dp"),
        P("pipe", None),
    )
    out_specs = (
        P("pipe", None, "dp", "tensor", None),
        P("pipe", None, "dp", "tensor", None),
        P("pipe", None, "dp", "tensor"),
        P("pipe", "tensor", "dp"),
        P("pipe", None),
        P("pipe", "dp", None, "tensor"),
        P("pipe", None, "tensor"),
        P("pipe", "tensor", "dp"),
        P("pipe", None),
        P("pipe", "dp", "tensor"),
        P("pipe", "tensor"),
        P("pipe", "tensor", "dp"),
        P("pipe", None),
    )
    return jax.shard_map(
        on_device, mesh=mesh, in_specs=in_specs, out_specs=out_specs, check_vma=False
    )
```

```python
import functools

import jax
import jax.numpy as jnp
from jax import lax
from jax.experimental import pallas as pl
from jax.experimental.pallas import tpu as pltpu
from jax.sharding import PartitionSpec as P

HEAD = 64
EPS = 1e-06
F32 = jnp.float32
BF16 = jnp.bfloat16
LINE = 4
VMEM_BYTES = 24 * 1024 * 1024
GELU_A = 0.7978845608028654
GELU_B = 0.044715


def swap(value, axis, mask):
    pairs = [(source, source ^ mask) for source in range(lax.axis_size(axis))]
    return lax.ppermute(value, axis, pairs)


def exchange(parts, axis):
    return [parts[0]] + [swap(parts[k], axis, k) for k in range(1, len(parts))]


def gather(value, axis):
    return exchange([value] * lax.axis_size(axis), axis)


def tree_sum(parts):
    parts = list(parts)
    while len(parts) > 1:
        parts = [parts[k] + parts[k + 1] for k in range(0, len(parts), 2)]
    return parts[0]


def trade(rows, axis):
    return lax.all_to_all(rows, axis, 0, 0, tiled=True)


def shape(dims, dtype):
    return jax.ShapeDtypeStruct(dims, dtype)


def run(name, body, outs, args, place=None):
    specs = [pl.BlockSpec(memory_space=pltpu.VMEM) for _ in args]
    if place is not None:
        specs = [pl.BlockSpec(memory_space=pltpu.SMEM)] + specs
        args = [place] + list(args)
    return pl.pallas_call(
        body,
        out_shape=outs,
        in_specs=specs,
        out_specs=[pl.BlockSpec(memory_space=pltpu.VMEM) for _ in outs],
        compiler_params=pltpu.CompilerParams(vmem_limit_bytes=VMEM_BYTES),
        name=name,
    )(*args)


def dot(left, right):
    return jnp.dot(left, right, preferred_element_type=F32)


def dot_t(left, right):
    return lax.dot_general(left, right, (((1,), (1,)), ((), ())), preferred_element_type=F32)


def t_dot(left, right):
    return lax.dot_general(left, right, (((0,), (0,)), ((), ())), preferred_element_type=F32)


def normalize(values):
    centred = values - jnp.mean(values, axis=-1, keepdims=True)
    rstd = lax.rsqrt(jnp.mean(centred * centred, axis=-1, keepdims=True) + EPS)
    return centred * rstd, rstd


def normalize_back(grad, normed, rstd):
    return rstd * (
        grad
        - jnp.mean(grad, axis=-1, keepdims=True)
        - normed * jnp.mean(grad * normed, axis=-1, keepdims=True)
    )


def total(refs):
    return tree_sum([ref[...].astype(F32) for ref in refs])


def column_sum(values):
    return jnp.sum(values, axis=0, keepdims=True)


def part(mod_ref, index):
    width = mod_ref.shape[1] // 6
    return mod_ref[:, index * width : (index + 1) * width]


def gelu(pre):
    return 0.5 * pre * (1.0 + jnp.tanh(GELU_A * (pre + GELU_B * (pre * pre * pre))))


def gelu_slope(pre):
    square = pre * pre
    bent = jnp.tanh(GELU_A * (pre + GELU_B * (square * pre)))
    return 0.5 * (1.0 + bent) + 0.5 * pre * (1.0 - bent * bent) * (
        GELU_A * (1.0 + 3.0 * GELU_B * square)
    )


def block_sum(ref, own):
    count = ref.shape[0] // own
    return tree_sum([ref[k * own : (k + 1) * own].astype(F32) for k in range(count)])


def copies(ref, values):
    own = values.shape[0]
    for k in range(ref.shape[0] // own):
        ref[k * own : (k + 1) * own] = values


def enter_body(place, tokens, cotangent, mod0, mod1, h_out, attn_in, g_y_out, g_shrunk):
    core = place[0]
    h = tokens[core].astype(F32)
    h_out[...] = h
    normed, _ = normalize(h)
    copies(attn_in, (normed * (1.0 + part(mod0, 1)) + part(mod0, 0)).astype(BF16))
    g_y = cotangent[core].astype(F32)
    g_y_out[...] = g_y
    copies(g_shrunk, (part(mod1, 5) * g_y).astype(BF16))


def pick_attn(place, own, received):
    first = place[0] == 0
    width = own.shape[1] // 2
    mine, other = own[...], received[...]
    front = jnp.where(first, mine, other)
    back = jnp.where(first, other, mine)
    return front, back[:, :width], back[:, width:]


def attn_body(place, rows_ref, w_own, w_received, bias, qkv_out, probs_out, mixed_out, partial):
    rows = rows_ref[...]
    w_front, w_value, w_out = pick_attn(place, w_own, w_received)
    width = w_value.shape[1]
    front = (dot(rows, w_front) + bias[:, : 2 * width]).astype(BF16)
    value = (dot(rows, w_value) + bias[:, 2 * width :]).astype(BF16)
    qkv_out[:, : 2 * width] = front
    qkv_out[:, 2 * width :] = value
    mixed = []
    for head in range(width // HEAD):
        at = head * HEAD
        query = front[:, at : at + HEAD]
        key = front[:, width + at : width + at + HEAD]
        scores = dot_t(query, key) * HEAD**-0.5
        powers = jnp.exp(scores - jnp.max(scores, axis=-1, keepdims=True))
        probs = powers / jnp.sum(powers, axis=-1, keepdims=True)
        probs_out[head] = probs
        mixed.append(dot(probs.astype(BF16), value[:, at : at + HEAD]))
    mixed = jnp.concatenate(mixed, axis=1).astype(BF16)
    mixed_out[...] = mixed
    partial[...] = dot_t(mixed, w_out).astype(BF16)


def middle_body(parts, bias, h, mod, attended_out, middle_out, mlp_in):
    attended = block_sum(parts, h.shape[0]) + bias[...]
    attended_out[...] = attended
    middle = h[...] + part(mod, 2) * attended
    middle_out[...] = middle
    normed, _ = normalize(middle)
    copies(mlp_in, (normed * (1.0 + part(mod, 4)) + part(mod, 3)).astype(BF16))


def mlp_body(rows_ref, w_own, w_received, bias, pre_out, hidden_out, partial):
    rows = rows_ref[...]
    half = w_own.shape[1] // 2
    shrunk = None
    for index, weight in enumerate((w_own, w_received)):
        at = index * half
        pre = dot(rows, weight[:, :half]) + bias[:, at : at + half]
        pre_out[:, at : at + half] = pre
        hidden = gelu(pre).astype(BF16)
        hidden_out[:, at : at + half] = hidden
        term = dot_t(hidden, weight[:, half:])
        shrunk = term if shrunk is None else shrunk + term
    partial[...] = shrunk.astype(BF16)


def mlp_both_body(
    rows_ref, g_rows_ref, w_own, w_received, bias, hidden_out, g_pre_out, bias_grad, partial, g_partial
):
    rows = rows_ref[...]
    g_rows = g_rows_ref[...]
    half = w_own.shape[1] // 2
    shrunk, g_in = None, None
    for index, weight in enumerate((w_own, w_received)):
        at = index * half
        pre = dot(rows, weight[:, :half]) + bias[:, at : at + half]
        hidden = gelu(pre).astype(BF16)
        hidden_out[:, at : at + half] = hidden
        g_pre = (dot(g_rows, weight[:, half:]) * gelu_slope(pre)).astype(BF16)
        g_pre_out[:, at : at + half] = g_pre
        bias_grad[:, at : at + half] = column_sum(g_pre.astype(F32))
        term = dot_t(hidden, weight[:, half:])
        g_term = dot_t(g_pre, weight[:, :half])
        shrunk = term if shrunk is None else shrunk + term
        g_in = g_term if g_in is None else g_in + g_term
    g_partial[...] = g_in.astype(BF16)
    partial[...] = shrunk.astype(BF16)


def mlp_back_body(g_rows_ref, w_own, w_received, pre_ref, g_pre_out, bias_grad, g_partial):
    g_rows = g_rows_ref[...]
    half = w_own.shape[1] // 2
    g_in = None
    for index, weight in enumerate((w_own, w_received)):
        at = index * half
        pre = pre_ref[:, at : at + half]
        g_pre = (dot(g_rows, weight[:, half:]) * gelu_slope(pre)).astype(BF16)
        g_pre_out[:, at : at + half] = g_pre
        bias_grad[:, at : at + half] = column_sum(g_pre.astype(F32))
        g_term = dot_t(g_pre, weight[:, :half])
        g_in = g_term if g_in is None else g_in + g_term
    g_partial[...] = g_in.astype(BF16)


def between_body(parts, bias, middle, mod0, mod1, shrunk_out, passed_out, h_out, attn_in):
    shrunk = block_sum(parts, middle.shape[0]) + bias[...]
    shrunk_out[...] = shrunk
    passed = (middle[...] + part(mod0, 5) * shrunk).astype(BF16)
    passed_out[...] = passed
    h = passed.astype(F32)
    h_out[...] = h
    normed, _ = normalize(h)
    copies(attn_in, (normed * (1.0 + part(mod1, 1)) + part(mod1, 0)).astype(BF16))


def leave_body(parts, bias, middle, mod, g_y_ref, y_out, g_gate, bias_grad):
    shrunk = block_sum(parts, middle.shape[0]) + bias[...]
    y_out[...] = (middle[...] + part(mod, 5) * shrunk).astype(BF16)
    g_gate[...] = column_sum(g_y_ref[...] * shrunk)
    bias_grad[...] = column_sum((part(mod, 5) * g_y_ref[...]).astype(BF16).astype(F32))


def middle_back_body(
    parts,
    middle,
    mod,
    g_y,
    attended,
    g_middle_out,
    g_attended_out,
    g_shift,
    g_scale,
    g_gate,
    bias_grad,
):
    g_in = block_sum(parts, middle.shape[0])
    normed, rstd = normalize(middle[...])
    g_shift[...] = column_sum(g_in)
    g_scale[...] = column_sum(g_in * normed)
    g_middle = g_y[...] + normalize_back(g_in * (1.0 + part(mod, 4)), normed, rstd)
    g_middle_out[...] = g_middle
    g_gate[...] = column_sum(g_middle * attended[...])
    g_attended = (part(mod, 2) * g_middle).astype(BF16)
    copies(g_attended_out, g_attended)
    bias_grad[...] = column_sum(g_attended.astype(F32))


def attn_back_body(
    place, g_rows_ref, w_own, w_received, qkv, probs_ref, g_joint_out, bias_grad, g_partial
):
    g_rows = g_rows_ref[...]
    w_front, w_value, w_out = pick_attn(place, w_own, w_received)
    width = w_value.shape[1]
    g_mixed = dot(g_rows, w_out).astype(BF16)
    g_query, g_key, g_value = [], [], []
    for head in range(width // HEAD):
        at = head * HEAD
        query = qkv[:, at : at + HEAD]
        key = qkv[:, width + at : width + at + HEAD]
        value = qkv[:, 2 * width + at : 2 * width + at + HEAD]
        probs = probs_ref[head]
        g_head = g_mixed[:, at : at + HEAD]
        g_probs = dot_t(g_head, value)
        row_dot = jnp.sum(probs * g_probs, axis=-1, keepdims=True)
        g_scores = (probs * (g_probs - row_dot)).astype(BF16)
        g_value.append(t_dot(probs.astype(BF16), g_head))
        g_query.append(dot(g_scores, key) * HEAD**-0.5)
        g_key.append(t_dot(g_scores, query) * HEAD**-0.5)
    g_front = jnp.concatenate(g_query + g_key, axis=1).astype(BF16)
    g_value = jnp.concatenate(g_value, axis=1).astype(BF16)
    g_joint_out[:, : 2 * width] = g_front
    g_joint_out[:, 2 * width :] = g_value
    bias_grad[:, :width] = column_sum(g_front[:, :width].astype(F32))
    bias_grad[:, width:] = column_sum(g_value.astype(F32))
    g_partial[...] = (dot_t(g_front, w_front) + dot_t(g_value, w_value)).astype(BF16)


def input_grad(parts, h, mod, g_middle, g_shift, g_scale):
    g_in = block_sum(parts, h.shape[0])
    normed, rstd = normalize(h[...])
    g_shift[...] = column_sum(g_in)
    g_scale[...] = column_sum(g_in * normed)
    return (g_middle[...] + normalize_back(g_in * (1.0 + part(mod, 1)), normed, rstd)).astype(BF16)


def between_back_body(
    parts,
    h,
    mod1,
    mod0,
    g_middle,
    shrunk,
    g_h_out,
    g_y_out,
    g_shrunk_out,
    g_shift,
    g_scale,
    g_gate,
    bias_grad,
):
    g_h = input_grad(parts, h, mod1, g_middle, g_shift, g_scale)
    g_h_out[...] = g_h
    g_y = g_h.astype(F32)
    g_y_out[...] = g_y
    g_gate[...] = column_sum(g_y * shrunk[...])
    g_shrunk = (part(mod0, 5) * g_y).astype(BF16)
    copies(g_shrunk_out, g_shrunk)
    bias_grad[...] = column_sum(g_shrunk.astype(F32))


def finish_back_body(parts, h, mod, g_middle, g_h_out, g_shift, g_scale):
    g_h_out[...] = input_grad(parts, h, mod, g_middle, g_shift, g_scale)


def mlp_weights_body(rows, g_pre, g_rows, hidden, keep, give):
    half = keep.shape[1] // 2
    keep[:, :half] = t_dot(rows[...], g_pre[:, :half])
    keep[:, half:] = t_dot(g_rows[...], hidden[:, :half])
    give[:, :half] = t_dot(rows[...], g_pre[:, half:]).astype(BF16)
    give[:, half:] = t_dot(g_rows[...], hidden[:, half:]).astype(BF16)


def attn_weights_body(place, rows, g_joint, g_rows, mixed, keep, give):
    width = mixed.shape[1]
    first = place[0] == 0
    front = t_dot(rows[...], g_joint[:, : 2 * width])
    back = jnp.concatenate(
        [t_dot(rows[...], g_joint[:, 2 * width :]), t_dot(g_rows[...], mixed[...])], axis=1
    )
    keep[...] = jnp.where(first, front, back)
    give[...] = jnp.where(first, back, front).astype(BF16)


def line_blocks(place, k, rows):
    return pl.ds(pl.multiple_of((place[1] ^ k) * rows, 16), rows)


def stack_body(place, *refs):
    out = refs[-1]
    for k, ref in enumerate(refs[:-1]):
        out[line_blocks(place, k, ref.shape[0])] = ref[...]


def line_parts_body(place, keep, received, near, far, own):
    rows = own.shape[0]

    def block(k):
        at = line_blocks(place, k, rows)
        return keep[at] + received[at].astype(F32)

    near[0] = block(1).astype(BF16)
    near[1] = block(3).astype(BF16)
    far[...] = block(2)
    own[...] = block(0)


def mod_first_body(a0, a1, a2, a3, weight, out):
    rows = jnp.concatenate([a0[...], a1[...], a2[...], a3[...]], axis=0)
    out[...] = dot(rows, weight[...])


def mod_sum_body(count, *refs):
    values = total(refs[:count])
    outs = refs[count:]
    micro = outs[0].shape[0]
    for k, out in enumerate(outs):
        out[...] = values[k * micro : (k + 1) * micro]


def mod_join_body(place, p0, p1, p2, p3, bias, mine, other, scratch):
    for k, ref in enumerate((p0, p1, p2, p3)):
        scratch[place[1] ^ k] = ref[...]
    values = jnp.concatenate([scratch[j] for j in range(LINE)], axis=1) + bias[...]
    first = place[0] == 0
    mine[...] = jnp.where(first, values[0:1], values[1:2])
    other[...] = jnp.where(first, values[1:2], values[0:1])


def pack_body(*refs):
    out, pieces = refs[-1], refs[:-1]
    count = len(pieces) // 2
    for row in range(2):
        at = 0
        for ref in pieces[row * count : (row + 1) * count]:
            out[row : row + 1, at : at + ref.shape[1]] = ref[...]
            at += ref.shape[1]


def grads_sum_body(count, place, *refs):
    parts = refs[:count]
    joint0, expand0, joint1, expand1, keep, give = refs[count:]
    first = place[0] == 0
    values = total(parts)
    hidden = expand0.shape[1]
    mod_width = values.shape[1] // 8 * 6
    rounded = values[:, :mod_width].astype(BF16).astype(F32)
    sums = values[:, mod_width:]
    half = hidden // 2

    def natural(ref):
        now = ref[...]
        return jnp.where(first, now, jnp.concatenate([now[:, half:], now[:, :half]], axis=1))

    rows = []
    for row, (joint, expand) in enumerate(((joint0, expand0), (joint1, expand1))):
        rows.append(
            jnp.concatenate(
                [rounded[row : row + 1], joint[...], natural(expand), sums[row : row + 1]], axis=1
            )
        )
    keep[...] = jnp.where(first, rows[0], rows[1])
    give[...] = jnp.where(first, rows[1], rows[0])


def grads_join_body(place, keep, received, out):
    mods = out.shape[1] - keep.shape[1]
    first = place[0] == 0
    own, other = keep[...], received[...]
    out[:, :mods] = jnp.where(first, own, other)[:, :mods]
    out[:, mods : 2 * mods] = jnp.where(first, other, own)[:, :mods]
    out[:, 2 * mods :] = own[:, mods:] + other[:, mods:]


def mod_back_body(place, g0, g1, g2, g3, a0, a1, a2, a3, weight, w_grad, b_grad, bias, c0, c1, c2, c3):
    columns = weight.shape[1]
    mods = columns * LINE
    grads = (g0, g1, g2, g3)
    at = pl.multiple_of(place[1] * columns, 128)
    rows = []
    for ref in grads:
        rows.append(ref[:, pl.ds(at, columns)])
        rows.append(ref[:, pl.ds(pl.multiple_of(at + mods, 128), columns)])
    picked = jnp.concatenate(rows, axis=0).astype(BF16)
    activated = jnp.concatenate([a0[...], a1[...], a2[...], a3[...]], axis=0)
    w_grad[...] = t_dot(activated, picked)
    act = dot_t(picked, weight[...])
    for k, out in enumerate((c0, c1, c2, c3)):
        out[...] = act[2 * k : 2 * k + 2]
    b_grad[...] = tree_sum([ref[:, :mods] + ref[:, mods : 2 * mods] for ref in grads])
    bias[...] = tree_sum([ref[:, 2 * mods :] for ref in grads])


def on_device(
    tokens,
    conditions,
    cotangent,
    modulation_weight,
    modulation_bias,
    joint_weight,
    joint_bias,
    output_weight,
    output_bias,
    expand_weight,
    expand_bias,
    shrink_weight,
    shrink_bias,
):
    core = lax.axis_index("pipe")
    first = core == 0
    line = lax.axis_index("dp")
    place = jnp.stack([core, line]).astype(jnp.int32)
    line_size = lax.axis_size("dp")
    count = lax.axis_size("tensor")
    direct = line_size == LINE
    micro, _, own, model = tokens.shape
    width = output_weight.shape[1]
    hidden = expand_weight.shape[2]
    chunk = model // line_size
    rows = own * count
    columns = modulation_weight.shape[2]
    mods = 6 * model
    bias_width = 2 * width + hidden + 2 * model
    own_rows = modulation_weight[0]

    def mine(pair):
        return jnp.where(first, pair[0], pair[1])

    def other(pair):
        return jnp.where(first, pair[1], pair[0])

    def both_layers(kept, received):
        return jnp.where(first, kept, received), jnp.where(first, received, kept)

    def after(value, earlier):
        return lax.optimization_barrier((value, earlier))[0]

    def tie(*values):
        return lax.optimization_barrier(values)

    attn_pack = jnp.concatenate(
        [joint_weight[0].reshape(chunk, 3 * width), output_weight[0].T], axis=1
    )
    shrink_t = shrink_weight[0].T
    expand = expand_weight[0]

    def column_half(index):
        return jnp.concatenate(
            [
                attn_pack[:, index * 2 * width : (index + 1) * 2 * width],
                expand[:, index * (hidden // 2) : (index + 1) * (hidden // 2)],
                shrink_t[:, index * (hidden // 2) : (index + 1) * (hidden // 2)],
            ],
            axis=1,
        )

    halves = (column_half(0), column_half(1))
    halves_of_layers = both_layers(mine(halves), swap(other(halves), "pipe", 1))
    split = 2 * width

    bias_pack = jnp.concatenate(
        [
            joint_bias[0].reshape(-1),
            expand_bias[0],
            output_bias[0],
            shrink_bias[0],
        ]
    )[None]
    bias_layers = both_layers(bias_pack, swap(bias_pack, "pipe", 1))
    biases = []
    for packed in bias_layers:
        at = 2 * width
        joint = jnp.concatenate(
            [packed[:, :width], jnp.zeros((1, width), F32), packed[:, width:at]], axis=1
        )
        grown = packed[:, at : at + hidden]
        rolled = jnp.concatenate([grown[:, hidden // 2 :], grown[:, : hidden // 2]], axis=1)
        grown = jnp.where(first, grown, rolled)
        at += hidden
        biases.append((joint, packed[:, at : at + model], grown, packed[:, at + model :]))

    activated = jax.nn.silu(conditions[:, 0].astype(F32)).astype(BF16)
    if direct:
        activated_all = gather(activated, "dp")
    else:
        activated_all = lax.all_gather(activated, "dp", axis=0).reshape(line_size * micro, -1)

    def along_line(value, earlier, at_once=False):
        if earlier is not None:
            value = after(value, earlier)
        if direct:
            near = swap(value, "dp", 1)
            far = swap(value, "dp", 2)
            farther = swap(value, "dp", 3) if at_once else swap(far, "dp", 1)
            lined = run(
                "stack_line",
                stack_body,
                [shape((model, value.shape[1]), BF16)],
                [value, near, far, farther],
                place,
            )[0]
            mark = (near, far, farther) if at_once else far
        else:
            lined = lax.all_gather(value, "dp", axis=0, tiled=True)
            mark = lined
        return (lined, swap(lined, "pipe", 1)), mark

    weights = []
    mark = activated_all
    for layer in range(2):
        attn, mark = along_line(halves_of_layers[layer][:, :split], mark, layer == 0)
        mlp, mark = along_line(halves_of_layers[layer][:, split:], mark)
        weights.append((attn, mlp))

    if direct:
        mod_partial = run(
            "mod_first",
            mod_first_body,
            [shape((micro * LINE, columns), F32)],
            activated_all + [own_rows],
        )[0]
        pieces = run(
            "mod_sum",
            functools.partial(mod_sum_body, count),
            [shape((micro, columns), F32)] * LINE,
            gather(mod_partial, "tensor"),
        )
        mod_mine, mod_other = pl.pallas_call(
            mod_join_body,
            out_shape=[shape((1, mods), F32)] * 2,
            in_specs=[pl.BlockSpec(memory_space=pltpu.SMEM)]
            + [pl.BlockSpec(memory_space=pltpu.VMEM)] * 5,
            out_specs=[pl.BlockSpec(memory_space=pltpu.VMEM)] * 2,
            scratch_shapes=[pltpu.VMEM((LINE, micro, columns), F32)],
            name="mod_join",
        )(place, *exchange(pieces, "dp"), modulation_bias)
    else:
        mod_partial = dot(activated_all, own_rows)
        mod_sum = tree_sum(gather(mod_partial, "tensor")).reshape(line_size, micro, -1)
        mod_layer = lax.all_to_all(mod_sum, "dp", split_axis=0, concat_axis=0)
        mod_layer = jnp.swapaxes(mod_layer, 0, 1).reshape(micro, -1) + modulation_bias
        mod_mine, mod_other = mine(mod_layer)[None], other(mod_layer)[None]
    mod0, mod1 = both_layers(mod_mine, swap(mod_other, "pipe", 1))

    own_f32 = shape((own, model), F32)
    own_bf16 = shape((own, model), BF16)
    wide_bf16 = shape((rows, model), BF16)
    hidden_bf16 = shape((rows, hidden), BF16)
    vector = shape((1, model), F32)
    hidden_vector = shape((1, hidden), F32)
    h0, attn_in, g_y1, g_shrunk1 = run(
        "enter",
        enter_body,
        [own_f32, wide_bf16, own_f32, wide_bf16],
        [tokens[:, 0], cotangent[:, 0], mod0, mod1],
        place,
    )

    def attention(attn_rows, weight, bias):
        qkv, probs, mixed, partial = run(
            "attention",
            attn_body,
            [
                shape((rows, 3 * width), BF16),
                shape((width // HEAD, rows, rows), F32),
                shape((rows, width), BF16),
                wide_bf16,
            ],
            [attn_rows, weight[0], weight[1], bias],
            place,
        )
        return (attn_rows, qkv, probs, mixed), trade(partial, "tensor")

    def middle_of(parts, bias, h, mod):
        return run(
            "middle", middle_body, [own_f32, own_f32, wide_bf16], [parts, bias, h, mod]
        )

    kept_attn0, parts = attention(trade(attn_in, "tensor"), weights[0][0], biases[0][0])
    attended0, middle0, mlp_in = middle_of(parts, biases[0][1], h0, mod0)
    mlp_rows0 = trade(mlp_in, "tensor")
    pre0, hidden0, partial = run(
        "feed_forward",
        mlp_body,
        [shape((rows, hidden), F32), hidden_bf16, wide_bf16],
        [mlp_rows0, weights[0][1][0], weights[0][1][1], biases[0][2]],
    )
    shrunk0, passed, h1, attn_in = run(
        "between",
        between_body,
        [own_f32, own_bf16, own_f32, wide_bf16],
        [trade(partial, "tensor"), biases[0][3], middle0, mod0, mod1],
    )

    g_rows1 = trade(g_shrunk1, "tensor")
    kept_attn1, parts = attention(trade(attn_in, "tensor"), weights[1][0], biases[1][0])
    attended1, middle1, mlp_in = middle_of(parts, biases[1][1], h1, mod1)
    mlp_rows1 = trade(mlp_in, "tensor")
    hidden1, g_pre1, expand_grad1, y_partial, g_partial = run(
        "feed_forward_both",
        mlp_both_body,
        [hidden_bf16, hidden_bf16, hidden_vector, wide_bf16, wide_bf16],
        [mlp_rows1, g_rows1, weights[1][1][0], weights[1][1][1], biases[1][2]],
    )

    def middle_back(parts, middle, mod, g_y, attended):
        return run(
            "middle_back",
            middle_back_body,
            [own_f32, wide_bf16] + [vector] * 4,
            [parts, middle, mod, g_y, attended],
        )

    def attention_back(g_rows, weight, kept):
        return run(
            "attention_back",
            attn_back_body,
            [shape((rows, 3 * width), BF16), shape((1, 2 * width), F32), wide_bf16],
            [g_rows, weight[0], weight[1], kept[1], kept[2]],
            place,
        )

    def mlp_weight_grads(mlp_rows, g_pre, g_rows, hidden_rows):
        return run(
            "mlp_weight_grads",
            mlp_weights_body,
            [shape((model, hidden), F32), shape((model, hidden), BF16)],
            [mlp_rows, g_pre, g_rows, hidden_rows],
        )

    def attn_weight_grads(kept, g_joint, g_rows):
        return run(
            "attn_weight_grads",
            attn_weights_body,
            [shape((model, 2 * width), F32), shape((model, 2 * width), BF16)],
            [kept[0], g_joint, g_rows, kept[3]],
            place,
        )

    def line_parts(keep, received):
        if not direct:
            return None, (keep + received.astype(F32)).astype(BF16), None
        wide = keep.shape[1]
        return run(
            "line_parts",
            line_parts_body,
            [shape((2, chunk, wide), BF16), shape((chunk, wide), F32), shape((chunk, wide), F32)],
            [keep, received],
            place,
        )

    def line_near(parts):
        return swap(parts[0], "dp", 1) if direct else parts[1]

    def line_far(parts, near):
        if not direct:
            return near
        return swap((parts[1] + near[1].astype(F32)).astype(BF16), "dp", 2)

    def line_total(parts, near, far):
        if not direct:
            return lax.psum_scatter(far, "dp", scatter_dimension=0, tiled=True).astype(F32)
        return parts[2] + near[0].astype(F32) + far.astype(F32)

    y_parts = trade(y_partial, "tensor")
    g_parts = trade(g_partial, "tensor")
    keep_m1, give_m1 = mlp_weight_grads(mlp_rows1, g_pre1, g_rows1, hidden1)
    g_parts, give_m1 = tie(g_parts, give_m1)
    g_middle1, g_attended, g_shift_mlp1, g_scale_mlp1, g_gate_attn1, out_grad1 = middle_back(
        g_parts, middle1, mod1, g_y1, attended1
    )
    g_rows = trade(g_attended, "tensor")
    got_m1 = swap(give_m1, "pipe", 1)
    g_rows, got_m1 = tie(g_rows, got_m1)
    g_joint, joint_grad1, partial = attention_back(g_rows, weights[1][0], kept_attn1)
    parts = trade(partial, "tensor")
    parts_m1 = line_parts(keep_m1, got_m1)
    keep_a1, give_a1 = attn_weight_grads(kept_attn1, g_joint, g_rows)
    parts, parts_m1, give_a1 = tie(parts, parts_m1, give_a1)
    g_passed, g_y0, g_shrunk0, g_shift_attn1, g_scale_attn1, g_gate_mlp0, shrink_grad0 = run(
        "between_back",
        between_back_body,
        [own_bf16, own_f32, wide_bf16] + [vector] * 4,
        [parts, h1, mod1, mod0, g_middle1, shrunk0],
    )
    g_rows0 = trade(g_shrunk0, "tensor")
    near_m1 = line_near(parts_m1)
    got_a1 = swap(give_a1, "pipe", 1)
    g_rows0, got_a1 = tie(g_rows0, got_a1)

    g_pre0, expand_grad0, partial = run(
        "feed_forward_back",
        mlp_back_body,
        [hidden_bf16, hidden_vector, wide_bf16],
        [g_rows0, weights[0][1][0], weights[0][1][1], pre0],
    )
    parts = trade(partial, "tensor")
    parts_a1 = line_parts(keep_a1, got_a1)
    keep_m0, give_m0 = mlp_weight_grads(mlp_rows0, g_pre0, g_rows0, hidden0)
    parts, near_m1, parts_a1, give_m0 = tie(parts, near_m1, parts_a1, give_m0)
    g_middle0, g_attended, g_shift_mlp0, g_scale_mlp0, g_gate_attn0, out_grad0 = middle_back(
        parts, middle0, mod0, g_y0, attended0
    )
    g_rows = trade(g_attended, "tensor")
    far_m1 = line_far(parts_m1, near_m1)
    near_a1 = line_near(parts_a1)
    got_m0 = swap(give_m0, "pipe", 1)
    g_rows, got_m0 = tie(g_rows, got_m0)
    y1, g_gate_mlp1, shrink_grad1 = run(
        "leave",
        leave_body,
        [own_bf16, vector, vector],
        [y_parts, biases[1][3], middle1, mod1, g_y1],
    )
    g_joint, joint_grad0, partial = attention_back(g_rows, weights[0][0], kept_attn0)
    parts = trade(partial, "tensor")
    parts_m0 = line_parts(keep_m0, got_m0)
    keep_a0, give_a0 = attn_weight_grads(kept_attn0, g_joint, g_rows)
    parts, far_m1, near_a1, parts_m0, give_a0 = tie(parts, far_m1, near_a1, parts_m0, give_a0)
    g_h0, g_shift_attn0, g_scale_attn0 = run(
        "finish_back", finish_back_body, [own_bf16, vector, vector], [parts, h0, mod0, g_middle0]
    )
    near_m0 = line_near(parts_m0)
    far_a1 = line_far(parts_a1, near_a1)
    parts_a0 = line_parts(keep_a0, swap(give_a0, "pipe", 1))
    near_a0 = line_near(parts_a0)
    far_m0 = line_far(parts_m0, near_m0)
    far_a0 = line_far(parts_a0, near_a0)
    mlp_grad1 = line_total(parts_m1, near_m1, far_m1)
    attn_grad1 = line_total(parts_a1, near_a1, far_a1)
    mlp_grad0 = line_total(parts_m0, near_m0, far_m0)
    attn_grad0 = line_total(parts_a0, near_a0, far_a0)

    def own_layer_of_micros(pair):
        return jnp.stack(both_layers(mine(pair), swap(other(pair), "pipe", 1)))

    layer_outputs = own_layer_of_micros((passed, y1))
    input_grads = own_layer_of_micros((g_h0, g_passed))

    def own_columns(pair):
        return both_layers(mine(pair), swap(other(pair), "pipe", 1))

    mlp_halves = own_columns((mlp_grad0, mlp_grad1))
    half = hidden // 2
    expand_w_grad = jnp.concatenate([part[:, :half] for part in mlp_halves], axis=1)
    shrink_w_grad = jnp.concatenate([part[:, half:] for part in mlp_halves], axis=1).T
    front, back = own_columns((attn_grad0, attn_grad1))
    joint_w_grad = jnp.concatenate([front, back[:, :width]], axis=1).reshape(chunk, 3, width)
    output_w_grad = back[:, width:].T

    packed = run(
        "pack_grads",
        pack_body,
        [shape((2, mods + 2 * model), F32)],
        [
            g_shift_attn0,
            g_scale_attn0,
            g_gate_attn0,
            g_shift_mlp0,
            g_scale_mlp0,
            g_gate_mlp0,
            out_grad0,
            shrink_grad0,
            g_shift_attn1,
            g_scale_attn1,
            g_gate_attn1,
            g_shift_mlp1,
            g_scale_mlp1,
            g_gate_mlp1,
            out_grad1,
            shrink_grad1,
        ],
    )[0]
    keep, give = run(
        "grads_sum",
        functools.partial(grads_sum_body, count),
        [shape((1, mods + bias_width), F32)] * 2,
        gather(packed, "tensor") + [joint_grad0, expand_grad0, joint_grad1, expand_grad1],
        place,
    )
    joined = run(
        "grads_join",
        grads_join_body,
        [shape((1, 2 * mods + bias_width), F32)],
        [keep, swap(give, "pipe", 1)],
        place,
    )[0]
    if direct:
        outs = run(
            "mod_back",
            mod_back_body,
            [shape(own_rows.shape, F32), shape((1, mods), F32), shape((1, bias_width), F32)]
            + [shape((micro, own_rows.shape[0]), F32)] * LINE,
            gather(joined, "dp") + activated_all + [own_rows],
            place,
        )
        ada_grad, ada_bias_grad, bias_sum = outs[:3]
        act_grad = tree_sum(exchange(outs[3:], "dp"))
    else:
        joined_all = lax.all_gather(joined, "dp", axis=0, tiled=True)
        mod_grads = joined_all[:, : 2 * mods].reshape(line_size * micro, mods)
        bias_sum = jnp.sum(joined_all[:, 2 * mods :], axis=0, keepdims=True)
        ada_bias_grad = jnp.sum(mod_grads, axis=0, keepdims=True)
        picked = lax.dynamic_slice_in_dim(mod_grads, line * columns, columns, 1).astype(BF16)
        ada_grad = t_dot(activated_all, picked)
        act_partial = dot_t(picked, own_rows).reshape(line_size, micro, -1)
        act_grad = lax.psum_scatter(act_partial, "dp", scatter_dimension=0, tiled=False)
    _, silu_back = jax.vjp(jax.nn.silu, conditions[:, 0].astype(F32))
    cond_grad = silu_back(act_grad)[0]
    at = 2 * width
    return (
        layer_outputs[None, :, None],
        input_grads[None, :, None],
        cond_grad[None, :, None],
        ada_grad[None],
        ada_bias_grad,
        joint_w_grad[None],
        bias_sum[:, :at].reshape(1, 2, width),
        output_w_grad[None],
        bias_sum[:, at + hidden : at + hidden + model],
        expand_w_grad[None],
        bias_sum[:, at : at + hidden],
        shrink_w_grad[None],
        bias_sum[:, at + hidden + model :],
    )


def solution(mesh):
    in_specs = (
        P(None, "dp", "tensor", None),
        P(None, "dp", "tensor"),
        P(None, "dp", "tensor", None),
        P("pipe", "tensor", "dp"),
        P("pipe", None),
        P("pipe", "dp", None, "tensor"),
        P("pipe", None, "tensor"),
        P("pipe", "tensor", "dp"),
        P("pipe", None),
        P("pipe", "dp", "tensor"),
        P("pipe", "tensor"),
        P("pipe", "tensor", "dp"),
        P("pipe", None),
    )
    out_specs = (
        P("pipe", None, "dp", "tensor", None),
        P("pipe", None, "dp", "tensor", None),
        P("pipe", None, "dp", "tensor"),
        P("pipe", "tensor", "dp"),
        P("pipe", None),
        P("pipe", "dp", None, "tensor"),
        P("pipe", None, "tensor"),
        P("pipe", "tensor", "dp"),
        P("pipe", None),
        P("pipe", "dp", "tensor"),
        P("pipe", "tensor"),
        P("pipe", "tensor", "dp"),
        P("pipe", None),
    )
    return jax.shard_map(
        on_device, mesh=mesh, in_specs=in_specs, out_specs=out_specs, check_vma=False
    )
```

```python
import functools

import jax
import jax.numpy as jnp
from jax import lax
from jax.experimental import pallas as pl
from jax.experimental.pallas import tpu as pltpu
from jax.sharding import PartitionSpec as P

HEAD = 64
EPS = 1e-06
F32 = jnp.float32
BF16 = jnp.bfloat16
LINE = 4
VMEM_BYTES = 24 * 1024 * 1024
GELU_A = 0.7978845608028654
GELU_B = 0.044715


def swap(value, axis, mask):
    pairs = [(source, source ^ mask) for source in range(lax.axis_size(axis))]
    return lax.ppermute(value, axis, pairs)


def exchange(parts, axis):
    received = {k: swap(parts[k], axis, k) for k in range(len(parts) - 1, 0, -1)}
    return [parts[0]] + [received[k] for k in range(1, len(parts))]


def gather(value, axis):
    return exchange([value] * lax.axis_size(axis), axis)


def tree_sum(parts):
    parts = list(parts)
    while len(parts) > 1:
        parts = [parts[k] + parts[k + 1] for k in range(0, len(parts), 2)]
    return parts[0]


def shape(dims, dtype):
    return jax.ShapeDtypeStruct(dims, dtype)


def run(name, body, outs, args, place=None):
    specs = [pl.BlockSpec(memory_space=pltpu.VMEM) for _ in args]
    if place is not None:
        specs = [pl.BlockSpec(memory_space=pltpu.SMEM)] + specs
        args = [place] + list(args)
    return pl.pallas_call(
        body,
        out_shape=outs,
        in_specs=specs,
        out_specs=[pl.BlockSpec(memory_space=pltpu.VMEM) for _ in outs],
        compiler_params=pltpu.CompilerParams(vmem_limit_bytes=VMEM_BYTES),
        name=name,
    )(*args)


def dot(left, right):
    return jnp.dot(left, right, preferred_element_type=F32)


def dot_t(left, right):
    return lax.dot_general(left, right, (((1,), (1,)), ((), ())), preferred_element_type=F32)


def t_dot(left, right):
    return lax.dot_general(left, right, (((0,), (0,)), ((), ())), preferred_element_type=F32)


def normalize(values):
    centred = values - jnp.mean(values, axis=-1, keepdims=True)
    rstd = lax.rsqrt(jnp.mean(centred * centred, axis=-1, keepdims=True) + EPS)
    return centred * rstd, rstd


def normalize_back(grad, normed, rstd):
    return rstd * (
        grad
        - jnp.mean(grad, axis=-1, keepdims=True)
        - normed * jnp.mean(grad * normed, axis=-1, keepdims=True)
    )


def total(refs):
    return tree_sum([ref[...].astype(F32) for ref in refs])


def column_sum(values):
    return jnp.sum(values, axis=0, keepdims=True)


def part(mod_ref, index):
    width = mod_ref.shape[1] // 6
    return mod_ref[:, index * width : (index + 1) * width]


def gelu(pre):
    return 0.5 * pre * (1.0 + jnp.tanh(GELU_A * (pre + GELU_B * (pre * pre * pre))))


def gelu_slope(pre):
    square = pre * pre
    bent = jnp.tanh(GELU_A * (pre + GELU_B * (square * pre)))
    return 0.5 * (1.0 + bent) + 0.5 * pre * (1.0 - bent * bent) * (
        GELU_A * (1.0 + 3.0 * GELU_B * square)
    )


def put_rows(ref, refs):
    own = refs[0].shape[0]
    for k, source in enumerate(refs):
        ref[k * own : (k + 1) * own] = source[...]
    return ref[...]


def put_blocks(refs, values):
    own = refs[0].shape[0]
    for k, ref in enumerate(refs):
        ref[...] = values[k * own : (k + 1) * own].astype(ref.dtype)


def enter_body(place, tokens, cotangent, mod0, mod1, h_out, attn_in, g_y_out, g_shrunk):
    core = place[0]
    h = tokens[core].astype(F32)
    h_out[...] = h
    normed, _ = normalize(h)
    attn_in[...] = (normed * (1.0 + part(mod0, 1)) + part(mod0, 0)).astype(BF16)
    g_y = cotangent[core].astype(F32)
    g_y_out[...] = g_y
    g_shrunk[...] = (part(mod1, 5) * g_y).astype(BF16)


def pick_attn(place, own, received):
    first = place[0] == 0
    width = own.shape[1] // 2
    mine, other = own[...], received[...]
    front = jnp.where(first, mine, other)
    back = jnp.where(first, other, mine)
    return front, back[:, :width], back[:, width:]


def attn_body(count, place, *refs):
    chunks = refs[:count]
    w_own, w_received, bias = refs[count : count + 3]
    rows_out, qkv_out, probs_out, mixed_out = refs[count + 3 : count + 7]
    partial = refs[count + 7 :]
    rows = put_rows(rows_out, chunks)
    w_front, w_value, w_out = pick_attn(place, w_own, w_received)
    width = w_value.shape[1]
    front = (dot(rows, w_front) + bias[:, : 2 * width]).astype(BF16)
    value = (dot(rows, w_value) + bias[:, 2 * width :]).astype(BF16)
    qkv_out[:, : 2 * width] = front
    qkv_out[:, 2 * width :] = value
    mixed = []
    for head in range(width // HEAD):
        at = head * HEAD
        query = front[:, at : at + HEAD]
        key = front[:, width + at : width + at + HEAD]
        scores = dot_t(query, key) * HEAD**-0.5
        powers = jnp.exp(scores - jnp.max(scores, axis=-1, keepdims=True))
        probs = powers / jnp.sum(powers, axis=-1, keepdims=True)
        probs_out[head] = probs
        mixed.append(dot(probs.astype(BF16), value[:, at : at + HEAD]))
    mixed = jnp.concatenate(mixed, axis=1).astype(BF16)
    mixed_out[...] = mixed
    put_blocks(partial, dot_t(mixed, w_out))


def middle_body(count, *refs):
    parts, (bias, h, mod, attended_out, middle_out, mlp_in) = refs[:count], refs[count:]
    attended = total(parts) + bias[...]
    attended_out[...] = attended
    middle = h[...] + part(mod, 2) * attended
    middle_out[...] = middle
    normed, _ = normalize(middle)
    mlp_in[...] = (normed * (1.0 + part(mod, 4)) + part(mod, 3)).astype(BF16)


def mlp_body(count, *refs):
    chunks = refs[:count]
    w_own, w_received, bias, rows_out, pre_out, hidden_out = refs[count : count + 6]
    partial = refs[count + 6 :]
    rows = put_rows(rows_out, chunks)
    half = w_own.shape[1] // 2
    shrunk = None
    for index, weight in enumerate((w_own, w_received)):
        at = index * half
        pre = dot(rows, weight[:, :half]) + bias[:, at : at + half]
        pre_out[:, at : at + half] = pre
        hidden = gelu(pre).astype(BF16)
        hidden_out[:, at : at + half] = hidden
        term = dot_t(hidden, weight[:, half:])
        shrunk = term if shrunk is None else shrunk + term
    put_blocks(partial, shrunk)


def mlp_both_body(count, *refs):
    chunks, g_chunks = refs[:count], refs[count : 2 * count]
    w_own, w_received, bias, rows_out, g_rows_out, hidden_out, g_pre_out, bias_grad = refs[
        2 * count : 2 * count + 8
    ]
    partial = refs[2 * count + 8 : 3 * count + 8]
    g_partial = refs[3 * count + 8 :]
    rows = put_rows(rows_out, chunks)
    g_rows = put_rows(g_rows_out, g_chunks)
    half = w_own.shape[1] // 2
    shrunk, g_in = None, None
    for index, weight in enumerate((w_own, w_received)):
        at = index * half
        pre = dot(rows, weight[:, :half]) + bias[:, at : at + half]
        hidden = gelu(pre).astype(BF16)
        hidden_out[:, at : at + half] = hidden
        g_pre = (dot(g_rows, weight[:, half:]) * gelu_slope(pre)).astype(BF16)
        g_pre_out[:, at : at + half] = g_pre
        bias_grad[:, at : at + half] = column_sum(g_pre.astype(F32))
        term = dot_t(hidden, weight[:, half:])
        g_term = dot_t(g_pre, weight[:, :half])
        shrunk = term if shrunk is None else shrunk + term
        g_in = g_term if g_in is None else g_in + g_term
    put_blocks(g_partial, g_in)
    put_blocks(partial, shrunk)


def mlp_back_body(count, *refs):
    g_chunks = refs[:count]
    w_own, w_received, pre_ref, g_rows_out, g_pre_out, bias_grad = refs[count : count + 6]
    g_partial = refs[count + 6 :]
    g_rows = put_rows(g_rows_out, g_chunks)
    half = w_own.shape[1] // 2
    g_in = None
    for index, weight in enumerate((w_own, w_received)):
        at = index * half
        pre = pre_ref[:, at : at + half]
        g_pre = (dot(g_rows, weight[:, half:]) * gelu_slope(pre)).astype(BF16)
        g_pre_out[:, at : at + half] = g_pre
        bias_grad[:, at : at + half] = column_sum(g_pre.astype(F32))
        g_term = dot_t(g_pre, weight[:, :half])
        g_in = g_term if g_in is None else g_in + g_term
    put_blocks(g_partial, g_in)


def between_body(count, *refs):
    parts = refs[:count]
    bias, middle, mod0, mod1, shrunk_out, passed_out, h_out, attn_in = refs[count:]
    shrunk = total(parts) + bias[...]
    shrunk_out[...] = shrunk
    passed = (middle[...] + part(mod0, 5) * shrunk).astype(BF16)
    passed_out[...] = passed
    h = passed.astype(F32)
    h_out[...] = h
    normed, _ = normalize(h)
    attn_in[...] = (normed * (1.0 + part(mod1, 1)) + part(mod1, 0)).astype(BF16)


def leave_body(count, *refs):
    parts = refs[:count]
    bias, middle, mod, g_y_ref, g_shrunk, y_out, g_gate, bias_grad = refs[count:]
    shrunk = total(parts) + bias[...]
    y_out[...] = (middle[...] + part(mod, 5) * shrunk).astype(BF16)
    g_gate[...] = column_sum(g_y_ref[...] * shrunk)
    bias_grad[...] = column_sum(g_shrunk[...].astype(F32))


def middle_back_body(count, *refs):
    parts = refs[:count]
    middle, mod, g_y, attended, g_middle_out, g_attended_out, g_shift, g_scale, g_gate, bias_grad = refs[
        count:
    ]
    g_in = total(parts)
    normed, rstd = normalize(middle[...])
    g_shift[...] = column_sum(g_in)
    g_scale[...] = column_sum(g_in * normed)
    g_middle = g_y[...] + normalize_back(g_in * (1.0 + part(mod, 4)), normed, rstd)
    g_middle_out[...] = g_middle
    g_gate[...] = column_sum(g_middle * attended[...])
    g_attended = (part(mod, 2) * g_middle).astype(BF16)
    g_attended_out[...] = g_attended
    bias_grad[...] = column_sum(g_attended.astype(F32))


def attn_back_body(count, place, *refs):
    g_chunks = refs[:count]
    w_own, w_received, qkv, probs_ref = refs[count : count + 4]
    g_rows_out, g_joint_out, bias_grad = refs[count + 4 : count + 7]
    g_partial = refs[count + 7 :]
    g_rows = put_rows(g_rows_out, g_chunks)
    w_front, w_value, w_out = pick_attn(place, w_own, w_received)
    width = w_value.shape[1]
    g_mixed = dot(g_rows, w_out).astype(BF16)
    g_query, g_key, g_value = [], [], []
    for head in range(width // HEAD):
        at = head * HEAD
        query = qkv[:, at : at + HEAD]
        key = qkv[:, width + at : width + at + HEAD]
        value = qkv[:, 2 * width + at : 2 * width + at + HEAD]
        probs = probs_ref[head]
        g_head = g_mixed[:, at : at + HEAD]
        g_probs = dot_t(g_head, value)
        row_dot = jnp.sum(probs * g_probs, axis=-1, keepdims=True)
        g_scores = (probs * (g_probs - row_dot)).astype(BF16)
        g_value.append(t_dot(probs.astype(BF16), g_head))
        g_query.append(dot(g_scores, key) * HEAD**-0.5)
        g_key.append(t_dot(g_scores, query) * HEAD**-0.5)
    g_front = jnp.concatenate(g_query + g_key, axis=1).astype(BF16)
    g_value = jnp.concatenate(g_value, axis=1).astype(BF16)
    g_joint_out[:, : 2 * width] = g_front
    g_joint_out[:, 2 * width :] = g_value
    bias_grad[:, :width] = column_sum(g_front[:, :width].astype(F32))
    bias_grad[:, width:] = column_sum(g_value.astype(F32))
    put_blocks(g_partial, dot_t(g_front, w_front) + dot_t(g_value, w_value))


def input_grad(parts, h, mod, g_middle, g_shift, g_scale):
    g_in = total(parts)
    normed, rstd = normalize(h[...])
    g_shift[...] = column_sum(g_in)
    g_scale[...] = column_sum(g_in * normed)
    return (g_middle[...] + normalize_back(g_in * (1.0 + part(mod, 1)), normed, rstd)).astype(BF16)


def between_back_body(count, *refs):
    parts = refs[:count]
    h, mod1, mod0, g_middle, shrunk, g_h_out, g_y_out, g_shrunk_out = refs[count : count + 8]
    g_shift, g_scale, g_gate, bias_grad = refs[count + 8 :]
    g_h = input_grad(parts, h, mod1, g_middle, g_shift, g_scale)
    g_h_out[...] = g_h
    g_y = g_h.astype(F32)
    g_y_out[...] = g_y
    g_gate[...] = column_sum(g_y * shrunk[...])
    g_shrunk = (part(mod0, 5) * g_y).astype(BF16)
    g_shrunk_out[...] = g_shrunk
    bias_grad[...] = column_sum(g_shrunk.astype(F32))


def finish_back_body(count, *refs):
    parts = refs[:count]
    h, mod, g_middle, g_h_out, g_shift, g_scale = refs[count:]
    g_h_out[...] = input_grad(parts, h, mod, g_middle, g_shift, g_scale)


def mlp_weights_body(rows, g_pre, g_rows, hidden, keep, give):
    half = keep.shape[1] // 2
    keep[:, :half] = t_dot(rows[...], g_pre[:, :half])
    keep[:, half:] = t_dot(g_rows[...], hidden[:, :half])
    give[:, :half] = t_dot(rows[...], g_pre[:, half:]).astype(BF16)
    give[:, half:] = t_dot(g_rows[...], hidden[:, half:]).astype(BF16)


def attn_weights_body(place, rows, g_joint, g_rows, mixed, keep, give):
    width = mixed.shape[1]
    first = place[0] == 0
    front = t_dot(rows[...], g_joint[:, : 2 * width])
    back = jnp.concatenate(
        [t_dot(rows[...], g_joint[:, 2 * width :]), t_dot(g_rows[...], mixed[...])], axis=1
    )
    keep[...] = jnp.where(first, front, back)
    give[...] = jnp.where(first, back, front).astype(BF16)


def line_blocks(place, k, rows):
    return pl.ds(pl.multiple_of((place[1] ^ k) * rows, 16), rows)


def stack_body(place, *refs):
    out = refs[-1]
    for k, ref in enumerate(refs[:-1]):
        out[line_blocks(place, k, ref.shape[0])] = ref[...]


def line_parts_body(place, keep, received, near, far, own):
    rows = own.shape[0]

    def block(k):
        at = line_blocks(place, k, rows)
        return keep[at] + received[at].astype(F32)

    near[0] = block(1).astype(BF16)
    near[1] = block(3).astype(BF16)
    far[...] = block(2)
    own[...] = block(0)


def line_total_body(place, own0, near0, far0, own1, near1, far1, mine, give):
    first = place[0] == 0
    total0 = own0[...] + near0[0].astype(F32) + far0[...].astype(F32)
    total1 = own1[...] + near1[0].astype(F32) + far1[...].astype(F32)
    mine[...] = jnp.where(first, total0, total1)
    give[...] = jnp.where(first, total1, total0)


def final_mlp_body(place, mine, received, expand_out, shrink_out):
    first = place[0] == 0
    half = mine.shape[1] // 2
    own, other = mine[...], received[...]
    for index, values in enumerate((jnp.where(first, own, other), jnp.where(first, other, own))):
        expand_out[:, index * half : (index + 1) * half] = values[:, :half]
        shrink_out[index * half : (index + 1) * half] = values[:, half:].T


def final_attn_body(place, mine, received, joint_out, out_out):
    first = place[0] == 0
    width = mine.shape[1] // 2
    own, other = mine[...], received[...]
    front, back = jnp.where(first, own, other), jnp.where(first, other, own)
    joint_out[:, : 2 * width] = front
    joint_out[:, 2 * width :] = back[:, :width]
    out_out[...] = back[:, width:].T


def mod_first_body(a0, a1, a2, a3, weight, out):
    rows = jnp.concatenate([a0[...], a1[...], a2[...], a3[...]], axis=0)
    out[...] = dot(rows, weight[...])


def mod_sum_body(count, *refs):
    values = total(refs[:count])
    outs = refs[count:]
    micro = outs[0].shape[0]
    for k, out in enumerate(outs):
        out[...] = values[k * micro : (k + 1) * micro]


def mod_join_body(place, p0, p1, p2, p3, bias, mine, other, scratch):
    for k, ref in enumerate((p0, p1, p2, p3)):
        scratch[place[1] ^ k] = ref[...]
    values = jnp.concatenate([scratch[j] for j in range(LINE)], axis=1) + bias[...]
    first = place[0] == 0
    mine[...] = jnp.where(first, values[0:1], values[1:2])
    other[...] = jnp.where(first, values[1:2], values[0:1])


def pack_body(*refs):
    out, pieces = refs[-1], refs[:-1]
    count = len(pieces) // 2
    for row in range(2):
        at = 0
        for ref in pieces[row * count : (row + 1) * count]:
            out[row : row + 1, at : at + ref.shape[1]] = ref[...]
            at += ref.shape[1]


def grads_sum_body(count, place, *refs):
    parts = refs[:count]
    joint0, expand0, joint1, expand1, keep, give = refs[count:]
    first = place[0] == 0
    values = total(parts)
    hidden = expand0.shape[1]
    mod_width = values.shape[1] // 8 * 6
    rounded = values[:, :mod_width].astype(BF16).astype(F32)
    sums = values[:, mod_width:]
    half = hidden // 2

    def natural(ref):
        now = ref[...]
        return jnp.where(first, now, jnp.concatenate([now[:, half:], now[:, :half]], axis=1))

    rows = []
    for row, (joint, expand) in enumerate(((joint0, expand0), (joint1, expand1))):
        rows.append(
            jnp.concatenate(
                [rounded[row : row + 1], joint[...], natural(expand), sums[row : row + 1]], axis=1
            )
        )
    keep[...] = jnp.where(first, rows[0], rows[1])
    give[...] = jnp.where(first, rows[1], rows[0])


def grads_join_body(place, keep, received, out):
    mods = out.shape[1] - keep.shape[1]
    first = place[0] == 0
    own, other = keep[...], received[...]
    out[:, :mods] = jnp.where(first, own, other)[:, :mods]
    out[:, mods : 2 * mods] = jnp.where(first, other, own)[:, :mods]
    out[:, 2 * mods :] = own[:, mods:] + other[:, mods:]


def mod_back_body(place, g0, g1, g2, g3, a0, a1, a2, a3, weight, w_grad, b_grad, bias, c0, c1, c2, c3):
    columns = weight.shape[1]
    mods = columns * LINE
    grads = (g0, g1, g2, g3)
    at = pl.multiple_of(place[1] * columns, 128)
    rows = []
    for ref in grads:
        rows.append(ref[:, pl.ds(at, columns)])
        rows.append(ref[:, pl.ds(pl.multiple_of(at + mods, 128), columns)])
    picked = jnp.concatenate(rows, axis=0).astype(BF16)
    activated = jnp.concatenate([a0[...], a1[...], a2[...], a3[...]], axis=0)
    w_grad[...] = t_dot(activated, picked)
    act = dot_t(picked, weight[...])
    for k, out in enumerate((c0, c1, c2, c3)):
        out[...] = act[2 * k : 2 * k + 2]
    b_grad[...] = tree_sum([ref[:, :mods] + ref[:, mods : 2 * mods] for ref in grads])
    bias[...] = tree_sum([ref[:, 2 * mods :] for ref in grads])


def on_device(
    tokens,
    conditions,
    cotangent,
    modulation_weight,
    modulation_bias,
    joint_weight,
    joint_bias,
    output_weight,
    output_bias,
    expand_weight,
    expand_bias,
    shrink_weight,
    shrink_bias,
):
    core = lax.axis_index("pipe")
    first = core == 0
    line = lax.axis_index("dp")
    place = jnp.stack([core, line]).astype(jnp.int32)
    line_size = lax.axis_size("dp")
    count = lax.axis_size("tensor")
    direct = line_size == LINE
    micro, _, own, model = tokens.shape
    width = output_weight.shape[1]
    hidden = expand_weight.shape[2]
    chunk = model // line_size
    rows = own * count
    columns = modulation_weight.shape[2]
    mods = 6 * model
    bias_width = 2 * width + hidden + 2 * model
    own_rows = modulation_weight[0]

    def mine(pair):
        return jnp.where(first, pair[0], pair[1])

    def other(pair):
        return jnp.where(first, pair[1], pair[0])

    def both_layers(kept, received):
        return jnp.where(first, kept, received), jnp.where(first, received, kept)

    def after(value, earlier):
        return lax.optimization_barrier((value, earlier))[0]

    def tie(*values):
        return lax.optimization_barrier(values)

    attn_pack = jnp.concatenate(
        [joint_weight[0].reshape(chunk, 3 * width), output_weight[0].T], axis=1
    )
    shrink_t = shrink_weight[0].T
    expand = expand_weight[0]

    def column_half(index):
        return jnp.concatenate(
            [
                attn_pack[:, index * 2 * width : (index + 1) * 2 * width],
                expand[:, index * (hidden // 2) : (index + 1) * (hidden // 2)],
                shrink_t[:, index * (hidden // 2) : (index + 1) * (hidden // 2)],
            ],
            axis=1,
        )

    halves = (column_half(0), column_half(1))
    halves_of_layers = both_layers(mine(halves), swap(other(halves), "pipe", 1))
    split = 2 * width

    bias_pack = jnp.concatenate(
        [
            joint_bias[0].reshape(-1),
            expand_bias[0],
            output_bias[0],
            shrink_bias[0],
        ]
    )[None]
    bias_layers = both_layers(bias_pack, swap(bias_pack, "pipe", 1))
    biases = []
    for packed in bias_layers:
        at = 2 * width
        joint = jnp.concatenate(
            [packed[:, :width], jnp.zeros((1, width), F32), packed[:, width:at]], axis=1
        )
        grown = packed[:, at : at + hidden]
        rolled = jnp.concatenate([grown[:, hidden // 2 :], grown[:, : hidden // 2]], axis=1)
        grown = jnp.where(first, grown, rolled)
        at += hidden
        biases.append((joint, packed[:, at : at + model], grown, packed[:, at + model :]))

    activated = jax.nn.silu(conditions[:, 0].astype(F32)).astype(BF16)
    if direct:
        activated_all = gather(activated, "dp")
    else:
        activated_all = lax.all_gather(activated, "dp", axis=0).reshape(line_size * micro, -1)

    def along_line(value):
        if direct:
            lined = run(
                "stack_line",
                stack_body,
                [shape((model, value.shape[1]), BF16)],
                gather(value, "dp"),
                place,
            )[0]
        else:
            lined = lax.all_gather(value, "dp", axis=0, tiled=True)
        return lined, swap(lined, "pipe", 1)

    def half_of(layer, mlp):
        return halves_of_layers[layer][:, split:] if mlp else halves_of_layers[layer][:, :split]

    w_attn0 = along_line(after(half_of(0, False), activated_all))

    if direct:
        mod_partial = run(
            "mod_first",
            mod_first_body,
            [shape((micro * LINE, columns), F32)],
            activated_all + [own_rows],
        )[0]
        pieces = run(
            "mod_sum",
            functools.partial(mod_sum_body, count),
            [shape((micro, columns), F32)] * LINE,
            gather(mod_partial, "tensor"),
        )
        mod_mine, mod_other = pl.pallas_call(
            mod_join_body,
            out_shape=[shape((1, mods), F32)] * 2,
            in_specs=[pl.BlockSpec(memory_space=pltpu.SMEM)]
            + [pl.BlockSpec(memory_space=pltpu.VMEM)] * 5,
            out_specs=[pl.BlockSpec(memory_space=pltpu.VMEM)] * 2,
            scratch_shapes=[pltpu.VMEM((LINE, micro, columns), F32)],
            name="mod_join",
        )(place, *exchange(pieces, "dp"), modulation_bias)
    else:
        mod_partial = dot(activated_all, own_rows)
        mod_sum = tree_sum(gather(mod_partial, "tensor")).reshape(line_size, micro, -1)
        mod_layer = lax.all_to_all(mod_sum, "dp", split_axis=0, concat_axis=0)
        mod_layer = jnp.swapaxes(mod_layer, 0, 1).reshape(micro, -1) + modulation_bias
        mod_mine, mod_other = mine(mod_layer)[None], other(mod_layer)[None]
    mod0, mod1 = both_layers(mod_mine, swap(mod_other, "pipe", 1))

    w_mlp0 = along_line(after(half_of(0, True), (mod0, w_attn0[0])))
    own_f32 = shape((own, model), F32)
    own_bf16 = shape((own, model), BF16)
    blocks = [own_bf16] * count
    wide_bf16 = shape((rows, model), BF16)
    hidden_bf16 = shape((rows, hidden), BF16)
    vector = shape((1, model), F32)
    hidden_vector = shape((1, hidden), F32)
    h0, attn_in, g_y1, g_shrunk1 = run(
        "enter",
        enter_body,
        [own_f32, own_bf16, own_f32, own_bf16],
        [tokens[:, 0], cotangent[:, 0], mod0, mod1],
        place,
    )

    def kernel(name, body, outs, args, where=None):
        return run(name, functools.partial(body, count), outs, args, where)

    def attention(attn_rows, weight, bias):
        outs = kernel(
            "attention",
            attn_body,
            [
                wide_bf16,
                shape((rows, 3 * width), BF16),
                shape((width // HEAD, rows, rows), F32),
                shape((rows, width), BF16),
            ]
            + blocks,
            attn_rows + [weight[0], weight[1], bias],
            place,
        )
        return outs[:4], exchange(outs[4:], "tensor")

    def middle_of(parts, bias, h, mod):
        return kernel(
            "middle", middle_body, [own_f32, own_f32, own_bf16], parts + [bias, h, mod]
        )

    kept_attn0, parts = attention(gather(attn_in, "tensor"), w_attn0, biases[0][0])
    attended0, middle0, mlp_in = middle_of(parts, biases[0][1], h0, mod0)
    mlp_rows0, half = tie(gather(mlp_in, "tensor"), half_of(1, False))
    w_attn1 = along_line(half)
    outs = kernel(
        "feed_forward",
        mlp_body,
        [wide_bf16, shape((rows, hidden), F32), hidden_bf16] + blocks,
        mlp_rows0 + [w_mlp0[0], w_mlp0[1], biases[0][2]],
    )
    mlp_rows0, pre0, hidden0 = outs[:3]
    parts, half = tie(exchange(outs[3:], "tensor"), half_of(1, True))
    w_mlp1 = along_line(half)
    shrunk0, passed, h1, attn_in = kernel(
        "between",
        between_body,
        [own_f32, own_bf16, own_f32, own_bf16],
        parts + [biases[0][3], middle0, mod0, mod1],
    )

    g_rows1 = gather(g_shrunk1, "tensor")
    kept_attn1, parts = attention(gather(attn_in, "tensor"), w_attn1, biases[1][0])
    attended1, middle1, mlp_in = middle_of(parts, biases[1][1], h1, mod1)
    outs = kernel(
        "feed_forward_both",
        mlp_both_body,
        [wide_bf16, wide_bf16, hidden_bf16, hidden_bf16, hidden_vector] + blocks + blocks,
        gather(mlp_in, "tensor") + g_rows1 + [w_mlp1[0], w_mlp1[1], biases[1][2]],
    )
    mlp_rows1, g_rows1, hidden1, g_pre1, expand_grad1 = outs[:5]
    y_partial, g_partial = outs[5 : 5 + count], outs[5 + count :]

    def middle_back(parts, middle, mod, g_y, attended):
        return kernel(
            "middle_back",
            middle_back_body,
            [own_f32, own_bf16] + [vector] * 4,
            parts + [middle, mod, g_y, attended],
        )

    def attention_back(g_rows, weight, kept):
        outs = kernel(
            "attention_back",
            attn_back_body,
            [wide_bf16, shape((rows, 3 * width), BF16), shape((1, 2 * width), F32)] + blocks,
            g_rows + [weight[0], weight[1], kept[1], kept[2]],
            place,
        )
        return outs[:3], exchange(outs[3:], "tensor")

    def line_parts(grads):
        keep, give = grads
        received = swap(give, "pipe", 1)
        if not direct:
            return None, (keep + received.astype(F32)).astype(BF16), None
        wide = keep.shape[1]
        return run(
            "line_parts",
            line_parts_body,
            [shape((2, chunk, wide), BF16), shape((chunk, wide), F32), shape((chunk, wide), F32)],
            [keep, received],
            place,
        )

    def mlp_weight_grads(mlp_rows, g_pre, g_rows, hidden_rows):
        return line_parts(
            run(
                "mlp_weight_grads",
                mlp_weights_body,
                [shape((model, hidden), F32), shape((model, hidden), BF16)],
                [mlp_rows, g_pre, g_rows, hidden_rows],
            )
        )

    def attn_weight_grads(kept, g_joint, g_rows):
        return line_parts(
            run(
                "attn_weight_grads",
                attn_weights_body,
                [shape((model, 2 * width), F32), shape((model, 2 * width), BF16)],
                [kept[0], g_joint, g_rows, kept[3]],
                place,
            )
        )

    def line_near(parts):
        return swap(parts[0], "dp", 1) if direct else parts[1]

    def line_far(parts, near):
        if not direct:
            return near
        return swap((parts[1] + near[1].astype(F32)).astype(BF16), "dp", 2)

    def line_total(first_layer, second_layer):
        if not direct:
            sums = [
                lax.psum_scatter(far, "dp", scatter_dimension=0, tiled=True).astype(F32)
                for _, _, far in (first_layer, second_layer)
            ]
            return mine(sums), swap(other(sums), "pipe", 1)
        args = [x for parts, near, far in (first_layer, second_layer) for x in (parts[2], near, far)]
        kept, given = run(
            "line_total", line_total_body, [shape(args[0].shape, F32)] * 2, args, place
        )
        return kept, swap(given, "pipe", 1)

    g_parts, y_partial, parts_m1 = tie(
        exchange(g_partial, "tensor"),
        y_partial,
        mlp_weight_grads(mlp_rows1, g_pre1, g_rows1, hidden1),
    )
    g_middle1, g_attended, g_shift_mlp1, g_scale_mlp1, g_gate_attn1, out_grad1 = middle_back(
        g_parts, middle1, mod1, g_y1, attended1
    )
    near_m1 = line_near(parts_m1)
    y_parts = exchange(y_partial, "tensor")
    (g_rows, g_joint, joint_grad1), parts = attention_back(
        gather(g_attended, "tensor"), w_attn1, kept_attn1
    )
    parts, near_m1, parts_a1 = tie(
        parts, near_m1, attn_weight_grads(kept_attn1, g_joint, g_rows)
    )
    g_passed, g_y0, g_shrunk0, g_shift_attn1, g_scale_attn1, g_gate_mlp0, shrink_grad0 = kernel(
        "between_back",
        between_back_body,
        [own_bf16, own_f32, own_bf16] + [vector] * 4,
        parts + [h1, mod1, mod0, g_middle1, shrunk0],
    )
    far_m1 = line_far(parts_m1, near_m1)
    near_a1 = line_near(parts_a1)

    outs = kernel(
        "feed_forward_back",
        mlp_back_body,
        [wide_bf16, hidden_bf16, hidden_vector] + blocks,
        gather(g_shrunk0, "tensor") + [w_mlp0[0], w_mlp0[1], pre0],
    )
    g_rows0, g_pre0, expand_grad0 = outs[:3]
    parts, far_m1, near_a1, parts_m0 = tie(
        exchange(outs[3:], "tensor"),
        far_m1,
        near_a1,
        mlp_weight_grads(mlp_rows0, g_pre0, g_rows0, hidden0),
    )
    g_middle0, g_attended, g_shift_mlp0, g_scale_mlp0, g_gate_attn0, out_grad0 = middle_back(
        parts, middle0, mod0, g_y0, attended0
    )
    near_m0 = line_near(parts_m0)
    far_a1 = line_far(parts_a1, near_a1)
    y1, g_gate_mlp1, shrink_grad1 = kernel(
        "leave",
        leave_body,
        [own_bf16, vector, vector],
        y_parts + [biases[1][3], middle1, mod1, g_y1, g_shrunk1],
    )
    (g_rows, g_joint, joint_grad0), parts = attention_back(
        gather(g_attended, "tensor"), w_attn0, kept_attn0
    )
    parts, far_a1, near_m0, parts_a0 = tie(
        parts, far_a1, near_m0, attn_weight_grads(kept_attn0, g_joint, g_rows)
    )
    g_h0, g_shift_attn0, g_scale_attn0 = kernel(
        "finish_back",
        finish_back_body,
        [own_bf16, vector, vector],
        parts + [h0, mod0, g_middle0],
    )
    far_m0 = line_far(parts_m0, near_m0)
    near_a0 = line_near(parts_a0)
    far_a0 = line_far(parts_a0, near_a0)
    mlp_halves = line_total((parts_m0, near_m0, far_m0), (parts_m1, near_m1, far_m1))
    attn_halves = line_total((parts_a0, near_a0, far_a0), (parts_a1, near_a1, far_a1))
    expand_w_grad, shrink_w_grad = run(
        "final_mlp",
        final_mlp_body,
        [shape((chunk, hidden), F32), shape((hidden, chunk), F32)],
        mlp_halves,
        place,
    )
    joint_w_grad, output_w_grad = run(
        "final_attn",
        final_attn_body,
        [shape((chunk, 3 * width), F32), shape((width, chunk), F32)],
        attn_halves,
        place,
    )
    joint_w_grad = joint_w_grad.reshape(chunk, 3, width)

    def own_layer_of_micros(pair):
        return jnp.stack(both_layers(mine(pair), swap(other(pair), "pipe", 1)))

    layer_outputs = own_layer_of_micros((passed, y1))
    input_grads = own_layer_of_micros((g_h0, g_passed))

    packed = run(
        "pack_grads",
        pack_body,
        [shape((2, mods + 2 * model), F32)],
        [
            g_shift_attn0,
            g_scale_attn0,
            g_gate_attn0,
            g_shift_mlp0,
            g_scale_mlp0,
            g_gate_mlp0,
            out_grad0,
            shrink_grad0,
            g_shift_attn1,
            g_scale_attn1,
            g_gate_attn1,
            g_shift_mlp1,
            g_scale_mlp1,
            g_gate_mlp1,
            out_grad1,
            shrink_grad1,
        ],
    )[0]
    keep, give = run(
        "grads_sum",
        functools.partial(grads_sum_body, count),
        [shape((1, mods + bias_width), F32)] * 2,
        gather(packed, "tensor") + [joint_grad0, expand_grad0, joint_grad1, expand_grad1],
        place,
    )
    joined = run(
        "grads_join",
        grads_join_body,
        [shape((1, 2 * mods + bias_width), F32)],
        [keep, swap(give, "pipe", 1)],
        place,
    )[0]
    if direct:
        outs = run(
            "mod_back",
            mod_back_body,
            [shape(own_rows.shape, F32), shape((1, mods), F32), shape((1, bias_width), F32)]
            + [shape((micro, own_rows.shape[0]), F32)] * LINE,
            gather(joined, "dp") + activated_all + [own_rows],
            place,
        )
        ada_grad, ada_bias_grad, bias_sum = outs[:3]
        act_grad = tree_sum(exchange(outs[3:], "dp"))
    else:
        joined_all = lax.all_gather(joined, "dp", axis=0, tiled=True)
        mod_grads = joined_all[:, : 2 * mods].reshape(line_size * micro, mods)
        bias_sum = jnp.sum(joined_all[:, 2 * mods :], axis=0, keepdims=True)
        ada_bias_grad = jnp.sum(mod_grads, axis=0, keepdims=True)
        picked = lax.dynamic_slice_in_dim(mod_grads, line * columns, columns, 1).astype(BF16)
        ada_grad = t_dot(activated_all, picked)
        act_partial = dot_t(picked, own_rows).reshape(line_size, micro, -1)
        act_grad = lax.psum_scatter(act_partial, "dp", scatter_dimension=0, tiled=False)
    _, silu_back = jax.vjp(jax.nn.silu, conditions[:, 0].astype(F32))
    cond_grad = silu_back(act_grad)[0]
    at = 2 * width
    return (
        layer_outputs[None, :, None],
        input_grads[None, :, None],
        cond_grad[None, :, None],
        ada_grad[None],
        ada_bias_grad,
        joint_w_grad[None],
        bias_sum[:, :at].reshape(1, 2, width),
        output_w_grad[None],
        bias_sum[:, at + hidden : at + hidden + model],
        expand_w_grad[None],
        bias_sum[:, at : at + hidden],
        shrink_w_grad[None],
        bias_sum[:, at + hidden + model :],
    )


def solution(mesh):
    in_specs = (
        P(None, "dp", "tensor", None),
        P(None, "dp", "tensor"),
        P(None, "dp", "tensor", None),
        P("pipe", "tensor", "dp"),
        P("pipe", None),
        P("pipe", "dp", None, "tensor"),
        P("pipe", None, "tensor"),
        P("pipe", "tensor", "dp"),
        P("pipe", None),
        P("pipe", "dp", "tensor"),
        P("pipe", "tensor"),
        P("pipe", "tensor", "dp"),
        P("pipe", None),
    )
    out_specs = (
        P("pipe", None, "dp", "tensor", None),
        P("pipe", None, "dp", "tensor", None),
        P("pipe", None, "dp", "tensor"),
        P("pipe", "tensor", "dp"),
        P("pipe", None),
        P("pipe", "dp", None, "tensor"),
        P("pipe", None, "tensor"),
        P("pipe", "tensor", "dp"),
        P("pipe", None),
        P("pipe", "dp", "tensor"),
        P("pipe", "tensor"),
        P("pipe", "tensor", "dp"),
        P("pipe", None),
    )
    return jax.shard_map(
        on_device, mesh=mesh, in_specs=in_specs, out_specs=out_specs, check_vma=False
    )
```

```python
import functools

import jax
import jax.numpy as jnp
from jax import lax
from jax.experimental import pallas as pl
from jax.experimental.pallas import tpu as pltpu
from jax.sharding import PartitionSpec as P

HEAD = 64
EPS = 1e-06
F32 = jnp.float32
BF16 = jnp.bfloat16
LINE = 4
VMEM_BYTES = 24 * 1024 * 1024
GELU_A = 0.7978845608028654
GELU_B = 0.044715


def swap(value, axis, mask):
    pairs = [(source, source ^ mask) for source in range(lax.axis_size(axis))]
    return lax.ppermute(value, axis, pairs)


def exchange(parts, axis):
    received = {k: swap(parts[k], axis, k) for k in range(len(parts) - 1, 0, -1)}
    return [parts[0]] + [received[k] for k in range(1, len(parts))]


def gather(value, axis):
    return exchange([value] * lax.axis_size(axis), axis)


def tree_sum(parts):
    parts = list(parts)
    while len(parts) > 1:
        parts = [parts[k] + parts[k + 1] for k in range(0, len(parts), 2)]
    return parts[0]


def shape(dims, dtype):
    return jax.ShapeDtypeStruct(dims, dtype)


def run(name, body, outs, args, place=None):
    specs = [pl.BlockSpec(memory_space=pltpu.VMEM) for _ in args]
    if place is not None:
        specs = [pl.BlockSpec(memory_space=pltpu.SMEM)] + specs
        args = [place] + list(args)
    return pl.pallas_call(
        body,
        out_shape=outs,
        in_specs=specs,
        out_specs=[pl.BlockSpec(memory_space=pltpu.VMEM) for _ in outs],
        compiler_params=pltpu.CompilerParams(vmem_limit_bytes=VMEM_BYTES),
        name=name,
    )(*args)


def dot(left, right):
    return jnp.dot(left, right, preferred_element_type=F32)


def dot_t(left, right):
    return lax.dot_general(left, right, (((1,), (1,)), ((), ())), preferred_element_type=F32)


def t_dot(left, right):
    return lax.dot_general(left, right, (((0,), (0,)), ((), ())), preferred_element_type=F32)


def normalize(values):
    centred = values - jnp.mean(values, axis=-1, keepdims=True)
    rstd = lax.rsqrt(jnp.mean(centred * centred, axis=-1, keepdims=True) + EPS)
    return centred * rstd, rstd


def normalize_back(grad, normed, rstd):
    return rstd * (
        grad
        - jnp.mean(grad, axis=-1, keepdims=True)
        - normed * jnp.mean(grad * normed, axis=-1, keepdims=True)
    )


def total(refs):
    return tree_sum([ref[...].astype(F32) for ref in refs])


def column_sum(values):
    return jnp.sum(values, axis=0, keepdims=True)


def part(mod_ref, index):
    width = mod_ref.shape[1] // 6
    return mod_ref[:, index * width : (index + 1) * width]


def gelu(pre):
    return 0.5 * pre * (1.0 + jnp.tanh(GELU_A * (pre + GELU_B * (pre * pre * pre))))


def gelu_slope(pre):
    square = pre * pre
    bent = jnp.tanh(GELU_A * (pre + GELU_B * (square * pre)))
    return 0.5 * (1.0 + bent) + 0.5 * pre * (1.0 - bent * bent) * (
        GELU_A * (1.0 + 3.0 * GELU_B * square)
    )


def put_rows(ref, refs):
    own = refs[0].shape[0]
    for k, source in enumerate(refs):
        ref[k * own : (k + 1) * own] = source[...]
    return ref[...]


def put_blocks(refs, values):
    own = refs[0].shape[0]
    for k, ref in enumerate(refs):
        ref[...] = values[k * own : (k + 1) * own].astype(ref.dtype)


def enter_body(place, tokens, cotangent, mod0, mod1, h_out, attn_in, g_y_out, g_shrunk):
    core = place[0]
    h = tokens[core].astype(F32)
    h_out[...] = h
    normed, _ = normalize(h)
    attn_in[...] = (normed * (1.0 + part(mod0, 1)) + part(mod0, 0)).astype(BF16)
    g_y = cotangent[core].astype(F32)
    g_y_out[...] = g_y
    g_shrunk[...] = (part(mod1, 5) * g_y).astype(BF16)


def pick_attn(place, own, received):
    first = place[0] == 0
    width = own.shape[1] // 2
    mine, other = own[...], received[...]
    front = jnp.where(first, mine, other)
    back = jnp.where(first, other, mine)
    return front, back[:, :width], back[:, width:]


def attn_body(count, place, *refs):
    chunks = refs[:count]
    w_own, w_received, bias = refs[count : count + 3]
    rows_out, qkv_out, probs_out, mixed_out = refs[count + 3 : count + 7]
    partial = refs[count + 7 :]
    rows = put_rows(rows_out, chunks)
    w_front, w_value, w_out = pick_attn(place, w_own, w_received)
    width = w_value.shape[1]
    front = (dot(rows, w_front) + bias[:, : 2 * width]).astype(BF16)
    value = (dot(rows, w_value) + bias[:, 2 * width :]).astype(BF16)
    qkv_out[:, : 2 * width] = front
    qkv_out[:, 2 * width :] = value
    mixed = []
    for head in range(width // HEAD):
        at = head * HEAD
        query = front[:, at : at + HEAD]
        key = front[:, width + at : width + at + HEAD]
        scores = dot_t(query, key) * HEAD**-0.5
        powers = jnp.exp(scores - jnp.max(scores, axis=-1, keepdims=True))
        probs = powers / jnp.sum(powers, axis=-1, keepdims=True)
        probs_out[head] = probs
        mixed.append(dot(probs.astype(BF16), value[:, at : at + HEAD]))
    mixed = jnp.concatenate(mixed, axis=1).astype(BF16)
    mixed_out[...] = mixed
    put_blocks(partial, dot_t(mixed, w_out))


def middle_body(count, *refs):
    parts, (bias, h, mod, attended_out, middle_out, mlp_in) = refs[:count], refs[count:]
    attended = total(parts) + bias[...]
    attended_out[...] = attended
    middle = h[...] + part(mod, 2) * attended
    middle_out[...] = middle
    normed, _ = normalize(middle)
    mlp_in[...] = (normed * (1.0 + part(mod, 4)) + part(mod, 3)).astype(BF16)


def mlp_body(count, *refs):
    chunks = refs[:count]
    w_own, w_received, bias, rows_out, pre_out, hidden_out = refs[count : count + 6]
    partial = refs[count + 6 :]
    rows = put_rows(rows_out, chunks)
    half = w_own.shape[1] // 2
    shrunk = None
    for index, weight in enumerate((w_own, w_received)):
        at = index * half
        pre = dot(rows, weight[:, :half]) + bias[:, at : at + half]
        pre_out[:, at : at + half] = pre
        hidden = gelu(pre).astype(BF16)
        hidden_out[:, at : at + half] = hidden
        term = dot_t(hidden, weight[:, half:])
        shrunk = term if shrunk is None else shrunk + term
    put_blocks(partial, shrunk)


def mlp_both_body(count, *refs):
    chunks, g_chunks = refs[:count], refs[count : 2 * count]
    w_own, w_received, bias, rows_out, g_rows_out, hidden_out, g_pre_out, bias_grad = refs[
        2 * count : 2 * count + 8
    ]
    partial = refs[2 * count + 8 : 3 * count + 8]
    g_partial = refs[3 * count + 8 :]
    rows = put_rows(rows_out, chunks)
    g_rows = put_rows(g_rows_out, g_chunks)
    half = w_own.shape[1] // 2
    shrunk, g_in = None, None
    for index, weight in enumerate((w_own, w_received)):
        at = index * half
        pre = dot(rows, weight[:, :half]) + bias[:, at : at + half]
        hidden = gelu(pre).astype(BF16)
        hidden_out[:, at : at + half] = hidden
        g_pre = (dot(g_rows, weight[:, half:]) * gelu_slope(pre)).astype(BF16)
        g_pre_out[:, at : at + half] = g_pre
        bias_grad[:, at : at + half] = column_sum(g_pre.astype(F32))
        term = dot_t(hidden, weight[:, half:])
        g_term = dot_t(g_pre, weight[:, :half])
        shrunk = term if shrunk is None else shrunk + term
        g_in = g_term if g_in is None else g_in + g_term
    put_blocks(g_partial, g_in)
    put_blocks(partial, shrunk)


def mlp_back_body(count, *refs):
    g_chunks = refs[:count]
    w_own, w_received, pre_ref, g_rows_out, g_pre_out, bias_grad = refs[count : count + 6]
    g_partial = refs[count + 6 :]
    g_rows = put_rows(g_rows_out, g_chunks)
    half = w_own.shape[1] // 2
    g_in = None
    for index, weight in enumerate((w_own, w_received)):
        at = index * half
        pre = pre_ref[:, at : at + half]
        g_pre = (dot(g_rows, weight[:, half:]) * gelu_slope(pre)).astype(BF16)
        g_pre_out[:, at : at + half] = g_pre
        bias_grad[:, at : at + half] = column_sum(g_pre.astype(F32))
        g_term = dot_t(g_pre, weight[:, :half])
        g_in = g_term if g_in is None else g_in + g_term
    put_blocks(g_partial, g_in)


def between_body(count, *refs):
    parts = refs[:count]
    bias, middle, mod0, mod1, shrunk_out, passed_out, h_out, attn_in = refs[count:]
    shrunk = total(parts) + bias[...]
    shrunk_out[...] = shrunk
    passed = (middle[...] + part(mod0, 5) * shrunk).astype(BF16)
    passed_out[...] = passed
    h = passed.astype(F32)
    h_out[...] = h
    normed, _ = normalize(h)
    attn_in[...] = (normed * (1.0 + part(mod1, 1)) + part(mod1, 0)).astype(BF16)


def leave_body(count, *refs):
    parts = refs[:count]
    bias, middle, mod, g_y_ref, g_shrunk, y_out, g_gate, bias_grad = refs[count:]
    shrunk = total(parts) + bias[...]
    y_out[...] = (middle[...] + part(mod, 5) * shrunk).astype(BF16)
    g_gate[...] = column_sum(g_y_ref[...] * shrunk)
    bias_grad[...] = column_sum(g_shrunk[...].astype(F32))


def middle_back_body(count, *refs):
    parts = refs[:count]
    middle, mod, g_y, attended, g_middle_out, g_attended_out, g_shift, g_scale, g_gate, bias_grad = refs[
        count:
    ]
    g_in = total(parts)
    normed, rstd = normalize(middle[...])
    g_shift[...] = column_sum(g_in)
    g_scale[...] = column_sum(g_in * normed)
    g_middle = g_y[...] + normalize_back(g_in * (1.0 + part(mod, 4)), normed, rstd)
    g_middle_out[...] = g_middle
    g_gate[...] = column_sum(g_middle * attended[...])
    g_attended = (part(mod, 2) * g_middle).astype(BF16)
    g_attended_out[...] = g_attended
    bias_grad[...] = column_sum(g_attended.astype(F32))


def attn_back_body(count, place, *refs):
    g_chunks = refs[:count]
    w_own, w_received, qkv, probs_ref = refs[count : count + 4]
    g_rows_out, g_joint_out, bias_grad = refs[count + 4 : count + 7]
    g_partial = refs[count + 7 :]
    g_rows = put_rows(g_rows_out, g_chunks)
    w_front, w_value, w_out = pick_attn(place, w_own, w_received)
    width = w_value.shape[1]
    g_mixed = dot(g_rows, w_out).astype(BF16)
    g_query, g_key, g_value = [], [], []
    for head in range(width // HEAD):
        at = head * HEAD
        query = qkv[:, at : at + HEAD]
        key = qkv[:, width + at : width + at + HEAD]
        value = qkv[:, 2 * width + at : 2 * width + at + HEAD]
        probs = probs_ref[head]
        g_head = g_mixed[:, at : at + HEAD]
        g_probs = dot_t(g_head, value)
        row_dot = jnp.sum(probs * g_probs, axis=-1, keepdims=True)
        g_scores = (probs * (g_probs - row_dot)).astype(BF16)
        g_value.append(t_dot(probs.astype(BF16), g_head))
        g_query.append(dot(g_scores, key) * HEAD**-0.5)
        g_key.append(t_dot(g_scores, query) * HEAD**-0.5)
    g_front = jnp.concatenate(g_query + g_key, axis=1).astype(BF16)
    g_value = jnp.concatenate(g_value, axis=1).astype(BF16)
    g_joint_out[:, : 2 * width] = g_front
    g_joint_out[:, 2 * width :] = g_value
    bias_grad[:, :width] = column_sum(g_front[:, :width].astype(F32))
    bias_grad[:, width:] = column_sum(g_value.astype(F32))
    put_blocks(g_partial, dot_t(g_front, w_front) + dot_t(g_value, w_value))


def input_grad(parts, h, mod, g_middle, g_shift, g_scale):
    g_in = total(parts)
    normed, rstd = normalize(h[...])
    g_shift[...] = column_sum(g_in)
    g_scale[...] = column_sum(g_in * normed)
    return (g_middle[...] + normalize_back(g_in * (1.0 + part(mod, 1)), normed, rstd)).astype(BF16)


def between_back_body(count, *refs):
    parts = refs[:count]
    h, mod1, mod0, g_middle, shrunk, g_h_out, g_y_out, g_shrunk_out = refs[count : count + 8]
    g_shift, g_scale, g_gate, bias_grad = refs[count + 8 :]
    g_h = input_grad(parts, h, mod1, g_middle, g_shift, g_scale)
    g_h_out[...] = g_h
    g_y = g_h.astype(F32)
    g_y_out[...] = g_y
    g_gate[...] = column_sum(g_y * shrunk[...])
    g_shrunk = (part(mod0, 5) * g_y).astype(BF16)
    g_shrunk_out[...] = g_shrunk
    bias_grad[...] = column_sum(g_shrunk.astype(F32))


def finish_back_body(count, *refs):
    parts = refs[:count]
    h, mod, g_middle, g_h_out, g_shift, g_scale = refs[count:]
    g_h_out[...] = input_grad(parts, h, mod, g_middle, g_shift, g_scale)


def mlp_weights_body(rows, g_pre, g_rows, hidden, keep, give):
    half = keep.shape[1] // 2
    keep[:, :half] = t_dot(rows[...], g_pre[:, :half])
    keep[:, half:] = t_dot(g_rows[...], hidden[:, :half])
    give[:, :half] = t_dot(rows[...], g_pre[:, half:]).astype(BF16)
    give[:, half:] = t_dot(g_rows[...], hidden[:, half:]).astype(BF16)


def attn_weights_body(place, rows, g_joint, g_rows, mixed, keep, give):
    width = mixed.shape[1]
    first = place[0] == 0
    front = t_dot(rows[...], g_joint[:, : 2 * width])
    back = jnp.concatenate(
        [t_dot(rows[...], g_joint[:, 2 * width :]), t_dot(g_rows[...], mixed[...])], axis=1
    )
    keep[...] = jnp.where(first, front, back)
    give[...] = jnp.where(first, back, front).astype(BF16)


def line_blocks(place, k, rows):
    return pl.ds(pl.multiple_of((place[1] ^ k) * rows, 16), rows)


def stack_body(place, pair, other_pair, out):
    rows = pair.shape[1]
    for k, block in enumerate((pair[0], other_pair[0], pair[1], other_pair[1])):
        out[line_blocks(place, k, rows)] = block


def line_parts_body(place, keep, received, *outs):
    rows, wide = outs[2].shape

    for piece in range(len(outs) // 3):
        near, far, own = outs[3 * piece : 3 * piece + 3]
        columns = slice(piece * wide, (piece + 1) * wide)

        def block(k):
            at = line_blocks(place, k, rows)
            return keep[at, columns] + received[at, columns].astype(F32)

        near[0] = block(1).astype(BF16)
        near[1] = block(3).astype(BF16)
        far[...] = block(2)
        own[...] = block(0)


def final_mlp_body(place, mine, received, expand_out, shrink_out):
    first = place[0] == 0
    half = mine.shape[1] // 2
    own, other = mine[...].astype(F32), received[...].astype(F32)
    for index, values in enumerate((jnp.where(first, own, other), jnp.where(first, other, own))):
        expand_out[:, index * half : (index + 1) * half] = values[:, :half]
        shrink_out[index * half : (index + 1) * half] = values[:, half:].T


def final_attn_body(place, mine, received, joint_out, out_out):
    first = place[0] == 0
    width = mine.shape[1] // 2
    own, other = mine[...].astype(F32), received[...].astype(F32)
    front, back = jnp.where(first, own, other), jnp.where(first, other, own)
    joint_out[:, : 2 * width] = front
    joint_out[:, 2 * width :] = back[:, :width]
    out_out[...] = back[:, width:].T


def mod_first_body(a0, a1, a2, a3, weight, out):
    rows = jnp.concatenate([a0[...], a1[...], a2[...], a3[...]], axis=0)
    out[...] = dot(rows, weight[...])


def mod_sum_body(count, *refs):
    values = total(refs[:count])
    outs = refs[count:]
    micro = outs[0].shape[0]
    for k, out in enumerate(outs):
        out[...] = values[k * micro : (k + 1) * micro]


def mod_join_body(place, p0, p1, p2, p3, bias, mine, other, scratch):
    for k, ref in enumerate((p0, p1, p2, p3)):
        scratch[place[1] ^ k] = ref[...]
    values = jnp.concatenate([scratch[j] for j in range(LINE)], axis=1) + bias[...]
    first = place[0] == 0
    mine[...] = jnp.where(first, values[0:1], values[1:2])
    other[...] = jnp.where(first, values[1:2], values[0:1])


def pack_body(*refs):
    out, pieces = refs[-1], refs[:-1]
    count = len(pieces) // 2
    for row in range(2):
        at = 0
        for ref in pieces[row * count : (row + 1) * count]:
            out[row : row + 1, at : at + ref.shape[1]] = ref[...]
            at += ref.shape[1]


def grads_sum_body(count, place, *refs):
    parts = refs[:count]
    joint0, expand0, joint1, expand1, keep, give = refs[count:]
    first = place[0] == 0
    values = total(parts)
    hidden = expand0.shape[1]
    mod_width = values.shape[1] // 8 * 6
    rounded = values[:, :mod_width].astype(BF16).astype(F32)
    sums = values[:, mod_width:]
    half = hidden // 2

    def natural(ref):
        now = ref[...]
        return jnp.where(first, now, jnp.concatenate([now[:, half:], now[:, :half]], axis=1))

    rows = []
    for row, (joint, expand) in enumerate(((joint0, expand0), (joint1, expand1))):
        rows.append(
            jnp.concatenate(
                [rounded[row : row + 1], joint[...], natural(expand), sums[row : row + 1]], axis=1
            )
        )
    keep[...] = jnp.where(first, rows[0], rows[1])
    give[...] = jnp.where(first, rows[1], rows[0])


def grads_join_body(place, keep, received, out):
    mods = out.shape[1] - keep.shape[1]
    first = place[0] == 0
    own, other = keep[...], received[...]
    out[:, :mods] = jnp.where(first, own, other)[:, :mods]
    out[:, mods : 2 * mods] = jnp.where(first, other, own)[:, :mods]
    out[:, 2 * mods :] = own[:, mods:] + other[:, mods:]


def mod_back_body(place, g0, g1, g2, g3, a0, a1, a2, a3, weight, w_grad, b_grad, bias, c0, c1, c2, c3):
    columns = weight.shape[1]
    mods = columns * LINE
    grads = (g0, g1, g2, g3)
    at = pl.multiple_of(place[1] * columns, 128)
    rows = []
    for ref in grads:
        rows.append(ref[:, pl.ds(at, columns)])
        rows.append(ref[:, pl.ds(pl.multiple_of(at + mods, 128), columns)])
    picked = jnp.concatenate(rows, axis=0).astype(BF16)
    activated = jnp.concatenate([a0[...], a1[...], a2[...], a3[...]], axis=0)
    w_grad[...] = t_dot(activated, picked)
    act = dot_t(picked, weight[...])
    for k, out in enumerate((c0, c1, c2, c3)):
        out[...] = act[2 * k : 2 * k + 2]
    b_grad[...] = tree_sum([ref[:, :mods] + ref[:, mods : 2 * mods] for ref in grads])
    bias[...] = tree_sum([ref[:, 2 * mods :] for ref in grads])


def on_device(
    tokens,
    conditions,
    cotangent,
    modulation_weight,
    modulation_bias,
    joint_weight,
    joint_bias,
    output_weight,
    output_bias,
    expand_weight,
    expand_bias,
    shrink_weight,
    shrink_bias,
):
    core = lax.axis_index("pipe")
    first = core == 0
    line = lax.axis_index("dp")
    place = jnp.stack([core, line]).astype(jnp.int32)
    line_size = lax.axis_size("dp")
    count = lax.axis_size("tensor")
    direct = line_size == LINE
    micro, _, own, model = tokens.shape
    width = output_weight.shape[1]
    hidden = expand_weight.shape[2]
    chunk = model // line_size
    rows = own * count
    columns = modulation_weight.shape[2]
    mods = 6 * model
    bias_width = 2 * width + hidden + 2 * model
    own_rows = modulation_weight[0]

    def mine(pair):
        return jnp.where(first, pair[0], pair[1])

    def other(pair):
        return jnp.where(first, pair[1], pair[0])

    def both_layers(kept, received):
        return jnp.where(first, kept, received), jnp.where(first, received, kept)

    def after(value, earlier):
        return lax.optimization_barrier((value, earlier))[0]

    def tie(*values):
        return lax.optimization_barrier(values)

    attn_pack = jnp.concatenate(
        [joint_weight[0].reshape(chunk, 3 * width), output_weight[0].T], axis=1
    )
    shrink_t = shrink_weight[0].T
    expand = expand_weight[0]

    def column_half(index):
        return jnp.concatenate(
            [
                attn_pack[:, index * 2 * width : (index + 1) * 2 * width],
                expand[:, index * (hidden // 2) : (index + 1) * (hidden // 2)],
                shrink_t[:, index * (hidden // 2) : (index + 1) * (hidden // 2)],
            ],
            axis=1,
        )

    halves = (column_half(0), column_half(1))
    halves_of_layers = both_layers(mine(halves), swap(other(halves), "pipe", 1))
    split = 2 * width

    bias_pack = jnp.concatenate(
        [
            joint_bias[0].reshape(-1),
            expand_bias[0],
            output_bias[0],
            shrink_bias[0],
        ]
    )[None]
    bias_layers = both_layers(bias_pack, swap(bias_pack, "pipe", 1))
    biases = []
    for packed in bias_layers:
        at = 2 * width
        joint = jnp.concatenate(
            [packed[:, :width], jnp.zeros((1, width), F32), packed[:, width:at]], axis=1
        )
        grown = packed[:, at : at + hidden]
        rolled = jnp.concatenate([grown[:, hidden // 2 :], grown[:, : hidden // 2]], axis=1)
        grown = jnp.where(first, grown, rolled)
        at += hidden
        biases.append((joint, packed[:, at : at + model], grown, packed[:, at + model :]))

    activated = jax.nn.silu(conditions[:, 0].astype(F32)).astype(BF16)
    if direct:
        activated_all = gather(activated, "dp")
    else:
        activated_all = lax.all_gather(activated, "dp", axis=0).reshape(line_size * micro, -1)

    def along_line(value):
        return lax.all_gather(value, "dp", axis=0, tiled=True)

    def line_first(value):
        return jnp.stack([value, swap(value, "dp", 2)]) if direct else value

    def line_second(pair):
        if not direct:
            return along_line(pair)
        return run(
            "stack_line",
            stack_body,
            [shape((model, pair.shape[2]), BF16)],
            [pair, swap(pair, "dp", 1)],
            place,
        )[0]

    def both_cores(lined, ready):
        lined = after(lined, ready)
        return lined, swap(lined, "pipe", 1)

    def half_of(layer, mlp):
        return halves_of_layers[layer][:, split:] if mlp else halves_of_layers[layer][:, :split]

    lined_a0 = along_line(half_of(0, False))

    if direct:
        mod_partial = run(
            "mod_first",
            mod_first_body,
            [shape((micro * LINE, columns), F32)],
            activated_all + [own_rows],
        )[0]
        mod_partials, lined_a0 = tie(gather(mod_partial, "tensor"), lined_a0)
        w_attn0 = both_cores(lined_a0, mod_partials)
        lined_m0 = along_line(after(half_of(0, True), lined_a0))
        pieces = run(
            "mod_sum",
            functools.partial(mod_sum_body, count),
            [shape((micro, columns), F32)] * LINE,
            mod_partials,
        )
        mod_mine, mod_other = pl.pallas_call(
            mod_join_body,
            out_shape=[shape((1, mods), F32)] * 2,
            in_specs=[pl.BlockSpec(memory_space=pltpu.SMEM)]
            + [pl.BlockSpec(memory_space=pltpu.VMEM)] * 5,
            out_specs=[pl.BlockSpec(memory_space=pltpu.VMEM)] * 2,
            scratch_shapes=[pltpu.VMEM((LINE, micro, columns), F32)],
            name="mod_join",
        )(place, *exchange(pieces, "dp"), modulation_bias)
    else:
        mod_partial = dot(activated_all, own_rows)
        mod_partials = gather(mod_partial, "tensor")
        w_attn0 = both_cores(lined_a0, mod_partials)
        lined_m0 = along_line(after(half_of(0, True), lined_a0))
        mod_sum = tree_sum(mod_partials).reshape(line_size, micro, -1)
        mod_layer = lax.all_to_all(mod_sum, "dp", split_axis=0, concat_axis=0)
        mod_layer = jnp.swapaxes(mod_layer, 0, 1).reshape(micro, -1) + modulation_bias
        mod_mine, mod_other = mine(mod_layer)[None], other(mod_layer)[None]
    mod0, mod1 = both_layers(mod_mine, swap(mod_other, "pipe", 1))

    pair_a1 = line_first(after(half_of(1, False), mod0))
    own_f32 = shape((own, model), F32)
    own_bf16 = shape((own, model), BF16)
    blocks = [own_bf16] * count
    wide_bf16 = shape((rows, model), BF16)
    hidden_bf16 = shape((rows, hidden), BF16)
    vector = shape((1, model), F32)
    hidden_vector = shape((1, hidden), F32)
    h0, attn_in, g_y1, g_shrunk1 = run(
        "enter",
        enter_body,
        [own_f32, own_bf16, own_f32, own_bf16],
        [tokens[:, 0], cotangent[:, 0], mod0, mod1],
        place,
    )

    def kernel(name, body, outs, args, where=None):
        return run(name, functools.partial(body, count), outs, args, where)

    def attention(attn_rows, weight, bias):
        outs = kernel(
            "attention",
            attn_body,
            [
                wide_bf16,
                shape((rows, 3 * width), BF16),
                shape((width // HEAD, rows, rows), F32),
                shape((rows, width), BF16),
            ]
            + blocks,
            attn_rows + [weight[0], weight[1], bias],
            place,
        )
        return outs[:4], exchange(outs[4:], "tensor")

    def middle_of(parts, bias, h, mod):
        return kernel(
            "middle", middle_body, [own_f32, own_f32, own_bf16], parts + [bias, h, mod]
        )

    attn_rows, pair_a1 = tie(gather(attn_in, "tensor"), pair_a1)
    lined_a1 = line_second(pair_a1)
    kept_attn0, parts = attention(attn_rows, w_attn0, biases[0][0])
    w_mlp0 = both_cores(lined_m0, parts)
    lined_m1 = along_line(after(half_of(1, True), w_mlp0[0]))
    attended0, middle0, mlp_in = middle_of(parts, biases[0][1], h0, mod0)
    mlp_rows0 = gather(mlp_in, "tensor")
    w_attn1 = both_cores(lined_a1, mlp_rows0)
    outs = kernel(
        "feed_forward",
        mlp_body,
        [wide_bf16, shape((rows, hidden), F32), hidden_bf16] + blocks,
        mlp_rows0 + [w_mlp0[0], w_mlp0[1], biases[0][2]],
    )
    mlp_rows0, pre0, hidden0 = outs[:3]
    shrunk0, passed, h1, attn_in = kernel(
        "between",
        between_body,
        [own_f32, own_bf16, own_f32, own_bf16],
        exchange(outs[3:], "tensor") + [biases[0][3], middle0, mod0, mod1],
    )

    g_rows1 = gather(g_shrunk1, "tensor")
    kept_attn1, parts = attention(gather(attn_in, "tensor"), w_attn1, biases[1][0])
    w_mlp1 = both_cores(lined_m1, parts)
    attended1, middle1, mlp_in = middle_of(parts, biases[1][1], h1, mod1)
    outs = kernel(
        "feed_forward_both",
        mlp_both_body,
        [wide_bf16, wide_bf16, hidden_bf16, hidden_bf16, hidden_vector] + blocks + blocks,
        gather(mlp_in, "tensor") + g_rows1 + [w_mlp1[0], w_mlp1[1], biases[1][2]],
    )
    mlp_rows1, g_rows1, hidden1, g_pre1, expand_grad1 = outs[:5]
    y_partial, g_partial = outs[5 : 5 + count], outs[5 + count :]

    def middle_back(parts, middle, mod, g_y, attended):
        return kernel(
            "middle_back",
            middle_back_body,
            [own_f32, own_bf16] + [vector] * 4,
            parts + [middle, mod, g_y, attended],
        )

    def attention_back(g_rows, weight, kept):
        outs = kernel(
            "attention_back",
            attn_back_body,
            [wide_bf16, shape((rows, 3 * width), BF16), shape((1, 2 * width), F32)] + blocks,
            g_rows + [weight[0], weight[1], kept[1], kept[2]],
            place,
        )
        return outs[:3], exchange(outs[3:], "tensor")

    def chip_sum(grads):
        keep, give = grads
        return (keep + swap(give, "pipe", 1).astype(F32)).astype(BF16)

    def line_sum(whole):
        return lax.psum_scatter(whole, "dp", scatter_dimension=0, tiled=True)

    def line_parts(grads, pieces):
        keep, give = grads
        wide = keep.shape[1] // pieces
        if not direct:
            whole = chip_sum(grads)
            return [[whole[:, k * wide : (k + 1) * wide]] for k in range(pieces)]
        outs = run(
            "line_parts",
            line_parts_body,
            [shape((2, chunk, wide), BF16), shape((chunk, wide), F32), shape((chunk, wide), F32)]
            * pieces,
            [keep, swap(give, "pipe", 1)],
            place,
        )
        return [outs[3 * k : 3 * k + 3] for k in range(pieces)]

    def line_near(parts):
        return swap(parts[0], "dp", 1) if direct else parts[0]

    def line_far(parts, near):
        if not direct:
            return line_sum(near)
        return swap((parts[1] + near[1].astype(F32)).astype(BF16), "dp", 2)

    def line_total(parts, near, far):
        if not direct:
            return far
        return (parts[2] + near[0].astype(F32) + far.astype(F32)).astype(BF16)

    def own_halves(pair):
        return mine(pair), swap(other(pair), "pipe", 1)

    def mlp_weight_grads(mlp_rows, g_pre, g_rows, hidden_rows):
        return run(
            "mlp_weight_grads",
            mlp_weights_body,
            [shape((model, hidden), F32), shape((model, hidden), BF16)],
            [mlp_rows, g_pre, g_rows, hidden_rows],
        )

    def attn_weight_grads(kept, g_joint, g_rows):
        return run(
            "attn_weight_grads",
            attn_weights_body,
            [shape((model, 2 * width), F32), shape((model, 2 * width), BF16)],
            [kept[0], g_joint, g_rows, kept[3]],
            place,
        )

    g_parts, y_partial, (parts_e1, parts_s1) = tie(
        exchange(g_partial, "tensor"),
        y_partial,
        line_parts(mlp_weight_grads(mlp_rows1, g_pre1, g_rows1, hidden1), 2),
    )
    near_e1 = line_near(parts_e1)
    g_middle1, g_attended, g_shift_mlp1, g_scale_mlp1, g_gate_attn1, out_grad1 = middle_back(
        g_parts, middle1, mod1, g_y1, attended1
    )
    y_parts = exchange(y_partial, "tensor")
    g_rows, near_e1, parts_e1, parts_s1 = tie(
        gather(g_attended, "tensor"), near_e1, parts_e1, parts_s1
    )
    far_e1 = line_far(parts_e1, near_e1)
    near_s1 = line_near(parts_s1)
    (g_rows, g_joint, joint_grad1), parts = attention_back(g_rows, w_attn1, kept_attn1)
    parts, (parts_a1,), far_e1, near_s1, parts_s1 = tie(
        parts,
        line_parts(attn_weight_grads(kept_attn1, g_joint, g_rows), 1),
        far_e1,
        near_s1,
        parts_s1,
    )
    near_a1 = line_near(parts_a1)
    far_s1 = line_far(parts_s1, near_s1)
    g_passed, g_y0, g_shrunk0, g_shift_attn1, g_scale_attn1, g_gate_mlp0, shrink_grad0 = kernel(
        "between_back",
        between_back_body,
        [own_bf16, own_f32, own_bf16] + [vector] * 4,
        parts + [h1, mod1, mod0, g_middle1, shrunk0],
    )

    g_rows0, near_a1, far_s1, parts_a1 = tie(
        gather(g_shrunk0, "tensor"), near_a1, far_s1, parts_a1
    )
    far_a1 = line_far(parts_a1, near_a1)
    outs = kernel(
        "feed_forward_back",
        mlp_back_body,
        [wide_bf16, hidden_bf16, hidden_vector] + blocks,
        g_rows0 + [w_mlp0[0], w_mlp0[1], pre0],
    )
    g_rows0, g_pre0, expand_grad0 = outs[:3]
    parts, (parts_e0, parts_s0), far_a1 = tie(
        exchange(outs[3:], "tensor"),
        line_parts(mlp_weight_grads(mlp_rows0, g_pre0, g_rows0, hidden0), 2),
        far_a1,
    )
    near_e0 = line_near(parts_e0)
    g_middle0, g_attended, g_shift_mlp0, g_scale_mlp0, g_gate_attn0, out_grad0 = middle_back(
        parts, middle0, mod0, g_y0, attended0
    )
    y1, g_gate_mlp1, shrink_grad1 = kernel(
        "leave",
        leave_body,
        [own_bf16, vector, vector],
        y_parts + [biases[1][3], middle1, mod1, g_y1, g_shrunk1],
    )
    g_rows, near_e0, parts_e0, parts_s0 = tie(
        gather(g_attended, "tensor"), near_e0, parts_e0, parts_s0
    )
    far_e0 = line_far(parts_e0, near_e0)
    near_s0 = line_near(parts_s0)
    (g_rows, g_joint, joint_grad0), parts = attention_back(g_rows, w_attn0, kept_attn0)
    parts, (parts_a0,), far_e0, near_s0, parts_s0 = tie(
        parts,
        line_parts(attn_weight_grads(kept_attn0, g_joint, g_rows), 1),
        far_e0,
        near_s0,
        parts_s0,
    )
    near_a0 = line_near(parts_a0)
    far_s0 = line_far(parts_s0, near_s0)
    g_h0, g_shift_attn0, g_scale_attn0 = kernel(
        "finish_back",
        finish_back_body,
        [own_bf16, vector, vector],
        parts + [h0, mod0, g_middle0],
    )
    def own_layer_of_micros(pair):
        return jnp.stack(both_layers(mine(pair), swap(other(pair), "pipe", 1)))

    layer_outputs = own_layer_of_micros((passed, y1))
    input_grads = own_layer_of_micros((g_h0, g_passed))

    packed = run(
        "pack_grads",
        pack_body,
        [shape((2, mods + 2 * model), F32)],
        [
            g_shift_attn0,
            g_scale_attn0,
            g_gate_attn0,
            g_shift_mlp0,
            g_scale_mlp0,
            g_gate_mlp0,
            out_grad0,
            shrink_grad0,
            g_shift_attn1,
            g_scale_attn1,
            g_gate_attn1,
            g_shift_mlp1,
            g_scale_mlp1,
            g_gate_mlp1,
            out_grad1,
            shrink_grad1,
        ],
    )[0]
    packed_all, near_a0, far_s0, parts_a0 = tie(
        gather(packed, "tensor"), near_a0, far_s0, parts_a0
    )
    far_a0 = line_far(parts_a0, near_a0)
    keep, give = run(
        "grads_sum",
        functools.partial(grads_sum_body, count),
        [shape((1, mods + bias_width), F32)] * 2,
        packed_all + [joint_grad0, expand_grad0, joint_grad1, expand_grad1],
        place,
    )
    joined = run(
        "grads_join",
        grads_join_body,
        [shape((1, 2 * mods + bias_width), F32)],
        [keep, swap(give, "pipe", 1)],
        place,
    )[0]
    joined_all = gather(joined, "dp") if direct else lax.all_gather(joined, "dp", axis=0, tiled=True)
    joined_all, far_a0 = tie(joined_all, far_a0)
    mlp_grad0, mlp_grad1 = (
        jnp.concatenate([line_total(*first_piece), line_total(*second_piece)], axis=1)
        for first_piece, second_piece in (
            ((parts_e0, near_e0, far_e0), (parts_s0, near_s0, far_s0)),
            ((parts_e1, near_e1, far_e1), (parts_s1, near_s1, far_s1)),
        )
    )
    attn_grad0 = line_total(parts_a0, near_a0, far_a0)
    attn_grad1 = line_total(parts_a1, near_a1, far_a1)
    expand_w_grad, shrink_w_grad = run(
        "final_mlp",
        final_mlp_body,
        [shape((chunk, hidden), F32), shape((hidden, chunk), F32)],
        own_halves((mlp_grad0, mlp_grad1)),
        place,
    )
    joint_w_grad, output_w_grad = run(
        "final_attn",
        final_attn_body,
        [shape((chunk, 3 * width), F32), shape((width, chunk), F32)],
        own_halves((attn_grad0, attn_grad1)),
        place,
    )
    joint_w_grad = joint_w_grad.reshape(chunk, 3, width)

    if direct:
        outs = run(
            "mod_back",
            mod_back_body,
            [shape(own_rows.shape, F32), shape((1, mods), F32), shape((1, bias_width), F32)]
            + [shape((micro, own_rows.shape[0]), F32)] * LINE,
            joined_all + activated_all + [own_rows],
            place,
        )
        ada_grad, ada_bias_grad, bias_sum = outs[:3]
        act_grad = tree_sum(exchange(outs[3:], "dp"))
    else:
        mod_grads = joined_all[:, : 2 * mods].reshape(line_size * micro, mods)
        bias_sum = jnp.sum(joined_all[:, 2 * mods :], axis=0, keepdims=True)
        ada_bias_grad = jnp.sum(mod_grads, axis=0, keepdims=True)
        picked = lax.dynamic_slice_in_dim(mod_grads, line * columns, columns, 1).astype(BF16)
        ada_grad = t_dot(activated_all, picked)
        act_partial = dot_t(picked, own_rows).reshape(line_size, micro, -1)
        act_grad = lax.psum_scatter(act_partial, "dp", scatter_dimension=0, tiled=False)
    _, silu_back = jax.vjp(jax.nn.silu, conditions[:, 0].astype(F32))
    cond_grad = silu_back(act_grad)[0]
    at = 2 * width
    return (
        layer_outputs[None, :, None],
        input_grads[None, :, None],
        cond_grad[None, :, None],
        ada_grad[None],
        ada_bias_grad,
        joint_w_grad[None],
        bias_sum[:, :at].reshape(1, 2, width),
        output_w_grad[None],
        bias_sum[:, at + hidden : at + hidden + model],
        expand_w_grad[None],
        bias_sum[:, at : at + hidden],
        shrink_w_grad[None],
        bias_sum[:, at + hidden + model :],
    )


def solution(mesh):
    in_specs = (
        P(None, "dp", "tensor", None),
        P(None, "dp", "tensor"),
        P(None, "dp", "tensor", None),
        P("pipe", "tensor", "dp"),
        P("pipe", None),
        P("pipe", "dp", None, "tensor"),
        P("pipe", None, "tensor"),
        P("pipe", "tensor", "dp"),
        P("pipe", None),
        P("pipe", "dp", "tensor"),
        P("pipe", "tensor"),
        P("pipe", "tensor", "dp"),
        P("pipe", None),
    )
    out_specs = (
        P("pipe", None, "dp", "tensor", None),
        P("pipe", None, "dp", "tensor", None),
        P("pipe", None, "dp", "tensor"),
        P("pipe", "tensor", "dp"),
        P("pipe", None),
        P("pipe", "dp", None, "tensor"),
        P("pipe", None, "tensor"),
        P("pipe", "tensor", "dp"),
        P("pipe", None),
        P("pipe", "dp", "tensor"),
        P("pipe", "tensor"),
        P("pipe", "tensor", "dp"),
        P("pipe", None),
    )
    return jax.shard_map(
        on_device, mesh=mesh, in_specs=in_specs, out_specs=out_specs, check_vma=False
    )
```

```python
import functools

import jax
import jax.numpy as jnp
from jax import lax
from jax.experimental import pallas as pl
from jax.experimental.pallas import tpu as pltpu
from jax.sharding import PartitionSpec as P

HEAD = 64
EPS = 1e-06
F32 = jnp.float32
BF16 = jnp.bfloat16
LINE = 4
VMEM_BYTES = 24 * 1024 * 1024
GELU_A = 0.7978845608028654
GELU_B = 0.044715


def swap(value, axis, mask):
    pairs = [(source, source ^ mask) for source in range(lax.axis_size(axis))]
    return lax.ppermute(value, axis, pairs)


def exchange(parts, axis):
    received = {k: swap(parts[k], axis, k) for k in range(len(parts) - 1, 0, -1)}
    return [parts[0]] + [received[k] for k in range(1, len(parts))]


def gather(value, axis):
    return exchange([value] * lax.axis_size(axis), axis)


def tree_sum(parts):
    parts = list(parts)
    while len(parts) > 1:
        parts = [parts[k] + parts[k + 1] for k in range(0, len(parts), 2)]
    return parts[0]


def shape(dims, dtype):
    return jax.ShapeDtypeStruct(dims, dtype)


def run(name, body, outs, args, place=None):
    specs = [pl.BlockSpec(memory_space=pltpu.VMEM) for _ in args]
    if place is not None:
        specs = [pl.BlockSpec(memory_space=pltpu.SMEM)] + specs
        args = [place] + list(args)
    return pl.pallas_call(
        body,
        out_shape=outs,
        in_specs=specs,
        out_specs=[pl.BlockSpec(memory_space=pltpu.VMEM) for _ in outs],
        compiler_params=pltpu.CompilerParams(vmem_limit_bytes=VMEM_BYTES),
        name=name,
    )(*args)


def dot(left, right):
    return jnp.dot(left, right, preferred_element_type=F32)


def dot_t(left, right):
    return lax.dot_general(left, right, (((1,), (1,)), ((), ())), preferred_element_type=F32)


def t_dot(left, right):
    return lax.dot_general(left, right, (((0,), (0,)), ((), ())), preferred_element_type=F32)


def normalize(values):
    centred = values - jnp.mean(values, axis=-1, keepdims=True)
    rstd = lax.rsqrt(jnp.mean(centred * centred, axis=-1, keepdims=True) + EPS)
    return centred * rstd, rstd


def normalize_back(grad, normed, rstd):
    return rstd * (
        grad
        - jnp.mean(grad, axis=-1, keepdims=True)
        - normed * jnp.mean(grad * normed, axis=-1, keepdims=True)
    )


def total(refs):
    return tree_sum([ref[...].astype(F32) for ref in refs])


def column_sum(values):
    return jnp.sum(values, axis=0, keepdims=True)


def part(mod_ref, index):
    width = mod_ref.shape[1] // 6
    return mod_ref[:, index * width : (index + 1) * width]


def gelu(pre):
    return 0.5 * pre * (1.0 + jnp.tanh(GELU_A * (pre + GELU_B * (pre * pre * pre))))


def gelu_slope(pre):
    square = pre * pre
    bent = jnp.tanh(GELU_A * (pre + GELU_B * (square * pre)))
    return 0.5 * (1.0 + bent) + 0.5 * pre * (1.0 - bent * bent) * (
        GELU_A * (1.0 + 3.0 * GELU_B * square)
    )


def put_rows(ref, refs):
    own = refs[0].shape[0]
    for k, source in enumerate(refs):
        ref[k * own : (k + 1) * own] = source[...]
    return ref[...]


def put_blocks(refs, values):
    own = refs[0].shape[0]
    for k, ref in enumerate(refs):
        ref[...] = values[k * own : (k + 1) * own].astype(ref.dtype)


def enter_body(place, tokens, cotangent, mod0, mod1, h_out, attn_in, g_y_out, g_shrunk):
    core = place[0]
    h = tokens[core].astype(F32)
    h_out[...] = h
    normed, _ = normalize(h)
    attn_in[...] = (normed * (1.0 + part(mod0, 1)) + part(mod0, 0)).astype(BF16)
    g_y = cotangent[core].astype(F32)
    g_y_out[...] = g_y
    g_shrunk[...] = (part(mod1, 5) * g_y).astype(BF16)


def pick_attn(place, own, received):
    first = place[0] == 0
    width = own.shape[1] // 2
    mine, other = own[...], received[...]
    front = jnp.where(first, mine, other)
    back = jnp.where(first, other, mine)
    return front, back[:, :width], back[:, width:]


def attn_body(count, place, *refs):
    chunks = refs[:count]
    w_own, w_received, bias = refs[count : count + 3]
    rows_out, qkv_out, probs_out, mixed_out = refs[count + 3 : count + 7]
    partial = refs[count + 7 :]
    rows = put_rows(rows_out, chunks)
    w_front, w_value, w_out = pick_attn(place, w_own, w_received)
    width = w_value.shape[1]
    front = (dot(rows, w_front) + bias[:, : 2 * width]).astype(BF16)
    value = (dot(rows, w_value) + bias[:, 2 * width :]).astype(BF16)
    qkv_out[:, : 2 * width] = front
    qkv_out[:, 2 * width :] = value
    mixed = []
    for head in range(width // HEAD):
        at = head * HEAD
        query = front[:, at : at + HEAD]
        key = front[:, width + at : width + at + HEAD]
        scores = dot_t(query, key) * HEAD**-0.5
        powers = jnp.exp(scores - jnp.max(scores, axis=-1, keepdims=True))
        probs = powers / jnp.sum(powers, axis=-1, keepdims=True)
        probs_out[head] = probs
        mixed.append(dot(probs.astype(BF16), value[:, at : at + HEAD]))
    mixed = jnp.concatenate(mixed, axis=1).astype(BF16)
    mixed_out[...] = mixed
    put_blocks(partial, dot_t(mixed, w_out))


def middle_body(count, *refs):
    parts, (bias, h, mod, attended_out, middle_out, mlp_in) = refs[:count], refs[count:]
    attended = total(parts) + bias[...]
    attended_out[...] = attended
    middle = h[...] + part(mod, 2) * attended
    middle_out[...] = middle
    normed, _ = normalize(middle)
    mlp_in[...] = (normed * (1.0 + part(mod, 4)) + part(mod, 3)).astype(BF16)


def mlp_body(count, *refs):
    chunks = refs[:count]
    w_own, w_received, bias, rows_out, pre_out, hidden_out = refs[count : count + 6]
    partial = refs[count + 6 :]
    rows = put_rows(rows_out, chunks)
    half = w_own.shape[1] // 2
    shrunk = None
    for index, weight in enumerate((w_own, w_received)):
        at = index * half
        pre = dot(rows, weight[:, :half]) + bias[:, at : at + half]
        pre_out[:, at : at + half] = pre
        hidden = gelu(pre).astype(BF16)
        hidden_out[:, at : at + half] = hidden
        term = dot_t(hidden, weight[:, half:])
        shrunk = term if shrunk is None else shrunk + term
    put_blocks(partial, shrunk)


def mlp_both_body(count, *refs):
    chunks, g_chunks = refs[:count], refs[count : 2 * count]
    w_own, w_received, bias, rows_out, g_rows_out, hidden_out, g_pre_out, bias_grad = refs[
        2 * count : 2 * count + 8
    ]
    partial = refs[2 * count + 8 : 3 * count + 8]
    g_partial = refs[3 * count + 8 :]
    rows = put_rows(rows_out, chunks)
    g_rows = put_rows(g_rows_out, g_chunks)
    half = w_own.shape[1] // 2
    shrunk, g_in = None, None
    for index, weight in enumerate((w_own, w_received)):
        at = index * half
        pre = dot(rows, weight[:, :half]) + bias[:, at : at + half]
        hidden = gelu(pre).astype(BF16)
        hidden_out[:, at : at + half] = hidden
        g_pre = (dot(g_rows, weight[:, half:]) * gelu_slope(pre)).astype(BF16)
        g_pre_out[:, at : at + half] = g_pre
        bias_grad[:, at : at + half] = column_sum(g_pre.astype(F32))
        term = dot_t(hidden, weight[:, half:])
        g_term = dot_t(g_pre, weight[:, :half])
        shrunk = term if shrunk is None else shrunk + term
        g_in = g_term if g_in is None else g_in + g_term
    put_blocks(g_partial, g_in)
    put_blocks(partial, shrunk)


def mlp_back_body(count, *refs):
    g_chunks = refs[:count]
    w_own, w_received, pre_ref, g_rows_out, g_pre_out, bias_grad = refs[count : count + 6]
    g_partial = refs[count + 6 :]
    g_rows = put_rows(g_rows_out, g_chunks)
    half = w_own.shape[1] // 2
    g_in = None
    for index, weight in enumerate((w_own, w_received)):
        at = index * half
        pre = pre_ref[:, at : at + half]
        g_pre = (dot(g_rows, weight[:, half:]) * gelu_slope(pre)).astype(BF16)
        g_pre_out[:, at : at + half] = g_pre
        bias_grad[:, at : at + half] = column_sum(g_pre.astype(F32))
        g_term = dot_t(g_pre, weight[:, :half])
        g_in = g_term if g_in is None else g_in + g_term
    put_blocks(g_partial, g_in)


def between_body(count, *refs):
    parts = refs[:count]
    bias, middle, mod0, mod1, shrunk_out, passed_out, h_out, attn_in = refs[count:]
    shrunk = total(parts) + bias[...]
    shrunk_out[...] = shrunk
    passed = (middle[...] + part(mod0, 5) * shrunk).astype(BF16)
    passed_out[...] = passed
    h = passed.astype(F32)
    h_out[...] = h
    normed, _ = normalize(h)
    attn_in[...] = (normed * (1.0 + part(mod1, 1)) + part(mod1, 0)).astype(BF16)


def leave_body(count, *refs):
    parts = refs[:count]
    bias, middle, mod, g_y_ref, g_shrunk, y_out, g_gate, bias_grad = refs[count:]
    shrunk = total(parts) + bias[...]
    y_out[...] = (middle[...] + part(mod, 5) * shrunk).astype(BF16)
    g_gate[...] = column_sum(g_y_ref[...] * shrunk)
    bias_grad[...] = column_sum(g_shrunk[...].astype(F32))


def middle_back_body(count, *refs):
    parts = refs[:count]
    middle, mod, g_y, attended, g_middle_out, g_attended_out, g_shift, g_scale, g_gate, bias_grad = refs[
        count:
    ]
    g_in = total(parts)
    normed, rstd = normalize(middle[...])
    g_shift[...] = column_sum(g_in)
    g_scale[...] = column_sum(g_in * normed)
    g_middle = g_y[...] + normalize_back(g_in * (1.0 + part(mod, 4)), normed, rstd)
    g_middle_out[...] = g_middle
    g_gate[...] = column_sum(g_middle * attended[...])
    g_attended = (part(mod, 2) * g_middle).astype(BF16)
    g_attended_out[...] = g_attended
    bias_grad[...] = column_sum(g_attended.astype(F32))


def attn_back_body(count, place, *refs):
    g_chunks = refs[:count]
    w_own, w_received, qkv, probs_ref = refs[count : count + 4]
    g_rows_out, g_joint_out, bias_grad = refs[count + 4 : count + 7]
    g_partial = refs[count + 7 :]
    g_rows = put_rows(g_rows_out, g_chunks)
    w_front, w_value, w_out = pick_attn(place, w_own, w_received)
    width = w_value.shape[1]
    g_mixed = dot(g_rows, w_out).astype(BF16)
    g_query, g_key, g_value = [], [], []
    for head in range(width // HEAD):
        at = head * HEAD
        query = qkv[:, at : at + HEAD]
        key = qkv[:, width + at : width + at + HEAD]
        value = qkv[:, 2 * width + at : 2 * width + at + HEAD]
        probs = probs_ref[head]
        g_head = g_mixed[:, at : at + HEAD]
        g_probs = dot_t(g_head, value)
        row_dot = jnp.sum(probs * g_probs, axis=-1, keepdims=True)
        g_scores = (probs * (g_probs - row_dot)).astype(BF16)
        g_value.append(t_dot(probs.astype(BF16), g_head))
        g_query.append(dot(g_scores, key) * HEAD**-0.5)
        g_key.append(t_dot(g_scores, query) * HEAD**-0.5)
    g_front = jnp.concatenate(g_query + g_key, axis=1).astype(BF16)
    g_value = jnp.concatenate(g_value, axis=1).astype(BF16)
    g_joint_out[:, : 2 * width] = g_front
    g_joint_out[:, 2 * width :] = g_value
    bias_grad[:, :width] = column_sum(g_front[:, :width].astype(F32))
    bias_grad[:, width:] = column_sum(g_value.astype(F32))
    put_blocks(g_partial, dot_t(g_front, w_front) + dot_t(g_value, w_value))


def input_grad(parts, h, mod, g_middle, g_shift, g_scale):
    g_in = total(parts)
    normed, rstd = normalize(h[...])
    g_shift[...] = column_sum(g_in)
    g_scale[...] = column_sum(g_in * normed)
    return (g_middle[...] + normalize_back(g_in * (1.0 + part(mod, 1)), normed, rstd)).astype(BF16)


def between_back_body(count, *refs):
    parts = refs[:count]
    h, mod1, mod0, g_middle, shrunk, g_h_out, g_y_out, g_shrunk_out = refs[count : count + 8]
    g_shift, g_scale, g_gate, bias_grad = refs[count + 8 :]
    g_h = input_grad(parts, h, mod1, g_middle, g_shift, g_scale)
    g_h_out[...] = g_h
    g_y = g_h.astype(F32)
    g_y_out[...] = g_y
    g_gate[...] = column_sum(g_y * shrunk[...])
    g_shrunk = (part(mod0, 5) * g_y).astype(BF16)
    g_shrunk_out[...] = g_shrunk
    bias_grad[...] = column_sum(g_shrunk.astype(F32))


def finish_back_body(count, *refs):
    parts = refs[:count]
    h, mod, g_middle, g_h_out, g_shift, g_scale = refs[count:]
    g_h_out[...] = input_grad(parts, h, mod, g_middle, g_shift, g_scale)


def mlp_weights_body(rows, g_pre, g_rows, hidden, keep, give):
    half = keep.shape[1] // 2
    keep[:, :half] = t_dot(rows[...], g_pre[:, :half])
    keep[:, half:] = t_dot(g_rows[...], hidden[:, :half])
    give[:, :half] = t_dot(rows[...], g_pre[:, half:]).astype(BF16)
    give[:, half:] = t_dot(g_rows[...], hidden[:, half:]).astype(BF16)


def attn_weights_body(place, rows, g_joint, g_rows, mixed, keep, give):
    width = mixed.shape[1]
    first = place[0] == 0
    front = t_dot(rows[...], g_joint[:, : 2 * width])
    back = jnp.concatenate(
        [t_dot(rows[...], g_joint[:, 2 * width :]), t_dot(g_rows[...], mixed[...])], axis=1
    )
    keep[...] = jnp.where(first, front, back)
    give[...] = jnp.where(first, back, front).astype(BF16)


def line_blocks(place, k, rows):
    return pl.ds(pl.multiple_of((place[1] ^ k) * rows, 16), rows)


def stack_body(place, *refs):
    out = refs[-1]
    pieces = len(refs) // 2
    _, rows, wide = refs[0].shape
    for piece in range(pieces):
        pair, other = refs[piece], refs[pieces + piece]
        columns = slice(piece * wide, (piece + 1) * wide)
        for k, block in enumerate((pair[0], other[0], pair[1], other[1])):
            out[line_blocks(place, k, rows), columns] = block


def line_parts_body(place, keep, received, *outs):
    rows, wide = outs[2].shape

    for piece in range(len(outs) // 3):
        near, far, own = outs[3 * piece : 3 * piece + 3]
        columns = slice(piece * wide, (piece + 1) * wide)

        def block(k):
            at = line_blocks(place, k, rows)
            return keep[at, columns] + received[at, columns].astype(F32)

        near[0] = block(1).astype(BF16)
        near[1] = block(3).astype(BF16)
        far[...] = block(2)
        own[...] = block(0)


def final_mlp_body(place, mine, received, expand_out, shrink_out):
    first = place[0] == 0
    half = mine.shape[1] // 2
    own, other = mine[...].astype(F32), received[...].astype(F32)
    for index, values in enumerate((jnp.where(first, own, other), jnp.where(first, other, own))):
        expand_out[:, index * half : (index + 1) * half] = values[:, :half]
        shrink_out[index * half : (index + 1) * half] = values[:, half:].T


def final_attn_body(place, mine, received, joint_out, out_out):
    first = place[0] == 0
    width = mine.shape[1] // 2
    own, other = mine[...].astype(F32), received[...].astype(F32)
    front, back = jnp.where(first, own, other), jnp.where(first, other, own)
    joint_out[:, : 2 * width] = front
    joint_out[:, 2 * width :] = back[:, :width]
    out_out[...] = back[:, width:].T


def mod_first_body(a0, a1, a2, a3, weight, out):
    rows = jnp.concatenate([a0[...], a1[...], a2[...], a3[...]], axis=0)
    out[...] = dot(rows, weight[...])


def mod_sum_body(count, *refs):
    values = total(refs[:count])
    outs = refs[count:]
    micro = outs[0].shape[0]
    for k, out in enumerate(outs):
        out[...] = values[k * micro : (k + 1) * micro]


def mod_join_body(place, p0, p1, p2, p3, bias, mine, other, scratch):
    for k, ref in enumerate((p0, p1, p2, p3)):
        scratch[place[1] ^ k] = ref[...]
    values = jnp.concatenate([scratch[j] for j in range(LINE)], axis=1) + bias[...]
    first = place[0] == 0
    mine[...] = jnp.where(first, values[0:1], values[1:2])
    other[...] = jnp.where(first, values[1:2], values[0:1])


def pack_body(*refs):
    out, pieces = refs[-1], refs[:-1]
    count = len(pieces) // 2
    for row in range(2):
        at = 0
        for ref in pieces[row * count : (row + 1) * count]:
            out[row : row + 1, at : at + ref.shape[1]] = ref[...]
            at += ref.shape[1]


def grads_sum_body(count, place, *refs):
    parts = refs[:count]
    joint0, expand0, joint1, expand1, keep, give = refs[count:]
    first = place[0] == 0
    values = total(parts)
    hidden = expand0.shape[1]
    mod_width = values.shape[1] // 8 * 6
    rounded = values[:, :mod_width].astype(BF16).astype(F32)
    sums = values[:, mod_width:]
    half = hidden // 2

    def natural(ref):
        now = ref[...]
        return jnp.where(first, now, jnp.concatenate([now[:, half:], now[:, :half]], axis=1))

    rows = []
    for row, (joint, expand) in enumerate(((joint0, expand0), (joint1, expand1))):
        rows.append(
            jnp.concatenate(
                [rounded[row : row + 1], joint[...], natural(expand), sums[row : row + 1]], axis=1
            )
        )
    keep[...] = jnp.where(first, rows[0], rows[1])
    give[...] = jnp.where(first, rows[1], rows[0])


def grads_join_body(place, keep, received, out):
    mods = out.shape[1] - keep.shape[1]
    first = place[0] == 0
    own, other = keep[...], received[...]
    out[:, :mods] = jnp.where(first, own, other)[:, :mods]
    out[:, mods : 2 * mods] = jnp.where(first, other, own)[:, :mods]
    out[:, 2 * mods :] = own[:, mods:] + other[:, mods:]


def mod_back_body(place, g0, g1, g2, g3, a0, a1, a2, a3, weight, w_grad, b_grad, bias, c0, c1, c2, c3):
    columns = weight.shape[1]
    mods = columns * LINE
    grads = (g0, g1, g2, g3)
    at = pl.multiple_of(place[1] * columns, 128)
    rows = []
    for ref in grads:
        rows.append(ref[:, pl.ds(at, columns)])
        rows.append(ref[:, pl.ds(pl.multiple_of(at + mods, 128), columns)])
    picked = jnp.concatenate(rows, axis=0).astype(BF16)
    activated = jnp.concatenate([a0[...], a1[...], a2[...], a3[...]], axis=0)
    w_grad[...] = t_dot(activated, picked)
    act = dot_t(picked, weight[...])
    for k, out in enumerate((c0, c1, c2, c3)):
        out[...] = act[2 * k : 2 * k + 2]
    b_grad[...] = tree_sum([ref[:, :mods] + ref[:, mods : 2 * mods] for ref in grads])
    bias[...] = tree_sum([ref[:, 2 * mods :] for ref in grads])


def on_device(
    tokens,
    conditions,
    cotangent,
    modulation_weight,
    modulation_bias,
    joint_weight,
    joint_bias,
    output_weight,
    output_bias,
    expand_weight,
    expand_bias,
    shrink_weight,
    shrink_bias,
):
    core = lax.axis_index("pipe")
    first = core == 0
    line = lax.axis_index("dp")
    place = jnp.stack([core, line]).astype(jnp.int32)
    line_size = lax.axis_size("dp")
    count = lax.axis_size("tensor")
    direct = line_size == LINE
    micro, _, own, model = tokens.shape
    width = output_weight.shape[1]
    hidden = expand_weight.shape[2]
    chunk = model // line_size
    rows = own * count
    columns = modulation_weight.shape[2]
    mods = 6 * model
    bias_width = 2 * width + hidden + 2 * model
    own_rows = modulation_weight[0]

    def mine(pair):
        return jnp.where(first, pair[0], pair[1])

    def other(pair):
        return jnp.where(first, pair[1], pair[0])

    def both_layers(kept, received):
        return jnp.where(first, kept, received), jnp.where(first, received, kept)

    def after(value, earlier):
        return lax.optimization_barrier((value, earlier))[0]

    def tie(*values):
        return lax.optimization_barrier(values)

    attn_pack = jnp.concatenate(
        [joint_weight[0].reshape(chunk, 3 * width), output_weight[0].T], axis=1
    )
    shrink_t = shrink_weight[0].T
    expand = expand_weight[0]

    def column_half(index):
        return jnp.concatenate(
            [
                attn_pack[:, index * 2 * width : (index + 1) * 2 * width],
                expand[:, index * (hidden // 2) : (index + 1) * (hidden // 2)],
                shrink_t[:, index * (hidden // 2) : (index + 1) * (hidden // 2)],
            ],
            axis=1,
        )

    halves = (column_half(0), column_half(1))
    halves_of_layers = both_layers(mine(halves), swap(other(halves), "pipe", 1))
    split = 2 * width

    bias_pack = jnp.concatenate(
        [
            joint_bias[0].reshape(-1),
            expand_bias[0],
            output_bias[0],
            shrink_bias[0],
        ]
    )[None]
    bias_layers = both_layers(bias_pack, swap(bias_pack, "pipe", 1))
    biases = []
    for packed in bias_layers:
        at = 2 * width
        joint = jnp.concatenate(
            [packed[:, :width], jnp.zeros((1, width), F32), packed[:, width:at]], axis=1
        )
        grown = packed[:, at : at + hidden]
        rolled = jnp.concatenate([grown[:, hidden // 2 :], grown[:, : hidden // 2]], axis=1)
        grown = jnp.where(first, grown, rolled)
        at += hidden
        biases.append((joint, packed[:, at : at + model], grown, packed[:, at + model :]))

    activated = jax.nn.silu(conditions[:, 0].astype(F32)).astype(BF16)
    if direct:
        activated_all = gather(activated, "dp")
    else:
        activated_all = lax.all_gather(activated, "dp", axis=0).reshape(line_size * micro, -1)

    def line_first(value):
        return jnp.stack([value, swap(value, "dp", 2)]) if direct else value

    def line_second(pair):
        if direct:
            return swap(pair, "dp", 1)
        return lax.all_gather(pair, "dp", axis=0, tiled=True)

    def both_cores(pairs, others):
        if direct:
            wide = sum(pair.shape[2] for pair in pairs)
            lined = run(
                "stack_line", stack_body, [shape((model, wide), BF16)], pairs + others, place
            )[0]
        else:
            lined = jnp.concatenate(others, axis=1)
        return lined, swap(lined, "pipe", 1)

    def piece_of(layer, index):
        return halves_of_layers[layer][:, index * split : (index + 1) * split]

    first_a0 = line_first(piece_of(0, 0))

    if direct:
        mod_partial = run(
            "mod_first",
            mod_first_body,
            [shape((micro * LINE, columns), F32)],
            activated_all + [own_rows],
        )[0]
        mod_partials, first_a0 = tie(gather(mod_partial, "tensor"), first_a0)
        second_a0 = line_second(first_a0)
        first_e0 = line_first(after(piece_of(0, 1), first_a0))
        pieces = run(
            "mod_sum",
            functools.partial(mod_sum_body, count),
            [shape((micro, columns), F32)] * LINE,
            mod_partials,
        )
        pieces, second_a0 = tie(exchange(pieces, "dp"), second_a0)
        mod_mine, mod_other = pl.pallas_call(
            mod_join_body,
            out_shape=[shape((1, mods), F32)] * 2,
            in_specs=[pl.BlockSpec(memory_space=pltpu.SMEM)]
            + [pl.BlockSpec(memory_space=pltpu.VMEM)] * 5,
            out_specs=[pl.BlockSpec(memory_space=pltpu.VMEM)] * 2,
            scratch_shapes=[pltpu.VMEM((LINE, micro, columns), F32)],
            name="mod_join",
        )(place, *pieces, modulation_bias)
    else:
        mod_partial = dot(activated_all, own_rows)
        mod_partials = gather(mod_partial, "tensor")
        second_a0 = line_second(first_a0)
        first_e0 = line_first(piece_of(0, 1))
        mod_sum = tree_sum(mod_partials).reshape(line_size, micro, -1)
        mod_layer = lax.all_to_all(mod_sum, "dp", split_axis=0, concat_axis=0)
        mod_layer = jnp.swapaxes(mod_layer, 0, 1).reshape(micro, -1) + modulation_bias
        mod_mine, mod_other = mine(mod_layer)[None], other(mod_layer)[None]
    mod0, mod1 = both_layers(mod_mine, swap(mod_other, "pipe", 1))

    w_attn0 = both_cores([first_a0], [second_a0])
    mod0, mod1, first_e0 = tie(mod0, mod1, first_e0)
    second_e0 = line_second(first_e0)
    first_s0 = line_first(after(piece_of(0, 2), first_e0))
    own_f32 = shape((own, model), F32)
    own_bf16 = shape((own, model), BF16)
    blocks = [own_bf16] * count
    wide_bf16 = shape((rows, model), BF16)
    hidden_bf16 = shape((rows, hidden), BF16)
    vector = shape((1, model), F32)
    hidden_vector = shape((1, hidden), F32)
    h0, attn_in, g_y1, g_shrunk1 = run(
        "enter",
        enter_body,
        [own_f32, own_bf16, own_f32, own_bf16],
        [tokens[:, 0], cotangent[:, 0], mod0, mod1],
        place,
    )

    def kernel(name, body, outs, args, where=None):
        return run(name, functools.partial(body, count), outs, args, where)

    def attention(attn_rows, weight, bias):
        outs = kernel(
            "attention",
            attn_body,
            [
                wide_bf16,
                shape((rows, 3 * width), BF16),
                shape((width // HEAD, rows, rows), F32),
                shape((rows, width), BF16),
            ]
            + blocks,
            attn_rows + [weight[0], weight[1], bias],
            place,
        )
        return outs[:4], exchange(outs[4:], "tensor")

    def middle_of(parts, bias, h, mod):
        return kernel(
            "middle", middle_body, [own_f32, own_f32, own_bf16], parts + [bias, h, mod]
        )

    attn_rows, second_e0, first_s0 = tie(gather(attn_in, "tensor"), second_e0, first_s0)
    second_s0 = line_second(first_s0)
    first_a1 = line_first(after(piece_of(1, 0), first_s0))
    kept_attn0, parts = attention(attn_rows, w_attn0, biases[0][0])
    parts, second_s0, first_a1 = tie(parts, second_s0, first_a1)
    w_mlp0 = both_cores([first_e0, first_s0], [second_e0, second_s0])
    second_a1 = line_second(first_a1)
    first_e1 = line_first(after(piece_of(1, 1), first_a1))
    attended0, middle0, mlp_in = middle_of(parts, biases[0][1], h0, mod0)
    mlp_rows0, second_a1, first_e1 = tie(gather(mlp_in, "tensor"), second_a1, first_e1)
    w_attn1 = both_cores([first_a1], [second_a1])
    second_e1 = line_second(first_e1)
    first_s1 = line_first(after(piece_of(1, 2), first_e1))
    outs = kernel(
        "feed_forward",
        mlp_body,
        [wide_bf16, shape((rows, hidden), F32), hidden_bf16] + blocks,
        mlp_rows0 + [w_mlp0[0], w_mlp0[1], biases[0][2]],
    )
    mlp_rows0, pre0, hidden0 = outs[:3]
    parts, second_e1, first_s1 = tie(exchange(outs[3:], "tensor"), second_e1, first_s1)
    second_s1 = line_second(first_s1)
    shrunk0, passed, h1, attn_in = kernel(
        "between",
        between_body,
        [own_f32, own_bf16, own_f32, own_bf16],
        parts + [biases[0][3], middle0, mod0, mod1],
    )

    g_rows1 = gather(g_shrunk1, "tensor")
    attn_rows, second_s1 = tie(gather(attn_in, "tensor"), second_s1)
    w_mlp1 = both_cores([first_e1, first_s1], [second_e1, second_s1])
    kept_attn1, parts = attention(attn_rows, w_attn1, biases[1][0])
    attended1, middle1, mlp_in = middle_of(parts, biases[1][1], h1, mod1)
    outs = kernel(
        "feed_forward_both",
        mlp_both_body,
        [wide_bf16, wide_bf16, hidden_bf16, hidden_bf16, hidden_vector] + blocks + blocks,
        gather(mlp_in, "tensor") + g_rows1 + [w_mlp1[0], w_mlp1[1], biases[1][2]],
    )
    mlp_rows1, g_rows1, hidden1, g_pre1, expand_grad1 = outs[:5]
    y_partial, g_partial = outs[5 : 5 + count], outs[5 + count :]

    def middle_back(parts, middle, mod, g_y, attended):
        return kernel(
            "middle_back",
            middle_back_body,
            [own_f32, own_bf16] + [vector] * 4,
            parts + [middle, mod, g_y, attended],
        )

    def attention_back(g_rows, weight, kept):
        outs = kernel(
            "attention_back",
            attn_back_body,
            [wide_bf16, shape((rows, 3 * width), BF16), shape((1, 2 * width), F32)] + blocks,
            g_rows + [weight[0], weight[1], kept[1], kept[2]],
            place,
        )
        return outs[:3], exchange(outs[3:], "tensor")

    def chip_sum(grads):
        keep, give = grads
        return (keep + swap(give, "pipe", 1).astype(F32)).astype(BF16)

    def line_sum(whole):
        return lax.psum_scatter(whole, "dp", scatter_dimension=0, tiled=True)

    def line_parts(grads, pieces):
        keep, give = grads
        wide = keep.shape[1] // pieces
        if not direct:
            whole = chip_sum(grads)
            return [[whole[:, k * wide : (k + 1) * wide]] for k in range(pieces)]
        outs = run(
            "line_parts",
            line_parts_body,
            [shape((2, chunk, wide), BF16), shape((chunk, wide), F32), shape((chunk, wide), F32)]
            * pieces,
            [keep, swap(give, "pipe", 1)],
            place,
        )
        return [outs[3 * k : 3 * k + 3] for k in range(pieces)]

    def line_near(parts):
        return swap(parts[0], "dp", 1) if direct else parts[0]

    def line_far(parts, near):
        if not direct:
            return line_sum(near)
        return swap((parts[1] + near[1].astype(F32)).astype(BF16), "dp", 2)

    def line_total(parts, near, far):
        if not direct:
            return far
        return (parts[2] + near[0].astype(F32) + far.astype(F32)).astype(BF16)

    def own_halves(pair):
        return mine(pair), swap(other(pair), "pipe", 1)

    def mlp_weight_grads(mlp_rows, g_pre, g_rows, hidden_rows):
        return run(
            "mlp_weight_grads",
            mlp_weights_body,
            [shape((model, hidden), F32), shape((model, hidden), BF16)],
            [mlp_rows, g_pre, g_rows, hidden_rows],
        )

    def attn_weight_grads(kept, g_joint, g_rows):
        return run(
            "attn_weight_grads",
            attn_weights_body,
            [shape((model, 2 * width), F32), shape((model, 2 * width), BF16)],
            [kept[0], g_joint, g_rows, kept[3]],
            place,
        )

    g_parts, y_partial, (parts_e1, parts_s1) = tie(
        exchange(g_partial, "tensor"),
        y_partial,
        line_parts(mlp_weight_grads(mlp_rows1, g_pre1, g_rows1, hidden1), 2),
    )
    near_e1 = line_near(parts_e1)
    g_middle1, g_attended, g_shift_mlp1, g_scale_mlp1, g_gate_attn1, out_grad1 = middle_back(
        g_parts, middle1, mod1, g_y1, attended1
    )
    y_parts = exchange(y_partial, "tensor")
    g_rows, near_e1, parts_e1, parts_s1 = tie(
        gather(g_attended, "tensor"), near_e1, parts_e1, parts_s1
    )
    far_e1 = line_far(parts_e1, near_e1)
    near_s1 = line_near(parts_s1)
    (g_rows, g_joint, joint_grad1), parts = attention_back(g_rows, w_attn1, kept_attn1)
    parts, (parts_a1,), far_e1, near_s1, parts_s1 = tie(
        parts,
        line_parts(attn_weight_grads(kept_attn1, g_joint, g_rows), 1),
        far_e1,
        near_s1,
        parts_s1,
    )
    near_a1 = line_near(parts_a1)
    far_s1 = line_far(parts_s1, near_s1)
    g_passed, g_y0, g_shrunk0, g_shift_attn1, g_scale_attn1, g_gate_mlp0, shrink_grad0 = kernel(
        "between_back",
        between_back_body,
        [own_bf16, own_f32, own_bf16] + [vector] * 4,
        parts + [h1, mod1, mod0, g_middle1, shrunk0],
    )

    g_rows0, near_a1, far_s1, parts_a1 = tie(
        gather(g_shrunk0, "tensor"), near_a1, far_s1, parts_a1
    )
    far_a1 = line_far(parts_a1, near_a1)
    outs = kernel(
        "feed_forward_back",
        mlp_back_body,
        [wide_bf16, hidden_bf16, hidden_vector] + blocks,
        g_rows0 + [w_mlp0[0], w_mlp0[1], pre0],
    )
    g_rows0, g_pre0, expand_grad0 = outs[:3]
    parts, (parts_e0, parts_s0), far_a1 = tie(
        exchange(outs[3:], "tensor"),
        line_parts(mlp_weight_grads(mlp_rows0, g_pre0, g_rows0, hidden0), 2),
        far_a1,
    )
    near_e0 = line_near(parts_e0)
    g_middle0, g_attended, g_shift_mlp0, g_scale_mlp0, g_gate_attn0, out_grad0 = middle_back(
        parts, middle0, mod0, g_y0, attended0
    )
    y1, g_gate_mlp1, shrink_grad1 = kernel(
        "leave",
        leave_body,
        [own_bf16, vector, vector],
        y_parts + [biases[1][3], middle1, mod1, g_y1, g_shrunk1],
    )
    g_rows, near_e0, parts_e0, parts_s0 = tie(
        gather(g_attended, "tensor"), near_e0, parts_e0, parts_s0
    )
    far_e0 = line_far(parts_e0, near_e0)
    near_s0 = line_near(parts_s0)
    (g_rows, g_joint, joint_grad0), parts = attention_back(g_rows, w_attn0, kept_attn0)
    (parts_a0,) = line_parts(attn_weight_grads(kept_attn0, g_joint, g_rows), 1)
    g_h0, g_shift_attn0, g_scale_attn0 = kernel(
        "finish_back",
        finish_back_body,
        [own_bf16, vector, vector],
        parts + [h0, mod0, g_middle0],
    )
    def own_layer_of_micros(pair):
        return jnp.stack(both_layers(mine(pair), swap(other(pair), "pipe", 1)))

    layer_outputs = own_layer_of_micros((passed, y1))
    input_grads = own_layer_of_micros((g_h0, g_passed))

    packed = run(
        "pack_grads",
        pack_body,
        [shape((2, mods + 2 * model), F32)],
        [
            g_shift_attn0,
            g_scale_attn0,
            g_gate_attn0,
            g_shift_mlp0,
            g_scale_mlp0,
            g_gate_mlp0,
            out_grad0,
            shrink_grad0,
            g_shift_attn1,
            g_scale_attn1,
            g_gate_attn1,
            g_shift_mlp1,
            g_scale_mlp1,
            g_gate_mlp1,
            out_grad1,
            shrink_grad1,
        ],
    )[0]
    packed_all, parts_a0, far_e0, near_s0, parts_s0 = tie(
        gather(packed, "tensor"), parts_a0, far_e0, near_s0, parts_s0
    )
    near_a0 = line_near(parts_a0)
    far_s0 = line_far(parts_s0, near_s0)
    keep, give = run(
        "grads_sum",
        functools.partial(grads_sum_body, count),
        [shape((1, mods + bias_width), F32)] * 2,
        packed_all + [joint_grad0, expand_grad0, joint_grad1, expand_grad1],
        place,
    )
    joined = run(
        "grads_join",
        grads_join_body,
        [shape((1, 2 * mods + bias_width), F32)],
        [keep, swap(give, "pipe", 1)],
        place,
    )[0]
    joined_all = gather(joined, "dp") if direct else lax.all_gather(joined, "dp", axis=0, tiled=True)
    joined_all, near_a0, far_s0 = tie(joined_all, near_a0, far_s0)
    far_a0 = line_far(parts_a0, near_a0)
    mlp_grad0, mlp_grad1 = (
        jnp.concatenate([line_total(*first_piece), line_total(*second_piece)], axis=1)
        for first_piece, second_piece in (
            ((parts_e0, near_e0, far_e0), (parts_s0, near_s0, far_s0)),
            ((parts_e1, near_e1, far_e1), (parts_s1, near_s1, far_s1)),
        )
    )
    attn_grad0 = line_total(parts_a0, near_a0, far_a0)
    attn_grad1 = line_total(parts_a1, near_a1, far_a1)
    expand_w_grad, shrink_w_grad = run(
        "final_mlp",
        final_mlp_body,
        [shape((chunk, hidden), F32), shape((hidden, chunk), F32)],
        own_halves((mlp_grad0, mlp_grad1)),
        place,
    )
    joint_w_grad, output_w_grad = run(
        "final_attn",
        final_attn_body,
        [shape((chunk, 3 * width), F32), shape((width, chunk), F32)],
        own_halves((attn_grad0, attn_grad1)),
        place,
    )
    joint_w_grad = joint_w_grad.reshape(chunk, 3, width)

    if direct:
        outs = run(
            "mod_back",
            mod_back_body,
            [shape(own_rows.shape, F32), shape((1, mods), F32), shape((1, bias_width), F32)]
            + [shape((micro, own_rows.shape[0]), F32)] * LINE,
            joined_all + activated_all + [own_rows],
            place,
        )
        ada_grad, ada_bias_grad, bias_sum = outs[:3]
        act_grad = tree_sum(exchange(outs[3:], "dp"))
    else:
        mod_grads = joined_all[:, : 2 * mods].reshape(line_size * micro, mods)
        bias_sum = jnp.sum(joined_all[:, 2 * mods :], axis=0, keepdims=True)
        ada_bias_grad = jnp.sum(mod_grads, axis=0, keepdims=True)
        picked = lax.dynamic_slice_in_dim(mod_grads, line * columns, columns, 1).astype(BF16)
        ada_grad = t_dot(activated_all, picked)
        act_partial = dot_t(picked, own_rows).reshape(line_size, micro, -1)
        act_grad = lax.psum_scatter(act_partial, "dp", scatter_dimension=0, tiled=False)
    _, silu_back = jax.vjp(jax.nn.silu, conditions[:, 0].astype(F32))
    cond_grad = silu_back(act_grad)[0]
    at = 2 * width
    return (
        layer_outputs[None, :, None],
        input_grads[None, :, None],
        cond_grad[None, :, None],
        ada_grad[None],
        ada_bias_grad,
        joint_w_grad[None],
        bias_sum[:, :at].reshape(1, 2, width),
        output_w_grad[None],
        bias_sum[:, at + hidden : at + hidden + model],
        expand_w_grad[None],
        bias_sum[:, at : at + hidden],
        shrink_w_grad[None],
        bias_sum[:, at + hidden + model :],
    )


def solution(mesh):
    in_specs = (
        P(None, "dp", "tensor", None),
        P(None, "dp", "tensor"),
        P(None, "dp", "tensor", None),
        P("pipe", "tensor", "dp"),
        P("pipe", None),
        P("pipe", "dp", None, "tensor"),
        P("pipe", None, "tensor"),
        P("pipe", "tensor", "dp"),
        P("pipe", None),
        P("pipe", "dp", "tensor"),
        P("pipe", "tensor"),
        P("pipe", "tensor", "dp"),
        P("pipe", None),
    )
    out_specs = (
        P("pipe", None, "dp", "tensor", None),
        P("pipe", None, "dp", "tensor", None),
        P("pipe", None, "dp", "tensor"),
        P("pipe", "tensor", "dp"),
        P("pipe", None),
        P("pipe", "dp", None, "tensor"),
        P("pipe", None, "tensor"),
        P("pipe", "tensor", "dp"),
        P("pipe", None),
        P("pipe", "dp", "tensor"),
        P("pipe", "tensor"),
        P("pipe", "tensor", "dp"),
        P("pipe", None),
    )
    return jax.shard_map(
        on_device, mesh=mesh, in_specs=in_specs, out_specs=out_specs, check_vma=False
    )
```

```python
import functools

import jax
import jax.numpy as jnp
from jax import lax
from jax.experimental import pallas as pl
from jax.experimental.pallas import tpu as pltpu
from jax.sharding import PartitionSpec as P

HEAD = 64
EPS = 1e-06
F32 = jnp.float32
BF16 = jnp.bfloat16
LINE = 4
VMEM_BYTES = 24 * 1024 * 1024
GELU_A = 0.7978845608028654
GELU_B = 0.044715


def swap(value, axis, mask):
    pairs = [(source, source ^ mask) for source in range(lax.axis_size(axis))]
    return lax.ppermute(value, axis, pairs)


def exchange(parts, axis):
    received = {k: swap(parts[k], axis, k) for k in range(len(parts) - 1, 0, -1)}
    return [parts[0]] + [received[k] for k in range(1, len(parts))]


def gather(value, axis):
    return exchange([value] * lax.axis_size(axis), axis)


def tree_sum(parts):
    parts = list(parts)
    while len(parts) > 1:
        parts = [parts[k] + parts[k + 1] for k in range(0, len(parts), 2)]
    return parts[0]


def shape(dims, dtype):
    return jax.ShapeDtypeStruct(dims, dtype)


def run(name, body, outs, args, place=None):
    specs = [pl.BlockSpec(memory_space=pltpu.VMEM) for _ in args]
    if place is not None:
        specs = [pl.BlockSpec(memory_space=pltpu.SMEM)] + specs
        args = [place] + list(args)
    return pl.pallas_call(
        body,
        out_shape=outs,
        in_specs=specs,
        out_specs=[pl.BlockSpec(memory_space=pltpu.VMEM) for _ in outs],
        compiler_params=pltpu.CompilerParams(vmem_limit_bytes=VMEM_BYTES),
        name=name,
    )(*args)


def dot(left, right):
    return jnp.dot(left, right, preferred_element_type=F32)


def dot_t(left, right):
    return lax.dot_general(left, right, (((1,), (1,)), ((), ())), preferred_element_type=F32)


def t_dot(left, right):
    return lax.dot_general(left, right, (((0,), (0,)), ((), ())), preferred_element_type=F32)


def normalize(values):
    centred = values - jnp.mean(values, axis=-1, keepdims=True)
    rstd = lax.rsqrt(jnp.mean(centred * centred, axis=-1, keepdims=True) + EPS)
    return centred * rstd, rstd


def normalize_back(grad, normed, rstd):
    return rstd * (
        grad
        - jnp.mean(grad, axis=-1, keepdims=True)
        - normed * jnp.mean(grad * normed, axis=-1, keepdims=True)
    )


def total(refs):
    return tree_sum([ref[...].astype(F32) for ref in refs])


def column_sum(values):
    return jnp.sum(values, axis=0, keepdims=True)


def part(mod_ref, index):
    width = mod_ref.shape[1] // 6
    return mod_ref[:, index * width : (index + 1) * width]


def gelu(pre):
    return 0.5 * pre * (1.0 + jnp.tanh(GELU_A * (pre + GELU_B * (pre * pre * pre))))


def gelu_slope(pre):
    square = pre * pre
    bent = jnp.tanh(GELU_A * (pre + GELU_B * (square * pre)))
    return 0.5 * (1.0 + bent) + 0.5 * pre * (1.0 - bent * bent) * (
        GELU_A * (1.0 + 3.0 * GELU_B * square)
    )


def put_rows(ref, refs):
    own = refs[0].shape[0]
    for k, source in enumerate(refs):
        ref[k * own : (k + 1) * own] = source[...]
    return ref[...]


def put_blocks(refs, values):
    own = refs[0].shape[0]
    for k, ref in enumerate(refs):
        ref[...] = values[k * own : (k + 1) * own].astype(ref.dtype)


def enter_body(place, tokens, cotangent, mod0, mod1, h_out, attn_in, g_y_out, g_shrunk):
    core = place[0]
    h = tokens[core].astype(F32)
    h_out[...] = h
    normed, _ = normalize(h)
    attn_in[...] = (normed * (1.0 + part(mod0, 1)) + part(mod0, 0)).astype(BF16)
    g_y = cotangent[core].astype(F32)
    g_y_out[...] = g_y
    g_shrunk[...] = (part(mod1, 5) * g_y).astype(BF16)


def pack_weights_body(place, joint, out, expand, shrink_t, keep, give):
    first = place[0] == 0
    width = out.shape[0]
    half = expand.shape[1] // 2
    pieces = (
        (
            jnp.concatenate([joint[0].astype(F32), joint[1].astype(F32)], axis=1),
            jnp.concatenate([joint[2].astype(F32), out[...].astype(F32).T], axis=1),
        ),
        (expand[:, :half], expand[:, half:]),
        (shrink_t[:, :half], shrink_t[:, half:]),
    )
    at = 0
    for front, back in pieces:
        columns = slice(at, at + front.shape[1])
        keep[:, columns] = jnp.where(first, front, back).astype(BF16)
        give[:, columns] = jnp.where(first, back, front).astype(BF16)
        at += front.shape[1]


def weight_pieces_body(place, keep, received, *outs):
    first = place[0] == 0
    pieces = len(outs) // 2
    wide = outs[0].shape[1]
    for piece in range(pieces):
        own = keep[:, piece * wide : (piece + 1) * wide]
        other = received[:, piece * wide : (piece + 1) * wide]
        outs[piece][...] = jnp.where(first, own, other)
        outs[pieces + piece][...] = jnp.where(first, other, own)


def pick_attn(place, own, received):
    first = place[0] == 0
    width = own.shape[1] // 2
    mine, other = own[...], received[...]
    front = jnp.where(first, mine, other)
    back = jnp.where(first, other, mine)
    return front, back[:, :width], back[:, width:]


def attn_body(count, place, *refs):
    chunks = refs[:count]
    w_own, w_received, bias = refs[count : count + 3]
    rows_out, qkv_out, probs_out, mixed_out = refs[count + 3 : count + 7]
    partial = refs[count + 7 :]
    rows = put_rows(rows_out, chunks)
    w_front, w_value, w_out = pick_attn(place, w_own, w_received)
    width = w_value.shape[1]
    front = (dot(rows, w_front) + bias[:, : 2 * width]).astype(BF16)
    value = (dot(rows, w_value) + bias[:, 2 * width :]).astype(BF16)
    qkv_out[:, : 2 * width] = front
    qkv_out[:, 2 * width :] = value
    mixed = []
    for head in range(width // HEAD):
        at = head * HEAD
        query = front[:, at : at + HEAD]
        key = front[:, width + at : width + at + HEAD]
        scores = dot_t(query, key) * HEAD**-0.5
        powers = jnp.exp(scores - jnp.max(scores, axis=-1, keepdims=True))
        probs = powers / jnp.sum(powers, axis=-1, keepdims=True)
        probs_out[head] = probs
        mixed.append(dot(probs.astype(BF16), value[:, at : at + HEAD]))
    mixed = jnp.concatenate(mixed, axis=1).astype(BF16)
    mixed_out[...] = mixed
    put_blocks(partial, dot_t(mixed, w_out))


def middle_body(count, *refs):
    parts, (bias, h, mod, attended_out, middle_out, mlp_in) = refs[:count], refs[count:]
    attended = total(parts) + bias[...]
    attended_out[...] = attended
    middle = h[...] + part(mod, 2) * attended
    middle_out[...] = middle
    normed, _ = normalize(middle)
    mlp_in[...] = (normed * (1.0 + part(mod, 4)) + part(mod, 3)).astype(BF16)


def mlp_body(count, *refs):
    chunks = refs[:count]
    w_own, w_received, bias, rows_out, pre_out, hidden_out = refs[count : count + 6]
    partial = refs[count + 6 :]
    rows = put_rows(rows_out, chunks)
    half = w_own.shape[1] // 2
    shrunk = None
    for index, weight in enumerate((w_own, w_received)):
        at = index * half
        pre = dot(rows, weight[:, :half]) + bias[:, at : at + half]
        pre_out[:, at : at + half] = pre
        hidden = gelu(pre).astype(BF16)
        hidden_out[:, at : at + half] = hidden
        term = dot_t(hidden, weight[:, half:])
        shrunk = term if shrunk is None else shrunk + term
    put_blocks(partial, shrunk)


def mlp_both_body(count, *refs):
    chunks, g_chunks = refs[:count], refs[count : 2 * count]
    w_own, w_received, bias, rows_out, g_rows_out, hidden_out, g_pre_out, bias_grad = refs[
        2 * count : 2 * count + 8
    ]
    partial = refs[2 * count + 8 : 3 * count + 8]
    g_partial = refs[3 * count + 8 :]
    rows = put_rows(rows_out, chunks)
    g_rows = put_rows(g_rows_out, g_chunks)
    half = w_own.shape[1] // 2
    shrunk, g_in = None, None
    for index, weight in enumerate((w_own, w_received)):
        at = index * half
        pre = dot(rows, weight[:, :half]) + bias[:, at : at + half]
        hidden = gelu(pre).astype(BF16)
        hidden_out[:, at : at + half] = hidden
        g_pre = (dot(g_rows, weight[:, half:]) * gelu_slope(pre)).astype(BF16)
        g_pre_out[:, at : at + half] = g_pre
        bias_grad[:, at : at + half] = column_sum(g_pre.astype(F32))
        term = dot_t(hidden, weight[:, half:])
        g_term = dot_t(g_pre, weight[:, :half])
        shrunk = term if shrunk is None else shrunk + term
        g_in = g_term if g_in is None else g_in + g_term
    put_blocks(g_partial, g_in)
    put_blocks(partial, shrunk)


def mlp_back_body(count, *refs):
    g_chunks = refs[:count]
    w_own, w_received, pre_ref, g_rows_out, g_pre_out, bias_grad = refs[count : count + 6]
    g_partial = refs[count + 6 :]
    g_rows = put_rows(g_rows_out, g_chunks)
    half = w_own.shape[1] // 2
    g_in = None
    for index, weight in enumerate((w_own, w_received)):
        at = index * half
        pre = pre_ref[:, at : at + half]
        g_pre = (dot(g_rows, weight[:, half:]) * gelu_slope(pre)).astype(BF16)
        g_pre_out[:, at : at + half] = g_pre
        bias_grad[:, at : at + half] = column_sum(g_pre.astype(F32))
        g_term = dot_t(g_pre, weight[:, :half])
        g_in = g_term if g_in is None else g_in + g_term
    put_blocks(g_partial, g_in)


def between_body(count, *refs):
    parts = refs[:count]
    bias, middle, mod0, mod1, shrunk_out, passed_out, h_out, attn_in = refs[count:]
    shrunk = total(parts) + bias[...]
    shrunk_out[...] = shrunk
    passed = (middle[...] + part(mod0, 5) * shrunk).astype(BF16)
    passed_out[...] = passed
    h = passed.astype(F32)
    h_out[...] = h
    normed, _ = normalize(h)
    attn_in[...] = (normed * (1.0 + part(mod1, 1)) + part(mod1, 0)).astype(BF16)


def leave_body(count, *refs):
    parts = refs[:count]
    bias, middle, mod, g_y_ref, g_shrunk, y_out, g_gate, bias_grad = refs[count:]
    shrunk = total(parts) + bias[...]
    y_out[...] = (middle[...] + part(mod, 5) * shrunk).astype(BF16)
    g_gate[...] = column_sum(g_y_ref[...] * shrunk)
    bias_grad[...] = column_sum(g_shrunk[...].astype(F32))


def middle_back_body(count, *refs):
    parts = refs[:count]
    middle, mod, g_y, attended, g_middle_out, g_attended_out, g_shift, g_scale, g_gate, bias_grad = refs[
        count:
    ]
    g_in = total(parts)
    normed, rstd = normalize(middle[...])
    g_shift[...] = column_sum(g_in)
    g_scale[...] = column_sum(g_in * normed)
    g_middle = g_y[...] + normalize_back(g_in * (1.0 + part(mod, 4)), normed, rstd)
    g_middle_out[...] = g_middle
    g_gate[...] = column_sum(g_middle * attended[...])
    g_attended = (part(mod, 2) * g_middle).astype(BF16)
    g_attended_out[...] = g_attended
    bias_grad[...] = column_sum(g_attended.astype(F32))


def attn_back_body(count, place, *refs):
    g_chunks = refs[:count]
    w_own, w_received, qkv, probs_ref = refs[count : count + 4]
    g_rows_out, g_joint_out, bias_grad = refs[count + 4 : count + 7]
    g_partial = refs[count + 7 :]
    g_rows = put_rows(g_rows_out, g_chunks)
    w_front, w_value, w_out = pick_attn(place, w_own, w_received)
    width = w_value.shape[1]
    g_mixed = dot(g_rows, w_out).astype(BF16)
    g_query, g_key, g_value = [], [], []
    for head in range(width // HEAD):
        at = head * HEAD
        query = qkv[:, at : at + HEAD]
        key = qkv[:, width + at : width + at + HEAD]
        value = qkv[:, 2 * width + at : 2 * width + at + HEAD]
        probs = probs_ref[head]
        g_head = g_mixed[:, at : at + HEAD]
        g_probs = dot_t(g_head, value)
        row_dot = jnp.sum(probs * g_probs, axis=-1, keepdims=True)
        g_scores = (probs * (g_probs - row_dot)).astype(BF16)
        g_value.append(t_dot(probs.astype(BF16), g_head))
        g_query.append(dot(g_scores, key) * HEAD**-0.5)
        g_key.append(t_dot(g_scores, query) * HEAD**-0.5)
    g_front = jnp.concatenate(g_query + g_key, axis=1).astype(BF16)
    g_value = jnp.concatenate(g_value, axis=1).astype(BF16)
    g_joint_out[:, : 2 * width] = g_front
    g_joint_out[:, 2 * width :] = g_value
    bias_grad[:, :width] = column_sum(g_front[:, :width].astype(F32))
    bias_grad[:, width:] = column_sum(g_value.astype(F32))
    put_blocks(g_partial, dot_t(g_front, w_front) + dot_t(g_value, w_value))


def input_grad(parts, h, mod, g_middle, g_shift, g_scale):
    g_in = total(parts)
    normed, rstd = normalize(h[...])
    g_shift[...] = column_sum(g_in)
    g_scale[...] = column_sum(g_in * normed)
    return (g_middle[...] + normalize_back(g_in * (1.0 + part(mod, 1)), normed, rstd)).astype(BF16)


def between_back_body(count, *refs):
    parts = refs[:count]
    h, mod1, mod0, g_middle, shrunk, g_h_out, g_y_out, g_shrunk_out = refs[count : count + 8]
    g_shift, g_scale, g_gate, bias_grad = refs[count + 8 :]
    g_h = input_grad(parts, h, mod1, g_middle, g_shift, g_scale)
    g_h_out[...] = g_h
    g_y = g_h.astype(F32)
    g_y_out[...] = g_y
    g_gate[...] = column_sum(g_y * shrunk[...])
    g_shrunk = (part(mod0, 5) * g_y).astype(BF16)
    g_shrunk_out[...] = g_shrunk
    bias_grad[...] = column_sum(g_shrunk.astype(F32))


def finish_back_body(count, *refs):
    parts = refs[:count]
    h, mod, g_middle, g_h_out, g_shift, g_scale = refs[count:]
    g_h_out[...] = input_grad(parts, h, mod, g_middle, g_shift, g_scale)


def mlp_weights_body(rows, g_pre, g_rows, hidden, keep, give):
    half = keep.shape[1] // 2
    keep[:, :half] = t_dot(rows[...], g_pre[:, :half])
    keep[:, half:] = t_dot(g_rows[...], hidden[:, :half])
    give[:, :half] = t_dot(rows[...], g_pre[:, half:]).astype(BF16)
    give[:, half:] = t_dot(g_rows[...], hidden[:, half:]).astype(BF16)


def attn_weights_body(place, rows, g_joint, g_rows, mixed, keep, give):
    width = mixed.shape[1]
    first = place[0] == 0
    front = t_dot(rows[...], g_joint[:, : 2 * width])
    back = jnp.concatenate(
        [t_dot(rows[...], g_joint[:, 2 * width :]), t_dot(g_rows[...], mixed[...])], axis=1
    )
    keep[...] = jnp.where(first, front, back)
    give[...] = jnp.where(first, back, front).astype(BF16)


def line_blocks(place, k, rows):
    return pl.ds(pl.multiple_of((place[1] ^ k) * rows, 16), rows)


def stack_body(place, *refs):
    out = refs[-1]
    pieces = len(refs) // 2
    _, rows, wide = refs[0].shape
    for piece in range(pieces):
        pair, other = refs[piece], refs[pieces + piece]
        columns = slice(piece * wide, (piece + 1) * wide)
        for k, block in enumerate((pair[0], other[0], pair[1], other[1])):
            out[line_blocks(place, k, rows), columns] = block


def line_parts_body(place, keep, received, *outs):
    rows, wide = outs[2].shape

    for piece in range(len(outs) // 3):
        near, far, own = outs[3 * piece : 3 * piece + 3]
        columns = slice(piece * wide, (piece + 1) * wide)

        def block(k):
            at = line_blocks(place, k, rows)
            return keep[at, columns] + received[at, columns].astype(F32)

        near[0] = block(1).astype(BF16)
        near[1] = block(3).astype(BF16)
        far[...] = block(2)
        own[...] = block(0)


def final_mlp_body(place, mine, received, expand_out, shrink_t_out):
    first = place[0] == 0
    half = mine.shape[1] // 2
    own, other = mine[...].astype(F32), received[...].astype(F32)
    for index, values in enumerate((jnp.where(first, own, other), jnp.where(first, other, own))):
        expand_out[:, index * half : (index + 1) * half] = values[:, :half]
        shrink_t_out[:, index * half : (index + 1) * half] = values[:, half:]


def final_attn_body(place, mine, received, joint_out, out_out):
    first = place[0] == 0
    width = mine.shape[1] // 2
    own, other = mine[...].astype(F32), received[...].astype(F32)
    front, back = jnp.where(first, own, other), jnp.where(first, other, own)
    joint_out[0] = front[:, :width]
    joint_out[1] = front[:, width:]
    joint_out[2] = back[:, :width]
    out_out[...] = back[:, width:].T


def mod_first_body(a0, a1, a2, a3, weight, out):
    rows = jnp.concatenate([a0[...], a1[...], a2[...], a3[...]], axis=0)
    out[...] = dot(rows, weight[...])


def mod_sum_body(count, *refs):
    values = total(refs[:count])
    outs = refs[count:]
    micro = outs[0].shape[0]
    for k, out in enumerate(outs):
        out[...] = values[k * micro : (k + 1) * micro]


def mod_join_body(place, p0, p1, p2, p3, bias, mine, other, scratch):
    for k, ref in enumerate((p0, p1, p2, p3)):
        scratch[place[1] ^ k] = ref[...]
    values = jnp.concatenate([scratch[j] for j in range(LINE)], axis=1) + bias[...]
    first = place[0] == 0
    mine[...] = jnp.where(first, values[0:1], values[1:2])
    other[...] = jnp.where(first, values[1:2], values[0:1])


def pack_body(*refs):
    out, pieces = refs[-1], refs[:-1]
    count = len(pieces) // 2
    for row in range(2):
        at = 0
        for ref in pieces[row * count : (row + 1) * count]:
            out[row : row + 1, at : at + ref.shape[1]] = ref[...]
            at += ref.shape[1]


def grads_sum_body(count, place, *refs):
    parts = refs[:count]
    joint0, expand0, joint1, expand1, keep, give = refs[count:]
    first = place[0] == 0
    values = total(parts)
    hidden = expand0.shape[1]
    mod_width = values.shape[1] // 8 * 6
    rounded = values[:, :mod_width].astype(BF16).astype(F32)
    sums = values[:, mod_width:]
    half = hidden // 2

    def natural(ref):
        now = ref[...]
        return jnp.where(first, now, jnp.concatenate([now[:, half:], now[:, :half]], axis=1))

    rows = []
    for row, (joint, expand) in enumerate(((joint0, expand0), (joint1, expand1))):
        rows.append(
            jnp.concatenate(
                [rounded[row : row + 1], joint[...], natural(expand), sums[row : row + 1]], axis=1
            )
        )
    keep[...] = jnp.where(first, rows[0], rows[1])
    give[...] = jnp.where(first, rows[1], rows[0])


def grads_join_body(place, keep, received, out):
    mods = out.shape[1] - keep.shape[1]
    first = place[0] == 0
    own, other = keep[...], received[...]
    out[:, :mods] = jnp.where(first, own, other)[:, :mods]
    out[:, mods : 2 * mods] = jnp.where(first, other, own)[:, :mods]
    out[:, 2 * mods :] = own[:, mods:] + other[:, mods:]


def mod_back_body(place, g0, g1, g2, g3, a0, a1, a2, a3, weight, w_grad, b_grad, bias, c0, c1, c2, c3):
    columns = weight.shape[1]
    mods = columns * LINE
    grads = (g0, g1, g2, g3)
    at = pl.multiple_of(place[1] * columns, 128)
    rows = []
    for ref in grads:
        rows.append(ref[:, pl.ds(at, columns)])
        rows.append(ref[:, pl.ds(pl.multiple_of(at + mods, 128), columns)])
    picked = jnp.concatenate(rows, axis=0).astype(BF16)
    activated = jnp.concatenate([a0[...], a1[...], a2[...], a3[...]], axis=0)
    w_grad[...] = t_dot(activated, picked)
    act = dot_t(picked, weight[...])
    for k, out in enumerate((c0, c1, c2, c3)):
        out[...] = act[2 * k : 2 * k + 2]
    b_grad[...] = tree_sum([ref[:, :mods] + ref[:, mods : 2 * mods] for ref in grads])
    bias[...] = tree_sum([ref[:, 2 * mods :] for ref in grads])


def on_device(
    tokens,
    conditions,
    cotangent,
    modulation_weight,
    modulation_bias,
    joint_weight,
    joint_bias,
    output_weight,
    output_bias,
    expand_weight,
    expand_bias,
    shrink_weight,
    shrink_bias,
):
    core = lax.axis_index("pipe")
    first = core == 0
    line = lax.axis_index("dp")
    place = jnp.stack([core, line]).astype(jnp.int32)
    line_size = lax.axis_size("dp")
    count = lax.axis_size("tensor")
    direct = line_size == LINE
    micro, _, own, model = tokens.shape
    width = output_weight.shape[1]
    hidden = expand_weight.shape[2]
    chunk = model // line_size
    rows = own * count
    columns = modulation_weight.shape[2]
    mods = 6 * model
    bias_width = 2 * width + hidden + 2 * model
    own_rows = modulation_weight[0]

    def mine(pair):
        return jnp.where(first, pair[0], pair[1])

    def other(pair):
        return jnp.where(first, pair[1], pair[0])

    def both_layers(kept, received):
        return jnp.where(first, kept, received), jnp.where(first, received, kept)

    def after(value, earlier):
        return lax.optimization_barrier((value, earlier))[0]

    def tie(main, *rest):
        return lax.optimization_barrier((lax.optimization_barrier(main),) + rest)

    split = 2 * width
    pieces_shape = shape((chunk, split), BF16)
    keep, give = run(
        "pack_weights",
        pack_weights_body,
        [shape((chunk, split + 2 * (hidden // 2)), BF16)] * 2,
        [
            jnp.transpose(joint_weight[0], (1, 0, 2)),
            output_weight[0],
            expand_weight[0],
            shrink_weight[0].T,
        ],
        place,
    )
    line_pieces = run(
        "weight_pieces",
        weight_pieces_body,
        [pieces_shape] * 6,
        [keep, swap(give, "pipe", 1)],
        place,
    )

    bias_pack = jnp.concatenate(
        [
            joint_bias[0].reshape(-1),
            expand_bias[0],
            output_bias[0],
            shrink_bias[0],
        ]
    )[None]
    bias_layers = both_layers(bias_pack, swap(bias_pack, "pipe", 1))
    biases = []
    for packed in bias_layers:
        at = 2 * width
        joint = jnp.concatenate(
            [packed[:, :width], jnp.zeros((1, width), F32), packed[:, width:at]], axis=1
        )
        grown = packed[:, at : at + hidden]
        rolled = jnp.concatenate([grown[:, hidden // 2 :], grown[:, : hidden // 2]], axis=1)
        grown = jnp.where(first, grown, rolled)
        at += hidden
        biases.append((joint, packed[:, at : at + model], grown, packed[:, at + model :]))

    activated = jax.nn.silu(conditions[:, 0].astype(F32)).astype(BF16)
    if direct:
        activated_all = gather(activated, "dp")
    else:
        activated_all = lax.all_gather(activated, "dp", axis=0).reshape(line_size * micro, -1)

    def line_first(value):
        return jnp.stack([value, swap(value, "dp", 2)]) if direct else value

    def line_second(pair):
        if direct:
            return swap(pair, "dp", 1)
        return lax.all_gather(pair, "dp", axis=0, tiled=True)

    def both_cores(pairs, others):
        if direct:
            wide = sum(pair.shape[2] for pair in pairs)
            lined = run(
                "stack_line", stack_body, [shape((model, wide), BF16)], pairs + others, place
            )[0]
        else:
            lined = jnp.concatenate(others, axis=1)
        return lined, swap(lined, "pipe", 1)

    def piece_of(layer, index):
        return line_pieces[3 * layer + index]

    first_a0 = line_first(piece_of(0, 0))

    if direct:
        mod_partial = run(
            "mod_first",
            mod_first_body,
            [shape((micro * LINE, columns), F32)],
            activated_all + [own_rows],
        )[0]
        mod_partials, first_a0 = tie(gather(mod_partial, "tensor"), first_a0)
        second_a0 = line_second(first_a0)
        first_e0 = line_first(after(piece_of(0, 1), first_a0))
        pieces = run(
            "mod_sum",
            functools.partial(mod_sum_body, count),
            [shape((micro, columns), F32)] * LINE,
            mod_partials,
        )
        pieces, second_a0 = tie(exchange(pieces, "dp"), second_a0)
        mod_mine, mod_other = pl.pallas_call(
            mod_join_body,
            out_shape=[shape((1, mods), F32)] * 2,
            in_specs=[pl.BlockSpec(memory_space=pltpu.SMEM)]
            + [pl.BlockSpec(memory_space=pltpu.VMEM)] * 5,
            out_specs=[pl.BlockSpec(memory_space=pltpu.VMEM)] * 2,
            scratch_shapes=[pltpu.VMEM((LINE, micro, columns), F32)],
            name="mod_join",
        )(place, *pieces, modulation_bias)
    else:
        mod_partial = dot(activated_all, own_rows)
        mod_partials = gather(mod_partial, "tensor")
        second_a0 = line_second(first_a0)
        first_e0 = line_first(piece_of(0, 1))
        mod_sum = tree_sum(mod_partials).reshape(line_size, micro, -1)
        mod_layer = lax.all_to_all(mod_sum, "dp", split_axis=0, concat_axis=0)
        mod_layer = jnp.swapaxes(mod_layer, 0, 1).reshape(micro, -1) + modulation_bias
        mod_mine, mod_other = mine(mod_layer)[None], other(mod_layer)[None]
    mod0, mod1 = both_layers(mod_mine, swap(mod_other, "pipe", 1))

    w_attn0 = both_cores([first_a0], [second_a0])
    mod0, mod1, first_e0 = tie(mod0, mod1, first_e0)
    second_e0 = line_second(first_e0)
    first_s0 = line_first(after(piece_of(0, 2), first_e0))
    own_f32 = shape((own, model), F32)
    own_bf16 = shape((own, model), BF16)
    blocks = [own_bf16] * count
    wide_bf16 = shape((rows, model), BF16)
    hidden_bf16 = shape((rows, hidden), BF16)
    vector = shape((1, model), F32)
    hidden_vector = shape((1, hidden), F32)
    h0, attn_in, g_y1, g_shrunk1 = run(
        "enter",
        enter_body,
        [own_f32, own_bf16, own_f32, own_bf16],
        [tokens[:, 0], cotangent[:, 0], mod0, mod1],
        place,
    )

    def kernel(name, body, outs, args, where=None):
        return run(name, functools.partial(body, count), outs, args, where)

    def attention(attn_rows, weight, bias):
        outs = kernel(
            "attention",
            attn_body,
            [
                wide_bf16,
                shape((rows, 3 * width), BF16),
                shape((width // HEAD, rows, rows), F32),
                shape((rows, width), BF16),
            ]
            + blocks,
            attn_rows + [weight[0], weight[1], bias],
            place,
        )
        return outs[:4], exchange(outs[4:], "tensor")

    def middle_of(parts, bias, h, mod):
        return kernel(
            "middle", middle_body, [own_f32, own_f32, own_bf16], parts + [bias, h, mod]
        )

    attn_rows, second_e0, first_s0 = tie(gather(attn_in, "tensor"), second_e0, first_s0)
    second_s0 = line_second(first_s0)
    first_a1 = line_first(after(piece_of(1, 0), first_s0))
    kept_attn0, parts = attention(attn_rows, w_attn0, biases[0][0])
    parts, second_s0, first_a1 = tie(parts, second_s0, first_a1)
    w_mlp0 = both_cores([first_e0, first_s0], [second_e0, second_s0])
    second_a1 = line_second(first_a1)
    first_e1 = line_first(after(piece_of(1, 1), first_a1))
    attended0, middle0, mlp_in = middle_of(parts, biases[0][1], h0, mod0)
    g_rows1 = gather(after(g_shrunk1, parts), "tensor")
    mlp_rows0, second_a1, first_e1, g_rows1 = tie(
        gather(mlp_in, "tensor"), second_a1, first_e1, g_rows1
    )
    w_attn1 = both_cores([first_a1], [second_a1])
    second_e1 = line_second(first_e1)
    first_s1 = line_first(after(piece_of(1, 2), first_e1))
    outs = kernel(
        "feed_forward",
        mlp_body,
        [wide_bf16, shape((rows, hidden), F32), hidden_bf16] + blocks,
        mlp_rows0 + [w_mlp0[0], w_mlp0[1], biases[0][2]],
    )
    mlp_rows0, pre0, hidden0 = outs[:3]
    parts, second_e1, first_s1 = tie(exchange(outs[3:], "tensor"), second_e1, first_s1)
    second_s1 = line_second(first_s1)
    shrunk0, passed, h1, attn_in = kernel(
        "between",
        between_body,
        [own_f32, own_bf16, own_f32, own_bf16],
        parts + [biases[0][3], middle0, mod0, mod1],
    )

    (attn_rows, w_attn1), second_s1 = tie((gather(attn_in, "tensor"), w_attn1), second_s1)
    w_mlp1 = both_cores([first_e1, first_s1], [second_e1, second_s1])
    kept_attn1, parts = attention(attn_rows, w_attn1, biases[1][0])
    attended1, middle1, mlp_in = middle_of(parts, biases[1][1], h1, mod1)
    outs = kernel(
        "feed_forward_both",
        mlp_both_body,
        [wide_bf16, wide_bf16, hidden_bf16, hidden_bf16, hidden_vector] + blocks + blocks,
        gather(mlp_in, "tensor") + g_rows1 + [w_mlp1[0], w_mlp1[1], biases[1][2]],
    )
    mlp_rows1, g_rows1, hidden1, g_pre1, expand_grad1 = outs[:5]
    y_partial, g_partial = outs[5 : 5 + count], outs[5 + count :]

    def middle_back(parts, middle, mod, g_y, attended):
        return kernel(
            "middle_back",
            middle_back_body,
            [own_f32, own_bf16] + [vector] * 4,
            parts + [middle, mod, g_y, attended],
        )

    def attention_back(g_rows, weight, kept):
        outs = kernel(
            "attention_back",
            attn_back_body,
            [wide_bf16, shape((rows, 3 * width), BF16), shape((1, 2 * width), F32)] + blocks,
            g_rows + [weight[0], weight[1], kept[1], kept[2]],
            place,
        )
        return outs[:3], exchange(outs[3:], "tensor")

    def chip_sum(grads):
        keep, give = grads
        return (keep + swap(give, "pipe", 1).astype(F32)).astype(BF16)

    def line_sum(whole):
        return lax.psum_scatter(whole, "dp", scatter_dimension=0, tiled=True)

    def line_parts(grads, pieces):
        keep, give = grads
        wide = keep.shape[1] // pieces
        if not direct:
            whole = chip_sum(grads)
            return [[whole[:, k * wide : (k + 1) * wide]] for k in range(pieces)]
        outs = run(
            "line_parts",
            line_parts_body,
            [shape((2, chunk, wide), BF16), shape((chunk, wide), F32), shape((chunk, wide), F32)]
            * pieces,
            [keep, swap(give, "pipe", 1)],
            place,
        )
        return [outs[3 * k : 3 * k + 3] for k in range(pieces)]

    def line_near(parts):
        return swap(parts[0], "dp", 1) if direct else parts[0]

    def line_far(parts, near):
        if not direct:
            return line_sum(near)
        return swap((parts[1] + near[1].astype(F32)).astype(BF16), "dp", 2)

    def line_total(parts, near, far):
        if not direct:
            return far
        return (parts[2] + near[0].astype(F32) + far.astype(F32)).astype(BF16)

    def own_halves(pair):
        return mine(pair), swap(other(pair), "pipe", 1)

    def mlp_weight_grads(mlp_rows, g_pre, g_rows, hidden_rows):
        return run(
            "mlp_weight_grads",
            mlp_weights_body,
            [shape((model, hidden), F32), shape((model, hidden), BF16)],
            [mlp_rows, g_pre, g_rows, hidden_rows],
        )

    def attn_weight_grads(kept, g_joint, g_rows):
        return run(
            "attn_weight_grads",
            attn_weights_body,
            [shape((model, 2 * width), F32), shape((model, 2 * width), BF16)],
            [kept[0], g_joint, g_rows, kept[3]],
            place,
        )

    (g_parts, (parts_e1, parts_s1)), y_partial = tie(
        (
            exchange(g_partial, "tensor"),
            line_parts(mlp_weight_grads(mlp_rows1, g_pre1, g_rows1, hidden1), 2),
        ),
        y_partial,
    )
    near_e1 = line_near(parts_e1)
    g_middle1, g_attended, g_shift_mlp1, g_scale_mlp1, g_gate_attn1, out_grad1 = middle_back(
        g_parts, middle1, mod1, g_y1, attended1
    )
    y_parts = exchange(y_partial, "tensor")
    g_rows, near_e1, parts_e1, parts_s1 = tie(
        gather(g_attended, "tensor"), near_e1, parts_e1, parts_s1
    )
    far_e1 = line_far(parts_e1, near_e1)
    near_s1 = line_near(parts_s1)
    (g_rows, g_joint, joint_grad1), parts = attention_back(g_rows, w_attn1, kept_attn1)
    (parts, (parts_a1,)), far_e1, near_s1, parts_s1 = tie(
        (parts, line_parts(attn_weight_grads(kept_attn1, g_joint, g_rows), 1)),
        far_e1,
        near_s1,
        parts_s1,
    )
    near_a1 = line_near(parts_a1)
    far_s1 = line_far(parts_s1, near_s1)
    g_passed, g_y0, g_shrunk0, g_shift_attn1, g_scale_attn1, g_gate_mlp0, shrink_grad0 = kernel(
        "between_back",
        between_back_body,
        [own_bf16, own_f32, own_bf16] + [vector] * 4,
        parts + [h1, mod1, mod0, g_middle1, shrunk0],
    )

    g_rows0, near_a1, far_s1, parts_a1 = tie(
        gather(g_shrunk0, "tensor"), near_a1, far_s1, parts_a1
    )
    far_a1 = line_far(parts_a1, near_a1)
    outs = kernel(
        "feed_forward_back",
        mlp_back_body,
        [wide_bf16, hidden_bf16, hidden_vector] + blocks,
        g_rows0 + [w_mlp0[0], w_mlp0[1], pre0],
    )
    g_rows0, g_pre0, expand_grad0 = outs[:3]
    ((parts, (parts_e0, parts_s0)),) = tie(
        (
            exchange(outs[3:], "tensor"),
            line_parts(mlp_weight_grads(mlp_rows0, g_pre0, g_rows0, hidden0), 2),
        )
    )
    near_e0 = line_near(parts_e0)
    g_middle0, g_attended, g_shift_mlp0, g_scale_mlp0, g_gate_attn0, out_grad0 = middle_back(
        parts, middle0, mod0, g_y0, attended0
    )
    y1, g_gate_mlp1, shrink_grad1 = kernel(
        "leave",
        leave_body,
        [own_bf16, vector, vector],
        y_parts + [biases[1][3], middle1, mod1, g_y1, g_shrunk1],
    )
    g_rows, near_e0, parts_e0, parts_s0, far_a1 = tie(
        gather(g_attended, "tensor"), near_e0, parts_e0, parts_s0, far_a1
    )
    far_e0 = line_far(parts_e0, near_e0)
    near_s0 = line_near(parts_s0)
    (g_rows, g_joint, joint_grad0), parts = attention_back(g_rows, w_attn0, kept_attn0)
    (parts, (parts_a0,)), far_e0, near_s0, parts_s0 = tie(
        (parts, line_parts(attn_weight_grads(kept_attn0, g_joint, g_rows), 1)),
        far_e0,
        near_s0,
        parts_s0,
    )
    near_a0 = line_near(parts_a0)
    far_s0 = line_far(parts_s0, near_s0)
    g_h0, g_shift_attn0, g_scale_attn0 = kernel(
        "finish_back",
        finish_back_body,
        [own_bf16, vector, vector],
        parts + [h0, mod0, g_middle0],
    )
    def own_layer_of_micros(pair):
        return jnp.stack(both_layers(mine(pair), swap(other(pair), "pipe", 1)))

    layer_outputs = own_layer_of_micros((passed, y1))
    input_grads = own_layer_of_micros((g_h0, g_passed))

    packed = run(
        "pack_grads",
        pack_body,
        [shape((2, mods + 2 * model), F32)],
        [
            g_shift_attn0,
            g_scale_attn0,
            g_gate_attn0,
            g_shift_mlp0,
            g_scale_mlp0,
            g_gate_mlp0,
            out_grad0,
            shrink_grad0,
            g_shift_attn1,
            g_scale_attn1,
            g_gate_attn1,
            g_shift_mlp1,
            g_scale_mlp1,
            g_gate_mlp1,
            out_grad1,
            shrink_grad1,
        ],
    )[0]
    packed_all, near_a0, far_s0 = tie(gather(packed, "tensor"), near_a0, far_s0)
    far_a0 = line_far(parts_a0, near_a0)
    keep, give = run(
        "grads_sum",
        functools.partial(grads_sum_body, count),
        [shape((1, mods + bias_width), F32)] * 2,
        packed_all + [joint_grad0, expand_grad0, joint_grad1, expand_grad1],
        place,
    )
    joined = run(
        "grads_join",
        grads_join_body,
        [shape((1, 2 * mods + bias_width), F32)],
        [keep, swap(give, "pipe", 1)],
        place,
    )[0]
    joined_all = gather(joined, "dp") if direct else lax.all_gather(joined, "dp", axis=0, tiled=True)
    joined_all, far_a0 = tie(joined_all, far_a0)
    mlp_grad0, mlp_grad1 = (
        jnp.concatenate([line_total(*first_piece), line_total(*second_piece)], axis=1)
        for first_piece, second_piece in (
            ((parts_e0, near_e0, far_e0), (parts_s0, near_s0, far_s0)),
            ((parts_e1, near_e1, far_e1), (parts_s1, near_s1, far_s1)),
        )
    )
    attn_grad0 = line_total(parts_a0, near_a0, far_a0)
    attn_grad1 = line_total(parts_a1, near_a1, far_a1)
    expand_w_grad, shrink_t_grad = run(
        "final_mlp",
        final_mlp_body,
        [shape((chunk, hidden), F32)] * 2,
        own_halves((mlp_grad0, mlp_grad1)),
        place,
    )
    joint_w_grad, output_w_grad = run(
        "final_attn",
        final_attn_body,
        [shape((3, chunk, width), F32), shape((width, chunk), F32)],
        own_halves((attn_grad0, attn_grad1)),
        place,
    )

    if direct:
        outs = run(
            "mod_back",
            mod_back_body,
            [shape(own_rows.shape, F32), shape((1, mods), F32), shape((1, bias_width), F32)]
            + [shape((micro, own_rows.shape[0]), F32)] * LINE,
            joined_all + activated_all + [own_rows],
            place,
        )
        ada_grad, ada_bias_grad, bias_sum = outs[:3]
        act_grad = tree_sum(exchange(outs[3:], "dp"))
    else:
        mod_grads = joined_all[:, : 2 * mods].reshape(line_size * micro, mods)
        bias_sum = jnp.sum(joined_all[:, 2 * mods :], axis=0, keepdims=True)
        ada_bias_grad = jnp.sum(mod_grads, axis=0, keepdims=True)
        picked = lax.dynamic_slice_in_dim(mod_grads, line * columns, columns, 1).astype(BF16)
        ada_grad = t_dot(activated_all, picked)
        act_partial = dot_t(picked, own_rows).reshape(line_size, micro, -1)
        act_grad = lax.psum_scatter(act_partial, "dp", scatter_dimension=0, tiled=False)
    _, silu_back = jax.vjp(jax.nn.silu, conditions[:, 0].astype(F32))
    cond_grad = silu_back(act_grad)[0]
    at = 2 * width
    return (
        layer_outputs[None, :, None],
        input_grads[None, :, None],
        cond_grad[None, :, None],
        ada_grad[None],
        ada_bias_grad,
        jnp.transpose(joint_w_grad, (1, 0, 2))[None],
        bias_sum[:, :at].reshape(1, 2, width),
        output_w_grad[None],
        bias_sum[:, at + hidden : at + hidden + model],
        expand_w_grad[None],
        bias_sum[:, at : at + hidden],
        shrink_t_grad.T[None],
        bias_sum[:, at + hidden + model :],
    )


def solution(mesh):
    in_specs = (
        P(None, "dp", "tensor", None),
        P(None, "dp", "tensor"),
        P(None, "dp", "tensor", None),
        P("pipe", "tensor", "dp"),
        P("pipe", None),
        P("pipe", "dp", None, "tensor"),
        P("pipe", None, "tensor"),
        P("pipe", "tensor", "dp"),
        P("pipe", None),
        P("pipe", "dp", "tensor"),
        P("pipe", "tensor"),
        P("pipe", "tensor", "dp"),
        P("pipe", None),
    )
    out_specs = (
        P("pipe", None, "dp", "tensor", None),
        P("pipe", None, "dp", "tensor", None),
        P("pipe", None, "dp", "tensor"),
        P("pipe", "tensor", "dp"),
        P("pipe", None),
        P("pipe", "dp", None, "tensor"),
        P("pipe", None, "tensor"),
        P("pipe", "tensor", "dp"),
        P("pipe", None),
        P("pipe", "dp", "tensor"),
        P("pipe", "tensor"),
        P("pipe", "tensor", "dp"),
        P("pipe", None),
    )
    return jax.shard_map(
        on_device, mesh=mesh, in_specs=in_specs, out_specs=out_specs, check_vma=False
    )
```

```python
import functools

import jax
import jax.numpy as jnp
from jax import lax
from jax.experimental import pallas as pl
from jax.experimental.pallas import tpu as pltpu
from jax.sharding import PartitionSpec as P

HEAD = 64
EPS = 1e-06
F32 = jnp.float32
BF16 = jnp.bfloat16
LINE = 4
VMEM_BYTES = 24 * 1024 * 1024
GELU_A = 0.7978845608028654
GELU_B = 0.044715


def swap(value, axis, mask):
    pairs = [(source, source ^ mask) for source in range(lax.axis_size(axis))]
    return lax.ppermute(value, axis, pairs)


def exchange(parts, axis):
    received = {k: swap(parts[k], axis, k) for k in range(len(parts) - 1, 0, -1)}
    return [parts[0]] + [received[k] for k in range(1, len(parts))]


def gather(value, axis):
    return exchange([value] * lax.axis_size(axis), axis)


def tree_sum(parts):
    parts = list(parts)
    while len(parts) > 1:
        parts = [parts[k] + parts[k + 1] for k in range(0, len(parts), 2)]
    return parts[0]


def shape(dims, dtype):
    return jax.ShapeDtypeStruct(dims, dtype)


def run(name, body, outs, args, place=None):
    specs = [pl.BlockSpec(memory_space=pltpu.VMEM) for _ in args]
    if place is not None:
        specs = [pl.BlockSpec(memory_space=pltpu.SMEM)] + specs
        args = [place] + list(args)
    return pl.pallas_call(
        body,
        out_shape=outs,
        in_specs=specs,
        out_specs=[pl.BlockSpec(memory_space=pltpu.VMEM) for _ in outs],
        compiler_params=pltpu.CompilerParams(vmem_limit_bytes=VMEM_BYTES),
        name=name,
    )(*args)


def dot(left, right):
    return jnp.dot(left, right, preferred_element_type=F32)


def dot_t(left, right):
    return lax.dot_general(left, right, (((1,), (1,)), ((), ())), preferred_element_type=F32)


def t_dot(left, right):
    return lax.dot_general(left, right, (((0,), (0,)), ((), ())), preferred_element_type=F32)


def normalize(values):
    centred = values - jnp.mean(values, axis=-1, keepdims=True)
    rstd = lax.rsqrt(jnp.mean(centred * centred, axis=-1, keepdims=True) + EPS)
    return centred * rstd, rstd


def normalize_back(grad, normed, rstd):
    return rstd * (
        grad
        - jnp.mean(grad, axis=-1, keepdims=True)
        - normed * jnp.mean(grad * normed, axis=-1, keepdims=True)
    )


def total(refs):
    return tree_sum([ref[...].astype(F32) for ref in refs])


def column_sum(values):
    return jnp.sum(values, axis=0, keepdims=True)


def part(mod_ref, index):
    width = mod_ref.shape[1] // 6
    return mod_ref[:, index * width : (index + 1) * width]


def gelu(pre):
    return 0.5 * pre * (1.0 + jnp.tanh(GELU_A * (pre + GELU_B * (pre * pre * pre))))


def gelu_slope(pre):
    square = pre * pre
    bent = jnp.tanh(GELU_A * (pre + GELU_B * (square * pre)))
    return 0.5 * (1.0 + bent) + 0.5 * pre * (1.0 - bent * bent) * (
        GELU_A * (1.0 + 3.0 * GELU_B * square)
    )


def put_rows(ref, refs):
    own = refs[0].shape[0]
    for k, source in enumerate(refs):
        ref[k * own : (k + 1) * own] = source[...]
    return ref[...]


def put_blocks(refs, values):
    own = refs[0].shape[0]
    for k, ref in enumerate(refs):
        ref[...] = values[k * own : (k + 1) * own].astype(ref.dtype)


def enter_body(place, tokens, cotangent, mod0, mod1, h_out, attn_in, g_y_out, g_shrunk):
    core = place[0]
    h = tokens[core].astype(F32)
    h_out[...] = h
    normed, _ = normalize(h)
    attn_in[...] = (normed * (1.0 + part(mod0, 1)) + part(mod0, 0)).astype(BF16)
    g_y = cotangent[core].astype(F32)
    g_y_out[...] = g_y
    g_shrunk[...] = (part(mod1, 5) * g_y).astype(BF16)


def weight_pieces_body(place, keep, received, *outs):
    first = place[0] == 0
    pieces = len(outs) // 2
    wide = outs[0].shape[1]
    for piece in range(pieces):
        own = keep[:, piece * wide : (piece + 1) * wide]
        other = received[:, piece * wide : (piece + 1) * wide]
        outs[piece][...] = jnp.where(first, own, other)
        outs[pieces + piece][...] = jnp.where(first, other, own)


def pick_attn(place, own, received):
    first = place[0] == 0
    width = own.shape[1] // 2
    mine, other = own[...], received[...]
    front = jnp.where(first, mine, other)
    back = jnp.where(first, other, mine)
    return front, back[:, :width], back[:, width:]


def attn_body(count, place, *refs):
    chunks = refs[:count]
    w_own, w_received, bias = refs[count : count + 3]
    rows_out, qkv_out, probs_out, mixed_out = refs[count + 3 : count + 7]
    partial = refs[count + 7 :]
    rows = put_rows(rows_out, chunks)
    w_front, w_value, w_out = pick_attn(place, w_own, w_received)
    width = w_value.shape[1]
    front = (dot(rows, w_front) + bias[:, : 2 * width]).astype(BF16)
    value = (dot(rows, w_value) + bias[:, 2 * width :]).astype(BF16)
    qkv_out[:, : 2 * width] = front
    qkv_out[:, 2 * width :] = value
    mixed = []
    for head in range(width // HEAD):
        at = head * HEAD
        query = front[:, at : at + HEAD]
        key = front[:, width + at : width + at + HEAD]
        scores = dot_t(query, key) * HEAD**-0.5
        powers = jnp.exp(scores - jnp.max(scores, axis=-1, keepdims=True))
        probs = powers / jnp.sum(powers, axis=-1, keepdims=True)
        probs_out[head] = probs
        mixed.append(dot(probs.astype(BF16), value[:, at : at + HEAD]))
    mixed = jnp.concatenate(mixed, axis=1).astype(BF16)
    mixed_out[...] = mixed
    put_blocks(partial, dot_t(mixed, w_out))


def middle_body(count, *refs):
    parts, (bias, h, mod, attended_out, middle_out, mlp_in) = refs[:count], refs[count:]
    attended = total(parts) + bias[...]
    attended_out[...] = attended
    middle = h[...] + part(mod, 2) * attended
    middle_out[...] = middle
    normed, _ = normalize(middle)
    mlp_in[...] = (normed * (1.0 + part(mod, 4)) + part(mod, 3)).astype(BF16)


def mlp_body(count, *refs):
    chunks = refs[:count]
    w_own, w_received, bias, rows_out, pre_out, hidden_out = refs[count : count + 6]
    partial = refs[count + 6 :]
    rows = put_rows(rows_out, chunks)
    half = w_own.shape[1] // 2
    shrunk = None
    for index, weight in enumerate((w_own, w_received)):
        at = index * half
        pre = dot(rows, weight[:, :half]) + bias[:, at : at + half]
        pre_out[:, at : at + half] = pre
        hidden = gelu(pre).astype(BF16)
        hidden_out[:, at : at + half] = hidden
        term = dot_t(hidden, weight[:, half:])
        shrunk = term if shrunk is None else shrunk + term
    put_blocks(partial, shrunk)


def mlp_both_body(count, *refs):
    chunks, g_chunks = refs[:count], refs[count : 2 * count]
    w_own, w_received, bias, rows_out, g_rows_out, hidden_out, g_pre_out, bias_grad = refs[
        2 * count : 2 * count + 8
    ]
    partial = refs[2 * count + 8 : 3 * count + 8]
    g_partial = refs[3 * count + 8 :]
    rows = put_rows(rows_out, chunks)
    g_rows = put_rows(g_rows_out, g_chunks)
    half = w_own.shape[1] // 2
    shrunk, g_in = None, None
    for index, weight in enumerate((w_own, w_received)):
        at = index * half
        pre = dot(rows, weight[:, :half]) + bias[:, at : at + half]
        hidden = gelu(pre).astype(BF16)
        hidden_out[:, at : at + half] = hidden
        g_pre = (dot(g_rows, weight[:, half:]) * gelu_slope(pre)).astype(BF16)
        g_pre_out[:, at : at + half] = g_pre
        bias_grad[:, at : at + half] = column_sum(g_pre.astype(F32))
        term = dot_t(hidden, weight[:, half:])
        g_term = dot_t(g_pre, weight[:, :half])
        shrunk = term if shrunk is None else shrunk + term
        g_in = g_term if g_in is None else g_in + g_term
    put_blocks(g_partial, g_in)
    put_blocks(partial, shrunk)


def mlp_back_body(count, *refs):
    g_chunks = refs[:count]
    w_own, w_received, pre_ref, g_rows_out, g_pre_out, bias_grad = refs[count : count + 6]
    g_partial = refs[count + 6 :]
    g_rows = put_rows(g_rows_out, g_chunks)
    half = w_own.shape[1] // 2
    g_in = None
    for index, weight in enumerate((w_own, w_received)):
        at = index * half
        pre = pre_ref[:, at : at + half]
        g_pre = (dot(g_rows, weight[:, half:]) * gelu_slope(pre)).astype(BF16)
        g_pre_out[:, at : at + half] = g_pre
        bias_grad[:, at : at + half] = column_sum(g_pre.astype(F32))
        g_term = dot_t(g_pre, weight[:, :half])
        g_in = g_term if g_in is None else g_in + g_term
    put_blocks(g_partial, g_in)


def between_body(count, *refs):
    parts = refs[:count]
    bias, middle, mod0, mod1, shrunk_out, passed_out, h_out, attn_in = refs[count:]
    shrunk = total(parts) + bias[...]
    shrunk_out[...] = shrunk
    passed = (middle[...] + part(mod0, 5) * shrunk).astype(BF16)
    passed_out[...] = passed
    h = passed.astype(F32)
    h_out[...] = h
    normed, _ = normalize(h)
    attn_in[...] = (normed * (1.0 + part(mod1, 1)) + part(mod1, 0)).astype(BF16)


def leave_body(count, *refs):
    parts = refs[:count]
    bias, middle, mod, g_y_ref, g_shrunk, y_out, g_gate, bias_grad = refs[count:]
    shrunk = total(parts) + bias[...]
    y_out[...] = (middle[...] + part(mod, 5) * shrunk).astype(BF16)
    g_gate[...] = column_sum(g_y_ref[...] * shrunk)
    bias_grad[...] = column_sum(g_shrunk[...].astype(F32))


def middle_back_body(count, *refs):
    parts = refs[:count]
    middle, mod, g_y, attended, g_middle_out, g_attended_out, g_shift, g_scale, g_gate, bias_grad = refs[
        count:
    ]
    g_in = total(parts)
    normed, rstd = normalize(middle[...])
    g_shift[...] = column_sum(g_in)
    g_scale[...] = column_sum(g_in * normed)
    g_middle = g_y[...] + normalize_back(g_in * (1.0 + part(mod, 4)), normed, rstd)
    g_middle_out[...] = g_middle
    g_gate[...] = column_sum(g_middle * attended[...])
    g_attended = (part(mod, 2) * g_middle).astype(BF16)
    g_attended_out[...] = g_attended
    bias_grad[...] = column_sum(g_attended.astype(F32))


def attn_back_body(count, place, *refs):
    g_chunks = refs[:count]
    w_own, w_received, qkv, probs_ref = refs[count : count + 4]
    g_rows_out, g_joint_out, bias_grad = refs[count + 4 : count + 7]
    g_partial = refs[count + 7 :]
    g_rows = put_rows(g_rows_out, g_chunks)
    w_front, w_value, w_out = pick_attn(place, w_own, w_received)
    width = w_value.shape[1]
    g_mixed = dot(g_rows, w_out).astype(BF16)
    g_query, g_key, g_value = [], [], []
    for head in range(width // HEAD):
        at = head * HEAD
        query = qkv[:, at : at + HEAD]
        key = qkv[:, width + at : width + at + HEAD]
        value = qkv[:, 2 * width + at : 2 * width + at + HEAD]
        probs = probs_ref[head]
        g_head = g_mixed[:, at : at + HEAD]
        g_probs = dot_t(g_head, value)
        row_dot = jnp.sum(probs * g_probs, axis=-1, keepdims=True)
        g_scores = (probs * (g_probs - row_dot)).astype(BF16)
        g_value.append(t_dot(probs.astype(BF16), g_head))
        g_query.append(dot(g_scores, key) * HEAD**-0.5)
        g_key.append(t_dot(g_scores, query) * HEAD**-0.5)
    g_front = jnp.concatenate(g_query + g_key, axis=1).astype(BF16)
    g_value = jnp.concatenate(g_value, axis=1).astype(BF16)
    g_joint_out[:, : 2 * width] = g_front
    g_joint_out[:, 2 * width :] = g_value
    bias_grad[:, :width] = column_sum(g_front[:, :width].astype(F32))
    bias_grad[:, width:] = column_sum(g_value.astype(F32))
    put_blocks(g_partial, dot_t(g_front, w_front) + dot_t(g_value, w_value))


def input_grad(parts, h, mod, g_middle, g_shift, g_scale):
    g_in = total(parts)
    normed, rstd = normalize(h[...])
    g_shift[...] = column_sum(g_in)
    g_scale[...] = column_sum(g_in * normed)
    return (g_middle[...] + normalize_back(g_in * (1.0 + part(mod, 1)), normed, rstd)).astype(BF16)


def between_back_body(count, *refs):
    parts = refs[:count]
    h, mod1, mod0, g_middle, shrunk, g_h_out, g_y_out, g_shrunk_out = refs[count : count + 8]
    g_shift, g_scale, g_gate, bias_grad = refs[count + 8 :]
    g_h = input_grad(parts, h, mod1, g_middle, g_shift, g_scale)
    g_h_out[...] = g_h
    g_y = g_h.astype(F32)
    g_y_out[...] = g_y
    g_gate[...] = column_sum(g_y * shrunk[...])
    g_shrunk = (part(mod0, 5) * g_y).astype(BF16)
    g_shrunk_out[...] = g_shrunk
    bias_grad[...] = column_sum(g_shrunk.astype(F32))


def finish_back_body(count, *refs):
    parts = refs[:count]
    h, mod, g_middle, g_h_out, g_shift, g_scale = refs[count:]
    g_h_out[...] = input_grad(parts, h, mod, g_middle, g_shift, g_scale)


def mlp_weights_body(rows, g_pre, g_rows, hidden, keep, give):
    half = keep.shape[1] // 2
    keep[:, :half] = t_dot(rows[...], g_pre[:, :half])
    keep[:, half:] = t_dot(g_rows[...], hidden[:, :half])
    give[:, :half] = t_dot(rows[...], g_pre[:, half:]).astype(BF16)
    give[:, half:] = t_dot(g_rows[...], hidden[:, half:]).astype(BF16)


def attn_weights_body(place, rows, g_joint, g_rows, mixed, keep, give):
    width = mixed.shape[1]
    first = place[0] == 0
    front = t_dot(rows[...], g_joint[:, : 2 * width])
    back = jnp.concatenate(
        [t_dot(rows[...], g_joint[:, 2 * width :]), t_dot(g_rows[...], mixed[...])], axis=1
    )
    keep[...] = jnp.where(first, front, back)
    give[...] = jnp.where(first, back, front).astype(BF16)


def line_blocks(place, k, rows):
    return pl.ds(pl.multiple_of((place[1] ^ k) * rows, 16), rows)


def stack_body(place, *refs):
    out = refs[-1]
    pieces = len(refs) // 2
    _, rows, wide = refs[0].shape
    for piece in range(pieces):
        pair, other = refs[piece], refs[pieces + piece]
        columns = slice(piece * wide, (piece + 1) * wide)
        for k, block in enumerate((pair[0], other[0], pair[1], other[1])):
            out[line_blocks(place, k, rows), columns] = block


def line_parts_body(place, keep, received, *outs):
    rows, wide = outs[2].shape

    for piece in range(len(outs) // 3):
        near, far, own = outs[3 * piece : 3 * piece + 3]
        columns = slice(piece * wide, (piece + 1) * wide)

        def block(k):
            at = line_blocks(place, k, rows)
            return keep[at, columns] + received[at, columns].astype(F32)

        near[0] = block(1).astype(BF16)
        near[1] = block(3).astype(BF16)
        far[...] = block(2)
        own[...] = block(0)


def final_mlp_body(place, mine, received, expand_out, shrink_t_out):
    first = place[0] == 0
    half = mine.shape[1] // 2
    own, other = mine[...].astype(F32), received[...].astype(F32)
    for index, values in enumerate((jnp.where(first, own, other), jnp.where(first, other, own))):
        expand_out[:, index * half : (index + 1) * half] = values[:, :half]
        shrink_t_out[:, index * half : (index + 1) * half] = values[:, half:]


def final_attn_body(place, mine, received, joint_out, out_out):
    first = place[0] == 0
    width = mine.shape[1] // 2
    own, other = mine[...].astype(F32), received[...].astype(F32)
    front, back = jnp.where(first, own, other), jnp.where(first, other, own)
    joint_out[0] = front[:, :width]
    joint_out[1] = front[:, width:]
    joint_out[2] = back[:, :width]
    out_out[...] = back[:, width:].T


def mod_first_body(a0, a1, a2, a3, weight, out):
    rows = jnp.concatenate([a0[...], a1[...], a2[...], a3[...]], axis=0)
    out[...] = dot(rows, weight[...])


def mod_sum_body(count, *refs):
    values = total(refs[:count])
    outs = refs[count:]
    micro = outs[0].shape[0]
    for k, out in enumerate(outs):
        out[...] = values[k * micro : (k + 1) * micro]


def mod_join_body(place, p0, p1, p2, p3, bias, mine, other, scratch):
    for k, ref in enumerate((p0, p1, p2, p3)):
        scratch[place[1] ^ k] = ref[...]
    values = jnp.concatenate([scratch[j] for j in range(LINE)], axis=1) + bias[...]
    first = place[0] == 0
    mine[...] = jnp.where(first, values[0:1], values[1:2])
    other[...] = jnp.where(first, values[1:2], values[0:1])


def pack_body(*refs):
    out, pieces = refs[-1], refs[:-1]
    count = len(pieces) // 2
    for row in range(2):
        at = 0
        for ref in pieces[row * count : (row + 1) * count]:
            out[row : row + 1, at : at + ref.shape[1]] = ref[...]
            at += ref.shape[1]


def grads_sum_body(count, place, *refs):
    parts = refs[:count]
    joint0, expand0, joint1, expand1, keep, give = refs[count:]
    first = place[0] == 0
    values = total(parts)
    hidden = expand0.shape[1]
    mod_width = values.shape[1] // 8 * 6
    rounded = values[:, :mod_width].astype(BF16).astype(F32)
    sums = values[:, mod_width:]
    half = hidden // 2

    def natural(ref):
        now = ref[...]
        return jnp.where(first, now, jnp.concatenate([now[:, half:], now[:, :half]], axis=1))

    rows = []
    for row, (joint, expand) in enumerate(((joint0, expand0), (joint1, expand1))):
        rows.append(
            jnp.concatenate(
                [rounded[row : row + 1], joint[...], natural(expand), sums[row : row + 1]], axis=1
            )
        )
    keep[...] = jnp.where(first, rows[0], rows[1])
    give[...] = jnp.where(first, rows[1], rows[0])


def grads_join_body(place, keep, received, out):
    mods = out.shape[1] - keep.shape[1]
    first = place[0] == 0
    own, other = keep[...], received[...]
    out[:, :mods] = jnp.where(first, own, other)[:, :mods]
    out[:, mods : 2 * mods] = jnp.where(first, other, own)[:, :mods]
    out[:, 2 * mods :] = own[:, mods:] + other[:, mods:]


def mod_back_body(place, g0, g1, g2, g3, a0, a1, a2, a3, weight, w_grad, b_grad, bias, c0, c1, c2, c3):
    columns = weight.shape[1]
    mods = columns * LINE
    grads = (g0, g1, g2, g3)
    at = pl.multiple_of(place[1] * columns, 128)
    rows = []
    for ref in grads:
        rows.append(ref[:, pl.ds(at, columns)])
        rows.append(ref[:, pl.ds(pl.multiple_of(at + mods, 128), columns)])
    picked = jnp.concatenate(rows, axis=0).astype(BF16)
    activated = jnp.concatenate([a0[...], a1[...], a2[...], a3[...]], axis=0)
    w_grad[...] = t_dot(activated, picked)
    act = dot_t(picked, weight[...])
    for k, out in enumerate((c0, c1, c2, c3)):
        out[...] = act[2 * k : 2 * k + 2]
    b_grad[...] = tree_sum([ref[:, :mods] + ref[:, mods : 2 * mods] for ref in grads])
    bias[...] = tree_sum([ref[:, 2 * mods :] for ref in grads])


def on_device(
    tokens,
    conditions,
    cotangent,
    modulation_weight,
    modulation_bias,
    joint_weight,
    joint_bias,
    output_weight,
    output_bias,
    expand_weight,
    expand_bias,
    shrink_weight,
    shrink_bias,
):
    core = lax.axis_index("pipe")
    first = core == 0
    line = lax.axis_index("dp")
    place = jnp.stack([core, line]).astype(jnp.int32)
    line_size = lax.axis_size("dp")
    count = lax.axis_size("tensor")
    direct = line_size == LINE
    micro, _, own, model = tokens.shape
    width = output_weight.shape[1]
    hidden = expand_weight.shape[2]
    chunk = model // line_size
    rows = own * count
    columns = modulation_weight.shape[2]
    mods = 6 * model
    bias_width = 2 * width + hidden + 2 * model
    own_rows = modulation_weight[0]

    def mine(pair):
        return jnp.where(first, pair[0], pair[1])

    def other(pair):
        return jnp.where(first, pair[1], pair[0])

    def both_layers(kept, received):
        return jnp.where(first, kept, received), jnp.where(first, received, kept)

    def after(value, earlier):
        return lax.optimization_barrier((value, earlier))[0]

    def tie(main, *rest):
        return lax.optimization_barrier((main,) + rest)

    split = 2 * width
    pieces_shape = shape((chunk, split), BF16)
    joint_blocks = jnp.transpose(joint_weight[0], (1, 0, 2))
    expand, shrink_t = expand_weight[0], shrink_weight[0].T
    half = hidden // 2
    halves = (
        jnp.concatenate(
            [joint_blocks[0], joint_blocks[1], expand[:, :half], shrink_t[:, :half]], axis=1
        ),
        jnp.concatenate(
            [joint_blocks[2], output_weight[0].T, expand[:, half:], shrink_t[:, half:]], axis=1
        ),
    )
    keep, give = mine(halves), other(halves)
    line_pieces = run(
        "weight_pieces",
        weight_pieces_body,
        [pieces_shape] * 6,
        [keep, swap(give, "pipe", 1)],
        place,
    )

    bias_pack = jnp.concatenate(
        [
            joint_bias[0].reshape(-1),
            expand_bias[0],
            output_bias[0],
            shrink_bias[0],
        ]
    )[None]
    bias_layers = both_layers(bias_pack, swap(bias_pack, "pipe", 1))
    biases = []
    for packed in bias_layers:
        at = 2 * width
        joint = jnp.concatenate(
            [packed[:, :width], jnp.zeros((1, width), F32), packed[:, width:at]], axis=1
        )
        grown = packed[:, at : at + hidden]
        rolled = jnp.concatenate([grown[:, hidden // 2 :], grown[:, : hidden // 2]], axis=1)
        grown = jnp.where(first, grown, rolled)
        at += hidden
        biases.append((joint, packed[:, at : at + model], grown, packed[:, at + model :]))

    activated = jax.nn.silu(conditions[:, 0].astype(F32)).astype(BF16)
    if direct:
        activated_all = gather(activated, "dp")
    else:
        activated_all = lax.all_gather(activated, "dp", axis=0).reshape(line_size * micro, -1)

    def line_first(value):
        return (value, swap(value, "dp", 2)) if direct else value

    def line_second(pair):
        if not direct:
            return pair, lax.all_gather(pair, "dp", axis=0, tiled=True)
        stacked = jnp.stack(pair)
        return stacked, swap(stacked, "dp", 1)

    def both_cores(*steps):
        pairs, others = [step[0] for step in steps], [step[1] for step in steps]
        if direct:
            wide = sum(pair.shape[2] for pair in pairs)
            lined = run(
                "stack_line", stack_body, [shape((model, wide), BF16)], pairs + others, place
            )[0]
        else:
            lined = jnp.concatenate(others, axis=1)
        return lined, swap(lined, "pipe", 1)

    def piece_of(layer, index):
        return line_pieces[3 * layer + index]

    first_a0 = line_first(after(piece_of(0, 0), activated_all))

    if direct:
        mod_partial = run(
            "mod_first",
            mod_first_body,
            [shape((micro * LINE, columns), F32)],
            activated_all + [own_rows],
        )[0]
        mod_partials, first_a0 = tie(gather(mod_partial, "tensor"), first_a0)
        second_a0 = line_second(first_a0)
        first_e0 = line_first(after(piece_of(0, 1), first_a0))
        pieces = run(
            "mod_sum",
            functools.partial(mod_sum_body, count),
            [shape((micro, columns), F32)] * LINE,
            mod_partials,
        )
        pieces, second_a0 = tie(exchange(pieces, "dp"), second_a0)
        mod_mine, mod_other = pl.pallas_call(
            mod_join_body,
            out_shape=[shape((1, mods), F32)] * 2,
            in_specs=[pl.BlockSpec(memory_space=pltpu.SMEM)]
            + [pl.BlockSpec(memory_space=pltpu.VMEM)] * 5,
            out_specs=[pl.BlockSpec(memory_space=pltpu.VMEM)] * 2,
            scratch_shapes=[pltpu.VMEM((LINE, micro, columns), F32)],
            name="mod_join",
        )(place, *pieces, modulation_bias)
    else:
        mod_partial = dot(activated_all, own_rows)
        mod_partials = gather(mod_partial, "tensor")
        second_a0 = line_second(first_a0)
        first_e0 = line_first(piece_of(0, 1))
        mod_sum = tree_sum(mod_partials).reshape(line_size, micro, -1)
        mod_layer = lax.all_to_all(mod_sum, "dp", split_axis=0, concat_axis=0)
        mod_layer = jnp.swapaxes(mod_layer, 0, 1).reshape(micro, -1) + modulation_bias
        mod_mine, mod_other = mine(mod_layer)[None], other(mod_layer)[None]
    mod0, mod1 = both_layers(mod_mine, swap(mod_other, "pipe", 1))

    w_attn0 = both_cores(second_a0)
    mod0, mod1, first_e0 = tie(mod0, mod1, first_e0)
    second_e0 = line_second(first_e0)
    first_s0 = line_first(after(piece_of(0, 2), first_e0))
    own_f32 = shape((own, model), F32)
    own_bf16 = shape((own, model), BF16)
    blocks = [own_bf16] * count
    wide_bf16 = shape((rows, model), BF16)
    hidden_bf16 = shape((rows, hidden), BF16)
    vector = shape((1, model), F32)
    hidden_vector = shape((1, hidden), F32)
    h0, attn_in, g_y1, g_shrunk1 = run(
        "enter",
        enter_body,
        [own_f32, own_bf16, own_f32, own_bf16],
        [tokens[:, 0], cotangent[:, 0], mod0, mod1],
        place,
    )

    def kernel(name, body, outs, args, where=None):
        return run(name, functools.partial(body, count), outs, args, where)

    def attention(attn_rows, weight, bias):
        outs = kernel(
            "attention",
            attn_body,
            [
                wide_bf16,
                shape((rows, 3 * width), BF16),
                shape((width // HEAD, rows, rows), F32),
                shape((rows, width), BF16),
            ]
            + blocks,
            attn_rows + [weight[0], weight[1], bias],
            place,
        )
        return outs[:4], exchange(outs[4:], "tensor")

    def middle_of(parts, bias, h, mod):
        return kernel(
            "middle", middle_body, [own_f32, own_f32, own_bf16], parts + [bias, h, mod]
        )

    attn_rows, second_e0, first_s0 = tie(gather(attn_in, "tensor"), second_e0, first_s0)
    second_s0 = line_second(first_s0)
    first_a1 = line_first(after(piece_of(1, 0), first_s0))
    kept_attn0, parts = attention(attn_rows, w_attn0, biases[0][0])
    parts, second_s0, first_a1 = tie(parts, second_s0, first_a1)
    w_mlp0 = both_cores(second_e0, second_s0)
    second_a1 = line_second(first_a1)
    first_e1 = line_first(after(piece_of(1, 1), first_a1))
    attended0, middle0, mlp_in = middle_of(parts, biases[0][1], h0, mod0)
    g_rows1 = gather(after(g_shrunk1, parts), "tensor")
    mlp_rows0, second_a1, first_e1, g_rows1 = tie(
        gather(mlp_in, "tensor"), second_a1, first_e1, g_rows1
    )
    w_attn1 = both_cores(second_a1)
    second_e1 = line_second(first_e1)
    first_s1 = line_first(after(piece_of(1, 2), first_e1))
    outs = kernel(
        "feed_forward",
        mlp_body,
        [wide_bf16, shape((rows, hidden), F32), hidden_bf16] + blocks,
        mlp_rows0 + [w_mlp0[0], w_mlp0[1], biases[0][2]],
    )
    mlp_rows0, pre0, hidden0 = outs[:3]
    (parts,) = tie(exchange(outs[3:], "tensor"))
    parts, second_e1, first_s1 = tie(parts, second_e1, first_s1)
    second_s1 = line_second(first_s1)
    shrunk0, passed, h1, attn_in = kernel(
        "between",
        between_body,
        [own_f32, own_bf16, own_f32, own_bf16],
        parts + [biases[0][3], middle0, mod0, mod1],
    )

    (attn_rows, w_attn1), second_s1 = tie((gather(attn_in, "tensor"), w_attn1), second_s1)
    w_mlp1 = both_cores(second_e1, second_s1)
    kept_attn1, parts = attention(attn_rows, w_attn1, biases[1][0])
    attended1, middle1, mlp_in = middle_of(parts, biases[1][1], h1, mod1)
    outs = kernel(
        "feed_forward_both",
        mlp_both_body,
        [wide_bf16, wide_bf16, hidden_bf16, hidden_bf16, hidden_vector] + blocks + blocks,
        gather(mlp_in, "tensor") + g_rows1 + [w_mlp1[0], w_mlp1[1], biases[1][2]],
    )
    mlp_rows1, g_rows1, hidden1, g_pre1, expand_grad1 = outs[:5]
    y_partial, g_partial = outs[5 : 5 + count], outs[5 + count :]

    def middle_back(parts, middle, mod, g_y, attended):
        return kernel(
            "middle_back",
            middle_back_body,
            [own_f32, own_bf16] + [vector] * 4,
            parts + [middle, mod, g_y, attended],
        )

    def attention_back(g_rows, weight, kept):
        outs = kernel(
            "attention_back",
            attn_back_body,
            [wide_bf16, shape((rows, 3 * width), BF16), shape((1, 2 * width), F32)] + blocks,
            g_rows + [weight[0], weight[1], kept[1], kept[2]],
            place,
        )
        return outs[:3], exchange(outs[3:], "tensor")

    def chip_sum(grads):
        keep, give = grads
        return (keep + swap(give, "pipe", 1).astype(F32)).astype(BF16)

    def line_sum(whole):
        return lax.psum_scatter(whole, "dp", scatter_dimension=0, tiled=True)

    def line_parts(grads, pieces):
        keep, give = grads
        wide = keep.shape[1] // pieces
        if not direct:
            whole = chip_sum(grads)
            return [[whole[:, k * wide : (k + 1) * wide]] for k in range(pieces)]
        outs = run(
            "line_parts",
            line_parts_body,
            [shape((2, chunk, wide), BF16), shape((chunk, wide), F32), shape((chunk, wide), F32)]
            * pieces,
            [keep, swap(give, "pipe", 1)],
            place,
        )
        return [outs[3 * k : 3 * k + 3] for k in range(pieces)]

    def line_near(parts):
        return swap(parts[0], "dp", 1) if direct else parts[0]

    def line_far(parts, near):
        if not direct:
            return line_sum(near)
        return swap((parts[1] + near[1].astype(F32)).astype(BF16), "dp", 2)

    def line_total(parts, near, far):
        if not direct:
            return far
        return (parts[2] + near[0].astype(F32) + far.astype(F32)).astype(BF16)

    def own_halves(pair):
        return mine(pair), swap(other(pair), "pipe", 1)

    def mlp_weight_grads(mlp_rows, g_pre, g_rows, hidden_rows):
        return run(
            "mlp_weight_grads",
            mlp_weights_body,
            [shape((model, hidden), F32), shape((model, hidden), BF16)],
            [mlp_rows, g_pre, g_rows, hidden_rows],
        )

    def attn_weight_grads(kept, g_joint, g_rows):
        return run(
            "attn_weight_grads",
            attn_weights_body,
            [shape((model, 2 * width), F32), shape((model, 2 * width), BF16)],
            [kept[0], g_joint, g_rows, kept[3]],
            place,
        )

    (g_parts, (parts_e1, parts_s1)), y_partial = tie(
        (
            exchange(g_partial, "tensor"),
            line_parts(mlp_weight_grads(mlp_rows1, g_pre1, g_rows1, hidden1), 2),
        ),
        y_partial,
    )
    near_e1 = line_near(parts_e1)
    g_middle1, g_attended, g_shift_mlp1, g_scale_mlp1, g_gate_attn1, out_grad1 = middle_back(
        g_parts, middle1, mod1, g_y1, attended1
    )
    y_parts = exchange(y_partial, "tensor")
    g_rows, near_e1, parts_e1, parts_s1 = tie(
        gather(g_attended, "tensor"), near_e1, parts_e1, parts_s1
    )
    far_e1 = line_far(parts_e1, near_e1)
    near_s1 = line_near(parts_s1)
    (g_rows, g_joint, joint_grad1), parts = attention_back(g_rows, w_attn1, kept_attn1)
    (parts, (parts_a1,)), far_e1, near_s1, parts_s1 = tie(
        (parts, line_parts(attn_weight_grads(kept_attn1, g_joint, g_rows), 1)),
        far_e1,
        near_s1,
        parts_s1,
    )
    near_a1 = line_near(parts_a1)
    far_s1 = line_far(parts_s1, near_s1)
    g_passed, g_y0, g_shrunk0, g_shift_attn1, g_scale_attn1, g_gate_mlp0, shrink_grad0 = kernel(
        "between_back",
        between_back_body,
        [own_bf16, own_f32, own_bf16] + [vector] * 4,
        parts + [h1, mod1, mod0, g_middle1, shrunk0],
    )

    g_rows0, near_a1, far_s1, parts_a1 = tie(
        gather(g_shrunk0, "tensor"), near_a1, far_s1, parts_a1
    )
    far_a1 = line_far(parts_a1, near_a1)
    outs = kernel(
        "feed_forward_back",
        mlp_back_body,
        [wide_bf16, hidden_bf16, hidden_vector] + blocks,
        g_rows0 + [w_mlp0[0], w_mlp0[1], pre0],
    )
    g_rows0, g_pre0, expand_grad0 = outs[:3]
    parts, (parts_m0,) = tie(
        exchange(outs[3:], "tensor"),
        line_parts(mlp_weight_grads(mlp_rows0, g_pre0, g_rows0, hidden0), 1),
    )
    near_m0 = line_near(parts_m0)
    g_middle0, g_attended, g_shift_mlp0, g_scale_mlp0, g_gate_attn0, out_grad0 = middle_back(
        parts, middle0, mod0, g_y0, attended0
    )
    y1, g_gate_mlp1, shrink_grad1 = kernel(
        "leave",
        leave_body,
        [own_bf16, vector, vector],
        y_parts + [biases[1][3], middle1, mod1, g_y1, g_shrunk1],
    )
    g_rows, near_m0, far_a1 = tie(gather(g_attended, "tensor"), near_m0, far_a1)
    far_m0 = line_far(parts_m0, near_m0)
    (g_rows, g_joint, joint_grad0), parts = attention_back(g_rows, w_attn0, kept_attn0)
    parts, (parts_a0,) = tie(
        parts, line_parts(attn_weight_grads(kept_attn0, g_joint, g_rows), 1)
    )
    near_a0 = line_near(parts_a0)
    g_h0, g_shift_attn0, g_scale_attn0 = kernel(
        "finish_back",
        finish_back_body,
        [own_bf16, vector, vector],
        parts + [h0, mod0, g_middle0],
    )
    def own_layer_of_micros(pair):
        return jnp.stack(both_layers(mine(pair), swap(other(pair), "pipe", 1)))

    layer_outputs = own_layer_of_micros((passed, y1))
    input_grads = own_layer_of_micros((g_h0, g_passed))

    packed = run(
        "pack_grads",
        pack_body,
        [shape((2, mods + 2 * model), F32)],
        [
            g_shift_attn0,
            g_scale_attn0,
            g_gate_attn0,
            g_shift_mlp0,
            g_scale_mlp0,
            g_gate_mlp0,
            out_grad0,
            shrink_grad0,
            g_shift_attn1,
            g_scale_attn1,
            g_gate_attn1,
            g_shift_mlp1,
            g_scale_mlp1,
            g_gate_mlp1,
            out_grad1,
            shrink_grad1,
        ],
    )[0]
    packed_all, near_a0, far_m0 = tie(gather(packed, "tensor"), near_a0, far_m0)
    far_a0 = line_far(parts_a0, near_a0)
    keep, give = run(
        "grads_sum",
        functools.partial(grads_sum_body, count),
        [shape((1, mods + bias_width), F32)] * 2,
        packed_all + [joint_grad0, expand_grad0, joint_grad1, expand_grad1],
        place,
    )
    joined = run(
        "grads_join",
        grads_join_body,
        [shape((1, 2 * mods + bias_width), F32)],
        [keep, swap(give, "pipe", 1)],
        place,
    )[0]
    joined_all = gather(joined, "dp") if direct else lax.all_gather(joined, "dp", axis=0, tiled=True)
    joined_all, far_a0 = tie(joined_all, far_a0)
    mlp_grad0 = line_total(parts_m0, near_m0, far_m0)
    mlp_grad1 = jnp.concatenate(
        [line_total(parts_e1, near_e1, far_e1), line_total(parts_s1, near_s1, far_s1)], axis=1
    )
    attn_grad0 = line_total(parts_a0, near_a0, far_a0)
    attn_grad1 = line_total(parts_a1, near_a1, far_a1)
    expand_w_grad, shrink_t_grad = run(
        "final_mlp",
        final_mlp_body,
        [shape((chunk, hidden), F32)] * 2,
        own_halves((mlp_grad0, mlp_grad1)),
        place,
    )
    joint_w_grad, output_w_grad = run(
        "final_attn",
        final_attn_body,
        [shape((3, chunk, width), F32), shape((width, chunk), F32)],
        own_halves((attn_grad0, attn_grad1)),
        place,
    )

    if direct:
        outs = run(
            "mod_back",
            mod_back_body,
            [shape(own_rows.shape, F32), shape((1, mods), F32), shape((1, bias_width), F32)]
            + [shape((micro, own_rows.shape[0]), F32)] * LINE,
            joined_all + activated_all + [own_rows],
            place,
        )
        ada_grad, ada_bias_grad, bias_sum = outs[:3]
        act_grad = tree_sum(exchange(outs[3:], "dp"))
    else:
        mod_grads = joined_all[:, : 2 * mods].reshape(line_size * micro, mods)
        bias_sum = jnp.sum(joined_all[:, 2 * mods :], axis=0, keepdims=True)
        ada_bias_grad = jnp.sum(mod_grads, axis=0, keepdims=True)
        picked = lax.dynamic_slice_in_dim(mod_grads, line * columns, columns, 1).astype(BF16)
        ada_grad = t_dot(activated_all, picked)
        act_partial = dot_t(picked, own_rows).reshape(line_size, micro, -1)
        act_grad = lax.psum_scatter(act_partial, "dp", scatter_dimension=0, tiled=False)
    _, silu_back = jax.vjp(jax.nn.silu, conditions[:, 0].astype(F32))
    cond_grad = silu_back(act_grad)[0]
    at = 2 * width
    return (
        layer_outputs[None, :, None],
        input_grads[None, :, None],
        cond_grad[None, :, None],
        ada_grad[None],
        ada_bias_grad,
        jnp.transpose(joint_w_grad, (1, 0, 2))[None],
        bias_sum[:, :at].reshape(1, 2, width),
        output_w_grad[None],
        bias_sum[:, at + hidden : at + hidden + model],
        expand_w_grad[None],
        bias_sum[:, at : at + hidden],
        shrink_t_grad.T[None],
        bias_sum[:, at + hidden + model :],
    )


def solution(mesh):
    in_specs = (
        P(None, "dp", "tensor", None),
        P(None, "dp", "tensor"),
        P(None, "dp", "tensor", None),
        P("pipe", "tensor", "dp"),
        P("pipe", None),
        P("pipe", "dp", None, "tensor"),
        P("pipe", None, "tensor"),
        P("pipe", "tensor", "dp"),
        P("pipe", None),
        P("pipe", "dp", "tensor"),
        P("pipe", "tensor"),
        P("pipe", "tensor", "dp"),
        P("pipe", None),
    )
    out_specs = (
        P("pipe", None, "dp", "tensor", None),
        P("pipe", None, "dp", "tensor", None),
        P("pipe", None, "dp", "tensor"),
        P("pipe", "tensor", "dp"),
        P("pipe", None),
        P("pipe", "dp", None, "tensor"),
        P("pipe", None, "tensor"),
        P("pipe", "tensor", "dp"),
        P("pipe", None),
        P("pipe", "dp", "tensor"),
        P("pipe", "tensor"),
        P("pipe", "tensor", "dp"),
        P("pipe", None),
    )
    return jax.shard_map(
        on_device, mesh=mesh, in_specs=in_specs, out_specs=out_specs, check_vma=False
    )
```

```python
import functools

import jax
import jax.numpy as jnp
from jax import lax
from jax.experimental import pallas as pl
from jax.experimental.pallas import tpu as pltpu
from jax.sharding import PartitionSpec as P

HEAD = 64
EPS = 1e-06
F32 = jnp.float32
BF16 = jnp.bfloat16
LINE = 4
VMEM_BYTES = 24 * 1024 * 1024
GELU_A = 0.7978845608028654
GELU_B = 0.044715


def swap(value, axis, mask):
    pairs = [(source, source ^ mask) for source in range(lax.axis_size(axis))]
    return lax.ppermute(value, axis, pairs)


def exchange(parts, axis):
    received = {k: swap(parts[k], axis, k) for k in range(len(parts) - 1, 0, -1)}
    return [parts[0]] + [received[k] for k in range(1, len(parts))]


def gather(value, axis):
    return exchange([value] * lax.axis_size(axis), axis)


def tree_sum(parts):
    parts = list(parts)
    while len(parts) > 1:
        parts = [parts[k] + parts[k + 1] for k in range(0, len(parts), 2)]
    return parts[0]


def shape(dims, dtype):
    return jax.ShapeDtypeStruct(dims, dtype)


def run(name, body, outs, args, place=None):
    specs = [pl.BlockSpec(memory_space=pltpu.VMEM) for _ in args]
    if place is not None:
        specs = [pl.BlockSpec(memory_space=pltpu.SMEM)] + specs
        args = [place] + list(args)
    return pl.pallas_call(
        body,
        out_shape=outs,
        in_specs=specs,
        out_specs=[pl.BlockSpec(memory_space=pltpu.VMEM) for _ in outs],
        compiler_params=pltpu.CompilerParams(vmem_limit_bytes=VMEM_BYTES),
        name=name,
    )(*args)


def dot(left, right):
    return jnp.dot(left, right, preferred_element_type=F32)


def dot_t(left, right):
    return lax.dot_general(left, right, (((1,), (1,)), ((), ())), preferred_element_type=F32)


def t_dot(left, right):
    return lax.dot_general(left, right, (((0,), (0,)), ((), ())), preferred_element_type=F32)


def normalize(values):
    centred = values - jnp.mean(values, axis=-1, keepdims=True)
    rstd = lax.rsqrt(jnp.mean(centred * centred, axis=-1, keepdims=True) + EPS)
    return centred * rstd, rstd


def normalize_back(grad, normed, rstd):
    return rstd * (
        grad
        - jnp.mean(grad, axis=-1, keepdims=True)
        - normed * jnp.mean(grad * normed, axis=-1, keepdims=True)
    )


def total(refs):
    return tree_sum([ref[...].astype(F32) for ref in refs])


def column_sum(values):
    return jnp.sum(values, axis=0, keepdims=True)


def part(mod_ref, index):
    width = mod_ref.shape[1] // 6
    return mod_ref[:, index * width : (index + 1) * width]


def gelu(pre):
    return 0.5 * pre * (1.0 + jnp.tanh(GELU_A * (pre + GELU_B * (pre * pre * pre))))


def gelu_slope(pre):
    square = pre * pre
    bent = jnp.tanh(GELU_A * (pre + GELU_B * (square * pre)))
    return 0.5 * (1.0 + bent) + 0.5 * pre * (1.0 - bent * bent) * (
        GELU_A * (1.0 + 3.0 * GELU_B * square)
    )


def put_rows(ref, refs):
    own = refs[0].shape[0]
    for k, source in enumerate(refs):
        ref[k * own : (k + 1) * own] = source[...]
    return ref[...]


def put_blocks(refs, values):
    own = refs[0].shape[0]
    for k, ref in enumerate(refs):
        ref[...] = values[k * own : (k + 1) * own].astype(ref.dtype)


def enter_body(place, tokens, cotangent, mod0, mod1, h_out, attn_in, g_y_out, g_shrunk):
    core = place[0]
    h = tokens[core].astype(F32)
    h_out[...] = h
    normed, _ = normalize(h)
    attn_in[...] = (normed * (1.0 + part(mod0, 1)) + part(mod0, 0)).astype(BF16)
    g_y = cotangent[core].astype(F32)
    g_y_out[...] = g_y
    g_shrunk[...] = (part(mod1, 5) * g_y).astype(BF16)


def weight_pieces_body(place, keep, received, *outs):
    first = place[0] == 0
    pieces = len(outs) // 2
    wide = outs[0].shape[1]
    for piece in range(pieces):
        own = keep[:, piece * wide : (piece + 1) * wide]
        other = received[:, piece * wide : (piece + 1) * wide]
        outs[piece][...] = jnp.where(first, own, other)
        outs[pieces + piece][...] = jnp.where(first, other, own)


def pick_attn(place, own, received):
    first = place[0] == 0
    width = own.shape[1] // 2
    mine, other = own[...], received[...]
    front = jnp.where(first, mine, other)
    back = jnp.where(first, other, mine)
    return front, back[:, :width], back[:, width:]


def attn_body(count, place, *refs):
    chunks = refs[:count]
    w_own, w_received, bias = refs[count : count + 3]
    rows_out, qkv_out, probs_out, mixed_out = refs[count + 3 : count + 7]
    partial = refs[count + 7 :]
    rows = put_rows(rows_out, chunks)
    w_front, w_value, w_out = pick_attn(place, w_own, w_received)
    width = w_value.shape[1]
    front = (dot(rows, w_front) + bias[:, : 2 * width]).astype(BF16)
    value = (dot(rows, w_value) + bias[:, 2 * width :]).astype(BF16)
    qkv_out[:, : 2 * width] = front
    qkv_out[:, 2 * width :] = value
    mixed = []
    for head in range(width // HEAD):
        at = head * HEAD
        query = front[:, at : at + HEAD]
        key = front[:, width + at : width + at + HEAD]
        scores = dot_t(query, key) * HEAD**-0.5
        powers = jnp.exp(scores - jnp.max(scores, axis=-1, keepdims=True))
        probs = powers / jnp.sum(powers, axis=-1, keepdims=True)
        probs_out[head] = probs
        mixed.append(dot(probs.astype(BF16), value[:, at : at + HEAD]))
    mixed = jnp.concatenate(mixed, axis=1).astype(BF16)
    mixed_out[...] = mixed
    put_blocks(partial, dot_t(mixed, w_out))


def middle_body(count, *refs):
    parts, (bias, h, mod, attended_out, middle_out, mlp_in) = refs[:count], refs[count:]
    attended = total(parts) + bias[...]
    attended_out[...] = attended
    middle = h[...] + part(mod, 2) * attended
    middle_out[...] = middle
    normed, _ = normalize(middle)
    mlp_in[...] = (normed * (1.0 + part(mod, 4)) + part(mod, 3)).astype(BF16)


def mlp_body(count, *refs):
    chunks = refs[:count]
    w_own, w_received, bias, rows_out, pre_out, hidden_out = refs[count : count + 6]
    partial = refs[count + 6 :]
    rows = put_rows(rows_out, chunks)
    half = w_own.shape[1] // 2
    shrunk = None
    for index, weight in enumerate((w_own, w_received)):
        at = index * half
        pre = dot(rows, weight[:, :half]) + bias[:, at : at + half]
        pre_out[:, at : at + half] = pre
        hidden = gelu(pre).astype(BF16)
        hidden_out[:, at : at + half] = hidden
        term = dot_t(hidden, weight[:, half:])
        shrunk = term if shrunk is None else shrunk + term
    put_blocks(partial, shrunk)


def mlp_both_body(count, *refs):
    chunks, g_chunks = refs[:count], refs[count : 2 * count]
    w_own, w_received, bias, rows_out, g_rows_out, hidden_out, g_pre_out, bias_grad = refs[
        2 * count : 2 * count + 8
    ]
    partial = refs[2 * count + 8 : 3 * count + 8]
    g_partial = refs[3 * count + 8 :]
    rows = put_rows(rows_out, chunks)
    g_rows = put_rows(g_rows_out, g_chunks)
    half = w_own.shape[1] // 2
    shrunk, g_in = None, None
    for index, weight in enumerate((w_own, w_received)):
        at = index * half
        pre = dot(rows, weight[:, :half]) + bias[:, at : at + half]
        hidden = gelu(pre).astype(BF16)
        hidden_out[:, at : at + half] = hidden
        g_pre = (dot(g_rows, weight[:, half:]) * gelu_slope(pre)).astype(BF16)
        g_pre_out[:, at : at + half] = g_pre
        bias_grad[:, at : at + half] = column_sum(g_pre.astype(F32))
        term = dot_t(hidden, weight[:, half:])
        g_term = dot_t(g_pre, weight[:, :half])
        shrunk = term if shrunk is None else shrunk + term
        g_in = g_term if g_in is None else g_in + g_term
    put_blocks(g_partial, g_in)
    put_blocks(partial, shrunk)


def mlp_back_body(count, *refs):
    g_chunks = refs[:count]
    w_own, w_received, pre_ref, g_rows_out, g_pre_out, bias_grad = refs[count : count + 6]
    g_partial = refs[count + 6 :]
    g_rows = put_rows(g_rows_out, g_chunks)
    half = w_own.shape[1] // 2
    g_in = None
    for index, weight in enumerate((w_own, w_received)):
        at = index * half
        pre = pre_ref[:, at : at + half]
        g_pre = (dot(g_rows, weight[:, half:]) * gelu_slope(pre)).astype(BF16)
        g_pre_out[:, at : at + half] = g_pre
        bias_grad[:, at : at + half] = column_sum(g_pre.astype(F32))
        g_term = dot_t(g_pre, weight[:, :half])
        g_in = g_term if g_in is None else g_in + g_term
    put_blocks(g_partial, g_in)


def between_body(count, *refs):
    parts = refs[:count]
    bias, middle, mod0, mod1, shrunk_out, passed_out, h_out, attn_in = refs[count:]
    shrunk = total(parts) + bias[...]
    shrunk_out[...] = shrunk
    passed = (middle[...] + part(mod0, 5) * shrunk).astype(BF16)
    passed_out[...] = passed
    h = passed.astype(F32)
    h_out[...] = h
    normed, _ = normalize(h)
    attn_in[...] = (normed * (1.0 + part(mod1, 1)) + part(mod1, 0)).astype(BF16)


def leave_body(count, *refs):
    parts = refs[:count]
    bias, middle, mod, g_y_ref, g_shrunk, y_out, g_gate, bias_grad = refs[count:]
    shrunk = total(parts) + bias[...]
    y_out[...] = (middle[...] + part(mod, 5) * shrunk).astype(BF16)
    g_gate[...] = column_sum(g_y_ref[...] * shrunk)
    bias_grad[...] = column_sum(g_shrunk[...].astype(F32))


def middle_back_body(count, *refs):
    parts = refs[:count]
    middle, mod, g_y, attended, g_middle_out, g_attended_out, g_shift, g_scale, g_gate, bias_grad = refs[
        count:
    ]
    g_in = total(parts)
    normed, rstd = normalize(middle[...])
    g_shift[...] = column_sum(g_in)
    g_scale[...] = column_sum(g_in * normed)
    g_middle = g_y[...] + normalize_back(g_in * (1.0 + part(mod, 4)), normed, rstd)
    g_middle_out[...] = g_middle
    g_gate[...] = column_sum(g_middle * attended[...])
    g_attended = (part(mod, 2) * g_middle).astype(BF16)
    g_attended_out[...] = g_attended
    bias_grad[...] = column_sum(g_attended.astype(F32))


def attn_back_body(count, place, *refs):
    g_chunks = refs[:count]
    w_own, w_received, qkv, probs_ref = refs[count : count + 4]
    g_rows_out, g_joint_out, bias_grad = refs[count + 4 : count + 7]
    g_partial = refs[count + 7 :]
    g_rows = put_rows(g_rows_out, g_chunks)
    w_front, w_value, w_out = pick_attn(place, w_own, w_received)
    width = w_value.shape[1]
    g_mixed = dot(g_rows, w_out).astype(BF16)
    g_query, g_key, g_value = [], [], []
    for head in range(width // HEAD):
        at = head * HEAD
        query = qkv[:, at : at + HEAD]
        key = qkv[:, width + at : width + at + HEAD]
        value = qkv[:, 2 * width + at : 2 * width + at + HEAD]
        probs = probs_ref[head]
        g_head = g_mixed[:, at : at + HEAD]
        g_probs = dot_t(g_head, value)
        row_dot = jnp.sum(probs * g_probs, axis=-1, keepdims=True)
        g_scores = (probs * (g_probs - row_dot)).astype(BF16)
        g_value.append(t_dot(probs.astype(BF16), g_head))
        g_query.append(dot(g_scores, key) * HEAD**-0.5)
        g_key.append(t_dot(g_scores, query) * HEAD**-0.5)
    g_front = jnp.concatenate(g_query + g_key, axis=1).astype(BF16)
    g_value = jnp.concatenate(g_value, axis=1).astype(BF16)
    g_joint_out[:, : 2 * width] = g_front
    g_joint_out[:, 2 * width :] = g_value
    bias_grad[:, :width] = column_sum(g_front[:, :width].astype(F32))
    bias_grad[:, width:] = column_sum(g_value.astype(F32))
    put_blocks(g_partial, dot_t(g_front, w_front) + dot_t(g_value, w_value))


def input_grad(parts, h, mod, g_middle, g_shift, g_scale):
    g_in = total(parts)
    normed, rstd = normalize(h[...])
    g_shift[...] = column_sum(g_in)
    g_scale[...] = column_sum(g_in * normed)
    return (g_middle[...] + normalize_back(g_in * (1.0 + part(mod, 1)), normed, rstd)).astype(BF16)


def between_back_body(count, *refs):
    parts = refs[:count]
    h, mod1, mod0, g_middle, shrunk, g_h_out, g_y_out, g_shrunk_out = refs[count : count + 8]
    g_shift, g_scale, g_gate, bias_grad = refs[count + 8 :]
    g_h = input_grad(parts, h, mod1, g_middle, g_shift, g_scale)
    g_h_out[...] = g_h
    g_y = g_h.astype(F32)
    g_y_out[...] = g_y
    g_gate[...] = column_sum(g_y * shrunk[...])
    g_shrunk = (part(mod0, 5) * g_y).astype(BF16)
    g_shrunk_out[...] = g_shrunk
    bias_grad[...] = column_sum(g_shrunk.astype(F32))


def finish_back_body(count, *refs):
    parts = refs[:count]
    h, mod, g_middle, g_h_out, g_shift, g_scale = refs[count:]
    g_h_out[...] = input_grad(parts, h, mod, g_middle, g_shift, g_scale)


def mlp_weights_body(rows, g_pre, g_rows, hidden, keep, give):
    half = keep.shape[1] // 2
    keep[:, :half] = t_dot(rows[...], g_pre[:, :half])
    keep[:, half:] = t_dot(g_rows[...], hidden[:, :half])
    give[:, :half] = t_dot(rows[...], g_pre[:, half:]).astype(BF16)
    give[:, half:] = t_dot(g_rows[...], hidden[:, half:]).astype(BF16)


def attn_weights_body(place, rows, g_joint, g_rows, mixed, keep, give):
    width = mixed.shape[1]
    first = place[0] == 0
    front = t_dot(rows[...], g_joint[:, : 2 * width])
    back = jnp.concatenate(
        [t_dot(rows[...], g_joint[:, 2 * width :]), t_dot(g_rows[...], mixed[...])], axis=1
    )
    keep[...] = jnp.where(first, front, back)
    give[...] = jnp.where(first, back, front).astype(BF16)


def line_blocks(place, k, rows):
    return pl.ds(pl.multiple_of((place[1] ^ k) * rows, 16), rows)


def stack_body(place, *refs):
    out = refs[-1]
    pieces = len(refs) // 2
    _, rows, wide = refs[0].shape
    for piece in range(pieces):
        pair, other = refs[piece], refs[pieces + piece]
        columns = slice(piece * wide, (piece + 1) * wide)
        for k, block in enumerate((pair[0], other[0], pair[1], other[1])):
            out[line_blocks(place, k, rows), columns] = block


def line_parts_body(place, keep, received, *outs):
    rows, wide = outs[2].shape

    for piece in range(len(outs) // 3):
        near, far, own = outs[3 * piece : 3 * piece + 3]
        columns = slice(piece * wide, (piece + 1) * wide)

        def block(k):
            at = line_blocks(place, k, rows)
            return keep[at, columns] + received[at, columns].astype(F32)

        near[0] = block(1).astype(BF16)
        near[1] = block(3).astype(BF16)
        far[...] = block(2)
        own[...] = block(0)


def final_mlp_body(place, mine, received, expand_out, shrink_t_out):
    first = place[0] == 0
    half = mine.shape[1] // 2
    own, other = mine[...].astype(F32), received[...].astype(F32)
    for index, values in enumerate((jnp.where(first, own, other), jnp.where(first, other, own))):
        expand_out[:, index * half : (index + 1) * half] = values[:, :half]
        shrink_t_out[:, index * half : (index + 1) * half] = values[:, half:]


def final_attn_body(place, mine, received, joint_out, out_out):
    first = place[0] == 0
    width = mine.shape[1] // 2
    own, other = mine[...].astype(F32), received[...].astype(F32)
    front, back = jnp.where(first, own, other), jnp.where(first, other, own)
    joint_out[0] = front[:, :width]
    joint_out[1] = front[:, width:]
    joint_out[2] = back[:, :width]
    out_out[...] = back[:, width:].T


def mod_first_body(a0, a1, a2, a3, weight, out):
    rows = jnp.concatenate([a0[...], a1[...], a2[...], a3[...]], axis=0)
    out[...] = dot(rows, weight[...])


def mod_sum_body(count, *refs):
    values = total(refs[:count])
    outs = refs[count:]
    micro = outs[0].shape[0]
    for k, out in enumerate(outs):
        out[...] = values[k * micro : (k + 1) * micro]


def mod_join_body(place, p0, p1, p2, p3, bias, mine, other, scratch):
    for k, ref in enumerate((p0, p1, p2, p3)):
        scratch[place[1] ^ k] = ref[...]
    values = jnp.concatenate([scratch[j] for j in range(LINE)], axis=1) + bias[...]
    first = place[0] == 0
    mine[...] = jnp.where(first, values[0:1], values[1:2])
    other[...] = jnp.where(first, values[1:2], values[0:1])


def pack_body(*refs):
    out, pieces = refs[-1], refs[:-1]
    count = len(pieces) // 2
    for row in range(2):
        at = 0
        for ref in pieces[row * count : (row + 1) * count]:
            out[row : row + 1, at : at + ref.shape[1]] = ref[...]
            at += ref.shape[1]


def grads_sum_body(count, place, *refs):
    parts = refs[:count]
    joint0, expand0, joint1, expand1, keep, give = refs[count:]
    first = place[0] == 0
    values = total(parts)
    hidden = expand0.shape[1]
    mod_width = values.shape[1] // 8 * 6
    rounded = values[:, :mod_width].astype(BF16).astype(F32)
    sums = values[:, mod_width:]
    half = hidden // 2

    def natural(ref):
        now = ref[...]
        return jnp.where(first, now, jnp.concatenate([now[:, half:], now[:, :half]], axis=1))

    rows = []
    for row, (joint, expand) in enumerate(((joint0, expand0), (joint1, expand1))):
        rows.append(
            jnp.concatenate(
                [rounded[row : row + 1], joint[...], natural(expand), sums[row : row + 1]], axis=1
            )
        )
    keep[...] = jnp.where(first, rows[0], rows[1])
    give[...] = jnp.where(first, rows[1], rows[0])


def grads_join_body(place, keep, received, out):
    mods = out.shape[1] - keep.shape[1]
    first = place[0] == 0
    own, other = keep[...], received[...]
    out[:, :mods] = jnp.where(first, own, other)[:, :mods].astype(BF16)
    out[:, mods : 2 * mods] = jnp.where(first, other, own)[:, :mods].astype(BF16)
    out[:, 2 * mods :] = (own[:, mods:] + other[:, mods:]).astype(BF16)


def mod_back_body(place, g0, g1, g2, g3, a0, a1, a2, a3, weight, w_grad, b_grad, bias, c0, c1, c2, c3):
    columns = weight.shape[1]
    mods = columns * LINE
    grads = (g0, g1, g2, g3)
    at = pl.multiple_of(place[1] * columns, 128)
    rows = []
    for ref in grads:
        rows.append(ref[:, pl.ds(at, columns)].astype(F32))
        rows.append(ref[:, pl.ds(pl.multiple_of(at + mods, 128), columns)].astype(F32))
    picked = jnp.concatenate(rows, axis=0).astype(BF16)
    activated = jnp.concatenate([a0[...], a1[...], a2[...], a3[...]], axis=0)
    w_grad[...] = t_dot(activated, picked)
    act = dot_t(picked, weight[...])
    for k, out in enumerate((c0, c1, c2, c3)):
        out[...] = act[2 * k : 2 * k + 2]
    b_grad[...] = tree_sum(
        [ref[:, :mods].astype(F32) + ref[:, mods : 2 * mods].astype(F32) for ref in grads]
    )
    bias[...] = tree_sum([ref[:, 2 * mods :].astype(F32) for ref in grads])


def on_device(
    tokens,
    conditions,
    cotangent,
    modulation_weight,
    modulation_bias,
    joint_weight,
    joint_bias,
    output_weight,
    output_bias,
    expand_weight,
    expand_bias,
    shrink_weight,
    shrink_bias,
):
    core = lax.axis_index("pipe")
    first = core == 0
    line = lax.axis_index("dp")
    place = jnp.stack([core, line]).astype(jnp.int32)
    line_size = lax.axis_size("dp")
    count = lax.axis_size("tensor")
    direct = line_size == LINE
    micro, _, own, model = tokens.shape
    width = output_weight.shape[1]
    hidden = expand_weight.shape[2]
    chunk = model // line_size
    rows = own * count
    columns = modulation_weight.shape[2]
    mods = 6 * model
    bias_width = 2 * width + hidden + 2 * model
    own_rows = modulation_weight[0]

    def mine(pair):
        return jnp.where(first, pair[0], pair[1])

    def other(pair):
        return jnp.where(first, pair[1], pair[0])

    def both_layers(kept, received):
        return jnp.where(first, kept, received), jnp.where(first, received, kept)

    def after(value, earlier):
        return lax.optimization_barrier((value, earlier))[0]

    def tie(main, *rest):
        return lax.optimization_barrier((main,) + rest)

    split = 2 * width
    pieces_shape = shape((chunk, split), BF16)
    joint_blocks = jnp.transpose(joint_weight[0], (1, 0, 2))
    expand, shrink_t = expand_weight[0], shrink_weight[0].T
    half = hidden // 2
    halves = (
        jnp.concatenate(
            [joint_blocks[0], joint_blocks[1], expand[:, :half], shrink_t[:, :half]], axis=1
        ),
        jnp.concatenate(
            [joint_blocks[2], output_weight[0].T, expand[:, half:], shrink_t[:, half:]], axis=1
        ),
    )
    keep, give = mine(halves), other(halves)
    line_pieces = run(
        "weight_pieces",
        weight_pieces_body,
        [pieces_shape] * 6,
        [keep, swap(give, "pipe", 1)],
        place,
    )

    bias_pack = jnp.concatenate(
        [
            joint_bias[0].reshape(-1),
            expand_bias[0],
            output_bias[0],
            shrink_bias[0],
        ]
    )[None]
    bias_layers = both_layers(bias_pack, swap(bias_pack, "pipe", 1))
    biases = []
    for packed in bias_layers:
        at = 2 * width
        joint = jnp.concatenate(
            [packed[:, :width], jnp.zeros((1, width), F32), packed[:, width:at]], axis=1
        )
        grown = packed[:, at : at + hidden]
        rolled = jnp.concatenate([grown[:, hidden // 2 :], grown[:, : hidden // 2]], axis=1)
        grown = jnp.where(first, grown, rolled)
        at += hidden
        biases.append((joint, packed[:, at : at + model], grown, packed[:, at + model :]))

    activated = jax.nn.silu(conditions[:, 0].astype(F32)).astype(BF16)
    if direct:
        activated_all = gather(activated, "dp")
    else:
        activated_all = lax.all_gather(activated, "dp", axis=0).reshape(line_size * micro, -1)

    def line_first(value):
        return (value, swap(value, "dp", 2)) if direct else value

    def line_second(pair):
        if not direct:
            return pair, lax.all_gather(pair, "dp", axis=0, tiled=True)
        stacked = jnp.stack(pair)
        return stacked, swap(stacked, "dp", 1)

    def both_cores(*steps):
        pairs, others = [step[0] for step in steps], [step[1] for step in steps]
        if direct:
            wide = sum(pair.shape[2] for pair in pairs)
            lined = run(
                "stack_line", stack_body, [shape((model, wide), BF16)], pairs + others, place
            )[0]
        else:
            lined = jnp.concatenate(others, axis=1)
        return lined, swap(lined, "pipe", 1)

    def piece_of(layer, index):
        return line_pieces[3 * layer + index]

    first_a0 = line_first(after(piece_of(0, 0), activated_all))

    if direct:
        mod_partial = run(
            "mod_first",
            mod_first_body,
            [shape((micro * LINE, columns), F32)],
            activated_all + [own_rows],
        )[0]
        mod_partials, first_a0 = tie(gather(mod_partial, "tensor"), first_a0)
        second_a0 = line_second(first_a0)
        first_e0 = line_first(after(piece_of(0, 1), first_a0))
        pieces = run(
            "mod_sum",
            functools.partial(mod_sum_body, count),
            [shape((micro, columns), F32)] * LINE,
            mod_partials,
        )
        pieces, second_a0 = tie(exchange(pieces, "dp"), second_a0)
        mod_mine, mod_other = pl.pallas_call(
            mod_join_body,
            out_shape=[shape((1, mods), F32)] * 2,
            in_specs=[pl.BlockSpec(memory_space=pltpu.SMEM)]
            + [pl.BlockSpec(memory_space=pltpu.VMEM)] * 5,
            out_specs=[pl.BlockSpec(memory_space=pltpu.VMEM)] * 2,
            scratch_shapes=[pltpu.VMEM((LINE, micro, columns), F32)],
            name="mod_join",
        )(place, *pieces, modulation_bias)
    else:
        mod_partial = dot(activated_all, own_rows)
        mod_partials = gather(mod_partial, "tensor")
        second_a0 = line_second(first_a0)
        first_e0 = line_first(piece_of(0, 1))
        mod_sum = tree_sum(mod_partials).reshape(line_size, micro, -1)
        mod_layer = lax.all_to_all(mod_sum, "dp", split_axis=0, concat_axis=0)
        mod_layer = jnp.swapaxes(mod_layer, 0, 1).reshape(micro, -1) + modulation_bias
        mod_mine, mod_other = mine(mod_layer)[None], other(mod_layer)[None]
    mod0, mod1 = both_layers(mod_mine, swap(mod_other, "pipe", 1))

    w_attn0 = both_cores(second_a0)
    own_f32 = shape((own, model), F32)
    own_bf16 = shape((own, model), BF16)
    blocks = [own_bf16] * count
    wide_bf16 = shape((rows, model), BF16)
    hidden_bf16 = shape((rows, hidden), BF16)
    vector = shape((1, model), F32)
    hidden_vector = shape((1, hidden), F32)
    h0, attn_in, g_y1, g_shrunk1 = run(
        "enter",
        enter_body,
        [own_f32, own_bf16, own_f32, own_bf16],
        [tokens[:, 0], cotangent[:, 0], mod0, mod1],
        place,
    )

    def kernel(name, body, outs, args, where=None):
        return run(name, functools.partial(body, count), outs, args, where)

    def attention(attn_rows, weight, bias):
        outs = kernel(
            "attention",
            attn_body,
            [
                wide_bf16,
                shape((rows, 3 * width), BF16),
                shape((width // HEAD, rows, rows), F32),
                shape((rows, width), BF16),
            ]
            + blocks,
            attn_rows + [weight[0], weight[1], bias],
            place,
        )
        return outs[:4], exchange(outs[4:], "tensor")

    def middle_of(parts, bias, h, mod):
        return kernel(
            "middle", middle_body, [own_f32, own_f32, own_bf16], parts + [bias, h, mod]
        )

    attn_rows, first_e0 = tie(gather(attn_in, "tensor"), first_e0)
    second_e0 = line_second(first_e0)
    first_s0 = line_first(after(piece_of(0, 2), first_e0))
    kept_attn0, parts = attention(attn_rows, w_attn0, biases[0][0])
    parts, second_e0, first_s0 = tie(parts, second_e0, first_s0)
    second_s0 = line_second(first_s0)
    first_a1 = line_first(after(piece_of(1, 0), first_s0))
    attended0, middle0, mlp_in = middle_of(parts, biases[0][1], h0, mod0)
    mlp_rows0, second_s0, first_a1 = tie(gather(mlp_in, "tensor"), second_s0, first_a1)
    w_mlp0 = both_cores(second_e0, second_s0)
    second_a1 = line_second(first_a1)
    first_e1 = line_first(after(piece_of(1, 1), first_a1))
    g_rows1 = gather(after(g_shrunk1, mlp_rows0), "tensor")
    w_mlp0, g_rows1 = tie(w_mlp0, g_rows1)
    outs = kernel(
        "feed_forward",
        mlp_body,
        [wide_bf16, shape((rows, hidden), F32), hidden_bf16] + blocks,
        mlp_rows0 + [w_mlp0[0], w_mlp0[1], biases[0][2]],
    )
    mlp_rows0, pre0, hidden0 = outs[:3]
    (parts,) = tie(exchange(outs[3:], "tensor"))
    parts, second_a1, first_e1 = tie(parts, second_a1, first_e1)
    w_attn1 = both_cores(second_a1)
    second_e1 = line_second(first_e1)
    first_s1 = line_first(after(piece_of(1, 2), first_e1))
    shrunk0, passed, h1, attn_in = kernel(
        "between",
        between_body,
        [own_f32, own_bf16, own_f32, own_bf16],
        parts + [biases[0][3], middle0, mod0, mod1],
    )

    (attn_rows, w_attn1), second_e1, first_s1 = tie(
        (gather(attn_in, "tensor"), w_attn1), second_e1, first_s1
    )
    second_s1 = line_second(first_s1)
    kept_attn1, parts = attention(attn_rows, w_attn1, biases[1][0])
    parts, second_s1 = tie(parts, second_s1)
    w_mlp1 = both_cores(second_e1, second_s1)
    attended1, middle1, mlp_in = middle_of(parts, biases[1][1], h1, mod1)
    outs = kernel(
        "feed_forward_both",
        mlp_both_body,
        [wide_bf16, wide_bf16, hidden_bf16, hidden_bf16, hidden_vector] + blocks + blocks,
        gather(mlp_in, "tensor") + g_rows1 + [w_mlp1[0], w_mlp1[1], biases[1][2]],
    )
    mlp_rows1, g_rows1, hidden1, g_pre1, expand_grad1 = outs[:5]
    y_partial, g_partial = outs[5 : 5 + count], outs[5 + count :]

    def middle_back(parts, middle, mod, g_y, attended):
        return kernel(
            "middle_back",
            middle_back_body,
            [own_f32, own_bf16] + [vector] * 4,
            parts + [middle, mod, g_y, attended],
        )

    def attention_back(g_rows, weight, kept):
        outs = kernel(
            "attention_back",
            attn_back_body,
            [wide_bf16, shape((rows, 3 * width), BF16), shape((1, 2 * width), F32)] + blocks,
            g_rows + [weight[0], weight[1], kept[1], kept[2]],
            place,
        )
        return outs[:3], exchange(outs[3:], "tensor")

    def chip_sum(grads):
        keep, give = grads
        return (keep + swap(give, "pipe", 1).astype(F32)).astype(BF16)

    def line_sum(whole):
        return lax.psum_scatter(whole, "dp", scatter_dimension=0, tiled=True)

    def line_parts(grads, pieces):
        keep, give = grads
        wide = keep.shape[1] // pieces
        if not direct:
            whole = chip_sum(grads)
            return [[whole[:, k * wide : (k + 1) * wide]] for k in range(pieces)]
        outs = run(
            "line_parts",
            line_parts_body,
            [shape((2, chunk, wide), BF16), shape((chunk, wide), F32), shape((chunk, wide), F32)]
            * pieces,
            [keep, swap(give, "pipe", 1)],
            place,
        )
        return [outs[3 * k : 3 * k + 3] for k in range(pieces)]

    def line_near(parts):
        return swap(parts[0], "dp", 1) if direct else parts[0]

    def line_far(parts, near):
        if not direct:
            return line_sum(near)
        return swap((parts[1] + near[1].astype(F32)).astype(BF16), "dp", 2)

    def line_total(parts, near, far):
        if not direct:
            return far
        return (parts[2] + near[0].astype(F32) + far.astype(F32)).astype(BF16)

    def own_halves(pair):
        return mine(pair), swap(other(pair), "pipe", 1)

    def mlp_weight_grads(mlp_rows, g_pre, g_rows, hidden_rows):
        return run(
            "mlp_weight_grads",
            mlp_weights_body,
            [shape((model, hidden), F32), shape((model, hidden), BF16)],
            [mlp_rows, g_pre, g_rows, hidden_rows],
        )

    def attn_weight_grads(kept, g_joint, g_rows):
        return run(
            "attn_weight_grads",
            attn_weights_body,
            [shape((model, 2 * width), F32), shape((model, 2 * width), BF16)],
            [kept[0], g_joint, g_rows, kept[3]],
            place,
        )

    (g_parts, (parts_e1, parts_s1)), y_partial = tie(
        (
            exchange(g_partial, "tensor"),
            line_parts(mlp_weight_grads(mlp_rows1, g_pre1, g_rows1, hidden1), 2),
        ),
        y_partial,
    )
    near_e1 = line_near(parts_e1)
    g_middle1, g_attended, g_shift_mlp1, g_scale_mlp1, g_gate_attn1, out_grad1 = middle_back(
        g_parts, middle1, mod1, g_y1, attended1
    )
    y_parts = exchange(y_partial, "tensor")
    g_rows, near_e1, parts_e1, parts_s1 = tie(
        gather(g_attended, "tensor"), near_e1, parts_e1, parts_s1
    )
    far_e1 = line_far(parts_e1, near_e1)
    near_s1 = line_near(parts_s1)
    (g_rows, g_joint, joint_grad1), parts = attention_back(g_rows, w_attn1, kept_attn1)
    (parts, (parts_a1,)), far_e1, near_s1, parts_s1 = tie(
        (parts, line_parts(attn_weight_grads(kept_attn1, g_joint, g_rows), 1)),
        far_e1,
        near_s1,
        parts_s1,
    )
    near_a1 = line_near(parts_a1)
    far_s1 = line_far(parts_s1, near_s1)
    g_passed, g_y0, g_shrunk0, g_shift_attn1, g_scale_attn1, g_gate_mlp0, shrink_grad0 = kernel(
        "between_back",
        between_back_body,
        [own_bf16, own_f32, own_bf16] + [vector] * 4,
        parts + [h1, mod1, mod0, g_middle1, shrunk0],
    )

    g_rows0, near_a1, far_s1, parts_a1 = tie(
        gather(g_shrunk0, "tensor"), near_a1, far_s1, parts_a1
    )
    far_a1 = line_far(parts_a1, near_a1)
    outs = kernel(
        "feed_forward_back",
        mlp_back_body,
        [wide_bf16, hidden_bf16, hidden_vector] + blocks,
        g_rows0 + [w_mlp0[0], w_mlp0[1], pre0],
    )
    g_rows0, g_pre0, expand_grad0 = outs[:3]
    parts, (parts_m0,) = tie(
        exchange(outs[3:], "tensor"),
        line_parts(mlp_weight_grads(mlp_rows0, g_pre0, g_rows0, hidden0), 1),
    )
    near_m0 = line_near(parts_m0)
    g_middle0, g_attended, g_shift_mlp0, g_scale_mlp0, g_gate_attn0, out_grad0 = middle_back(
        parts, middle0, mod0, g_y0, attended0
    )
    y1, g_gate_mlp1, shrink_grad1 = kernel(
        "leave",
        leave_body,
        [own_bf16, vector, vector],
        y_parts + [biases[1][3], middle1, mod1, g_y1, g_shrunk1],
    )
    g_rows, near_m0 = tie(gather(g_attended, "tensor"), near_m0)
    far_m0 = line_far(parts_m0, near_m0)
    (g_rows, g_joint, joint_grad0), parts = attention_back(g_rows, w_attn0, kept_attn0)
    parts, far_m0, g_joint, g_rows = tie(parts, far_m0, g_joint, g_rows)
    (parts_a0,) = line_parts(attn_weight_grads(kept_attn0, g_joint, g_rows), 1)
    g_h0, g_shift_attn0, g_scale_attn0 = kernel(
        "finish_back",
        finish_back_body,
        [own_bf16, vector, vector],
        parts + [h0, mod0, g_middle0],
    )
    def own_layer_of_micros(pair):
        return jnp.stack(both_layers(mine(pair), swap(other(pair), "pipe", 1)))

    layer_outputs = own_layer_of_micros((passed, y1))
    input_grads = own_layer_of_micros((g_h0, g_passed))

    packed = run(
        "pack_grads",
        pack_body,
        [shape((2, mods + 2 * model), F32)],
        [
            g_shift_attn0,
            g_scale_attn0,
            g_gate_attn0,
            g_shift_mlp0,
            g_scale_mlp0,
            g_gate_mlp0,
            out_grad0,
            shrink_grad0,
            g_shift_attn1,
            g_scale_attn1,
            g_gate_attn1,
            g_shift_mlp1,
            g_scale_mlp1,
            g_gate_mlp1,
            out_grad1,
            shrink_grad1,
        ],
    )[0]
    packed_all, parts_a0, far_a1 = tie(gather(packed, "tensor"), parts_a0, far_a1)
    near_a0 = line_near(parts_a0)
    keep, give = run(
        "grads_sum",
        functools.partial(grads_sum_body, count),
        [shape((1, mods + bias_width), F32)] * 2,
        packed_all + [joint_grad0, expand_grad0, joint_grad1, expand_grad1],
        place,
    )
    joined = run(
        "grads_join",
        grads_join_body,
        [shape((1, 2 * mods + bias_width), BF16)],
        [keep, swap(give, "pipe", 1)],
        place,
    )[0]
    joined_all = gather(joined, "dp") if direct else lax.all_gather(joined, "dp", axis=0, tiled=True)
    joined_all, near_a0 = tie(joined_all, near_a0)
    far_a0 = line_far(parts_a0, near_a0)
    mlp_grad0 = line_total(parts_m0, near_m0, far_m0)
    mlp_grad1 = jnp.concatenate(
        [line_total(parts_e1, near_e1, far_e1), line_total(parts_s1, near_s1, far_s1)], axis=1
    )
    attn_grad0 = line_total(parts_a0, near_a0, far_a0)
    attn_grad1 = line_total(parts_a1, near_a1, far_a1)
    expand_w_grad, shrink_t_grad = run(
        "final_mlp",
        final_mlp_body,
        [shape((chunk, hidden), F32)] * 2,
        own_halves((mlp_grad0, mlp_grad1)),
        place,
    )
    joint_w_grad, output_w_grad = run(
        "final_attn",
        final_attn_body,
        [shape((3, chunk, width), F32), shape((width, chunk), F32)],
        own_halves((attn_grad0, attn_grad1)),
        place,
    )

    if direct:
        outs = run(
            "mod_back",
            mod_back_body,
            [shape(own_rows.shape, F32), shape((1, mods), F32), shape((1, bias_width), F32)]
            + [shape((micro, own_rows.shape[0]), F32)] * LINE,
            joined_all + activated_all + [own_rows],
            place,
        )
        ada_grad, ada_bias_grad, bias_sum = outs[:3]
        act_grad = tree_sum(exchange(outs[3:], "dp"))
    else:
        mod_grads = joined_all[:, : 2 * mods].reshape(line_size * micro, mods)
        bias_sum = jnp.sum(joined_all[:, 2 * mods :].astype(F32), axis=0, keepdims=True)
        ada_bias_grad = jnp.sum(mod_grads.astype(F32), axis=0, keepdims=True)
        picked = lax.dynamic_slice_in_dim(mod_grads, line * columns, columns, 1).astype(BF16)
        ada_grad = t_dot(activated_all, picked)
        act_partial = dot_t(picked, own_rows).reshape(line_size, micro, -1)
        act_grad = lax.psum_scatter(act_partial, "dp", scatter_dimension=0, tiled=False)
    _, silu_back = jax.vjp(jax.nn.silu, conditions[:, 0].astype(F32))
    cond_grad = silu_back(act_grad)[0]
    at = 2 * width
    return (
        layer_outputs[None, :, None],
        input_grads[None, :, None],
        cond_grad[None, :, None],
        ada_grad[None],
        ada_bias_grad,
        jnp.transpose(joint_w_grad, (1, 0, 2))[None],
        bias_sum[:, :at].reshape(1, 2, width),
        output_w_grad[None],
        bias_sum[:, at + hidden : at + hidden + model],
        expand_w_grad[None],
        bias_sum[:, at : at + hidden],
        shrink_t_grad.T[None],
        bias_sum[:, at + hidden + model :],
    )


def solution(mesh):
    in_specs = (
        P(None, "dp", "tensor", None),
        P(None, "dp", "tensor"),
        P(None, "dp", "tensor", None),
        P("pipe", "tensor", "dp"),
        P("pipe", None),
        P("pipe", "dp", None, "tensor"),
        P("pipe", None, "tensor"),
        P("pipe", "tensor", "dp"),
        P("pipe", None),
        P("pipe", "dp", "tensor"),
        P("pipe", "tensor"),
        P("pipe", "tensor", "dp"),
        P("pipe", None),
    )
    out_specs = (
        P("pipe", None, "dp", "tensor", None),
        P("pipe", None, "dp", "tensor", None),
        P("pipe", None, "dp", "tensor"),
        P("pipe", "tensor", "dp"),
        P("pipe", None),
        P("pipe", "dp", None, "tensor"),
        P("pipe", None, "tensor"),
        P("pipe", "tensor", "dp"),
        P("pipe", None),
        P("pipe", "dp", "tensor"),
        P("pipe", "tensor"),
        P("pipe", "tensor", "dp"),
        P("pipe", None),
    )
    return jax.shard_map(
        on_device, mesh=mesh, in_specs=in_specs, out_specs=out_specs, check_vma=False
    )
```

```python
import functools

import jax
import jax.numpy as jnp
from jax import lax
from jax.experimental import pallas as pl
from jax.experimental.pallas import tpu as pltpu
from jax.sharding import PartitionSpec as P

HEAD = 64
EPS = 1e-06
F32 = jnp.float32
BF16 = jnp.bfloat16
LINE = 4
VMEM_BYTES = 24 * 1024 * 1024
GELU_A = 0.7978845608028654
GELU_B = 0.044715


def swap(value, axis, mask):
    pairs = [(source, source ^ mask) for source in range(lax.axis_size(axis))]
    return lax.ppermute(value, axis, pairs)


def exchange(parts, axis):
    received = {k: swap(parts[k], axis, k) for k in range(len(parts) - 1, 0, -1)}
    return [parts[0]] + [received[k] for k in range(1, len(parts))]


def gather(value, axis):
    return exchange([value] * lax.axis_size(axis), axis)


def tree_sum(parts):
    parts = list(parts)
    while len(parts) > 1:
        parts = [parts[k] + parts[k + 1] for k in range(0, len(parts), 2)]
    return parts[0]


def shape(dims, dtype):
    return jax.ShapeDtypeStruct(dims, dtype)


def run(name, body, outs, args, place=None):
    specs = [pl.BlockSpec(memory_space=pltpu.VMEM) for _ in args]
    if place is not None:
        specs = [pl.BlockSpec(memory_space=pltpu.SMEM)] + specs
        args = [place] + list(args)
    return pl.pallas_call(
        body,
        out_shape=outs,
        in_specs=specs,
        out_specs=[pl.BlockSpec(memory_space=pltpu.VMEM) for _ in outs],
        compiler_params=pltpu.CompilerParams(vmem_limit_bytes=VMEM_BYTES),
        name=name,
    )(*args)


def dot(left, right):
    return jnp.dot(left, right, preferred_element_type=F32)


def dot_t(left, right):
    return lax.dot_general(left, right, (((1,), (1,)), ((), ())), preferred_element_type=F32)


def t_dot(left, right):
    return lax.dot_general(left, right, (((0,), (0,)), ((), ())), preferred_element_type=F32)


def normalize(values):
    centred = values - jnp.mean(values, axis=-1, keepdims=True)
    rstd = lax.rsqrt(jnp.mean(centred * centred, axis=-1, keepdims=True) + EPS)
    return centred * rstd, rstd


def normalize_back(grad, normed, rstd):
    return rstd * (
        grad
        - jnp.mean(grad, axis=-1, keepdims=True)
        - normed * jnp.mean(grad * normed, axis=-1, keepdims=True)
    )


def total(refs):
    return tree_sum([ref[...].astype(F32) for ref in refs])


def column_sum(values):
    return jnp.sum(values, axis=0, keepdims=True)


def part(mod_ref, index):
    width = mod_ref.shape[1] // 6
    return mod_ref[:, index * width : (index + 1) * width]


def gelu(pre):
    return 0.5 * pre * (1.0 + jnp.tanh(GELU_A * (pre + GELU_B * (pre * pre * pre))))


def gelu_slope(pre):
    square = pre * pre
    bent = jnp.tanh(GELU_A * (pre + GELU_B * (square * pre)))
    return 0.5 * (1.0 + bent) + 0.5 * pre * (1.0 - bent * bent) * (
        GELU_A * (1.0 + 3.0 * GELU_B * square)
    )


def put_rows(ref, refs):
    own = refs[0].shape[0]
    for k, source in enumerate(refs):
        ref[k * own : (k + 1) * own] = source[...]
    return ref[...]


def put_blocks(refs, values):
    own = refs[0].shape[0]
    for k, ref in enumerate(refs):
        ref[...] = values[k * own : (k + 1) * own].astype(ref.dtype)


def enter_body(place, tokens, cotangent, mod0, mod1, h_out, attn_in, g_y_out, g_shrunk):
    core = place[0]
    h = tokens[core].astype(F32)
    h_out[...] = h
    normed, _ = normalize(h)
    attn_in[...] = (normed * (1.0 + part(mod0, 1)) + part(mod0, 0)).astype(BF16)
    g_y = cotangent[core].astype(F32)
    g_y_out[...] = g_y
    g_shrunk[...] = (part(mod1, 5) * g_y).astype(BF16)


def weight_pieces_body(place, keep, received, *outs):
    first = place[0] == 0
    pieces = len(outs) // 2
    wide = outs[0].shape[1]
    for piece in range(pieces):
        own = keep[:, piece * wide : (piece + 1) * wide]
        other = received[:, piece * wide : (piece + 1) * wide]
        outs[piece][...] = jnp.where(first, own, other)
        outs[pieces + piece][...] = jnp.where(first, other, own)


def pick_attn(place, own, received):
    first = place[0] == 0
    width = own.shape[1] // 2
    mine, other = own[...], received[...]
    front = jnp.where(first, mine, other)
    back = jnp.where(first, other, mine)
    return front, back[:, :width], back[:, width:]


def attn_body(count, place, *refs):
    chunks = refs[:count]
    w_own, w_received, bias = refs[count : count + 3]
    rows_out, qkv_out, probs_out, mixed_out = refs[count + 3 : count + 7]
    partial = refs[count + 7 :]
    rows = put_rows(rows_out, chunks)
    w_front, w_value, w_out = pick_attn(place, w_own, w_received)
    width = w_value.shape[1]
    front = (dot(rows, w_front) + bias[:, : 2 * width]).astype(BF16)
    value = (dot(rows, w_value) + bias[:, 2 * width :]).astype(BF16)
    qkv_out[:, : 2 * width] = front
    qkv_out[:, 2 * width :] = value
    mixed = []
    for head in range(width // HEAD):
        at = head * HEAD
        query = front[:, at : at + HEAD]
        key = front[:, width + at : width + at + HEAD]
        scores = dot_t(query, key) * HEAD**-0.5
        powers = jnp.exp(scores - jnp.max(scores, axis=-1, keepdims=True))
        probs = powers / jnp.sum(powers, axis=-1, keepdims=True)
        probs_out[head] = probs
        mixed.append(dot(probs.astype(BF16), value[:, at : at + HEAD]))
    mixed = jnp.concatenate(mixed, axis=1).astype(BF16)
    mixed_out[...] = mixed
    put_blocks(partial, dot_t(mixed, w_out))


def middle_body(count, *refs):
    parts, (bias, h, mod, attended_out, middle_out, mlp_in) = refs[:count], refs[count:]
    attended = total(parts) + bias[...]
    attended_out[...] = attended
    middle = h[...] + part(mod, 2) * attended
    middle_out[...] = middle
    normed, _ = normalize(middle)
    mlp_in[...] = (normed * (1.0 + part(mod, 4)) + part(mod, 3)).astype(BF16)


def mlp_body(count, *refs):
    chunks = refs[:count]
    w_own, w_received, bias, rows_out, pre_out, hidden_out = refs[count : count + 6]
    partial = refs[count + 6 :]
    rows = put_rows(rows_out, chunks)
    half = w_own.shape[1] // 2
    shrunk = None
    for index, weight in enumerate((w_own, w_received)):
        at = index * half
        pre = dot(rows, weight[:, :half]) + bias[:, at : at + half]
        pre_out[:, at : at + half] = pre
        hidden = gelu(pre).astype(BF16)
        hidden_out[:, at : at + half] = hidden
        term = dot_t(hidden, weight[:, half:])
        shrunk = term if shrunk is None else shrunk + term
    put_blocks(partial, shrunk)


def mlp_both_body(count, *refs):
    chunks, g_chunks = refs[:count], refs[count : 2 * count]
    w_own, w_received, bias, rows_out, g_rows_out, hidden_out, g_pre_out, bias_grad = refs[
        2 * count : 2 * count + 8
    ]
    partial = refs[2 * count + 8 : 3 * count + 8]
    g_partial = refs[3 * count + 8 :]
    rows = put_rows(rows_out, chunks)
    g_rows = put_rows(g_rows_out, g_chunks)
    half = w_own.shape[1] // 2
    shrunk, g_in = None, None
    for index, weight in enumerate((w_own, w_received)):
        at = index * half
        pre = dot(rows, weight[:, :half]) + bias[:, at : at + half]
        hidden = gelu(pre).astype(BF16)
        hidden_out[:, at : at + half] = hidden
        g_pre = (dot(g_rows, weight[:, half:]) * gelu_slope(pre)).astype(BF16)
        g_pre_out[:, at : at + half] = g_pre
        bias_grad[:, at : at + half] = column_sum(g_pre.astype(F32))
        term = dot_t(hidden, weight[:, half:])
        g_term = dot_t(g_pre, weight[:, :half])
        shrunk = term if shrunk is None else shrunk + term
        g_in = g_term if g_in is None else g_in + g_term
    put_blocks(g_partial, g_in)
    put_blocks(partial, shrunk)


def mlp_back_body(count, *refs):
    g_chunks = refs[:count]
    w_own, w_received, pre_ref, g_rows_out, g_pre_out, bias_grad = refs[count : count + 6]
    g_partial = refs[count + 6 :]
    g_rows = put_rows(g_rows_out, g_chunks)
    half = w_own.shape[1] // 2
    g_in = None
    for index, weight in enumerate((w_own, w_received)):
        at = index * half
        pre = pre_ref[:, at : at + half]
        g_pre = (dot(g_rows, weight[:, half:]) * gelu_slope(pre)).astype(BF16)
        g_pre_out[:, at : at + half] = g_pre
        bias_grad[:, at : at + half] = column_sum(g_pre.astype(F32))
        g_term = dot_t(g_pre, weight[:, :half])
        g_in = g_term if g_in is None else g_in + g_term
    put_blocks(g_partial, g_in)


def between_body(count, *refs):
    parts = refs[:count]
    bias, middle, mod0, mod1, shrunk_out, passed_out, h_out, attn_in = refs[count:]
    shrunk = total(parts) + bias[...]
    shrunk_out[...] = shrunk
    passed = (middle[...] + part(mod0, 5) * shrunk).astype(BF16)
    passed_out[...] = passed
    h = passed.astype(F32)
    h_out[...] = h
    normed, _ = normalize(h)
    attn_in[...] = (normed * (1.0 + part(mod1, 1)) + part(mod1, 0)).astype(BF16)


def leave_body(count, *refs):
    parts = refs[:count]
    bias, middle, mod, g_y_ref, g_shrunk, y_out, g_gate, bias_grad = refs[count:]
    shrunk = total(parts) + bias[...]
    y_out[...] = (middle[...] + part(mod, 5) * shrunk).astype(BF16)
    g_gate[...] = column_sum(g_y_ref[...] * shrunk)
    bias_grad[...] = column_sum(g_shrunk[...].astype(F32))


def middle_back_body(count, *refs):
    parts = refs[:count]
    middle, mod, g_y, attended, g_middle_out, g_attended_out, g_shift, g_scale, g_gate, bias_grad = refs[
        count:
    ]
    g_in = total(parts)
    normed, rstd = normalize(middle[...])
    g_shift[...] = column_sum(g_in)
    g_scale[...] = column_sum(g_in * normed)
    g_middle = g_y[...] + normalize_back(g_in * (1.0 + part(mod, 4)), normed, rstd)
    g_middle_out[...] = g_middle
    g_gate[...] = column_sum(g_middle * attended[...])
    g_attended = (part(mod, 2) * g_middle).astype(BF16)
    g_attended_out[...] = g_attended
    bias_grad[...] = column_sum(g_attended.astype(F32))


def attn_back_body(count, place, *refs):
    g_chunks = refs[:count]
    w_own, w_received, qkv, probs_ref = refs[count : count + 4]
    g_rows_out, g_joint_out, bias_grad = refs[count + 4 : count + 7]
    g_partial = refs[count + 7 :]
    g_rows = put_rows(g_rows_out, g_chunks)
    w_front, w_value, w_out = pick_attn(place, w_own, w_received)
    width = w_value.shape[1]
    g_mixed = dot(g_rows, w_out).astype(BF16)
    g_query, g_key, g_value = [], [], []
    for head in range(width // HEAD):
        at = head * HEAD
        query = qkv[:, at : at + HEAD]
        key = qkv[:, width + at : width + at + HEAD]
        value = qkv[:, 2 * width + at : 2 * width + at + HEAD]
        probs = probs_ref[head]
        g_head = g_mixed[:, at : at + HEAD]
        g_probs = dot_t(g_head, value)
        row_dot = jnp.sum(probs * g_probs, axis=-1, keepdims=True)
        g_scores = (probs * (g_probs - row_dot)).astype(BF16)
        g_value.append(t_dot(probs.astype(BF16), g_head))
        g_query.append(dot(g_scores, key) * HEAD**-0.5)
        g_key.append(t_dot(g_scores, query) * HEAD**-0.5)
    g_front = jnp.concatenate(g_query + g_key, axis=1).astype(BF16)
    g_value = jnp.concatenate(g_value, axis=1).astype(BF16)
    g_joint_out[:, : 2 * width] = g_front
    g_joint_out[:, 2 * width :] = g_value
    bias_grad[:, :width] = column_sum(g_front[:, :width].astype(F32))
    bias_grad[:, width:] = column_sum(g_value.astype(F32))
    put_blocks(g_partial, dot_t(g_front, w_front) + dot_t(g_value, w_value))


def input_grad(parts, h, mod, g_middle, g_shift, g_scale):
    g_in = total(parts)
    normed, rstd = normalize(h[...])
    g_shift[...] = column_sum(g_in)
    g_scale[...] = column_sum(g_in * normed)
    return (g_middle[...] + normalize_back(g_in * (1.0 + part(mod, 1)), normed, rstd)).astype(BF16)


def between_back_body(count, *refs):
    parts = refs[:count]
    h, mod1, mod0, g_middle, shrunk, g_h_out, g_y_out, g_shrunk_out = refs[count : count + 8]
    g_shift, g_scale, g_gate, bias_grad = refs[count + 8 :]
    g_h = input_grad(parts, h, mod1, g_middle, g_shift, g_scale)
    g_h_out[...] = g_h
    g_y = g_h.astype(F32)
    g_y_out[...] = g_y
    g_gate[...] = column_sum(g_y * shrunk[...])
    g_shrunk = (part(mod0, 5) * g_y).astype(BF16)
    g_shrunk_out[...] = g_shrunk
    bias_grad[...] = column_sum(g_shrunk.astype(F32))


def finish_back_body(count, *refs):
    parts = refs[:count]
    h, mod, g_middle, g_h_out, g_shift, g_scale = refs[count:]
    g_h_out[...] = input_grad(parts, h, mod, g_middle, g_shift, g_scale)


def mlp_weights_body(rows, g_pre, g_rows, hidden, keep, give):
    half = keep.shape[1] // 2
    keep[:, :half] = t_dot(rows[...], g_pre[:, :half])
    keep[:, half:] = t_dot(g_rows[...], hidden[:, :half])
    give[:, :half] = t_dot(rows[...], g_pre[:, half:]).astype(BF16)
    give[:, half:] = t_dot(g_rows[...], hidden[:, half:]).astype(BF16)


def attn_weights_body(place, rows, g_joint, g_rows, mixed, keep, give):
    width = mixed.shape[1]
    first = place[0] == 0
    front = t_dot(rows[...], g_joint[:, : 2 * width])
    back = jnp.concatenate(
        [t_dot(rows[...], g_joint[:, 2 * width :]), t_dot(g_rows[...], mixed[...])], axis=1
    )
    keep[...] = jnp.where(first, front, back)
    give[...] = jnp.where(first, back, front).astype(BF16)


def line_blocks(place, k, rows):
    return pl.ds(pl.multiple_of((place[1] ^ k) * rows, 16), rows)


def stack_body(place, *refs):
    out = refs[-1]
    pieces = len(refs) // 2
    _, rows, wide = refs[0].shape
    for piece in range(pieces):
        pair, other = refs[piece], refs[pieces + piece]
        columns = slice(piece * wide, (piece + 1) * wide)
        for k, block in enumerate((pair[0], other[0], pair[1], other[1])):
            out[line_blocks(place, k, rows), columns] = block


def line_parts_body(place, keep, received, *outs):
    rows, wide = outs[2].shape

    for piece in range(len(outs) // 3):
        near, far, own = outs[3 * piece : 3 * piece + 3]
        columns = slice(piece * wide, (piece + 1) * wide)

        def block(k):
            at = line_blocks(place, k, rows)
            return keep[at, columns] + received[at, columns].astype(F32)

        near[0] = block(1).astype(BF16)
        near[1] = block(3).astype(BF16)
        far[...] = block(2)
        own[...] = block(0)


def final_mlp_body(place, mine, received, expand_out, shrink_t_out):
    first = place[0] == 0
    half = mine.shape[1] // 2
    own, other = mine[...].astype(F32), received[...].astype(F32)
    for index, values in enumerate((jnp.where(first, own, other), jnp.where(first, other, own))):
        expand_out[:, index * half : (index + 1) * half] = values[:, :half]
        shrink_t_out[:, index * half : (index + 1) * half] = values[:, half:]


def final_attn_body(place, mine, received, joint_out, out_out):
    first = place[0] == 0
    width = mine.shape[1] // 2
    own, other = mine[...].astype(F32), received[...].astype(F32)
    front, back = jnp.where(first, own, other), jnp.where(first, other, own)
    joint_out[0] = front[:, :width]
    joint_out[1] = front[:, width:]
    joint_out[2] = back[:, :width]
    out_out[...] = back[:, width:].T


def mod_first_body(a0, a1, a2, a3, weight, out):
    rows = jnp.concatenate([a0[...], a1[...], a2[...], a3[...]], axis=0)
    out[...] = dot(rows, weight[...])


def mod_sum_body(count, *refs):
    values = total(refs[:count])
    outs = refs[count:]
    micro = outs[0].shape[0]
    for k, out in enumerate(outs):
        out[...] = values[k * micro : (k + 1) * micro]


def mod_join_body(place, p0, p1, p2, p3, bias, mine, other, scratch):
    for k, ref in enumerate((p0, p1, p2, p3)):
        scratch[place[1] ^ k] = ref[...]
    values = jnp.concatenate([scratch[j] for j in range(LINE)], axis=1) + bias[...]
    first = place[0] == 0
    mine[...] = jnp.where(first, values[0:1], values[1:2])
    other[...] = jnp.where(first, values[1:2], values[0:1])


def pack_body(*refs):
    out, pieces = refs[-1], refs[:-1]
    count = len(pieces) // 2
    for row in range(2):
        at = 0
        for ref in pieces[row * count : (row + 1) * count]:
            out[row : row + 1, at : at + ref.shape[1]] = ref[...]
            at += ref.shape[1]


def grads_sum_body(count, place, *refs):
    parts = refs[:count]
    joint0, expand0, joint1, expand1, keep, give = refs[count:]
    first = place[0] == 0
    values = total(parts)
    hidden = expand0.shape[1]
    mod_width = values.shape[1] // 8 * 6
    rounded = values[:, :mod_width].astype(BF16).astype(F32)
    sums = values[:, mod_width:]
    half = hidden // 2

    def natural(ref):
        now = ref[...]
        return jnp.where(first, now, jnp.concatenate([now[:, half:], now[:, :half]], axis=1))

    rows = []
    for row, (joint, expand) in enumerate(((joint0, expand0), (joint1, expand1))):
        rows.append(
            jnp.concatenate(
                [rounded[row : row + 1], joint[...], natural(expand), sums[row : row + 1]], axis=1
            )
        )
    keep[...] = jnp.where(first, rows[0], rows[1])
    give[...] = jnp.where(first, rows[1], rows[0])


def grads_join_body(place, keep, received, out):
    mods = out.shape[1] - keep.shape[1]
    first = place[0] == 0
    own, other = keep[...], received[...]
    out[:, :mods] = jnp.where(first, own, other)[:, :mods].astype(BF16)
    out[:, mods : 2 * mods] = jnp.where(first, other, own)[:, :mods].astype(BF16)
    out[:, 2 * mods :] = (own[:, mods:] + other[:, mods:]).astype(BF16)


def mod_back_body(place, g0, g1, g2, g3, a0, a1, a2, a3, weight, w_grad, b_grad, bias, c0, c1, c2, c3):
    columns = weight.shape[1]
    mods = columns * LINE
    grads = (g0, g1, g2, g3)
    at = pl.multiple_of(place[1] * columns, 128)
    rows = []
    for ref in grads:
        rows.append(ref[:, pl.ds(at, columns)].astype(F32))
        rows.append(ref[:, pl.ds(pl.multiple_of(at + mods, 128), columns)].astype(F32))
    picked = jnp.concatenate(rows, axis=0).astype(BF16)
    activated = jnp.concatenate([a0[...], a1[...], a2[...], a3[...]], axis=0)
    w_grad[...] = t_dot(activated, picked)
    act = dot_t(picked, weight[...])
    for k, out in enumerate((c0, c1, c2, c3)):
        out[...] = act[2 * k : 2 * k + 2]
    b_grad[...] = tree_sum(
        [ref[:, :mods].astype(F32) + ref[:, mods : 2 * mods].astype(F32) for ref in grads]
    )
    bias[...] = tree_sum([ref[:, 2 * mods :].astype(F32) for ref in grads])


def on_device(
    tokens,
    conditions,
    cotangent,
    modulation_weight,
    modulation_bias,
    joint_weight,
    joint_bias,
    output_weight,
    output_bias,
    expand_weight,
    expand_bias,
    shrink_weight,
    shrink_bias,
):
    core = lax.axis_index("pipe")
    first = core == 0
    line = lax.axis_index("dp")
    place = jnp.stack([core, line]).astype(jnp.int32)
    line_size = lax.axis_size("dp")
    count = lax.axis_size("tensor")
    direct = line_size == LINE
    micro, _, own, model = tokens.shape
    width = output_weight.shape[1]
    hidden = expand_weight.shape[2]
    chunk = model // line_size
    rows = own * count
    columns = modulation_weight.shape[2]
    mods = 6 * model
    bias_width = 2 * width + hidden + 2 * model
    own_rows = modulation_weight[0]

    def mine(pair):
        return jnp.where(first, pair[0], pair[1])

    def other(pair):
        return jnp.where(first, pair[1], pair[0])

    def both_layers(kept, received):
        return jnp.where(first, kept, received), jnp.where(first, received, kept)

    def after(value, earlier):
        return lax.optimization_barrier((value, earlier))[0]

    def tie(main, *rest):
        return lax.optimization_barrier((main,) + rest)

    split = 2 * width
    pieces_shape = shape((chunk, split), BF16)
    joint_blocks = jnp.transpose(joint_weight[0], (1, 0, 2))
    expand, shrink_t = expand_weight[0], shrink_weight[0].T
    half = hidden // 2
    halves = (
        jnp.concatenate(
            [joint_blocks[0], joint_blocks[1], expand[:, :half], shrink_t[:, :half]], axis=1
        ),
        jnp.concatenate(
            [joint_blocks[2], output_weight[0].T, expand[:, half:], shrink_t[:, half:]], axis=1
        ),
    )
    keep, give = mine(halves), other(halves)
    line_pieces = run(
        "weight_pieces",
        weight_pieces_body,
        [pieces_shape] * 6,
        [keep, swap(give, "pipe", 1)],
        place,
    )

    bias_pack = jnp.concatenate(
        [
            joint_bias[0].reshape(-1),
            expand_bias[0],
            output_bias[0],
            shrink_bias[0],
        ]
    )[None]
    bias_layers = both_layers(bias_pack, swap(bias_pack, "pipe", 1))
    biases = []
    for packed in bias_layers:
        at = 2 * width
        joint = jnp.concatenate(
            [packed[:, :width], jnp.zeros((1, width), F32), packed[:, width:at]], axis=1
        )
        grown = packed[:, at : at + hidden]
        rolled = jnp.concatenate([grown[:, hidden // 2 :], grown[:, : hidden // 2]], axis=1)
        grown = jnp.where(first, grown, rolled)
        at += hidden
        biases.append((joint, packed[:, at : at + model], grown, packed[:, at + model :]))

    activated = jax.nn.silu(conditions[:, 0].astype(F32)).astype(BF16)
    if direct:
        activated_all = gather(activated, "dp")
    else:
        activated_all = lax.all_gather(activated, "dp", axis=0).reshape(line_size * micro, -1)

    def line_first(value):
        return (value, swap(value, "dp", 2)) if direct else value

    def line_second(pair):
        if not direct:
            return pair, lax.all_gather(pair, "dp", axis=0, tiled=True)
        stacked = jnp.stack(pair)
        return stacked, swap(stacked, "dp", 1)

    def both_cores(*steps):
        pairs, others = [step[0] for step in steps], [step[1] for step in steps]
        if direct:
            wide = sum(pair.shape[2] for pair in pairs)
            lined = run(
                "stack_line", stack_body, [shape((model, wide), BF16)], pairs + others, place
            )[0]
        else:
            lined = jnp.concatenate(others, axis=1)
        return lined, swap(lined, "pipe", 1)

    def piece_of(layer, index):
        return line_pieces[3 * layer + index]

    first_a0 = line_first(after(piece_of(0, 0), activated_all))

    if direct:
        mod_partial = run(
            "mod_first",
            mod_first_body,
            [shape((micro * LINE, columns), F32)],
            activated_all + [own_rows],
        )[0]
        mod_partials, first_a0 = tie(gather(mod_partial, "tensor"), first_a0)
        second_a0 = line_second(first_a0)
        first_e0 = line_first(after(piece_of(0, 1), first_a0))
        pieces = run(
            "mod_sum",
            functools.partial(mod_sum_body, count),
            [shape((micro, columns), F32)] * LINE,
            mod_partials,
        )
        pieces, second_a0 = tie(exchange(pieces, "dp"), second_a0)
        mod_mine, mod_other = pl.pallas_call(
            mod_join_body,
            out_shape=[shape((1, mods), F32)] * 2,
            in_specs=[pl.BlockSpec(memory_space=pltpu.SMEM)]
            + [pl.BlockSpec(memory_space=pltpu.VMEM)] * 5,
            out_specs=[pl.BlockSpec(memory_space=pltpu.VMEM)] * 2,
            scratch_shapes=[pltpu.VMEM((LINE, micro, columns), F32)],
            name="mod_join",
        )(place, *pieces, modulation_bias)
    else:
        mod_partial = dot(activated_all, own_rows)
        mod_partials = gather(mod_partial, "tensor")
        second_a0 = line_second(first_a0)
        first_e0 = line_first(piece_of(0, 1))
        mod_sum = tree_sum(mod_partials).reshape(line_size, micro, -1)
        mod_layer = lax.all_to_all(mod_sum, "dp", split_axis=0, concat_axis=0)
        mod_layer = jnp.swapaxes(mod_layer, 0, 1).reshape(micro, -1) + modulation_bias
        mod_mine, mod_other = mine(mod_layer)[None], other(mod_layer)[None]
    mod0, mod1 = both_layers(mod_mine, swap(mod_other, "pipe", 1))

    w_attn0 = both_cores(second_a0)
    own_f32 = shape((own, model), F32)
    own_bf16 = shape((own, model), BF16)
    blocks = [own_bf16] * count
    wide_bf16 = shape((rows, model), BF16)
    hidden_bf16 = shape((rows, hidden), BF16)
    vector = shape((1, model), F32)
    hidden_vector = shape((1, hidden), F32)
    h0, attn_in, g_y1, g_shrunk1 = run(
        "enter",
        enter_body,
        [own_f32, own_bf16, own_f32, own_bf16],
        [tokens[:, 0], cotangent[:, 0], mod0, mod1],
        place,
    )

    def kernel(name, body, outs, args, where=None):
        return run(name, functools.partial(body, count), outs, args, where)

    def attention(attn_rows, weight, bias):
        outs = kernel(
            "attention",
            attn_body,
            [
                wide_bf16,
                shape((rows, 3 * width), BF16),
                shape((width // HEAD, rows, rows), F32),
                shape((rows, width), BF16),
            ]
            + blocks,
            attn_rows + [weight[0], weight[1], bias],
            place,
        )
        return outs[:4], exchange(outs[4:], "tensor")

    def middle_of(parts, bias, h, mod):
        return kernel(
            "middle", middle_body, [own_f32, own_f32, own_bf16], parts + [bias, h, mod]
        )

    attn_rows, first_e0 = tie(gather(attn_in, "tensor"), first_e0)
    second_e0 = line_second(first_e0)
    first_s0 = line_first(after(piece_of(0, 2), first_e0))
    kept_attn0, parts = attention(attn_rows, w_attn0, biases[0][0])
    parts, second_e0, first_s0 = tie(parts, second_e0, first_s0)
    second_s0 = line_second(first_s0)
    first_a1 = line_first(after(piece_of(1, 0), first_s0))
    attended0, middle0, mlp_in = middle_of(parts, biases[0][1], h0, mod0)
    mlp_rows0, second_s0, first_a1 = tie(gather(mlp_in, "tensor"), second_s0, first_a1)
    w_mlp0 = both_cores(second_e0, second_s0)
    second_a1 = line_second(first_a1)
    first_e1 = line_first(after(piece_of(1, 1), first_a1))
    g_rows1 = gather(after(g_shrunk1, mlp_rows0), "tensor")
    outs = kernel(
        "feed_forward",
        mlp_body,
        [wide_bf16, shape((rows, hidden), F32), hidden_bf16] + blocks,
        mlp_rows0 + [w_mlp0[0], w_mlp0[1], biases[0][2]],
    )
    outs, g_rows1 = tie(outs, g_rows1)
    mlp_rows0, pre0, hidden0 = outs[:3]
    (parts,) = tie(exchange(outs[3:], "tensor"))
    parts, second_a1, first_e1 = tie(parts, second_a1, first_e1)
    w_attn1 = both_cores(second_a1)
    second_e1 = line_second(first_e1)
    first_s1 = line_first(after(piece_of(1, 2), first_e1))
    shrunk0, passed, h1, attn_in = kernel(
        "between",
        between_body,
        [own_f32, own_bf16, own_f32, own_bf16],
        parts + [biases[0][3], middle0, mod0, mod1],
    )

    (attn_rows, w_attn1), second_e1, first_s1 = tie(
        (gather(attn_in, "tensor"), w_attn1), second_e1, first_s1
    )
    second_s1 = line_second(first_s1)
    kept_attn1, parts = attention(attn_rows, w_attn1, biases[1][0])
    parts, second_s1 = tie(parts, second_s1)
    w_mlp1 = both_cores(second_e1, second_s1)
    attended1, middle1, mlp_in = middle_of(parts, biases[1][1], h1, mod1)
    outs = kernel(
        "feed_forward_both",
        mlp_both_body,
        [wide_bf16, wide_bf16, hidden_bf16, hidden_bf16, hidden_vector] + blocks + blocks,
        gather(mlp_in, "tensor") + g_rows1 + [w_mlp1[0], w_mlp1[1], biases[1][2]],
    )
    mlp_rows1, g_rows1, hidden1, g_pre1, expand_grad1 = outs[:5]
    y_partial, g_partial = outs[5 : 5 + count], outs[5 + count :]

    def middle_back(parts, middle, mod, g_y, attended):
        return kernel(
            "middle_back",
            middle_back_body,
            [own_f32, own_bf16] + [vector] * 4,
            parts + [middle, mod, g_y, attended],
        )

    def attention_back(g_rows, weight, kept):
        outs = kernel(
            "attention_back",
            attn_back_body,
            [wide_bf16, shape((rows, 3 * width), BF16), shape((1, 2 * width), F32)] + blocks,
            g_rows + [weight[0], weight[1], kept[1], kept[2]],
            place,
        )
        return outs[:3], exchange(outs[3:], "tensor")

    def chip_sum(grads):
        keep, give = grads
        return (keep + swap(give, "pipe", 1).astype(F32)).astype(BF16)

    def line_sum(whole):
        return lax.psum_scatter(whole, "dp", scatter_dimension=0, tiled=True)

    def line_parts(grads, pieces):
        keep, give = grads
        wide = keep.shape[1] // pieces
        if not direct:
            whole = chip_sum(grads)
            return [[whole[:, k * wide : (k + 1) * wide]] for k in range(pieces)]
        outs = run(
            "line_parts",
            line_parts_body,
            [shape((2, chunk, wide), BF16), shape((chunk, wide), F32), shape((chunk, wide), F32)]
            * pieces,
            [keep, swap(give, "pipe", 1)],
            place,
        )
        return [outs[3 * k : 3 * k + 3] for k in range(pieces)]

    def line_near(parts):
        return swap(parts[0], "dp", 1) if direct else parts[0]

    def line_far(parts, near):
        if not direct:
            return line_sum(near)
        return swap((parts[1] + near[1].astype(F32)).astype(BF16), "dp", 2)

    def line_total(parts, near, far):
        if not direct:
            return far
        return (parts[2] + near[0].astype(F32) + far.astype(F32)).astype(BF16)

    def own_halves(pair):
        return mine(pair), swap(other(pair), "pipe", 1)

    def mlp_weight_grads(mlp_rows, g_pre, g_rows, hidden_rows):
        return run(
            "mlp_weight_grads",
            mlp_weights_body,
            [shape((model, hidden), F32), shape((model, hidden), BF16)],
            [mlp_rows, g_pre, g_rows, hidden_rows],
        )

    def attn_weight_grads(kept, g_joint, g_rows):
        return run(
            "attn_weight_grads",
            attn_weights_body,
            [shape((model, 2 * width), F32), shape((model, 2 * width), BF16)],
            [kept[0], g_joint, g_rows, kept[3]],
            place,
        )

    (g_parts, (parts_e1, parts_s1)), y_partial = tie(
        (
            exchange(g_partial, "tensor"),
            line_parts(mlp_weight_grads(mlp_rows1, g_pre1, g_rows1, hidden1), 2),
        ),
        y_partial,
    )
    near_e1 = line_near(parts_e1)
    g_middle1, g_attended, g_shift_mlp1, g_scale_mlp1, g_gate_attn1, out_grad1 = middle_back(
        g_parts, middle1, mod1, g_y1, attended1
    )
    y_parts = exchange(y_partial, "tensor")
    g_rows, near_e1, parts_e1, parts_s1 = tie(
        gather(g_attended, "tensor"), near_e1, parts_e1, parts_s1
    )
    far_e1 = line_far(parts_e1, near_e1)
    near_s1 = line_near(parts_s1)
    (g_rows, g_joint, joint_grad1), parts = attention_back(g_rows, w_attn1, kept_attn1)
    (parts, (parts_a1,)), far_e1, near_s1, parts_s1 = tie(
        (parts, line_parts(attn_weight_grads(kept_attn1, g_joint, g_rows), 1)),
        far_e1,
        near_s1,
        parts_s1,
    )
    near_a1 = line_near(parts_a1)
    far_s1 = line_far(parts_s1, near_s1)
    g_passed, g_y0, g_shrunk0, g_shift_attn1, g_scale_attn1, g_gate_mlp0, shrink_grad0 = kernel(
        "between_back",
        between_back_body,
        [own_bf16, own_f32, own_bf16] + [vector] * 4,
        parts + [h1, mod1, mod0, g_middle1, shrunk0],
    )

    g_rows0, near_a1, far_s1, parts_a1 = tie(
        gather(g_shrunk0, "tensor"), near_a1, far_s1, parts_a1
    )
    outs = kernel(
        "feed_forward_back",
        mlp_back_body,
        [wide_bf16, hidden_bf16, hidden_vector] + blocks,
        g_rows0 + [w_mlp0[0], w_mlp0[1], pre0],
    )
    g_rows0, g_pre0, expand_grad0 = outs[:3]
    parts, (parts_m0,) = tie(
        exchange(outs[3:], "tensor"),
        line_parts(mlp_weight_grads(mlp_rows0, g_pre0, g_rows0, hidden0), 1),
    )
    near_m0 = line_near(parts_m0)
    g_middle0, g_attended, g_shift_mlp0, g_scale_mlp0, g_gate_attn0, out_grad0 = middle_back(
        parts, middle0, mod0, g_y0, attended0
    )
    y1, g_gate_mlp1, shrink_grad1 = kernel(
        "leave",
        leave_body,
        [own_bf16, vector, vector],
        y_parts + [biases[1][3], middle1, mod1, g_y1, g_shrunk1],
    )
    g_rows, near_m0 = tie(gather(g_attended, "tensor"), near_m0)
    far_m0 = line_far(parts_m0, near_m0)
    (g_rows, g_joint, joint_grad0), parts = attention_back(g_rows, w_attn0, kept_attn0)
    parts, far_m0, g_joint, g_rows, near_a1 = tie(parts, far_m0, g_joint, g_rows, near_a1)
    far_a1 = line_far(parts_a1, near_a1)
    (parts_a0,) = line_parts(attn_weight_grads(kept_attn0, g_joint, g_rows), 1)
    g_h0, g_shift_attn0, g_scale_attn0 = kernel(
        "finish_back",
        finish_back_body,
        [own_bf16, vector, vector],
        parts + [h0, mod0, g_middle0],
    )
    def own_layer_of_micros(pair):
        return jnp.stack(both_layers(mine(pair), swap(other(pair), "pipe", 1)))

    layer_outputs = own_layer_of_micros((passed, y1))
    input_grads = own_layer_of_micros((g_h0, g_passed))

    packed = run(
        "pack_grads",
        pack_body,
        [shape((2, mods + 2 * model), F32)],
        [
            g_shift_attn0,
            g_scale_attn0,
            g_gate_attn0,
            g_shift_mlp0,
            g_scale_mlp0,
            g_gate_mlp0,
            out_grad0,
            shrink_grad0,
            g_shift_attn1,
            g_scale_attn1,
            g_gate_attn1,
            g_shift_mlp1,
            g_scale_mlp1,
            g_gate_mlp1,
            out_grad1,
            shrink_grad1,
        ],
    )[0]
    packed_all, far_a1 = tie(gather(packed, "tensor"), far_a1)
    near_a0 = line_near(parts_a0)
    keep, give = run(
        "grads_sum",
        functools.partial(grads_sum_body, count),
        [shape((1, mods + bias_width), F32)] * 2,
        packed_all + [joint_grad0, expand_grad0, joint_grad1, expand_grad1],
        place,
    )
    received, near_a0 = tie(swap(give, "pipe", 1), near_a0)
    far_a0 = line_far(parts_a0, near_a0)
    joined = run(
        "grads_join",
        grads_join_body,
        [shape((1, 2 * mods + bias_width), BF16)],
        [keep, received],
        place,
    )[0]
    joined_all = gather(joined, "dp") if direct else lax.all_gather(joined, "dp", axis=0, tiled=True)
    joined_all, far_a0 = tie(joined_all, far_a0)
    mlp_grad0 = line_total(parts_m0, near_m0, far_m0)
    mlp_grad1 = jnp.concatenate(
        [line_total(parts_e1, near_e1, far_e1), line_total(parts_s1, near_s1, far_s1)], axis=1
    )
    attn_grad0 = line_total(parts_a0, near_a0, far_a0)
    attn_grad1 = line_total(parts_a1, near_a1, far_a1)
    expand_w_grad, shrink_t_grad = run(
        "final_mlp",
        final_mlp_body,
        [shape((chunk, hidden), F32)] * 2,
        own_halves((mlp_grad0, mlp_grad1)),
        place,
    )
    joint_w_grad, output_w_grad = run(
        "final_attn",
        final_attn_body,
        [shape((3, chunk, width), F32), shape((width, chunk), F32)],
        own_halves((attn_grad0, attn_grad1)),
        place,
    )

    if direct:
        outs = run(
            "mod_back",
            mod_back_body,
            [shape(own_rows.shape, F32), shape((1, mods), F32), shape((1, bias_width), F32)]
            + [shape((micro, own_rows.shape[0]), F32)] * LINE,
            joined_all + activated_all + [own_rows],
            place,
        )
        ada_grad, ada_bias_grad, bias_sum = outs[:3]
        act_grad = tree_sum(exchange(outs[3:], "dp"))
    else:
        mod_grads = joined_all[:, : 2 * mods].reshape(line_size * micro, mods)
        bias_sum = jnp.sum(joined_all[:, 2 * mods :].astype(F32), axis=0, keepdims=True)
        ada_bias_grad = jnp.sum(mod_grads.astype(F32), axis=0, keepdims=True)
        picked = lax.dynamic_slice_in_dim(mod_grads, line * columns, columns, 1).astype(BF16)
        ada_grad = t_dot(activated_all, picked)
        act_partial = dot_t(picked, own_rows).reshape(line_size, micro, -1)
        act_grad = lax.psum_scatter(act_partial, "dp", scatter_dimension=0, tiled=False)
    _, silu_back = jax.vjp(jax.nn.silu, conditions[:, 0].astype(F32))
    cond_grad = silu_back(act_grad)[0]
    at = 2 * width
    return (
        layer_outputs[None, :, None],
        input_grads[None, :, None],
        cond_grad[None, :, None],
        ada_grad[None],
        ada_bias_grad,
        jnp.transpose(joint_w_grad, (1, 0, 2))[None],
        bias_sum[:, :at].reshape(1, 2, width),
        output_w_grad[None],
        bias_sum[:, at + hidden : at + hidden + model],
        expand_w_grad[None],
        bias_sum[:, at : at + hidden],
        shrink_t_grad.T[None],
        bias_sum[:, at + hidden + model :],
    )


def solution(mesh):
    in_specs = (
        P(None, "dp", "tensor", None),
        P(None, "dp", "tensor"),
        P(None, "dp", "tensor", None),
        P("pipe", "tensor", "dp"),
        P("pipe", None),
        P("pipe", "dp", None, "tensor"),
        P("pipe", None, "tensor"),
        P("pipe", "tensor", "dp"),
        P("pipe", None),
        P("pipe", "dp", "tensor"),
        P("pipe", "tensor"),
        P("pipe", "tensor", "dp"),
        P("pipe", None),
    )
    out_specs = (
        P("pipe", None, "dp", "tensor", None),
        P("pipe", None, "dp", "tensor", None),
        P("pipe", None, "dp", "tensor"),
        P("pipe", "tensor", "dp"),
        P("pipe", None),
        P("pipe", "dp", None, "tensor"),
        P("pipe", None, "tensor"),
        P("pipe", "tensor", "dp"),
        P("pipe", None),
        P("pipe", "dp", "tensor"),
        P("pipe", "tensor"),
        P("pipe", "tensor", "dp"),
        P("pipe", None),
    )
    return jax.shard_map(
        on_device, mesh=mesh, in_specs=in_specs, out_specs=out_specs, check_vma=False
    )
```

```python
import functools

import jax
import jax.numpy as jnp
from jax import lax
from jax.experimental import pallas as pl
from jax.experimental.pallas import tpu as pltpu
from jax.sharding import PartitionSpec as P

HEAD = 64
EPS = 1e-06
F32 = jnp.float32
BF16 = jnp.bfloat16
LINE = 4
VMEM_BYTES = 24 * 1024 * 1024
GELU_A = 0.7978845608028654
GELU_B = 0.044715


def swap(value, axis, mask):
    pairs = [(source, source ^ mask) for source in range(lax.axis_size(axis))]
    return lax.ppermute(value, axis, pairs)


def exchange(parts, axis):
    received = {k: swap(parts[k], axis, k) for k in range(len(parts) - 1, 0, -1)}
    return [parts[0]] + [received[k] for k in range(1, len(parts))]


def gather(value, axis):
    return exchange([value] * lax.axis_size(axis), axis)


def tree_sum(parts):
    parts = list(parts)
    while len(parts) > 1:
        parts = [parts[k] + parts[k + 1] for k in range(0, len(parts), 2)]
    return parts[0]


def shape(dims, dtype):
    return jax.ShapeDtypeStruct(dims, dtype)


def run(name, body, outs, args, place=None):
    specs = [pl.BlockSpec(memory_space=pltpu.VMEM) for _ in args]
    if place is not None:
        specs = [pl.BlockSpec(memory_space=pltpu.SMEM)] + specs
        args = [place] + list(args)
    return pl.pallas_call(
        body,
        out_shape=outs,
        in_specs=specs,
        out_specs=[pl.BlockSpec(memory_space=pltpu.VMEM) for _ in outs],
        compiler_params=pltpu.CompilerParams(vmem_limit_bytes=VMEM_BYTES),
        name=name,
    )(*args)


def dot(left, right):
    return jnp.dot(left, right, preferred_element_type=F32)


def dot_t(left, right):
    return lax.dot_general(left, right, (((1,), (1,)), ((), ())), preferred_element_type=F32)


def t_dot(left, right):
    return lax.dot_general(left, right, (((0,), (0,)), ((), ())), preferred_element_type=F32)


def normalize(values):
    centred = values - jnp.mean(values, axis=-1, keepdims=True)
    rstd = lax.rsqrt(jnp.mean(centred * centred, axis=-1, keepdims=True) + EPS)
    return centred * rstd, rstd


def normalize_back(grad, normed, rstd):
    return rstd * (
        grad
        - jnp.mean(grad, axis=-1, keepdims=True)
        - normed * jnp.mean(grad * normed, axis=-1, keepdims=True)
    )


def total(refs):
    return tree_sum([ref[...].astype(F32) for ref in refs])


def column_sum(values):
    return jnp.sum(values, axis=0, keepdims=True)


def part(mod_ref, index):
    width = mod_ref.shape[1] // 6
    return mod_ref[:, index * width : (index + 1) * width]


def gelu(pre):
    return 0.5 * pre * (1.0 + jnp.tanh(GELU_A * (pre + GELU_B * (pre * pre * pre))))


def gelu_slope(pre):
    square = pre * pre
    bent = jnp.tanh(GELU_A * (pre + GELU_B * (square * pre)))
    return 0.5 * (1.0 + bent) + 0.5 * pre * (1.0 - bent * bent) * (
        GELU_A * (1.0 + 3.0 * GELU_B * square)
    )


def put_rows(ref, refs):
    own = refs[0].shape[0]
    for k, source in enumerate(refs):
        ref[k * own : (k + 1) * own] = source[...]
    return ref[...]


def put_blocks(refs, values):
    own = refs[0].shape[0]
    for k, ref in enumerate(refs):
        ref[...] = values[k * own : (k + 1) * own].astype(ref.dtype)


def enter_body(place, tokens, cotangent, mod0, mod1, h_out, attn_in, g_y_out, g_shrunk):
    core = place[0]
    h = tokens[core].astype(F32)
    h_out[...] = h
    normed, _ = normalize(h)
    attn_in[...] = (normed * (1.0 + part(mod0, 1)) + part(mod0, 0)).astype(BF16)
    g_y = cotangent[core].astype(F32)
    g_y_out[...] = g_y
    g_shrunk[...] = (part(mod1, 5) * g_y).astype(BF16)


def weight_pieces_body(place, keep, received, *outs):
    first = place[0] == 0
    pieces = len(outs) // 2
    wide = outs[0].shape[1]
    for piece in range(pieces):
        own = keep[:, piece * wide : (piece + 1) * wide]
        other = received[:, piece * wide : (piece + 1) * wide]
        outs[piece][...] = jnp.where(first, own, other)
        outs[pieces + piece][...] = jnp.where(first, other, own)


def pick_attn(place, own, received):
    first = place[0] == 0
    width = own.shape[1] // 2
    mine, other = own[...], received[...]
    front = jnp.where(first, mine, other)
    back = jnp.where(first, other, mine)
    return front, back[:, :width], back[:, width:]


def attn_body(count, place, *refs):
    chunks = refs[:count]
    w_own, w_received, bias = refs[count : count + 3]
    rows_out, qkv_out, probs_out, mixed_out = refs[count + 3 : count + 7]
    partial = refs[count + 7 :]
    rows = put_rows(rows_out, chunks)
    w_front, w_value, w_out = pick_attn(place, w_own, w_received)
    width = w_value.shape[1]
    front = (dot(rows, w_front) + bias[:, : 2 * width]).astype(BF16)
    value = (dot(rows, w_value) + bias[:, 2 * width :]).astype(BF16)
    qkv_out[:, : 2 * width] = front
    qkv_out[:, 2 * width :] = value
    mixed = []
    for head in range(width // HEAD):
        at = head * HEAD
        query = front[:, at : at + HEAD]
        key = front[:, width + at : width + at + HEAD]
        scores = dot_t(query, key) * HEAD**-0.5
        powers = jnp.exp(scores - jnp.max(scores, axis=-1, keepdims=True))
        probs = powers / jnp.sum(powers, axis=-1, keepdims=True)
        probs_out[head] = probs
        mixed.append(dot(probs.astype(BF16), value[:, at : at + HEAD]))
    mixed = jnp.concatenate(mixed, axis=1).astype(BF16)
    mixed_out[...] = mixed
    put_blocks(partial, dot_t(mixed, w_out))


def middle_body(count, *refs):
    parts, (bias, h, mod, attended_out, middle_out, mlp_in) = refs[:count], refs[count:]
    attended = total(parts) + bias[...]
    attended_out[...] = attended
    middle = h[...] + part(mod, 2) * attended
    middle_out[...] = middle
    normed, _ = normalize(middle)
    mlp_in[...] = (normed * (1.0 + part(mod, 4)) + part(mod, 3)).astype(BF16)


def mlp_body(count, *refs):
    chunks = refs[:count]
    w_own, w_received, bias, rows_out, pre_out, hidden_out = refs[count : count + 6]
    partial = refs[count + 6 :]
    rows = put_rows(rows_out, chunks)
    half = w_own.shape[1] // 2
    shrunk = None
    for index, weight in enumerate((w_own, w_received)):
        at = index * half
        pre = dot(rows, weight[:, :half]) + bias[:, at : at + half]
        pre_out[:, at : at + half] = pre
        hidden = gelu(pre).astype(BF16)
        hidden_out[:, at : at + half] = hidden
        term = dot_t(hidden, weight[:, half:])
        shrunk = term if shrunk is None else shrunk + term
    put_blocks(partial, shrunk)


def mlp_both_body(count, *refs):
    chunks, g_chunks = refs[:count], refs[count : 2 * count]
    w_own, w_received, bias, rows_out, g_rows_out, hidden_out, g_pre_out, bias_grad = refs[
        2 * count : 2 * count + 8
    ]
    partial = refs[2 * count + 8 : 3 * count + 8]
    g_partial = refs[3 * count + 8 :]
    rows = put_rows(rows_out, chunks)
    g_rows = put_rows(g_rows_out, g_chunks)
    half = w_own.shape[1] // 2
    shrunk, g_in = None, None
    for index, weight in enumerate((w_own, w_received)):
        at = index * half
        pre = dot(rows, weight[:, :half]) + bias[:, at : at + half]
        hidden = gelu(pre).astype(BF16)
        hidden_out[:, at : at + half] = hidden
        g_pre = (dot(g_rows, weight[:, half:]) * gelu_slope(pre)).astype(BF16)
        g_pre_out[:, at : at + half] = g_pre
        bias_grad[:, at : at + half] = column_sum(g_pre.astype(F32))
        term = dot_t(hidden, weight[:, half:])
        g_term = dot_t(g_pre, weight[:, :half])
        shrunk = term if shrunk is None else shrunk + term
        g_in = g_term if g_in is None else g_in + g_term
    put_blocks(g_partial, g_in)
    put_blocks(partial, shrunk)


def mlp_back_body(count, *refs):
    g_chunks = refs[:count]
    w_own, w_received, pre_ref, g_rows_out, g_pre_out, bias_grad = refs[count : count + 6]
    g_partial = refs[count + 6 :]
    g_rows = put_rows(g_rows_out, g_chunks)
    half = w_own.shape[1] // 2
    g_in = None
    for index, weight in enumerate((w_own, w_received)):
        at = index * half
        pre = pre_ref[:, at : at + half]
        g_pre = (dot(g_rows, weight[:, half:]) * gelu_slope(pre)).astype(BF16)
        g_pre_out[:, at : at + half] = g_pre
        bias_grad[:, at : at + half] = column_sum(g_pre.astype(F32))
        g_term = dot_t(g_pre, weight[:, :half])
        g_in = g_term if g_in is None else g_in + g_term
    put_blocks(g_partial, g_in)


def between_body(count, *refs):
    parts = refs[:count]
    bias, middle, mod0, mod1, shrunk_out, passed_out, h_out, attn_in = refs[count:]
    shrunk = total(parts) + bias[...]
    shrunk_out[...] = shrunk
    passed = (middle[...] + part(mod0, 5) * shrunk).astype(BF16)
    passed_out[...] = passed
    h = passed.astype(F32)
    h_out[...] = h
    normed, _ = normalize(h)
    attn_in[...] = (normed * (1.0 + part(mod1, 1)) + part(mod1, 0)).astype(BF16)


def leave_body(count, *refs):
    parts = refs[:count]
    bias, middle, mod, g_y_ref, g_shrunk, y_out, g_gate, bias_grad = refs[count:]
    shrunk = total(parts) + bias[...]
    y_out[...] = (middle[...] + part(mod, 5) * shrunk).astype(BF16)
    g_gate[...] = column_sum(g_y_ref[...] * shrunk)
    bias_grad[...] = column_sum(g_shrunk[...].astype(F32))


def middle_back_body(count, *refs):
    parts = refs[:count]
    middle, mod, g_y, attended, g_middle_out, g_attended_out, g_shift, g_scale, g_gate, bias_grad = refs[
        count:
    ]
    g_in = total(parts)
    normed, rstd = normalize(middle[...])
    g_shift[...] = column_sum(g_in)
    g_scale[...] = column_sum(g_in * normed)
    g_middle = g_y[...] + normalize_back(g_in * (1.0 + part(mod, 4)), normed, rstd)
    g_middle_out[...] = g_middle
    g_gate[...] = column_sum(g_middle * attended[...])
    g_attended = (part(mod, 2) * g_middle).astype(BF16)
    g_attended_out[...] = g_attended
    bias_grad[...] = column_sum(g_attended.astype(F32))


def attn_back_body(count, place, *refs):
    g_chunks = refs[:count]
    w_own, w_received, qkv, probs_ref = refs[count : count + 4]
    g_rows_out, g_joint_out, bias_grad = refs[count + 4 : count + 7]
    g_partial = refs[count + 7 :]
    g_rows = put_rows(g_rows_out, g_chunks)
    w_front, w_value, w_out = pick_attn(place, w_own, w_received)
    width = w_value.shape[1]
    g_mixed = dot(g_rows, w_out).astype(BF16)
    g_query, g_key, g_value = [], [], []
    for head in range(width // HEAD):
        at = head * HEAD
        query = qkv[:, at : at + HEAD]
        key = qkv[:, width + at : width + at + HEAD]
        value = qkv[:, 2 * width + at : 2 * width + at + HEAD]
        probs = probs_ref[head]
        g_head = g_mixed[:, at : at + HEAD]
        g_probs = dot_t(g_head, value)
        row_dot = jnp.sum(probs * g_probs, axis=-1, keepdims=True)
        g_scores = (probs * (g_probs - row_dot)).astype(BF16)
        g_value.append(t_dot(probs.astype(BF16), g_head))
        g_query.append(dot(g_scores, key) * HEAD**-0.5)
        g_key.append(t_dot(g_scores, query) * HEAD**-0.5)
    g_front = jnp.concatenate(g_query + g_key, axis=1).astype(BF16)
    g_value = jnp.concatenate(g_value, axis=1).astype(BF16)
    g_joint_out[:, : 2 * width] = g_front
    g_joint_out[:, 2 * width :] = g_value
    bias_grad[:, :width] = column_sum(g_front[:, :width].astype(F32))
    bias_grad[:, width:] = column_sum(g_value.astype(F32))
    put_blocks(g_partial, dot_t(g_front, w_front) + dot_t(g_value, w_value))


def input_grad(parts, h, mod, g_middle, g_shift, g_scale):
    g_in = total(parts)
    normed, rstd = normalize(h[...])
    g_shift[...] = column_sum(g_in)
    g_scale[...] = column_sum(g_in * normed)
    return (g_middle[...] + normalize_back(g_in * (1.0 + part(mod, 1)), normed, rstd)).astype(BF16)


def between_back_body(count, *refs):
    parts = refs[:count]
    h, mod1, mod0, g_middle, shrunk, g_h_out, g_y_out, g_shrunk_out = refs[count : count + 8]
    g_shift, g_scale, g_gate, bias_grad = refs[count + 8 :]
    g_h = input_grad(parts, h, mod1, g_middle, g_shift, g_scale)
    g_h_out[...] = g_h
    g_y = g_h.astype(F32)
    g_y_out[...] = g_y
    g_gate[...] = column_sum(g_y * shrunk[...])
    g_shrunk = (part(mod0, 5) * g_y).astype(BF16)
    g_shrunk_out[...] = g_shrunk
    bias_grad[...] = column_sum(g_shrunk.astype(F32))


def finish_back_body(count, *refs):
    parts = refs[:count]
    h, mod, g_middle, g_h_out, g_shift, g_scale = refs[count:]
    g_h_out[...] = input_grad(parts, h, mod, g_middle, g_shift, g_scale)


def mlp_weights_body(rows, g_pre, g_rows, hidden, keep, give):
    half = keep.shape[1] // 2
    keep[:, :half] = t_dot(rows[...], g_pre[:, :half])
    keep[:, half:] = t_dot(g_rows[...], hidden[:, :half])
    give[:, :half] = t_dot(rows[...], g_pre[:, half:]).astype(BF16)
    give[:, half:] = t_dot(g_rows[...], hidden[:, half:]).astype(BF16)


def attn_weights_body(place, rows, g_joint, g_rows, mixed, keep, give):
    width = mixed.shape[1]
    first = place[0] == 0
    front = t_dot(rows[...], g_joint[:, : 2 * width])
    back = jnp.concatenate(
        [t_dot(rows[...], g_joint[:, 2 * width :]), t_dot(g_rows[...], mixed[...])], axis=1
    )
    keep[...] = jnp.where(first, front, back)
    give[...] = jnp.where(first, back, front).astype(BF16)


def line_blocks(place, k, rows):
    return pl.ds(pl.multiple_of((place[1] ^ k) * rows, 16), rows)


def stack_body(place, *refs):
    out = refs[-1]
    pieces = len(refs) // 2
    _, rows, wide = refs[0].shape
    for piece in range(pieces):
        pair, other = refs[piece], refs[pieces + piece]
        columns = slice(piece * wide, (piece + 1) * wide)
        for k, block in enumerate((pair[0], other[0], pair[1], other[1])):
            out[line_blocks(place, k, rows), columns] = block


def line_parts_body(place, keep, received, *outs):
    rows, wide = outs[2].shape

    for piece in range(len(outs) // 3):
        near, far, own = outs[3 * piece : 3 * piece + 3]
        columns = slice(piece * wide, (piece + 1) * wide)

        def block(k):
            at = line_blocks(place, k, rows)
            return keep[at, columns] + received[at, columns].astype(F32)

        near[0] = block(1).astype(BF16)
        near[1] = block(3).astype(BF16)
        far[...] = block(2)
        own[...] = block(0)


def final_mlp_body(place, mine, received, expand_out, shrink_t_out):
    first = place[0] == 0
    half = mine.shape[1] // 2
    own, other = mine[...].astype(F32), received[...].astype(F32)
    for index, values in enumerate((jnp.where(first, own, other), jnp.where(first, other, own))):
        expand_out[:, index * half : (index + 1) * half] = values[:, :half]
        shrink_t_out[:, index * half : (index + 1) * half] = values[:, half:]


def final_attn_body(place, mine, received, joint_out, out_out):
    first = place[0] == 0
    width = mine.shape[1] // 2
    own, other = mine[...].astype(F32), received[...].astype(F32)
    front, back = jnp.where(first, own, other), jnp.where(first, other, own)
    joint_out[0] = front[:, :width]
    joint_out[1] = front[:, width:]
    joint_out[2] = back[:, :width]
    out_out[...] = back[:, width:].T


def mod_first_body(a0, a1, a2, a3, weight, out):
    rows = jnp.concatenate([a0[...], a1[...], a2[...], a3[...]], axis=0)
    out[...] = dot(rows, weight[...])


def mod_sum_body(count, *refs):
    values = total(refs[:count])
    outs = refs[count:]
    micro = outs[0].shape[0]
    for k, out in enumerate(outs):
        out[...] = values[k * micro : (k + 1) * micro]


def mod_join_body(place, p0, p1, p2, p3, bias, mine, other, scratch):
    for k, ref in enumerate((p0, p1, p2, p3)):
        scratch[place[1] ^ k] = ref[...]
    values = jnp.concatenate([scratch[j] for j in range(LINE)], axis=1) + bias[...]
    first = place[0] == 0
    mine[...] = jnp.where(first, values[0:1], values[1:2])
    other[...] = jnp.where(first, values[1:2], values[0:1])


def pack_body(*refs):
    out, pieces = refs[-1], refs[:-1]
    count = len(pieces) // 2
    for row in range(2):
        at = 0
        for ref in pieces[row * count : (row + 1) * count]:
            out[row : row + 1, at : at + ref.shape[1]] = ref[...]
            at += ref.shape[1]


def grads_sum_body(count, place, *refs):
    parts = refs[:count]
    joint0, expand0, joint1, expand1, keep, give = refs[count:]
    first = place[0] == 0
    values = total(parts)
    hidden = expand0.shape[1]
    mod_width = values.shape[1] // 8 * 6
    rounded = values[:, :mod_width].astype(BF16).astype(F32)
    sums = values[:, mod_width:]
    half = hidden // 2

    def natural(ref):
        now = ref[...]
        return jnp.where(first, now, jnp.concatenate([now[:, half:], now[:, :half]], axis=1))

    rows = []
    for row, (joint, expand) in enumerate(((joint0, expand0), (joint1, expand1))):
        rows.append(
            jnp.concatenate(
                [rounded[row : row + 1], joint[...], natural(expand), sums[row : row + 1]], axis=1
            )
        )
    keep[...] = jnp.where(first, rows[0], rows[1])
    give[...] = jnp.where(first, rows[1], rows[0])


def grads_join_body(place, keep, received, out):
    mods = out.shape[1] - keep.shape[1]
    first = place[0] == 0
    own, other = keep[...], received[...]
    out[:, :mods] = jnp.where(first, own, other)[:, :mods].astype(BF16)
    out[:, mods : 2 * mods] = jnp.where(first, other, own)[:, :mods].astype(BF16)
    out[:, 2 * mods :] = (own[:, mods:] + other[:, mods:]).astype(BF16)


def mod_back_body(place, g0, g1, g2, g3, a0, a1, a2, a3, weight, w_grad, b_grad, bias, c0, c1, c2, c3):
    columns = weight.shape[1]
    mods = columns * LINE
    grads = (g0, g1, g2, g3)
    at = pl.multiple_of(place[1] * columns, 128)
    rows = []
    for ref in grads:
        rows.append(ref[:, pl.ds(at, columns)].astype(F32))
        rows.append(ref[:, pl.ds(pl.multiple_of(at + mods, 128), columns)].astype(F32))
    picked = jnp.concatenate(rows, axis=0).astype(BF16)
    activated = jnp.concatenate([a0[...], a1[...], a2[...], a3[...]], axis=0)
    w_grad[...] = t_dot(activated, picked)
    act = dot_t(picked, weight[...])
    for k, out in enumerate((c0, c1, c2, c3)):
        out[...] = act[2 * k : 2 * k + 2]
    b_grad[...] = tree_sum(
        [ref[:, :mods].astype(F32) + ref[:, mods : 2 * mods].astype(F32) for ref in grads]
    )
    bias[...] = tree_sum([ref[:, 2 * mods :].astype(F32) for ref in grads])


def on_device(
    tokens,
    conditions,
    cotangent,
    modulation_weight,
    modulation_bias,
    joint_weight,
    joint_bias,
    output_weight,
    output_bias,
    expand_weight,
    expand_bias,
    shrink_weight,
    shrink_bias,
):
    core = lax.axis_index("pipe")
    first = core == 0
    line = lax.axis_index("dp")
    place = jnp.stack([core, line]).astype(jnp.int32)
    line_size = lax.axis_size("dp")
    count = lax.axis_size("tensor")
    direct = line_size == LINE
    micro, _, own, model = tokens.shape
    width = output_weight.shape[1]
    hidden = expand_weight.shape[2]
    chunk = model // line_size
    rows = own * count
    columns = modulation_weight.shape[2]
    mods = 6 * model
    bias_width = 2 * width + hidden + 2 * model
    own_rows = modulation_weight[0]

    def mine(pair):
        return jnp.where(first, pair[0], pair[1])

    def other(pair):
        return jnp.where(first, pair[1], pair[0])

    def both_layers(kept, received):
        return jnp.where(first, kept, received), jnp.where(first, received, kept)

    def after(value, earlier):
        return lax.optimization_barrier((value, earlier))[0]

    def tie(main, *rest):
        return lax.optimization_barrier((main,) + rest)

    split = 2 * width
    pieces_shape = shape((chunk, split), BF16)
    joint_blocks = jnp.transpose(joint_weight[0], (1, 0, 2))
    expand, shrink_t = expand_weight[0], shrink_weight[0].T
    half = hidden // 2
    halves = (
        jnp.concatenate(
            [joint_blocks[0], joint_blocks[1], expand[:, :half], shrink_t[:, :half]], axis=1
        ),
        jnp.concatenate(
            [joint_blocks[2], output_weight[0].T, expand[:, half:], shrink_t[:, half:]], axis=1
        ),
    )
    keep, give = mine(halves), other(halves)
    line_pieces = run(
        "weight_pieces",
        weight_pieces_body,
        [pieces_shape] * 6,
        [keep, swap(give, "pipe", 1)],
        place,
    )

    bias_pack = jnp.concatenate(
        [
            joint_bias[0].reshape(-1),
            expand_bias[0],
            output_bias[0],
            shrink_bias[0],
        ]
    )[None]
    bias_layers = both_layers(bias_pack, swap(bias_pack, "pipe", 1))
    biases = []
    for packed in bias_layers:
        at = 2 * width
        joint = jnp.concatenate(
            [packed[:, :width], jnp.zeros((1, width), F32), packed[:, width:at]], axis=1
        )
        grown = packed[:, at : at + hidden]
        rolled = jnp.concatenate([grown[:, hidden // 2 :], grown[:, : hidden // 2]], axis=1)
        grown = jnp.where(first, grown, rolled)
        at += hidden
        biases.append((joint, packed[:, at : at + model], grown, packed[:, at + model :]))

    activated = jax.nn.silu(conditions[:, 0].astype(F32)).astype(BF16)
    if direct:
        activated_all = gather(activated, "dp")
    else:
        activated_all = lax.all_gather(activated, "dp", axis=0).reshape(line_size * micro, -1)

    def line_first(value):
        return (value, swap(value, "dp", 2)) if direct else value

    def line_second(pair):
        if not direct:
            return pair, lax.all_gather(pair, "dp", axis=0, tiled=True)
        stacked = jnp.stack(pair)
        return stacked, swap(stacked, "dp", 1)

    def both_cores(*steps):
        pairs, others = [step[0] for step in steps], [step[1] for step in steps]
        if direct:
            wide = sum(pair.shape[2] for pair in pairs)
            lined = run(
                "stack_line", stack_body, [shape((model, wide), BF16)], pairs + others, place
            )[0]
        else:
            lined = jnp.concatenate(others, axis=1)
        return lined, swap(lined, "pipe", 1)

    def piece_of(layer, index):
        return line_pieces[3 * layer + index]

    first_a0 = line_first(after(piece_of(0, 0), activated_all))

    if direct:
        mod_partial = run(
            "mod_first",
            mod_first_body,
            [shape((micro * LINE, columns), F32)],
            activated_all + [own_rows],
        )[0]
        mod_partials, first_a0 = tie(gather(mod_partial, "tensor"), first_a0)
        second_a0 = line_second(first_a0)
        first_e0 = line_first(after(piece_of(0, 1), first_a0))
        pieces = run(
            "mod_sum",
            functools.partial(mod_sum_body, count),
            [shape((micro, columns), F32)] * LINE,
            mod_partials,
        )
        pieces, second_a0 = tie(exchange(pieces, "dp"), second_a0)
        mod_mine, mod_other = pl.pallas_call(
            mod_join_body,
            out_shape=[shape((1, mods), F32)] * 2,
            in_specs=[pl.BlockSpec(memory_space=pltpu.SMEM)]
            + [pl.BlockSpec(memory_space=pltpu.VMEM)] * 5,
            out_specs=[pl.BlockSpec(memory_space=pltpu.VMEM)] * 2,
            scratch_shapes=[pltpu.VMEM((LINE, micro, columns), F32)],
            name="mod_join",
        )(place, *pieces, modulation_bias)
    else:
        mod_partial = dot(activated_all, own_rows)
        mod_partials = gather(mod_partial, "tensor")
        second_a0 = line_second(first_a0)
        first_e0 = line_first(piece_of(0, 1))
        mod_sum = tree_sum(mod_partials).reshape(line_size, micro, -1)
        mod_layer = lax.all_to_all(mod_sum, "dp", split_axis=0, concat_axis=0)
        mod_layer = jnp.swapaxes(mod_layer, 0, 1).reshape(micro, -1) + modulation_bias
        mod_mine, mod_other = mine(mod_layer)[None], other(mod_layer)[None]
    mod0, mod1 = both_layers(mod_mine, swap(mod_other, "pipe", 1))

    w_attn0 = both_cores(second_a0)
    own_f32 = shape((own, model), F32)
    own_bf16 = shape((own, model), BF16)
    blocks = [own_bf16] * count
    wide_bf16 = shape((rows, model), BF16)
    hidden_bf16 = shape((rows, hidden), BF16)
    vector = shape((1, model), F32)
    hidden_vector = shape((1, hidden), F32)
    h0, attn_in, g_y1, g_shrunk1 = run(
        "enter",
        enter_body,
        [own_f32, own_bf16, own_f32, own_bf16],
        [tokens[:, 0], cotangent[:, 0], mod0, mod1],
        place,
    )

    def kernel(name, body, outs, args, where=None):
        return run(name, functools.partial(body, count), outs, args, where)

    def attention(attn_rows, weight, bias):
        outs = kernel(
            "attention",
            attn_body,
            [
                wide_bf16,
                shape((rows, 3 * width), BF16),
                shape((width // HEAD, rows, rows), F32),
                shape((rows, width), BF16),
            ]
            + blocks,
            attn_rows + [weight[0], weight[1], bias],
            place,
        )
        return outs[:4], exchange(outs[4:], "tensor")

    def middle_of(parts, bias, h, mod):
        return kernel(
            "middle", middle_body, [own_f32, own_f32, own_bf16], parts + [bias, h, mod]
        )

    attn_rows, first_e0 = tie(gather(attn_in, "tensor"), first_e0)
    second_e0 = line_second(first_e0)
    first_s0 = line_first(after(piece_of(0, 2), first_e0))
    kept_attn0, parts = attention(attn_rows, w_attn0, biases[0][0])
    parts, second_e0, first_s0 = tie(parts, second_e0, first_s0)
    second_s0 = line_second(first_s0)
    first_a1 = line_first(after(piece_of(1, 0), first_s0))
    attended0, middle0, mlp_in = middle_of(parts, biases[0][1], h0, mod0)
    mlp_rows0, second_s0, first_a1 = tie(gather(mlp_in, "tensor"), second_s0, first_a1)
    w_mlp0 = both_cores(second_e0, second_s0)
    second_a1 = line_second(first_a1)
    first_e1 = line_first(after(piece_of(1, 1), first_a1))
    g_rows1 = gather(after(g_shrunk1, mlp_rows0), "tensor")
    outs = kernel(
        "feed_forward",
        mlp_body,
        [wide_bf16, shape((rows, hidden), F32), hidden_bf16] + blocks,
        mlp_rows0 + [w_mlp0[0], w_mlp0[1], biases[0][2]],
    )
    outs, g_rows1 = tie(outs, g_rows1)
    mlp_rows0, pre0, hidden0 = outs[:3]
    (parts,) = tie(exchange(outs[3:], "tensor"))
    parts, second_a1, first_e1 = tie(parts, second_a1, first_e1)
    w_attn1 = both_cores(second_a1)
    second_e1 = line_second(first_e1)
    first_s1 = line_first(after(piece_of(1, 2), first_e1))
    shrunk0, passed, h1, attn_in = kernel(
        "between",
        between_body,
        [own_f32, own_bf16, own_f32, own_bf16],
        parts + [biases[0][3], middle0, mod0, mod1],
    )

    (attn_rows, w_attn1), second_e1, first_s1 = tie(
        (gather(attn_in, "tensor"), w_attn1), second_e1, first_s1
    )
    second_s1 = line_second(first_s1)
    kept_attn1, parts = attention(attn_rows, w_attn1, biases[1][0])
    parts, second_s1 = tie(parts, second_s1)
    w_mlp1 = both_cores(second_e1, second_s1)
    attended1, middle1, mlp_in = middle_of(parts, biases[1][1], h1, mod1)
    outs = kernel(
        "feed_forward_both",
        mlp_both_body,
        [wide_bf16, wide_bf16, hidden_bf16, hidden_bf16, hidden_vector] + blocks + blocks,
        gather(mlp_in, "tensor") + g_rows1 + [w_mlp1[0], w_mlp1[1], biases[1][2]],
    )
    mlp_rows1, g_rows1, hidden1, g_pre1, expand_grad1 = outs[:5]
    y_partial, g_partial = outs[5 : 5 + count], outs[5 + count :]

    def middle_back(parts, middle, mod, g_y, attended):
        return kernel(
            "middle_back",
            middle_back_body,
            [own_f32, own_bf16] + [vector] * 4,
            parts + [middle, mod, g_y, attended],
        )

    def attention_back(g_rows, weight, kept):
        outs = kernel(
            "attention_back",
            attn_back_body,
            [wide_bf16, shape((rows, 3 * width), BF16), shape((1, 2 * width), F32)] + blocks,
            g_rows + [weight[0], weight[1], kept[1], kept[2]],
            place,
        )
        return outs[:3], exchange(outs[3:], "tensor")

    def chip_sum(grads):
        keep, give = grads
        return (keep + swap(give, "pipe", 1).astype(F32)).astype(BF16)

    def line_sum(whole):
        return lax.psum_scatter(whole, "dp", scatter_dimension=0, tiled=True)

    def line_parts(grads, pieces):
        keep, give = grads
        wide = keep.shape[1] // pieces
        if not direct:
            whole = chip_sum(grads)
            return [[whole[:, k * wide : (k + 1) * wide]] for k in range(pieces)]
        outs = run(
            "line_parts",
            line_parts_body,
            [shape((2, chunk, wide), BF16), shape((chunk, wide), F32), shape((chunk, wide), F32)]
            * pieces,
            [keep, swap(give, "pipe", 1)],
            place,
        )
        return [outs[3 * k : 3 * k + 3] for k in range(pieces)]

    def line_near(parts):
        return swap(parts[0], "dp", 1) if direct else parts[0]

    def line_far(parts, near):
        if not direct:
            return line_sum(near)
        return swap((parts[1] + near[1].astype(F32)).astype(BF16), "dp", 2)

    def line_total(parts, near, far):
        if not direct:
            return far
        return (parts[2] + near[0].astype(F32) + far.astype(F32)).astype(BF16)

    def own_halves(pair):
        return mine(pair), swap(other(pair), "pipe", 1)

    def mlp_weight_grads(mlp_rows, g_pre, g_rows, hidden_rows):
        return run(
            "mlp_weight_grads",
            mlp_weights_body,
            [shape((model, hidden), F32), shape((model, hidden), BF16)],
            [mlp_rows, g_pre, g_rows, hidden_rows],
        )

    def attn_weight_grads(kept, g_joint, g_rows):
        return run(
            "attn_weight_grads",
            attn_weights_body,
            [shape((model, 2 * width), F32), shape((model, 2 * width), BF16)],
            [kept[0], g_joint, g_rows, kept[3]],
            place,
        )

    (g_parts, (parts_e1, parts_s1)), y_partial = tie(
        (
            exchange(g_partial, "tensor"),
            line_parts(mlp_weight_grads(mlp_rows1, g_pre1, g_rows1, hidden1), 2),
        ),
        y_partial,
    )
    near_e1 = line_near(parts_e1)
    g_middle1, g_attended, g_shift_mlp1, g_scale_mlp1, g_gate_attn1, out_grad1 = middle_back(
        g_parts, middle1, mod1, g_y1, attended1
    )
    y_parts = exchange(y_partial, "tensor")
    g_rows, near_e1, parts_e1, parts_s1 = tie(
        gather(g_attended, "tensor"), near_e1, parts_e1, parts_s1
    )
    far_e1 = line_far(parts_e1, near_e1)
    near_s1 = line_near(parts_s1)
    (g_rows, g_joint, joint_grad1), parts = attention_back(g_rows, w_attn1, kept_attn1)
    (parts, (parts_a1,)), far_e1, near_s1, parts_s1 = tie(
        (parts, line_parts(attn_weight_grads(kept_attn1, g_joint, g_rows), 1)),
        far_e1,
        near_s1,
        parts_s1,
    )
    near_a1 = line_near(parts_a1)
    far_s1 = line_far(parts_s1, near_s1)
    g_passed, g_y0, g_shrunk0, g_shift_attn1, g_scale_attn1, g_gate_mlp0, shrink_grad0 = kernel(
        "between_back",
        between_back_body,
        [own_bf16, own_f32, own_bf16] + [vector] * 4,
        parts + [h1, mod1, mod0, g_middle1, shrunk0],
    )

    g_rows0, near_a1, far_s1, parts_a1 = tie(
        gather(g_shrunk0, "tensor"), near_a1, far_s1, parts_a1
    )
    outs = kernel(
        "feed_forward_back",
        mlp_back_body,
        [wide_bf16, hidden_bf16, hidden_vector] + blocks,
        g_rows0 + [w_mlp0[0], w_mlp0[1], pre0],
    )
    g_rows0, g_pre0, expand_grad0 = outs[:3]
    parts, (parts_m0,) = tie(
        exchange(outs[3:], "tensor"),
        line_parts(mlp_weight_grads(mlp_rows0, g_pre0, g_rows0, hidden0), 1),
    )
    near_m0 = line_near(parts_m0)
    g_middle0, g_attended, g_shift_mlp0, g_scale_mlp0, g_gate_attn0, out_grad0 = middle_back(
        parts, middle0, mod0, g_y0, attended0
    )
    y1, g_gate_mlp1, shrink_grad1 = kernel(
        "leave",
        leave_body,
        [own_bf16, vector, vector],
        y_parts + [biases[1][3], middle1, mod1, g_y1, g_shrunk1],
    )
    g_rows, near_m0 = tie(gather(g_attended, "tensor"), near_m0)
    far_m0 = line_far(parts_m0, near_m0)
    (g_rows, g_joint, joint_grad0), parts = attention_back(g_rows, w_attn0, kept_attn0)
    parts, far_m0, g_joint, g_rows, near_a1 = tie(parts, far_m0, g_joint, g_rows, near_a1)
    far_a1 = line_far(parts_a1, near_a1)
    (parts_a0,) = line_parts(attn_weight_grads(kept_attn0, g_joint, g_rows), 1)
    g_h0, g_shift_attn0, g_scale_attn0 = kernel(
        "finish_back",
        finish_back_body,
        [own_bf16, vector, vector],
        parts + [h0, mod0, g_middle0],
    )
    def own_layer_of_micros(pair):
        return jnp.stack(both_layers(mine(pair), swap(other(pair), "pipe", 1)))

    layer_outputs = own_layer_of_micros((passed, y1))
    input_grads = own_layer_of_micros((g_h0, g_passed))

    packed = run(
        "pack_grads",
        pack_body,
        [shape((2, mods + 2 * model), F32)],
        [
            g_shift_attn0,
            g_scale_attn0,
            g_gate_attn0,
            g_shift_mlp0,
            g_scale_mlp0,
            g_gate_mlp0,
            out_grad0,
            shrink_grad0,
            g_shift_attn1,
            g_scale_attn1,
            g_gate_attn1,
            g_shift_mlp1,
            g_scale_mlp1,
            g_gate_mlp1,
            out_grad1,
            shrink_grad1,
        ],
    )[0]
    packed_all = gather(packed, "tensor")
    near_a0 = line_near(parts_a0)
    keep, give = run(
        "grads_sum",
        functools.partial(grads_sum_body, count),
        [shape((1, mods + bias_width), F32)] * 2,
        packed_all + [joint_grad0, expand_grad0, joint_grad1, expand_grad1],
        place,
    )
    received, far_a1 = tie(swap(give, "pipe", 1), far_a1)
    joined = run(
        "grads_join",
        grads_join_body,
        [shape((1, 2 * mods + bias_width), BF16)],
        [keep, received],
        place,
    )[0]
    joined_all = gather(joined, "dp") if direct else lax.all_gather(joined, "dp", axis=0, tiled=True)
    joined_all, near_a0 = tie(joined_all, near_a0)
    far_a0 = line_far(parts_a0, near_a0)
    mlp_grad0 = line_total(parts_m0, near_m0, far_m0)
    mlp_grad1 = jnp.concatenate(
        [line_total(parts_e1, near_e1, far_e1), line_total(parts_s1, near_s1, far_s1)], axis=1
    )
    attn_grad0 = line_total(parts_a0, near_a0, far_a0)
    attn_grad1 = line_total(parts_a1, near_a1, far_a1)
    expand_w_grad, shrink_t_grad = run(
        "final_mlp",
        final_mlp_body,
        [shape((chunk, hidden), F32)] * 2,
        own_halves((mlp_grad0, mlp_grad1)),
        place,
    )
    joint_w_grad, output_w_grad = run(
        "final_attn",
        final_attn_body,
        [shape((3, chunk, width), F32), shape((width, chunk), F32)],
        own_halves((attn_grad0, attn_grad1)),
        place,
    )

    if direct:
        outs = run(
            "mod_back",
            mod_back_body,
            [shape(own_rows.shape, F32), shape((1, mods), F32), shape((1, bias_width), F32)]
            + [shape((micro, own_rows.shape[0]), F32)] * LINE,
            joined_all + activated_all + [own_rows],
            place,
        )
        ada_grad, ada_bias_grad, bias_sum = outs[:3]
        act_parts, joint_w_grad, output_w_grad = tie(
            exchange(outs[3:], "dp"), joint_w_grad, output_w_grad
        )
        act_grad = tree_sum(act_parts)
    else:
        mod_grads = joined_all[:, : 2 * mods].reshape(line_size * micro, mods)
        bias_sum = jnp.sum(joined_all[:, 2 * mods :].astype(F32), axis=0, keepdims=True)
        ada_bias_grad = jnp.sum(mod_grads.astype(F32), axis=0, keepdims=True)
        picked = lax.dynamic_slice_in_dim(mod_grads, line * columns, columns, 1).astype(BF16)
        ada_grad = t_dot(activated_all, picked)
        act_partial = dot_t(picked, own_rows).reshape(line_size, micro, -1)
        act_grad = lax.psum_scatter(act_partial, "dp", scatter_dimension=0, tiled=False)
    _, silu_back = jax.vjp(jax.nn.silu, conditions[:, 0].astype(F32))
    cond_grad = silu_back(act_grad)[0]
    at = 2 * width
    return (
        layer_outputs[None, :, None],
        input_grads[None, :, None],
        cond_grad[None, :, None],
        ada_grad[None],
        ada_bias_grad,
        jnp.transpose(joint_w_grad, (1, 0, 2))[None],
        bias_sum[:, :at].reshape(1, 2, width),
        output_w_grad[None],
        bias_sum[:, at + hidden : at + hidden + model],
        expand_w_grad[None],
        bias_sum[:, at : at + hidden],
        shrink_t_grad.T[None],
        bias_sum[:, at + hidden + model :],
    )


def solution(mesh):
    in_specs = (
        P(None, "dp", "tensor", None),
        P(None, "dp", "tensor"),
        P(None, "dp", "tensor", None),
        P("pipe", "tensor", "dp"),
        P("pipe", None),
        P("pipe", "dp", None, "tensor"),
        P("pipe", None, "tensor"),
        P("pipe", "tensor", "dp"),
        P("pipe", None),
        P("pipe", "dp", "tensor"),
        P("pipe", "tensor"),
        P("pipe", "tensor", "dp"),
        P("pipe", None),
    )
    out_specs = (
        P("pipe", None, "dp", "tensor", None),
        P("pipe", None, "dp", "tensor", None),
        P("pipe", None, "dp", "tensor"),
        P("pipe", "tensor", "dp"),
        P("pipe", None),
        P("pipe", "dp", None, "tensor"),
        P("pipe", None, "tensor"),
        P("pipe", "tensor", "dp"),
        P("pipe", None),
        P("pipe", "dp", "tensor"),
        P("pipe", "tensor"),
        P("pipe", "tensor", "dp"),
        P("pipe", None),
    )
    return jax.shard_map(
        on_device, mesh=mesh, in_specs=in_specs, out_specs=out_specs, check_vma=False
    )
```

```python
import functools

import jax
import jax.numpy as jnp
from jax import lax
from jax.experimental import pallas as pl
from jax.experimental.pallas import tpu as pltpu
from jax.sharding import PartitionSpec as P

HEAD = 64
EPS = 1e-06
F32 = jnp.float32
BF16 = jnp.bfloat16
LINE = 4
VMEM_BYTES = 24 * 1024 * 1024
GELU_A = 0.7978845608028654
GELU_B = 0.044715


def swap(value, axis, mask):
    pairs = [(source, source ^ mask) for source in range(lax.axis_size(axis))]
    return lax.ppermute(value, axis, pairs)


def exchange(parts, axis):
    received = {k: swap(parts[k], axis, k) for k in range(len(parts) - 1, 0, -1)}
    return [parts[0]] + [received[k] for k in range(1, len(parts))]


def gather(value, axis):
    return exchange([value] * lax.axis_size(axis), axis)


def tree_sum(parts):
    parts = list(parts)
    while len(parts) > 1:
        parts = [parts[k] + parts[k + 1] for k in range(0, len(parts), 2)]
    return parts[0]


def shape(dims, dtype):
    return jax.ShapeDtypeStruct(dims, dtype)


def run(name, body, outs, args, place=None):
    specs = [pl.BlockSpec(memory_space=pltpu.VMEM) for _ in args]
    if place is not None:
        specs = [pl.BlockSpec(memory_space=pltpu.SMEM)] + specs
        args = [place] + list(args)
    return pl.pallas_call(
        body,
        out_shape=outs,
        in_specs=specs,
        out_specs=[pl.BlockSpec(memory_space=pltpu.VMEM) for _ in outs],
        compiler_params=pltpu.CompilerParams(vmem_limit_bytes=VMEM_BYTES),
        name=name,
    )(*args)


def dot(left, right):
    return jnp.dot(left, right, preferred_element_type=F32)


def dot_t(left, right):
    return lax.dot_general(left, right, (((1,), (1,)), ((), ())), preferred_element_type=F32)


def t_dot(left, right):
    return lax.dot_general(left, right, (((0,), (0,)), ((), ())), preferred_element_type=F32)


def normalize(values):
    centred = values - jnp.mean(values, axis=-1, keepdims=True)
    rstd = lax.rsqrt(jnp.mean(centred * centred, axis=-1, keepdims=True) + EPS)
    return centred * rstd, rstd


def normalize_back(grad, normed, rstd):
    return rstd * (
        grad
        - jnp.mean(grad, axis=-1, keepdims=True)
        - normed * jnp.mean(grad * normed, axis=-1, keepdims=True)
    )


def total(refs):
    return tree_sum([ref[...].astype(F32) for ref in refs])


def column_sum(values):
    return jnp.sum(values, axis=0, keepdims=True)


def part(mod_ref, index):
    width = mod_ref.shape[1] // 6
    return mod_ref[:, index * width : (index + 1) * width]


def gelu(pre):
    return 0.5 * pre * (1.0 + jnp.tanh(GELU_A * (pre + GELU_B * (pre * pre * pre))))


def gelu_slope(pre):
    square = pre * pre
    bent = jnp.tanh(GELU_A * (pre + GELU_B * (square * pre)))
    return 0.5 * (1.0 + bent) + 0.5 * pre * (1.0 - bent * bent) * (
        GELU_A * (1.0 + 3.0 * GELU_B * square)
    )


def put_rows(ref, refs):
    own = refs[0].shape[0]
    for k, source in enumerate(refs):
        ref[k * own : (k + 1) * own] = source[...]
    return ref[...]


def put_blocks(refs, values):
    own = refs[0].shape[0]
    for k, ref in enumerate(refs):
        ref[...] = values[k * own : (k + 1) * own].astype(ref.dtype)


def enter_body(place, tokens, cotangent, mod0, mod1, h_out, attn_in, g_y_out, g_shrunk):
    core = place[0]
    h = tokens[core].astype(F32)
    h_out[...] = h
    normed, _ = normalize(h)
    attn_in[...] = (normed * (1.0 + part(mod0, 1)) + part(mod0, 0)).astype(BF16)
    g_y = cotangent[core].astype(F32)
    g_y_out[...] = g_y
    g_shrunk[...] = (part(mod1, 5) * g_y).astype(BF16)


def weight_pieces_body(place, keep, received, *outs):
    first = place[0] == 0
    pieces = len(outs) // 2
    wide = outs[0].shape[1]
    for piece in range(pieces):
        own = keep[:, piece * wide : (piece + 1) * wide]
        other = received[:, piece * wide : (piece + 1) * wide]
        outs[piece][...] = jnp.where(first, own, other)
        outs[pieces + piece][...] = jnp.where(first, other, own)


def pick_attn(place, own, received):
    first = place[0] == 0
    width = own.shape[1] // 2
    mine, other = own[...], received[...]
    front = jnp.where(first, mine, other)
    back = jnp.where(first, other, mine)
    return front, back[:, :width], back[:, width:]


def attn_body(count, place, *refs):
    chunks = refs[:count]
    w_own, w_received, bias = refs[count : count + 3]
    rows_out, qkv_out, probs_out, mixed_out = refs[count + 3 : count + 7]
    partial = refs[count + 7 :]
    rows = put_rows(rows_out, chunks)
    w_front, w_value, w_out = pick_attn(place, w_own, w_received)
    width = w_value.shape[1]
    front = (dot(rows, w_front) + bias[:, : 2 * width]).astype(BF16)
    value = (dot(rows, w_value) + bias[:, 2 * width :]).astype(BF16)
    qkv_out[:, : 2 * width] = front
    qkv_out[:, 2 * width :] = value
    mixed = []
    for head in range(width // HEAD):
        at = head * HEAD
        query = front[:, at : at + HEAD]
        key = front[:, width + at : width + at + HEAD]
        scores = dot_t(query, key) * HEAD**-0.5
        powers = jnp.exp(scores - jnp.max(scores, axis=-1, keepdims=True))
        probs = powers / jnp.sum(powers, axis=-1, keepdims=True)
        probs_out[head] = probs
        mixed.append(dot(probs.astype(BF16), value[:, at : at + HEAD]))
    mixed = jnp.concatenate(mixed, axis=1).astype(BF16)
    mixed_out[...] = mixed
    put_blocks(partial, dot_t(mixed, w_out))


def middle_body(count, *refs):
    parts, (bias, h, mod, attended_out, middle_out, mlp_in) = refs[:count], refs[count:]
    attended = total(parts) + bias[...]
    attended_out[...] = attended
    middle = h[...] + part(mod, 2) * attended
    middle_out[...] = middle
    normed, _ = normalize(middle)
    mlp_in[...] = (normed * (1.0 + part(mod, 4)) + part(mod, 3)).astype(BF16)


def mlp_body(count, *refs):
    chunks = refs[:count]
    w_own, w_received, bias, rows_out, pre_out, hidden_out = refs[count : count + 6]
    partial = refs[count + 6 :]
    rows = put_rows(rows_out, chunks)
    half = w_own.shape[1] // 2
    shrunk = None
    for index, weight in enumerate((w_own, w_received)):
        at = index * half
        pre = dot(rows, weight[:, :half]) + bias[:, at : at + half]
        pre_out[:, at : at + half] = pre
        hidden = gelu(pre).astype(BF16)
        hidden_out[:, at : at + half] = hidden
        term = dot_t(hidden, weight[:, half:])
        shrunk = term if shrunk is None else shrunk + term
    put_blocks(partial, shrunk)


def mlp_both_body(count, *refs):
    chunks, g_chunks = refs[:count], refs[count : 2 * count]
    w_own, w_received, bias, rows_out, g_rows_out, hidden_out, g_pre_out, bias_grad = refs[
        2 * count : 2 * count + 8
    ]
    partial = refs[2 * count + 8 : 3 * count + 8]
    g_partial = refs[3 * count + 8 :]
    rows = put_rows(rows_out, chunks)
    g_rows = put_rows(g_rows_out, g_chunks)
    half = w_own.shape[1] // 2
    shrunk, g_in = None, None
    for index, weight in enumerate((w_own, w_received)):
        at = index * half
        pre = dot(rows, weight[:, :half]) + bias[:, at : at + half]
        hidden = gelu(pre).astype(BF16)
        hidden_out[:, at : at + half] = hidden
        g_pre = (dot(g_rows, weight[:, half:]) * gelu_slope(pre)).astype(BF16)
        g_pre_out[:, at : at + half] = g_pre
        bias_grad[:, at : at + half] = column_sum(g_pre.astype(F32))
        term = dot_t(hidden, weight[:, half:])
        g_term = dot_t(g_pre, weight[:, :half])
        shrunk = term if shrunk is None else shrunk + term
        g_in = g_term if g_in is None else g_in + g_term
    put_blocks(g_partial, g_in)
    put_blocks(partial, shrunk)


def mlp_back_body(count, *refs):
    g_chunks = refs[:count]
    w_own, w_received, pre_ref, g_rows_out, g_pre_out, bias_grad = refs[count : count + 6]
    g_partial = refs[count + 6 :]
    g_rows = put_rows(g_rows_out, g_chunks)
    half = w_own.shape[1] // 2
    g_in = None
    for index, weight in enumerate((w_own, w_received)):
        at = index * half
        pre = pre_ref[:, at : at + half]
        g_pre = (dot(g_rows, weight[:, half:]) * gelu_slope(pre)).astype(BF16)
        g_pre_out[:, at : at + half] = g_pre
        bias_grad[:, at : at + half] = column_sum(g_pre.astype(F32))
        g_term = dot_t(g_pre, weight[:, :half])
        g_in = g_term if g_in is None else g_in + g_term
    put_blocks(g_partial, g_in)


def between_body(count, *refs):
    parts = refs[:count]
    bias, middle, mod0, mod1, shrunk_out, passed_out, h_out, attn_in = refs[count:]
    shrunk = total(parts) + bias[...]
    shrunk_out[...] = shrunk
    passed = (middle[...] + part(mod0, 5) * shrunk).astype(BF16)
    passed_out[...] = passed
    h = passed.astype(F32)
    h_out[...] = h
    normed, _ = normalize(h)
    attn_in[...] = (normed * (1.0 + part(mod1, 1)) + part(mod1, 0)).astype(BF16)


def leave_body(count, *refs):
    parts = refs[:count]
    bias, middle, mod, g_y_ref, g_shrunk, y_out, g_gate, bias_grad = refs[count:]
    shrunk = total(parts) + bias[...]
    y_out[...] = (middle[...] + part(mod, 5) * shrunk).astype(BF16)
    g_gate[...] = column_sum(g_y_ref[...] * shrunk)
    bias_grad[...] = column_sum(g_shrunk[...].astype(F32))


def middle_back_body(count, *refs):
    parts = refs[:count]
    middle, mod, g_y, attended, g_middle_out, g_attended_out, g_shift, g_scale, g_gate, bias_grad = refs[
        count:
    ]
    g_in = total(parts)
    normed, rstd = normalize(middle[...])
    g_shift[...] = column_sum(g_in)
    g_scale[...] = column_sum(g_in * normed)
    g_middle = g_y[...] + normalize_back(g_in * (1.0 + part(mod, 4)), normed, rstd)
    g_middle_out[...] = g_middle
    g_gate[...] = column_sum(g_middle * attended[...])
    g_attended = (part(mod, 2) * g_middle).astype(BF16)
    g_attended_out[...] = g_attended
    bias_grad[...] = column_sum(g_attended.astype(F32))


def attn_back_body(count, place, *refs):
    g_chunks = refs[:count]
    w_own, w_received, qkv, probs_ref = refs[count : count + 4]
    g_rows_out, g_joint_out, bias_grad = refs[count + 4 : count + 7]
    g_partial = refs[count + 7 :]
    g_rows = put_rows(g_rows_out, g_chunks)
    w_front, w_value, w_out = pick_attn(place, w_own, w_received)
    width = w_value.shape[1]
    g_mixed = dot(g_rows, w_out).astype(BF16)
    g_query, g_key, g_value = [], [], []
    for head in range(width // HEAD):
        at = head * HEAD
        query = qkv[:, at : at + HEAD]
        key = qkv[:, width + at : width + at + HEAD]
        value = qkv[:, 2 * width + at : 2 * width + at + HEAD]
        probs = probs_ref[head]
        g_head = g_mixed[:, at : at + HEAD]
        g_probs = dot_t(g_head, value)
        row_dot = jnp.sum(probs * g_probs, axis=-1, keepdims=True)
        g_scores = (probs * (g_probs - row_dot)).astype(BF16)
        g_value.append(t_dot(probs.astype(BF16), g_head))
        g_query.append(dot(g_scores, key) * HEAD**-0.5)
        g_key.append(t_dot(g_scores, query) * HEAD**-0.5)
    g_front = jnp.concatenate(g_query + g_key, axis=1).astype(BF16)
    g_value = jnp.concatenate(g_value, axis=1).astype(BF16)
    g_joint_out[:, : 2 * width] = g_front
    g_joint_out[:, 2 * width :] = g_value
    bias_grad[:, :width] = column_sum(g_front[:, :width].astype(F32))
    bias_grad[:, width:] = column_sum(g_value.astype(F32))
    put_blocks(g_partial, dot_t(g_front, w_front) + dot_t(g_value, w_value))


def input_grad(parts, h, mod, g_middle, g_shift, g_scale):
    g_in = total(parts)
    normed, rstd = normalize(h[...])
    g_shift[...] = column_sum(g_in)
    g_scale[...] = column_sum(g_in * normed)
    return (g_middle[...] + normalize_back(g_in * (1.0 + part(mod, 1)), normed, rstd)).astype(BF16)


def between_back_body(count, *refs):
    parts = refs[:count]
    h, mod1, mod0, g_middle, shrunk, g_h_out, g_y_out, g_shrunk_out = refs[count : count + 8]
    g_shift, g_scale, g_gate, bias_grad = refs[count + 8 :]
    g_h = input_grad(parts, h, mod1, g_middle, g_shift, g_scale)
    g_h_out[...] = g_h
    g_y = g_h.astype(F32)
    g_y_out[...] = g_y
    g_gate[...] = column_sum(g_y * shrunk[...])
    g_shrunk = (part(mod0, 5) * g_y).astype(BF16)
    g_shrunk_out[...] = g_shrunk
    bias_grad[...] = column_sum(g_shrunk.astype(F32))


def finish_back_body(count, *refs):
    parts = refs[:count]
    h, mod, g_middle, g_h_out, g_shift, g_scale = refs[count:]
    g_h_out[...] = input_grad(parts, h, mod, g_middle, g_shift, g_scale)


def mlp_weights_body(rows, g_pre, g_rows, hidden, keep, give):
    half = keep.shape[1] // 2
    keep[:, :half] = t_dot(rows[...], g_pre[:, :half])
    keep[:, half:] = t_dot(g_rows[...], hidden[:, :half])
    give[:, :half] = t_dot(rows[...], g_pre[:, half:]).astype(BF16)
    give[:, half:] = t_dot(g_rows[...], hidden[:, half:]).astype(BF16)


def attn_weights_body(place, rows, g_joint, g_rows, mixed, keep, give):
    width = mixed.shape[1]
    first = place[0] == 0
    front = t_dot(rows[...], g_joint[:, : 2 * width])
    back = jnp.concatenate(
        [t_dot(rows[...], g_joint[:, 2 * width :]), t_dot(g_rows[...], mixed[...])], axis=1
    )
    keep[...] = jnp.where(first, front, back)
    give[...] = jnp.where(first, back, front).astype(BF16)


def line_blocks(place, k, rows):
    return pl.ds(pl.multiple_of((place[1] ^ k) * rows, 16), rows)


def stack_body(place, *refs):
    out = refs[-1]
    pieces = len(refs) // 2
    _, rows, wide = refs[0].shape
    for piece in range(pieces):
        pair, other = refs[piece], refs[pieces + piece]
        columns = slice(piece * wide, (piece + 1) * wide)
        for k, block in enumerate((pair[0], other[0], pair[1], other[1])):
            out[line_blocks(place, k, rows), columns] = block


def line_parts_body(place, keep, received, *outs):
    rows, wide = outs[2].shape

    for piece in range(len(outs) // 3):
        near, far, own = outs[3 * piece : 3 * piece + 3]
        columns = slice(piece * wide, (piece + 1) * wide)

        def block(k):
            at = line_blocks(place, k, rows)
            return keep[at, columns] + received[at, columns].astype(F32)

        near[0] = block(1).astype(BF16)
        near[1] = block(3).astype(BF16)
        far[...] = block(2)
        own[...] = block(0)


def final_mlp_body(place, mine, received, expand_out, shrink_t_out):
    first = place[0] == 0
    half = mine.shape[1] // 2
    own, other = mine[...].astype(F32), received[...].astype(F32)
    for index, values in enumerate((jnp.where(first, own, other), jnp.where(first, other, own))):
        expand_out[:, index * half : (index + 1) * half] = values[:, :half]
        shrink_t_out[:, index * half : (index + 1) * half] = values[:, half:]


def final_attn_body(place, mine, received, joint_out, out_out):
    first = place[0] == 0
    width = mine.shape[1] // 2
    own, other = mine[...].astype(F32), received[...].astype(F32)
    front, back = jnp.where(first, own, other), jnp.where(first, other, own)
    joint_out[0] = front[:, :width]
    joint_out[1] = front[:, width:]
    joint_out[2] = back[:, :width]
    out_out[...] = back[:, width:].T


def mod_first_body(a0, a1, a2, a3, weight, out):
    rows = jnp.concatenate([a0[...], a1[...], a2[...], a3[...]], axis=0)
    out[...] = dot(rows, weight[...])


def mod_sum_body(count, *refs):
    values = total(refs[:count])
    outs = refs[count:]
    micro = outs[0].shape[0]
    for k, out in enumerate(outs):
        out[...] = values[k * micro : (k + 1) * micro]


def mod_join_body(place, p0, p1, p2, p3, bias, mine, other, scratch):
    for k, ref in enumerate((p0, p1, p2, p3)):
        scratch[place[1] ^ k] = ref[...]
    values = jnp.concatenate([scratch[j] for j in range(LINE)], axis=1) + bias[...]
    first = place[0] == 0
    mine[...] = jnp.where(first, values[0:1], values[1:2])
    other[...] = jnp.where(first, values[1:2], values[0:1])


def pack_body(*refs):
    out, pieces = refs[-1], refs[:-1]
    count = len(pieces) // 2
    for row in range(2):
        at = 0
        for ref in pieces[row * count : (row + 1) * count]:
            out[row : row + 1, at : at + ref.shape[1]] = ref[...]
            at += ref.shape[1]


def grads_sum_body(count, place, *refs):
    parts = refs[:count]
    joint0, expand0, joint1, expand1, keep, give = refs[count:]
    first = place[0] == 0
    values = total(parts)
    hidden = expand0.shape[1]
    mod_width = values.shape[1] // 8 * 6
    rounded = values[:, :mod_width].astype(BF16).astype(F32)
    sums = values[:, mod_width:]
    half = hidden // 2

    def natural(ref):
        now = ref[...]
        return jnp.where(first, now, jnp.concatenate([now[:, half:], now[:, :half]], axis=1))

    rows = []
    for row, (joint, expand) in enumerate(((joint0, expand0), (joint1, expand1))):
        rows.append(
            jnp.concatenate(
                [rounded[row : row + 1], joint[...], natural(expand), sums[row : row + 1]], axis=1
            )
        )
    keep[...] = jnp.where(first, rows[0], rows[1])
    give[...] = jnp.where(first, rows[1], rows[0])


def grads_join_body(place, keep, received, out):
    mods = out.shape[1] - keep.shape[1]
    first = place[0] == 0
    own, other = keep[...], received[...]
    out[:, :mods] = jnp.where(first, own, other)[:, :mods].astype(BF16)
    out[:, mods : 2 * mods] = jnp.where(first, other, own)[:, :mods].astype(BF16)
    out[:, 2 * mods :] = (own[:, mods:] + other[:, mods:]).astype(BF16)


def mod_back_body(place, g0, g1, g2, g3, a0, a1, a2, a3, weight, w_grad, b_grad, bias, c0, c1, c2, c3):
    columns = weight.shape[1]
    mods = columns * LINE
    grads = (g0, g1, g2, g3)
    at = pl.multiple_of(place[1] * columns, 128)
    rows = []
    for ref in grads:
        rows.append(ref[:, pl.ds(at, columns)].astype(F32))
        rows.append(ref[:, pl.ds(pl.multiple_of(at + mods, 128), columns)].astype(F32))
    picked = jnp.concatenate(rows, axis=0).astype(BF16)
    activated = jnp.concatenate([a0[...], a1[...], a2[...], a3[...]], axis=0)
    w_grad[...] = t_dot(activated, picked)
    act = dot_t(picked, weight[...])
    for k, out in enumerate((c0, c1, c2, c3)):
        out[...] = act[2 * k : 2 * k + 2]
    b_grad[...] = tree_sum(
        [ref[:, :mods].astype(F32) + ref[:, mods : 2 * mods].astype(F32) for ref in grads]
    )
    bias[...] = tree_sum([ref[:, 2 * mods :].astype(F32) for ref in grads])


def on_device(
    tokens,
    conditions,
    cotangent,
    modulation_weight,
    modulation_bias,
    joint_weight,
    joint_bias,
    output_weight,
    output_bias,
    expand_weight,
    expand_bias,
    shrink_weight,
    shrink_bias,
):
    core = lax.axis_index("pipe")
    first = core == 0
    line = lax.axis_index("dp")
    place = jnp.stack([core, line]).astype(jnp.int32)
    line_size = lax.axis_size("dp")
    count = lax.axis_size("tensor")
    direct = line_size == LINE
    micro, _, own, model = tokens.shape
    width = output_weight.shape[1]
    hidden = expand_weight.shape[2]
    chunk = model // line_size
    rows = own * count
    columns = modulation_weight.shape[2]
    mods = 6 * model
    bias_width = 2 * width + hidden + 2 * model
    own_rows = modulation_weight[0]

    def mine(pair):
        return jnp.where(first, pair[0], pair[1])

    def other(pair):
        return jnp.where(first, pair[1], pair[0])

    def both_layers(kept, received):
        return jnp.where(first, kept, received), jnp.where(first, received, kept)

    def after(value, earlier):
        return lax.optimization_barrier((value, earlier))[0]

    def tie(main, *rest):
        return lax.optimization_barrier((main,) + rest)

    split = 2 * width
    pieces_shape = shape((chunk, split), BF16)
    joint_blocks = jnp.transpose(joint_weight[0], (1, 0, 2))
    expand, shrink_t = expand_weight[0], shrink_weight[0].T
    half = hidden // 2
    halves = (
        jnp.concatenate(
            [joint_blocks[0], joint_blocks[1], expand[:, :half], shrink_t[:, :half]], axis=1
        ),
        jnp.concatenate(
            [joint_blocks[2], output_weight[0].T, expand[:, half:], shrink_t[:, half:]], axis=1
        ),
    )
    keep, give = mine(halves), other(halves)
    line_pieces = run(
        "weight_pieces",
        weight_pieces_body,
        [pieces_shape] * 6,
        [keep, swap(give, "pipe", 1)],
        place,
    )

    bias_pack = jnp.concatenate(
        [
            joint_bias[0].reshape(-1),
            expand_bias[0],
            output_bias[0],
            shrink_bias[0],
        ]
    )[None]
    bias_layers = both_layers(bias_pack, swap(bias_pack, "pipe", 1))
    biases = []
    for packed in bias_layers:
        at = 2 * width
        joint = jnp.concatenate(
            [packed[:, :width], jnp.zeros((1, width), F32), packed[:, width:at]], axis=1
        )
        grown = packed[:, at : at + hidden]
        rolled = jnp.concatenate([grown[:, hidden // 2 :], grown[:, : hidden // 2]], axis=1)
        grown = jnp.where(first, grown, rolled)
        at += hidden
        biases.append((joint, packed[:, at : at + model], grown, packed[:, at + model :]))

    activated = jax.nn.silu(conditions[:, 0].astype(F32)).astype(BF16)
    if direct:
        activated_all = gather(activated, "dp")
    else:
        activated_all = lax.all_gather(activated, "dp", axis=0).reshape(line_size * micro, -1)

    def line_first(value):
        return (value, swap(value, "dp", 2)) if direct else value

    def line_second(pair):
        if not direct:
            return pair, lax.all_gather(pair, "dp", axis=0, tiled=True)
        stacked = jnp.stack(pair)
        return stacked, swap(stacked, "dp", 1)

    def both_cores(*steps):
        pairs, others = [step[0] for step in steps], [step[1] for step in steps]
        if direct:
            wide = sum(pair.shape[2] for pair in pairs)
            lined = run(
                "stack_line", stack_body, [shape((model, wide), BF16)], pairs + others, place
            )[0]
        else:
            lined = jnp.concatenate(others, axis=1)
        return lined, swap(lined, "pipe", 1)

    def piece_of(layer, index):
        return line_pieces[3 * layer + index]

    first_a0 = line_first(after(piece_of(0, 0), activated_all))

    if direct:
        mod_partial = run(
            "mod_first",
            mod_first_body,
            [shape((micro * LINE, columns), F32)],
            activated_all + [own_rows],
        )[0]
        mod_partials, first_a0 = tie(gather(mod_partial, "tensor"), first_a0)
        second_a0 = line_second(first_a0)
        first_e0 = line_first(after(piece_of(0, 1), first_a0))
        pieces = run(
            "mod_sum",
            functools.partial(mod_sum_body, count),
            [shape((micro, columns), F32)] * LINE,
            mod_partials,
        )
        pieces, second_a0 = tie(exchange(pieces, "dp"), second_a0)
        mod_mine, mod_other = pl.pallas_call(
            mod_join_body,
            out_shape=[shape((1, mods), F32)] * 2,
            in_specs=[pl.BlockSpec(memory_space=pltpu.SMEM)]
            + [pl.BlockSpec(memory_space=pltpu.VMEM)] * 5,
            out_specs=[pl.BlockSpec(memory_space=pltpu.VMEM)] * 2,
            scratch_shapes=[pltpu.VMEM((LINE, micro, columns), F32)],
            name="mod_join",
        )(place, *pieces, modulation_bias)
    else:
        mod_partial = dot(activated_all, own_rows)
        mod_partials = gather(mod_partial, "tensor")
        second_a0 = line_second(first_a0)
        first_e0 = line_first(piece_of(0, 1))
        mod_sum = tree_sum(mod_partials).reshape(line_size, micro, -1)
        mod_layer = lax.all_to_all(mod_sum, "dp", split_axis=0, concat_axis=0)
        mod_layer = jnp.swapaxes(mod_layer, 0, 1).reshape(micro, -1) + modulation_bias
        mod_mine, mod_other = mine(mod_layer)[None], other(mod_layer)[None]
    mod0, mod1 = both_layers(mod_mine, swap(mod_other, "pipe", 1))

    w_attn0 = both_cores(second_a0)
    own_f32 = shape((own, model), F32)
    own_bf16 = shape((own, model), BF16)
    blocks = [own_bf16] * count
    wide_bf16 = shape((rows, model), BF16)
    hidden_bf16 = shape((rows, hidden), BF16)
    vector = shape((1, model), F32)
    hidden_vector = shape((1, hidden), F32)
    h0, attn_in, g_y1, g_shrunk1 = run(
        "enter",
        enter_body,
        [own_f32, own_bf16, own_f32, own_bf16],
        [tokens[:, 0], cotangent[:, 0], mod0, mod1],
        place,
    )

    def kernel(name, body, outs, args, where=None):
        return run(name, functools.partial(body, count), outs, args, where)

    def attention(attn_rows, weight, bias):
        outs = kernel(
            "attention",
            attn_body,
            [
                wide_bf16,
                shape((rows, 3 * width), BF16),
                shape((width // HEAD, rows, rows), F32),
                shape((rows, width), BF16),
            ]
            + blocks,
            attn_rows + [weight[0], weight[1], bias],
            place,
        )
        return outs[:4], exchange(outs[4:], "tensor")

    def middle_of(parts, bias, h, mod):
        return kernel(
            "middle", middle_body, [own_f32, own_f32, own_bf16], parts + [bias, h, mod]
        )

    attn_rows, first_e0 = tie(gather(attn_in, "tensor"), first_e0)
    second_e0 = line_second(first_e0)
    first_s0 = line_first(after(piece_of(0, 2), first_e0))
    kept_attn0, parts = attention(attn_rows, w_attn0, biases[0][0])
    parts, second_e0, first_s0 = tie(parts, second_e0, first_s0)
    second_s0 = line_second(first_s0)
    first_a1 = line_first(after(piece_of(1, 0), first_s0))
    attended0, middle0, mlp_in = middle_of(parts, biases[0][1], h0, mod0)
    mlp_rows0, second_s0, first_a1 = tie(gather(mlp_in, "tensor"), second_s0, first_a1)
    w_mlp0 = both_cores(second_e0, second_s0)
    second_a1 = line_second(first_a1)
    first_e1 = line_first(after(piece_of(1, 1), first_a1))
    g_rows1 = gather(after(g_shrunk1, mlp_rows0), "tensor")
    outs = kernel(
        "feed_forward",
        mlp_body,
        [wide_bf16, shape((rows, hidden), F32), hidden_bf16] + blocks,
        mlp_rows0 + [w_mlp0[0], w_mlp0[1], biases[0][2]],
    )
    outs, g_rows1 = tie(outs, g_rows1)
    mlp_rows0, pre0, hidden0 = outs[:3]
    (parts,) = tie(exchange(outs[3:], "tensor"))
    parts, second_a1, first_e1 = tie(parts, second_a1, first_e1)
    w_attn1 = both_cores(second_a1)
    second_e1 = line_second(first_e1)
    first_s1 = line_first(after(piece_of(1, 2), first_e1))
    shrunk0, passed, h1, attn_in = kernel(
        "between",
        between_body,
        [own_f32, own_bf16, own_f32, own_bf16],
        parts + [biases[0][3], middle0, mod0, mod1],
    )

    (attn_rows, w_attn1), second_e1, first_s1 = tie(
        (gather(attn_in, "tensor"), w_attn1), second_e1, first_s1
    )
    second_s1 = line_second(first_s1)
    kept_attn1, parts = attention(attn_rows, w_attn1, biases[1][0])
    parts, second_s1 = tie(parts, second_s1)
    w_mlp1 = both_cores(second_e1, second_s1)
    attended1, middle1, mlp_in = middle_of(parts, biases[1][1], h1, mod1)
    outs = kernel(
        "feed_forward_both",
        mlp_both_body,
        [wide_bf16, wide_bf16, hidden_bf16, hidden_bf16, hidden_vector] + blocks + blocks,
        gather(mlp_in, "tensor") + g_rows1 + [w_mlp1[0], w_mlp1[1], biases[1][2]],
    )
    mlp_rows1, g_rows1, hidden1, g_pre1, expand_grad1 = outs[:5]
    y_partial, g_partial = outs[5 : 5 + count], outs[5 + count :]

    def middle_back(parts, middle, mod, g_y, attended):
        return kernel(
            "middle_back",
            middle_back_body,
            [own_f32, own_bf16] + [vector] * 4,
            parts + [middle, mod, g_y, attended],
        )

    def attention_back(g_rows, weight, kept):
        outs = kernel(
            "attention_back",
            attn_back_body,
            [wide_bf16, shape((rows, 3 * width), BF16), shape((1, 2 * width), F32)] + blocks,
            g_rows + [weight[0], weight[1], kept[1], kept[2]],
            place,
        )
        return outs[:3], exchange(outs[3:], "tensor")

    def chip_sum(grads):
        keep, give = grads
        return (keep + swap(give, "pipe", 1).astype(F32)).astype(BF16)

    def line_sum(whole):
        return lax.psum_scatter(whole, "dp", scatter_dimension=0, tiled=True)

    def line_parts(grads, pieces):
        keep, give = grads
        wide = keep.shape[1] // pieces
        if not direct:
            whole = chip_sum(grads)
            return [[whole[:, k * wide : (k + 1) * wide]] for k in range(pieces)]
        outs = run(
            "line_parts",
            line_parts_body,
            [shape((2, chunk, wide), BF16), shape((chunk, wide), F32), shape((chunk, wide), F32)]
            * pieces,
            [keep, swap(give, "pipe", 1)],
            place,
        )
        return [outs[3 * k : 3 * k + 3] for k in range(pieces)]

    def line_near(parts):
        return swap(parts[0], "dp", 1) if direct else parts[0]

    def line_far(parts, near):
        if not direct:
            return line_sum(near)
        return swap((parts[1] + near[1].astype(F32)).astype(BF16), "dp", 2)

    def line_total(parts, near, far):
        if not direct:
            return far
        return (parts[2] + near[0].astype(F32) + far.astype(F32)).astype(BF16)

    def own_halves(pair):
        return mine(pair), swap(other(pair), "pipe", 1)

    def mlp_weight_grads(mlp_rows, g_pre, g_rows, hidden_rows):
        return run(
            "mlp_weight_grads",
            mlp_weights_body,
            [shape((model, hidden), F32), shape((model, hidden), BF16)],
            [mlp_rows, g_pre, g_rows, hidden_rows],
        )

    def attn_weight_grads(kept, g_joint, g_rows):
        return run(
            "attn_weight_grads",
            attn_weights_body,
            [shape((model, 2 * width), F32), shape((model, 2 * width), BF16)],
            [kept[0], g_joint, g_rows, kept[3]],
            place,
        )

    g_parts, (parts_m1,), y_partial = tie(
        exchange(g_partial, "tensor"),
        line_parts(mlp_weight_grads(mlp_rows1, g_pre1, g_rows1, hidden1), 1),
        y_partial,
    )
    near_m1 = line_near(parts_m1)
    g_middle1, g_attended, g_shift_mlp1, g_scale_mlp1, g_gate_attn1, out_grad1 = middle_back(
        g_parts, middle1, mod1, g_y1, attended1
    )
    y_parts = exchange(y_partial, "tensor")
    g_rows, near_m1 = tie(gather(g_attended, "tensor"), near_m1)
    far_m1 = line_far(parts_m1, near_m1)
    (g_rows, g_joint, joint_grad1), parts = attention_back(g_rows, w_attn1, kept_attn1)
    parts, (parts_a1,), far_m1 = tie(
        parts, line_parts(attn_weight_grads(kept_attn1, g_joint, g_rows), 1), far_m1
    )
    near_a1 = line_near(parts_a1)
    g_passed, g_y0, g_shrunk0, g_shift_attn1, g_scale_attn1, g_gate_mlp0, shrink_grad0 = kernel(
        "between_back",
        between_back_body,
        [own_bf16, own_f32, own_bf16] + [vector] * 4,
        parts + [h1, mod1, mod0, g_middle1, shrunk0],
    )

    g_rows0, near_a1 = tie(gather(g_shrunk0, "tensor"), near_a1)
    outs = kernel(
        "feed_forward_back",
        mlp_back_body,
        [wide_bf16, hidden_bf16, hidden_vector] + blocks,
        g_rows0 + [w_mlp0[0], w_mlp0[1], pre0],
    )
    g_rows0, g_pre0, expand_grad0 = outs[:3]
    parts, (parts_m0,) = tie(
        exchange(outs[3:], "tensor"),
        line_parts(mlp_weight_grads(mlp_rows0, g_pre0, g_rows0, hidden0), 1),
    )
    near_m0 = line_near(parts_m0)
    g_middle0, g_attended, g_shift_mlp0, g_scale_mlp0, g_gate_attn0, out_grad0 = middle_back(
        parts, middle0, mod0, g_y0, attended0
    )
    y1, g_gate_mlp1, shrink_grad1 = kernel(
        "leave",
        leave_body,
        [own_bf16, vector, vector],
        y_parts + [biases[1][3], middle1, mod1, g_y1, g_shrunk1],
    )
    g_rows, near_m0 = tie(gather(g_attended, "tensor"), near_m0)
    far_m0 = line_far(parts_m0, near_m0)
    (g_rows, g_joint, joint_grad0), parts = attention_back(g_rows, w_attn0, kept_attn0)
    parts, far_m0, g_joint, g_rows, near_a1 = tie(parts, far_m0, g_joint, g_rows, near_a1)
    far_a1 = line_far(parts_a1, near_a1)
    (parts_a0,) = line_parts(attn_weight_grads(kept_attn0, g_joint, g_rows), 1)
    g_h0, g_shift_attn0, g_scale_attn0 = kernel(
        "finish_back",
        finish_back_body,
        [own_bf16, vector, vector],
        parts + [h0, mod0, g_middle0],
    )
    def own_layer_of_micros(pair):
        return jnp.stack(both_layers(mine(pair), swap(other(pair), "pipe", 1)))

    layer_outputs = own_layer_of_micros((passed, y1))
    input_grads = own_layer_of_micros((g_h0, g_passed))

    packed = run(
        "pack_grads",
        pack_body,
        [shape((2, mods + 2 * model), F32)],
        [
            g_shift_attn0,
            g_scale_attn0,
            g_gate_attn0,
            g_shift_mlp0,
            g_scale_mlp0,
            g_gate_mlp0,
            out_grad0,
            shrink_grad0,
            g_shift_attn1,
            g_scale_attn1,
            g_gate_attn1,
            g_shift_mlp1,
            g_scale_mlp1,
            g_gate_mlp1,
            out_grad1,
            shrink_grad1,
        ],
    )[0]
    packed_all = gather(packed, "tensor")
    near_a0 = line_near(parts_a0)
    keep, give = run(
        "grads_sum",
        functools.partial(grads_sum_body, count),
        [shape((1, mods + bias_width), F32)] * 2,
        packed_all + [joint_grad0, expand_grad0, joint_grad1, expand_grad1],
        place,
    )
    received = swap(give, "pipe", 1)
    joined = run(
        "grads_join",
        grads_join_body,
        [shape((1, 2 * mods + bias_width), BF16)],
        [keep, received],
        place,
    )[0]
    joined_all = gather(joined, "dp") if direct else lax.all_gather(joined, "dp", axis=0, tiled=True)
    joined_all, near_a0, far_a1 = tie(joined_all, near_a0, far_a1)
    far_a0 = line_far(parts_a0, near_a0)
    mlp_grad0 = line_total(parts_m0, near_m0, far_m0)
    mlp_grad1 = line_total(parts_m1, near_m1, far_m1)
    attn_grad0 = line_total(parts_a0, near_a0, far_a0)
    attn_grad1 = line_total(parts_a1, near_a1, far_a1)
    expand_w_grad, shrink_t_grad = run(
        "final_mlp",
        final_mlp_body,
        [shape((chunk, hidden), F32)] * 2,
        own_halves((mlp_grad0, mlp_grad1)),
        place,
    )
    joint_w_grad, output_w_grad = run(
        "final_attn",
        final_attn_body,
        [shape((3, chunk, width), F32), shape((width, chunk), F32)],
        own_halves((attn_grad0, attn_grad1)),
        place,
    )

    if direct:
        outs = run(
            "mod_back",
            mod_back_body,
            [shape(own_rows.shape, F32), shape((1, mods), F32), shape((1, bias_width), F32)]
            + [shape((micro, own_rows.shape[0]), F32)] * LINE,
            joined_all + activated_all + [own_rows],
            place,
        )
        ada_grad, ada_bias_grad, bias_sum = outs[:3]
        act_parts, joint_w_grad, output_w_grad = tie(
            exchange(outs[3:], "dp"), joint_w_grad, output_w_grad
        )
        act_grad = tree_sum(act_parts)
    else:
        mod_grads = joined_all[:, : 2 * mods].reshape(line_size * micro, mods)
        bias_sum = jnp.sum(joined_all[:, 2 * mods :].astype(F32), axis=0, keepdims=True)
        ada_bias_grad = jnp.sum(mod_grads.astype(F32), axis=0, keepdims=True)
        picked = lax.dynamic_slice_in_dim(mod_grads, line * columns, columns, 1).astype(BF16)
        ada_grad = t_dot(activated_all, picked)
        act_partial = dot_t(picked, own_rows).reshape(line_size, micro, -1)
        act_grad = lax.psum_scatter(act_partial, "dp", scatter_dimension=0, tiled=False)
    _, silu_back = jax.vjp(jax.nn.silu, conditions[:, 0].astype(F32))
    cond_grad = silu_back(act_grad)[0]
    at = 2 * width
    return (
        layer_outputs[None, :, None],
        input_grads[None, :, None],
        cond_grad[None, :, None],
        ada_grad[None],
        ada_bias_grad,
        jnp.transpose(joint_w_grad, (1, 0, 2))[None],
        bias_sum[:, :at].reshape(1, 2, width),
        output_w_grad[None],
        bias_sum[:, at + hidden : at + hidden + model],
        expand_w_grad[None],
        bias_sum[:, at : at + hidden],
        shrink_t_grad.T[None],
        bias_sum[:, at + hidden + model :],
    )


def solution(mesh):
    in_specs = (
        P(None, "dp", "tensor", None),
        P(None, "dp", "tensor"),
        P(None, "dp", "tensor", None),
        P("pipe", "tensor", "dp"),
        P("pipe", None),
        P("pipe", "dp", None, "tensor"),
        P("pipe", None, "tensor"),
        P("pipe", "tensor", "dp"),
        P("pipe", None),
        P("pipe", "dp", "tensor"),
        P("pipe", "tensor"),
        P("pipe", "tensor", "dp"),
        P("pipe", None),
    )
    out_specs = (
        P("pipe", None, "dp", "tensor", None),
        P("pipe", None, "dp", "tensor", None),
        P("pipe", None, "dp", "tensor"),
        P("pipe", "tensor", "dp"),
        P("pipe", None),
        P("pipe", "dp", None, "tensor"),
        P("pipe", None, "tensor"),
        P("pipe", "tensor", "dp"),
        P("pipe", None),
        P("pipe", "dp", "tensor"),
        P("pipe", "tensor"),
        P("pipe", "tensor", "dp"),
        P("pipe", None),
    )
    return jax.shard_map(
        on_device, mesh=mesh, in_specs=in_specs, out_specs=out_specs, check_vma=False
    )
```
